32 devices in a mesh: ctx: 8 (over z, y), fsdp: 4 (over x, core).
Axes of the slice: x: 2, y: 2, z: 4, core: 2. Of those that a mesh axis runs over, the one named last changes fastest.
Arguments:
- tokens: bfloat16 [4, 16, 128, 1024], P('fsdp', None, 'ctx'), may hold values from -6 to 6
- lengths: int32 [4, 3], P('fsdp'), may hold values from 512 to 1024, as said below
- packing: int32 [4, 3], P('fsdp'), may hold values from 0 to 2, each once within a row
- query_w: bfloat16 [1024, 1024], P('fsdp'), may hold values from -0.1875 to 0.1875
- query_b: float32 [1024], replicated, may hold values from -3 to 3
- key_w: bfloat16 [1024, 1024], P('fsdp'), may hold values from -0.1875 to 0.1875
- value_w: bfloat16 [1024, 1024], P('fsdp'), may hold values from -0.1875 to 0.1875
- value_b: float32 [1024], replicated, may hold values from -3 to 3
- output_w: bfloat16 [1024, 1024], P('fsdp'), may hold values from -3 to 3
- output_b: float32 [1024], replicated, may hold values from -3 to 3
- attn_gain: float32 [1024], replicated, may hold values from 0.5 to 1.5
- attn_shift: float32 [1024], replicated, may hold values from -2 to 2
- expand_w: bfloat16 [1024, 4096], P('fsdp'), may hold values from -0.1875 to 0.1875
- expand_b: float32 [4096], replicated, may hold values from -3 to 3
- reduce_w: bfloat16 [4096, 1024], P('fsdp'), may hold values from -0.09375 to 0.09375
- reduce_b: float32 [1024], replicated, may hold values from -3 to 3
- ffn_gain: float32 [1024], replicated, may hold values from 0.5 to 1.5
- ffn_shift: float32 [1024], replicated, may hold values from -2 to 2
- cotangent: bfloat16 [4, 16, 128, 1024], P('fsdp', None, 'ctx'), may hold values from -6 to 6
Outputs:
- layer_out: bfloat16 [4, 16, 128, 1024], P('fsdp', None, 'ctx')
- grad_tokens: float32 [4, 16, 128, 1024], P('fsdp', None, 'ctx')
- grad_query_w: float32 [1024, 1024], P('fsdp')
- grad_query_b: float32 [1024], replicated
- grad_key_w: float32 [1024, 1024], P('fsdp')
- grad_value_w: float32 [1024, 1024], P('fsdp')
- grad_value_b: float32 [1024], replicated
- grad_output_w: float32 [1024, 1024], P('fsdp')
- grad_output_b: float32 [1024], replicated
- grad_attn_gain: float32 [1024], replicated
- grad_attn_shift: float32 [1024], replicated
- grad_expand_w: float32 [1024, 4096], P('fsdp')
- grad_expand_b: float32 [4096], replicated
- grad_reduce_w: float32 [4096, 1024], P('fsdp')
- grad_reduce_b: float32 [1024], replicated
- grad_ffn_gain: float32 [1024], replicated
- grad_ffn_shift: float32 [1024], replicated
The draws below stay inside these ranges and needn't reach their ends.
Inputs may be any that keep to these rules, and one draw needn't show every extreme that they name: Each row's 3 lengths sum to 2048. Each row of packing names every sequence once.
All inputs are finite; a program needn't handle non-finite values.
Results may differ from the reference program's by a relative error of at most 0.02.
Values may be sent and summed in bfloat16 or wider, within the bound.
A program may use at most 192 MiB of HBM per device.

```python
import math
from functools import partial
import jax
import jax.numpy as jnp
from jax import lax

D = 1024
H = 16
HD = 64
FF = 4096
NSEQ = 3
LAPS = 16
SPAN = 128
ROW_LEN = 2048
ROWS = 4
MIN_LEN = 512


def draw_lengths(key, part):
    key = jax.random.fold_in(key, 7)
    spare_len = ROW_LEN - NSEQ * MIN_LEN
    cut_point = jax.random.randint(key, (ROWS, 1), 0, spare_len + 1).astype(jnp.int32)
    first_row = (jnp.arange(ROWS, dtype=jnp.int32) == 0)[:, None]
    cut_point = jnp.where(first_row, 0, cut_point).astype(jnp.int32)
    least = jnp.full((ROWS, 1), MIN_LEN, jnp.int32)
    return jnp.concatenate([least, MIN_LEN + cut_point, MIN_LEN + spare_len - cut_point], axis=-1).astype(jnp.int32)


def level_of(key, dims, shards, smallest, high):
    factor_of, own = 1.0, jax.random.fold_in(key, 6)
    for dim, blocks in shards:
        draws = jnp.exp(jax.random.uniform(jax.random.fold_in(own, dim), (blocks,), jnp.float32, smallest / len(shards), high / len(shards)))
        factor_of = factor_of * jnp.repeat(draws, dims[dim] // blocks).reshape([-1 if axis == dim else 1 for axis in range(len(dims))])
    return factor_of


def gaussian(own_key, dims, scale, most, split=(), kind=jnp.bfloat16):
    loudness = level_of(own_key, dims, split, -0.22, 0.18) if split else 1.0
    values = jax.random.normal(own_key, dims, jnp.float32) * scale * loudness
    return jnp.minimum(jnp.maximum(values, -most), most).astype(kind)


def setup_inputs(seed: int = 0) -> dict:
    splits = jax.random.split(jax.random.key(seed), 20)
    tokens = gaussian(splits[0], (ROWS, LAPS, SPAN, D), 1.0, 6.0, ((0, 4), (2, 8)))
    lengths = draw_lengths(jax.random.fold_in(splits[19], 71), 0)
    packing = jax.vmap(lambda own: jax.random.permutation(own, NSEQ))(jax.random.split(splits[2], ROWS)).reshape((ROWS, NSEQ)).astype(jnp.int32)
    query_w = gaussian(splits[3], (D, D), D ** -0.5, 0.1875, ((0, 4),))
    query_b = gaussian(splits[4], (D,), 0.5, 3.0, (), jnp.float32)
    key_w = gaussian(splits[5], (D, D), D ** -0.5, 0.1875, ((0, 4),))
    value_w = gaussian(splits[6], (D, D), D ** -0.5, 0.1875, ((0, 4),))
    value_b = gaussian(splits[7], (D,), 0.5, 3.0, (), jnp.float32)
    output_w = gaussian(splits[8], (D, D), (max(1, D // 256)) ** -0.5, 3.0, ((0, 4),))
    output_b = gaussian(splits[9], (D,), 0.5, 3.0, (), jnp.float32)
    attn_gain = jnp.clip(1.0 + 0.1 * jax.random.normal(splits[10], (D,), jnp.float32), 0.5, 1.5)
    attn_shift = gaussian(splits[11], (D,), 0.3, 2.0, (), jnp.float32)
    expand_w = gaussian(splits[12], (D, FF), D ** -0.5, 0.1875, ((0, 4),))
    expand_b = gaussian(splits[13], (FF,), 0.5, 3.0, (), jnp.float32)
    reduce_w = gaussian(splits[14], (FF, D), FF ** -0.5, 0.09375, ((0, 4),))
    reduce_b = gaussian(splits[15], (D,), 0.5, 3.0, (), jnp.float32)
    ffn_gain = jnp.clip(1.0 + 0.1 * jax.random.normal(splits[16], (D,), jnp.float32), 0.5, 1.5)
    ffn_shift = gaussian(splits[17], (D,), 0.3, 2.0, (), jnp.float32)
    cotangent = gaussian(splits[18], (ROWS, LAPS, SPAN, D), 1.0, 6.0, ((0, 4), (2, 8)))
    return {"tokens": tokens, "lengths": lengths, "packing": packing, "query_w": query_w, "query_b": query_b, "key_w": key_w, "value_w": value_w, "value_b": value_b, "output_w": output_w, "output_b": output_b, "attn_gain": attn_gain, "attn_shift": attn_shift, "expand_w": expand_w, "expand_b": expand_b, "reduce_w": reduce_w, "reduce_b": reduce_b, "ffn_gain": ffn_gain, "ffn_shift": ffn_shift, "cotangent": cotangent}


HIGH = lax.Precision.HIGHEST

@jax.custom_vjp
def low(v):
    return lax.optimization_barrier(v.astype(jnp.bfloat16)).astype(jnp.float32)

@jax.custom_vjp
def low_back(v):
    return v

def low_keep(v):
    return (low(v), None)

def low_pass(kept, grad):
    return (grad,)

def back_keep(v):
    return (v, None)

def back_low(kept, grad):
    return (low(grad),)
low.defvjp(low_keep, low_pass)
low_back.defvjp(back_keep, back_low)

def matmul32(left, right):
    return jnp.dot(left, right, precision=HIGH, preferred_element_type=jnp.float32)

def layer_norm(hidden, gain, shift):
    mean_row = lax.optimization_barrier(jnp.mean(hidden, axis=-1, keepdims=True))
    centred = hidden - mean_row
    variance = lax.optimization_barrier(jnp.mean(centred * centred, axis=-1, keepdims=True))
    return centred * lax.rsqrt(variance + 1e-05) * gain + shift

def attend_block(query_block, seg_block, key_rows, value_rows, seg_row):
    scores = 0.125 * jnp.einsum('qhd,khd->hqk', query_block, key_rows, precision=HIGH)
    scores = low_back(scores)
    same_seg = (seg_block[:, None] == seg_row[None, :])[None]
    masked = jnp.where(same_seg, scores, -1e+30)
    row_max = lax.optimization_barrier(jnp.max(masked, axis=-1, keepdims=True))
    exp_scores = jnp.exp(masked - row_max)
    probs = low(exp_scores / lax.optimization_barrier(jnp.sum(exp_scores, axis=-1, keepdims=True)))
    return jnp.einsum('hqk,khd->qhd', probs, value_rows, precision=HIGH)

def attend_row(query_row, key_rows, value_rows, seg_row):
    q_block = math.gcd(ROW_LEN, 512)
    blocks = query_row.reshape(ROW_LEN // q_block, q_block, H, HD)
    seg_blocks = seg_row.reshape(ROW_LEN // q_block, q_block)
    block_fn = jax.checkpoint(lambda pair: attend_block(pair[0], pair[1], key_rows, value_rows, seg_row))
    return lax.map(block_fn, (blocks, seg_blocks)).reshape(ROW_LEN, H, HD)

def forward(segments, tokens_f, query_w, query_b, key_w, value_w, value_b, output_w, output_b, attn_gain, attn_shift, expand_w, expand_b, reduce_w, reduce_b, ffn_gain, ffn_shift):
    flat = tokens_f.reshape(ROWS * ROW_LEN, D)
    queries = low(low_back(matmul32(flat, query_w) + query_b))
    key_rows = low(low_back(matmul32(flat, key_w)))
    value_rows = low(low_back(matmul32(flat, value_w) + value_b))

    def shaped(array):
        return array.reshape(ROWS, ROW_LEN, H, HD)
    attended = lax.map(lambda item: attend_row(item[0], item[1], item[2], item[3]), (shaped(queries), shaped(key_rows), shaped(value_rows), segments))
    attended = low(low_back(attended.reshape(ROWS * ROW_LEN, D)))
    branch = low_back(matmul32(attended, output_w) + output_b)
    normed = layer_norm(flat + branch, attn_gain, attn_shift)
    pre_act = low_back(matmul32(low(normed), expand_w) + expand_b)
    hidden = low(jax.nn.gelu(pre_act, approximate=False))
    ffn_out = low_back(matmul32(hidden, reduce_w) + reduce_b)
    return layer_norm(normed + ffn_out, ffn_gain, ffn_shift).reshape(tokens_f.shape)

def reference(tokens, lengths, packing, query_w, query_b, key_w, value_w, value_b, output_w, output_b, attn_gain, attn_shift, expand_w, expand_b, reduce_w, reduce_b, ffn_gain, ffn_shift, cotangent):
    ordered = jnp.take_along_axis(lengths, packing, axis=1)
    slot_ends = jnp.cumsum(ordered, axis=1)
    position = jnp.arange(ROW_LEN, dtype=jnp.int32)
    segments = lax.optimization_barrier(jnp.sum((position[None, :, None] >= slot_ends[:, None, :]).astype(jnp.int32), axis=2))
    params = [param.astype(jnp.float32) for param in (query_w, query_b, key_w, value_w, value_b, output_w, output_b, attn_gain, attn_shift, expand_w, expand_b, reduce_w, reduce_b, ffn_gain, ffn_shift)]
    tokens_f = tokens.astype(jnp.float32).reshape(ROWS, ROW_LEN, D)
    result, pullback = jax.vjp(partial(forward, segments), tokens_f, *params)
    grads = pullback(cotangent.astype(jnp.float32).reshape(ROWS, ROW_LEN, D))
    return (result.reshape(tokens.shape).astype(jnp.bfloat16), grads[0].reshape(tokens.shape), grads[1], grads[2], grads[3], grads[4], grads[5], grads[6], grads[7], grads[8], grads[9], grads[10], grads[11], grads[12], grads[13], grads[14], grads[15])
```

```python
import jax
import jax.numpy as jnp
from jax import lax
from jax.sharding import PartitionSpec as P

H = 16
HD = 64


def from_behind(block, axis, distance):
    devices = range(lax.axis_size(axis))
    route = [((i - distance) % len(devices), i) for i in devices]
    return lax.ppermute(block, axis, route)


def dense(left, right):
    return jnp.dot(left, right, preferred_element_type=jnp.float32)


def dense_back(left, right):
    return lax.dot_general(
        left, right, (((1,), (1,)), ((), ())), preferred_element_type=jnp.float32
    )


def norm_fwd(hidden, gain, shift):
    mean_row = jnp.mean(hidden, axis=-1, keepdims=True)
    centred = hidden - mean_row
    variance = jnp.mean(centred * centred, axis=-1, keepdims=True)
    inv_std = lax.rsqrt(variance + 1e-05)
    x_hat = centred * inv_std
    return (x_hat * gain + shift, x_hat, inv_std)


def norm_back(incoming, x_hat, inv_std, gain):
    scaled = incoming * gain
    grad_in = inv_std * (
        scaled
        - jnp.mean(scaled, axis=-1, keepdims=True)
        - x_hat * jnp.mean(scaled * x_hat, axis=-1, keepdims=True)
    )
    return (grad_in, jnp.sum(incoming * x_hat, axis=0), jnp.sum(incoming, axis=0))


def gelu_slope(pre_act):
    return (
        0.5 * (1.0 + lax.erf(pre_act * 0.7071067811865476))
        + pre_act * jnp.exp(-0.5 * pre_act * pre_act) * 0.3989422804014327
    )


def online_update(running, query_heads, query_seg, key_rows, value_rows, key_seg):
    accum, run_max, run_sum = running
    rows_here = key_rows.shape[0]
    scores = 0.125 * jnp.einsum(
        "qhd,khd->hqk",
        query_heads,
        key_rows.reshape(rows_here, H, HD),
        preferred_element_type=jnp.float32,
    )
    same_seg = (query_seg[:, None] == key_seg[None, :])[None]
    masked = jnp.where(same_seg, scores, -1e30)
    new_max = jnp.maximum(run_max, jnp.max(masked, axis=-1))
    scale_old = jnp.exp(run_max - new_max)
    exp_scores = jnp.where(same_seg, jnp.exp(masked - new_max[:, :, None]), 0.0)
    run_sum = run_sum * scale_old + jnp.sum(exp_scores, axis=-1)
    update = jnp.einsum(
        "hqk,khd->qhd",
        exp_scores.astype(jnp.bfloat16),
        value_rows.reshape(rows_here, H, HD),
        preferred_element_type=jnp.float32,
    )
    accum = accum * scale_old.T[:, :, None] + update
    return (accum, new_max, run_sum)


def pair_grads(query_rows, grad_rows, log_sum, delta_row, query_seg, key_rows, value_rows, key_seg):
    q_heads = query_rows.reshape(-1, H, HD)
    g_heads = grad_rows.reshape(-1, H, HD)
    k_heads = key_rows.reshape(-1, H, HD)
    v_heads = value_rows.reshape(-1, H, HD)
    scores = 0.125 * jnp.einsum(
        "qhd,khd->hqk", q_heads, k_heads, preferred_element_type=jnp.float32
    )
    same_seg = (query_seg[:, None] == key_seg[None, :])[None]
    probs = jnp.where(
        same_seg, jnp.exp(jnp.where(same_seg, scores, -1e30) - log_sum[:, :, None]), 0.0
    )
    grad_prob = jnp.einsum("qhd,khd->hqk", g_heads, v_heads, preferred_element_type=jnp.float32)
    grad_score = (probs * (grad_prob - delta_row[:, :, None])).astype(jnp.bfloat16)
    grad_q = 0.125 * jnp.einsum(
        "hqk,khd->qhd", grad_score, k_heads, preferred_element_type=jnp.float32
    )
    grad_k = 0.125 * jnp.einsum(
        "hqk,qhd->khd", grad_score, q_heads, preferred_element_type=jnp.float32
    )
    grad_v = jnp.einsum(
        "hqk,qhd->khd", probs.astype(jnp.bfloat16), g_heads, preferred_element_type=jnp.float32
    )
    return (
        grad_q.reshape(query_rows.shape),
        grad_k.reshape(key_rows.shape),
        grad_v.reshape(key_rows.shape),
    )


def owner_rows(layer_in, layer_grad):
    return lax.psum_scatter(
        lax.dot_general(
            layer_in, layer_grad, (((0,), (0,)), ((), ())), preferred_element_type=jnp.float32
        ).astype(jnp.bfloat16),
        "fsdp",
        scatter_dimension=0,
        tiled=True,
    ).astype(jnp.float32)


def body(
    tokens,
    lengths,
    packing,
    query_w,
    query_b,
    key_w,
    value_w,
    value_b,
    output_w,
    output_b,
    attn_gain,
    attn_shift,
    expand_w,
    expand_b,
    reduce_w,
    reduce_b,
    ffn_gain,
    ffn_shift,
    cotangent,
):
    tok_shape = tokens.shape
    stripe = tok_shape[2]
    block_len = tok_shape[1] * tok_shape[2]
    model_width = tok_shape[3]
    n_ctx = lax.axis_size("ctx")
    ctx_index = lax.axis_index("ctx")
    seq_lens = lengths[0]
    slot_ids = packing[0]
    ordered = jnp.sum(
        jnp.where(
            slot_ids[:, None] == jnp.arange(seq_lens.shape[0], dtype=jnp.int32)[None, :],
            seq_lens[None, :],
            0,
        ),
        axis=1,
    )
    slots = jnp.arange(seq_lens.shape[0], dtype=jnp.int32)
    slot_ends = jnp.sum(jnp.where(slots[None, :] <= slots[:, None], ordered[None, :], 0), axis=1)
    gathered = jnp.arange(n_ctx * block_len, dtype=jnp.int32)
    owner_dev = gathered // block_len
    local_row = gathered % block_len
    position = local_row // stripe * (stripe * n_ctx) + owner_dev * stripe + local_row % stripe
    seg_all = jnp.sum((position[:, None] >= slot_ends[None, :]).astype(jnp.int32), axis=1)
    query_seg = lax.dynamic_slice_in_dim(seg_all, ctx_index * block_len, block_len)
    inputs = tokens.reshape(block_len, model_width)
    w_query, w_key, w_value, w_output, w_up, w_down = (
        lax.all_gather(query_w, "fsdp", axis=0, tiled=True),
        lax.all_gather(key_w, "fsdp", axis=0, tiled=True),
        lax.all_gather(value_w, "fsdp", axis=0, tiled=True),
        lax.all_gather(output_w, "fsdp", axis=0, tiled=True),
        lax.all_gather(expand_w, "fsdp", axis=0, tiled=True),
        lax.all_gather(reduce_w, "fsdp", axis=0, tiled=True),
    )
    queries = (dense(inputs, w_query) + query_b).astype(jnp.bfloat16)
    key_rows = dense(inputs, w_key).astype(jnp.bfloat16)
    values = (dense(inputs, w_value) + value_b).astype(jnp.bfloat16)
    query_heads = queries.reshape(block_len, H, HD)
    start_state = (
        jnp.zeros((block_len, H, HD), jnp.float32),
        jnp.full((H, block_len), -1e30, jnp.float32),
        jnp.zeros((H, block_len), jnp.float32),
    )
    key_piece = lax.all_gather(key_rows, "ctx", axis=0, tiled=True)
    value_piece = lax.all_gather(values, "ctx", axis=0, tiled=True)
    shards = key_piece.shape[0] // block_len

    def one_shard(index, inner):
        key_part = lax.dynamic_slice_in_dim(key_piece, index * block_len, block_len)
        value_part = lax.dynamic_slice_in_dim(value_piece, index * block_len, block_len)
        key_seg = lax.dynamic_slice_in_dim(seg_all, index * block_len, block_len)
        return online_update(inner, query_heads, query_seg, key_part, value_part, key_seg)

    accum, run_max, run_sum = lax.fori_loop(0, shards, one_shard, start_state)
    attended = (accum / run_sum.T[:, :, None]).reshape(block_len, model_width).astype(jnp.bfloat16)
    log_sum = run_max + jnp.log(run_sum)
    branch = dense(attended, w_output) + output_b
    normed, x_hat1, inv_std1 = norm_fwd(inputs.astype(jnp.float32) + branch, attn_gain, attn_shift)
    normed_low = normed.astype(jnp.bfloat16)
    pre_act = dense(normed_low, w_up) + expand_b
    hidden = jax.nn.gelu(pre_act, approximate=False).astype(jnp.bfloat16)
    ffn_out = dense(hidden, w_down) + reduce_b
    outputs, x_hat2, inv_std2 = norm_fwd(normed + ffn_out, ffn_gain, ffn_shift)
    layer_out = outputs.astype(jnp.bfloat16).reshape(tok_shape)
    upstream = cotangent.reshape(block_len, model_width).astype(jnp.float32)
    grad_mid2, grad_ffn_gain, grad_ffn_shift = norm_back(upstream, x_hat2, inv_std2, ffn_gain)
    grad_ffn = grad_mid2.astype(jnp.bfloat16)
    grad_reduce_b = jnp.sum(grad_ffn.astype(jnp.float32), axis=0)
    share_down = owner_rows(hidden, grad_ffn)
    grad_pre = (dense_back(grad_ffn, w_down) * gelu_slope(pre_act)).astype(jnp.bfloat16)
    grad_expand_b = jnp.sum(grad_pre.astype(jnp.float32), axis=0)
    share_up = owner_rows(normed_low, grad_pre)
    grad_normed = dense_back(grad_pre, w_up) + grad_mid2
    grad_mid1, grad_attn_gain, grad_attn_shift = norm_back(grad_normed, x_hat1, inv_std1, attn_gain)
    grad_branch = grad_mid1.astype(jnp.bfloat16)
    grad_output_b = jnp.sum(grad_branch.astype(jnp.float32), axis=0)
    share_out = owner_rows(attended, grad_branch)
    grad_att = dense_back(grad_branch, w_output).astype(jnp.bfloat16)
    delta_row = jnp.einsum(
        "qhd,qhd->hq",
        grad_att.astype(jnp.float32).reshape(block_len, H, HD),
        attended.astype(jnp.float32).reshape(block_len, H, HD),
    )
    zero_rows = jnp.zeros((block_len, model_width), jnp.float32)

    def key_step(step, state):
        visit_keys, visit_values, sum_k, sum_v, sum_q = state
        anchor = (ctx_index - step) % n_ctx
        key_seg = lax.dynamic_slice_in_dim(seg_all, anchor * block_len, block_len)
        part_q, part_k, part_v = pair_grads(
            queries, grad_att, log_sum, delta_row, query_seg, visit_keys, visit_values, key_seg
        )
        sum_q = sum_q + part_q
        visit_keys, visit_values = from_behind((visit_keys, visit_values), "ctx", 1)
        sum_k, sum_v = (
            from_behind((sum_k + part_k).astype(jnp.bfloat16), "ctx", 1).astype(jnp.float32),
            from_behind((sum_v + part_v).astype(jnp.bfloat16), "ctx", 1).astype(jnp.float32),
        )
        return (visit_keys, visit_values, sum_k, sum_v, sum_q)

    final = lax.fori_loop(0, n_ctx, key_step, (key_rows, values, zero_rows, zero_rows, zero_rows))
    sum_k, sum_v, sum_q = (final[2], final[3], final[4])
    grad_q = sum_q.astype(jnp.bfloat16)
    grad_k = sum_k.astype(jnp.bfloat16)
    grad_v = sum_v.astype(jnp.bfloat16)
    grad_query_b = jnp.sum(grad_q.astype(jnp.float32), axis=0)
    grad_value_b = jnp.sum(grad_v.astype(jnp.float32), axis=0)
    share_query = owner_rows(inputs, grad_q)
    share_key = owner_rows(inputs, grad_k)
    share_value = owner_rows(inputs, grad_v)
    grad_inputs = (
        dense_back(grad_q, w_query)
        + dense_back(grad_k, w_key)
        + dense_back(grad_v, w_value)
        + grad_mid1
    )
    share_query, share_key, share_value, share_out, share_up, share_down = lax.psum(
        (share_query, share_key, share_value, share_out, share_up, share_down), "ctx"
    )
    (
        grad_query_b,
        grad_value_b,
        grad_output_b,
        grad_attn_gain,
        grad_attn_shift,
        grad_expand_b,
        grad_reduce_b,
        grad_ffn_gain,
        grad_ffn_shift,
    ) = lax.psum(
        (
            grad_query_b,
            grad_value_b,
            grad_output_b,
            grad_attn_gain,
            grad_attn_shift,
            grad_expand_b,
            grad_reduce_b,
            grad_ffn_gain,
            grad_ffn_shift,
        ),
        ("ctx", "fsdp"),
    )
    return (
        layer_out,
        grad_inputs.reshape(tok_shape),
        share_query,
        grad_query_b,
        share_key,
        share_value,
        grad_value_b,
        share_out,
        grad_output_b,
        grad_attn_gain,
        grad_attn_shift,
        share_up,
        grad_expand_b,
        share_down,
        grad_reduce_b,
        grad_ffn_gain,
        grad_ffn_shift,
    )


def solution(mesh):
    return jax.shard_map(
        body,
        mesh=mesh,
        in_specs=(
            P("fsdp", None, "ctx", None),
            P("fsdp", None),
            P("fsdp", None),
            P("fsdp", None),
            P(),
            P("fsdp", None),
            P("fsdp", None),
            P(),
            P("fsdp", None),
            P(),
            P(),
            P(),
            P("fsdp", None),
            P(),
            P("fsdp", None),
            P(),
            P(),
            P(),
            P("fsdp", None, "ctx", None),
        ),
        out_specs=(
            P("fsdp", None, "ctx", None),
            P("fsdp", None, "ctx", None),
            P("fsdp", None),
            P(),
            P("fsdp", None),
            P("fsdp", None),
            P(),
            P("fsdp", None),
            P(),
            P(),
            P(),
            P("fsdp", None),
            P(),
            P("fsdp", None),
            P(),
            P(),
            P(),
        ),
        check_vma=False,
    )
```

```python
import functools
import jax
import jax.numpy as jnp
from jax import lax
from jax.experimental import pallas as pl
from jax.experimental.pallas import tpu as pltpu
from jax.sharding import PartitionSpec as P

H = 16
HD = 64
PAIR = 2 * HD
GROUP = 8
SWAP = (0, 2, 1, 3)
BF = jnp.bfloat16
F32 = jnp.float32


def dense(left, right):
    return jnp.dot(left, right, preferred_element_type=F32)


def dense_back(left, right):
    return lax.dot_general(left, right, (((1,), (1,)), ((), ())), preferred_element_type=F32)


def dense_in(left, right):
    return lax.dot_general(left, right, (((0,), (0,)), ((), ())), preferred_element_type=F32)


def norm_fwd(hidden, gain, shift):
    mean_row = jnp.mean(hidden, axis=-1, keepdims=True)
    centred = hidden - mean_row
    variance = jnp.mean(centred * centred, axis=-1, keepdims=True)
    inv_std = lax.rsqrt(variance + 1e-05)
    x_hat = centred * inv_std
    return (x_hat * gain + shift, x_hat, inv_std)


def norm_back(incoming, x_hat, inv_std, gain):
    scaled = incoming * gain
    grad_in = inv_std * (
        scaled
        - jnp.mean(scaled, axis=-1, keepdims=True)
        - x_hat * jnp.mean(scaled * x_hat, axis=-1, keepdims=True)
    )
    return (grad_in, jnp.sum(incoming * x_hat, axis=0), jnp.sum(incoming, axis=0))


def gelu_slope(pre_act):
    return (
        0.5 * (1.0 + lax.erf(pre_act * 0.7071067811865476))
        + pre_act * jnp.exp(-0.5 * pre_act * pre_act) * 0.3989422804014327
    )


def first_half(shape):
    return lax.broadcasted_iota(jnp.int32, shape, 1) < HD


def both_heads(block):
    left = first_half(block.shape)
    zero = jnp.zeros_like(block)
    return jnp.concatenate([jnp.where(left, block, zero), jnp.where(left, zero, block)], axis=0)


def by_head(stacked):
    rows = stacked.shape[0] // 2
    left = first_half((rows, stacked.shape[1]))
    return jnp.where(left, stacked[:rows], stacked[rows:])


def attend_kernel(bq, bk, chunks, lo_ref, hi_ref, q_ref, k_ref, v_ref, sq_ref, sk_ref, o_ref, lse_ref):
    nq = q_ref.shape[0] // bq
    per_chunk = k_ref.shape[0] // chunks // bk

    def q_step(i, carry):
        rows = pl.ds(pl.multiple_of(i * bq, bq), bq)
        q2 = both_heads(q_ref[rows, :] * BF(0.125))
        seg = sq_ref[rows, :]
        seg2 = jnp.concatenate([seg, seg], axis=0)

        def k_step(j, state):
            accum, run_max, run_sum = state
            keys = pl.ds(pl.multiple_of(j * bk, bk), bk)
            scores = dense_back(q2, k_ref[keys, :])
            same = seg2 == sk_ref[:, keys]
            scores = jnp.where(same, scores, -1e30)
            new_max = jnp.maximum(run_max, jnp.max(scores, axis=1, keepdims=True))
            probs = jnp.where(same, jnp.exp(scores - new_max), 0.0)
            scale = jnp.exp(run_max - new_max)
            run_sum = run_sum * scale + jnp.sum(probs, axis=1, keepdims=True)
            accum = accum * scale + dense(probs.astype(BF), v_ref[keys, :])
            return accum, new_max, run_sum

        state = (
            jnp.zeros((2 * bq, PAIR), F32),
            jnp.full((2 * bq, 1), -1e30, F32),
            jnp.zeros((2 * bq, 1), F32),
        )
        for s in range(chunks):
            base = s * per_chunk
            state = lax.fori_loop(base + lo_ref[i, s], base + hi_ref[i, s], k_step, state)
        accum, run_max, run_sum = state
        o_ref[rows, :] = by_head(accum / run_sum).astype(BF)
        lse_ref[pl.ds(pl.multiple_of(2 * i * bq, 2 * bq), 2 * bq), :] = run_max + jnp.log(run_sum)
        return carry

    lax.fori_loop(0, nq, q_step, 0)


def attend_back_kernel(
    bq, bk, chunks, lo_ref, hi_ref, q_ref, k_ref, v_ref, sq_ref, sk_ref, o_ref, lse_ref, g_ref,
    dq_ref, dk_ref, dv_ref, dk_sum, dv_sum,
):
    nq = q_ref.shape[0] // bq
    per_chunk = k_ref.shape[0] // chunks // bk
    dk_sum[...] = jnp.zeros_like(dk_sum)
    dv_sum[...] = jnp.zeros_like(dv_sum)

    def q_step(i, carry):
        rows = pl.ds(pl.multiple_of(i * bq, bq), bq)
        q2 = both_heads(q_ref[rows, :] * BF(0.125))
        grad = g_ref[rows, :]
        g2 = both_heads(grad)
        prod = grad.astype(F32) * o_ref[rows, :].astype(F32)
        left = first_half(prod.shape)
        delta = jnp.concatenate(
            [
                jnp.sum(jnp.where(left, prod, 0.0), axis=1, keepdims=True),
                jnp.sum(jnp.where(left, 0.0, prod), axis=1, keepdims=True),
            ],
            axis=0,
        )
        lse = lse_ref[pl.ds(pl.multiple_of(2 * i * bq, 2 * bq), 2 * bq), :]
        seg = sq_ref[rows, :]
        seg2 = jnp.concatenate([seg, seg], axis=0)

        def k_step(j, dq2):
            keys = pl.ds(pl.multiple_of(j * bk, bk), bk)
            key_rows = k_ref[keys, :]
            scores = dense_back(q2, key_rows)
            same = seg2 == sk_ref[:, keys]
            probs = jnp.where(same, jnp.exp(jnp.where(same, scores, -1e30) - lse), 0.0)
            grad_prob = dense_back(g2, v_ref[keys, :])
            grad_score = (probs * (grad_prob - delta)).astype(BF)
            dv_sum[keys, :] += dense_in(probs.astype(BF), g2)
            dk_sum[keys, :] += dense_in(grad_score, q2)
            return dq2 + dense(grad_score, key_rows)

        dq2 = jnp.zeros((2 * bq, PAIR), F32)
        for s in range(chunks):
            base = s * per_chunk
            dq2 = lax.fori_loop(base + lo_ref[i, s], base + hi_ref[i, s], k_step, dq2)
        dq_ref[rows, :] = (0.125 * by_head(dq2)).astype(BF)
        return carry

    lax.fori_loop(0, nq, q_step, 0)
    dk_ref[...] = dk_sum[...].astype(dk_ref.dtype)
    dv_ref[...] = dv_sum[...].astype(dv_ref.dtype)


SMEM = pl.BlockSpec(memory_space=pltpu.SMEM)
VMEM = pl.BlockSpec(memory_space=pltpu.VMEM)
BQ = 256
BK = 256


def attend(bounds, q, k, v, seg_q, seg_k, chunks):
    n = q.shape[0]
    return pl.pallas_call(
        functools.partial(attend_kernel, BQ, BK, chunks),
        out_shape=(jax.ShapeDtypeStruct((n, PAIR), BF), jax.ShapeDtypeStruct((2 * n, 1), F32)),
        in_specs=[SMEM, SMEM] + [VMEM] * 5,
        out_specs=(VMEM, VMEM),
        compiler_params=pltpu.CompilerParams(vmem_limit_bytes=48 * 2**20),
    )(*bounds, q, k, v, seg_q, seg_k)


def attend_back(bounds, q, k, v, seg_q, seg_k, out, lse, grad, chunks):
    n, m = q.shape[0], k.shape[0]
    kept = BF if chunks == 1 else F32
    return pl.pallas_call(
        functools.partial(attend_back_kernel, BQ, BK, chunks),
        out_shape=(
            jax.ShapeDtypeStruct((n, PAIR), BF),
            jax.ShapeDtypeStruct((m, PAIR), kept),
            jax.ShapeDtypeStruct((m, PAIR), kept),
        ),
        in_specs=[SMEM, SMEM] + [VMEM] * 8,
        out_specs=(VMEM, VMEM, VMEM),
        scratch_shapes=[pltpu.VMEM((m, PAIR), F32), pltpu.VMEM((m, PAIR), F32)],
        compiler_params=pltpu.CompilerParams(vmem_limit_bytes=56 * 2**20),
    )(*bounds, q, k, v, seg_q, seg_k, out, lse, grad)


def body(
    tokens, lengths, packing, query_w, query_b, key_w, value_w, value_b, output_w, output_b,
    attn_gain, attn_shift, expand_w, expand_b, reduce_w, reduce_b, ffn_gain, ffn_shift, cotangent,
):
    tok_shape = tokens.shape
    laps, stripe, width = tok_shape[1], tok_shape[2], tok_shape[3]
    mine = laps * stripe
    n_ctx = lax.axis_size("ctx")
    n_f = lax.axis_size("fsdp")
    per_group = n_ctx // n_f
    chunks = per_group // 2
    ctx = lax.axis_index("ctx")
    f = lax.axis_index("fsdp")
    g = ctx // per_group
    chunk = ctx % per_group // 2
    b = ctx % 2
    swap = jnp.array(SWAP, jnp.int32)
    u = swap[f] * 2 + b
    pairs = [[2 * j, 2 * j + 1] for j in range(n_ctx // 2)]

    route = []
    for c0 in range(n_ctx):
        for f0 in range(n_f):
            g0, b0 = divmod(c0, per_group)
            route.append((c0 * n_f + f0, (SWAP[f0] * per_group + b0) * n_f + SWAP[g0]))

    def relocate(block):
        return lax.ppermute(block, ("ctx", "fsdp"), route)

    def order(block):
        return jnp.stack([block[SWAP[i]] for i in range(n_f)])

    def gather_group(block):
        both = lax.all_gather(block, "ctx", axis_index_groups=pairs)
        everyone = order(lax.all_gather(both, "fsdp"))
        everyone = everyone.reshape(GROUP, laps, stripe, -1)
        return everyone.transpose(1, 0, 2, 3).reshape(GROUP * mine, -1)

    def swap_group(block):
        block = order(block.reshape(n_f, 2, mine, -1))
        block = lax.all_to_all(block, "fsdp", 0, 0)
        block = lax.all_to_all(block, "ctx", 1, 1, axis_index_groups=pairs)
        return order(block).reshape(GROUP, mine, -1)

    def to_tokens(block):
        parts = block.reshape(laps, GROUP, stripe, PAIR).transpose(1, 0, 2, 3).reshape(GROUP, mine, PAIR)
        return swap_group(parts).transpose(1, 0, 2).reshape(mine, width)

    def to_heads(block):
        parts = block.reshape(mine, GROUP, PAIR).transpose(1, 0, 2)
        got = swap_group(parts).reshape(GROUP, laps, stripe, PAIR)
        return got.transpose(1, 0, 2, 3).reshape(GROUP * mine, PAIR)

    def columns(w):
        return lax.all_to_all(w.reshape(w.shape[0], n_f, -1).transpose(1, 0, 2), "fsdp", 0, 0).reshape(
            n_f * w.shape[0], -1
        )

    def rows_back(w):
        return lax.all_to_all(w.reshape(n_f, w.shape[0] // n_f, w.shape[1]), "fsdp", 0, 0)

    row_id = swap[g]
    ordered_all = jnp.sum(
        jnp.where(
            packing[0][:, None] == jnp.arange(lengths.shape[1], dtype=jnp.int32)[None, :],
            lengths[0][None, :],
            0,
        ),
        axis=1,
    )
    ordered = lax.all_gather(ordered_all, "fsdp")[row_id]
    slots = jnp.arange(ordered.shape[0], dtype=jnp.int32)
    slot_ends = jnp.sum(jnp.where(slots[None, :] <= slots[:, None], ordered[None, :], 0), axis=1)
    span = GROUP * mine
    index = jnp.arange(span, dtype=jnp.int32)

    def segments(which):
        lap, rest = index // (GROUP * stripe), index % (GROUP * stripe)
        unit, place = rest // stripe, rest % stripe
        owner = unit // 2 * per_group + which * 2 + unit % 2
        position = lap * (n_ctx * stripe) + owner * stripe + place
        return jnp.sum((position[:, None] >= slot_ends[None, :]).astype(jnp.int32), axis=1)

    seg_q = segments(chunk)
    seg_k = jnp.concatenate([segments(s) for s in range(chunks)])
    q_first, q_last = seg_q[::BQ], seg_q[BQ - 1 :: BQ]
    k_first = seg_k[::BK].reshape(chunks, -1)
    k_last = seg_k[BK - 1 :: BK].reshape(chunks, -1)
    lo = jnp.sum((k_last[None] < q_first[:, None, None]).astype(jnp.int32), axis=2)
    hi = jnp.sum((k_first[None] <= q_last[:, None, None]).astype(jnp.int32), axis=2)
    bounds = (lo, hi)
    seg_q = seg_q[:, None]
    seg_k = seg_k[None, :]

    inputs = relocate(tokens.reshape(mine, width))
    upstream = relocate(cotangent.reshape(mine, width)).astype(F32)
    x_all = gather_group(inputs)
    w_three = jnp.stack([query_w, key_w, value_w]).reshape(3, -1, n_f, 2, PAIR)
    w_three = lax.dynamic_index_in_dim(w_three, b, 3, keepdims=False)
    w_three = order(w_three.transpose(2, 1, 0, 3).reshape(n_f, -1, 3 * PAIR))
    w_three = lax.all_to_all(w_three, "fsdp", 0, 0).reshape(width, 3 * PAIR)
    here = u * PAIR
    bias3 = jnp.concatenate(
        [
            lax.dynamic_slice_in_dim(query_b, here, PAIR),
            jnp.zeros((PAIR,), F32),
            lax.dynamic_slice_in_dim(value_b, here, PAIR),
        ]
    )
    three = (dense(x_all, w_three) + bias3).astype(BF)
    q, k_own, v_own = three[:, :PAIR], three[:, PAIR : 2 * PAIR], three[:, 2 * PAIR :]
    same_place = [
        [(gg * chunks + s) * 2 + bb for s in range(chunks)] for gg in range(n_f) for bb in range(2)
    ]
    if chunks == 1:
        k, v = k_own, v_own
    else:
        k = lax.all_gather(k_own, "ctx", axis_index_groups=same_place, tiled=True)
        v = lax.all_gather(v_own, "ctx", axis_index_groups=same_place, tiled=True)
    att_heads, lse = attend(bounds, q, k, v, seg_q, seg_k, chunks)

    w_output = lax.all_gather(output_w, "fsdp", axis=0, tiled=True)
    attended = to_tokens(att_heads)
    branch = dense(attended, w_output) + output_b
    normed, x_hat1, inv_std1 = norm_fwd(inputs.astype(F32) + branch, attn_gain, attn_shift)
    normed_low = lax.all_gather(normed.astype(BF), "fsdp", axis=0, tiled=True)

    w_up = columns(expand_w)
    units = w_up.shape[1]
    pre_act = dense(normed_low, w_up) + lax.dynamic_slice_in_dim(expand_b, f * units, units)
    hidden = jax.nn.gelu(pre_act, approximate=False).astype(BF)
    ffn_out = lax.psum_scatter(dense(hidden, reduce_w).astype(BF), "fsdp", tiled=True).astype(F32) + reduce_b
    outputs, x_hat2, inv_std2 = norm_fwd(normed + ffn_out, ffn_gain, ffn_shift)
    layer_out = relocate(outputs.astype(BF)).reshape(tok_shape)
    grad_mid2, grad_ffn_gain, grad_ffn_shift = norm_back(upstream, x_hat2, inv_std2, ffn_gain)
    grad_ffn_own = grad_mid2.astype(BF)
    grad_reduce_b = jnp.sum(grad_ffn_own.astype(F32), axis=0)
    grad_ffn = lax.all_gather(grad_ffn_own, "fsdp", axis=0, tiled=True)
    part_down = dense_in(hidden, grad_ffn).astype(BF)
    grad_pre = (dense_back(grad_ffn, reduce_w) * gelu_slope(pre_act)).astype(BF)
    grad_expand_b = lax.dynamic_update_slice_in_dim(
        jnp.zeros_like(expand_b), jnp.sum(grad_pre.astype(F32), axis=0), f * units, 0
    )
    part_up = dense_in(normed_low, grad_pre).astype(BF)
    grad_normed = lax.psum_scatter(dense_back(grad_pre, w_up).astype(BF), "fsdp", tiled=True).astype(F32) + grad_mid2
    grad_mid1, grad_attn_gain, grad_attn_shift = norm_back(grad_normed, x_hat1, inv_std1, attn_gain)
    grad_branch = grad_mid1.astype(BF)
    grad_output_b = jnp.sum(grad_branch.astype(F32), axis=0)
    part_out = lax.psum_scatter(dense_in(attended, grad_branch).astype(BF), "fsdp", tiled=True)
    grad_att = to_heads(dense_back(grad_branch, w_output).astype(BF))

    grad_q, grad_k, grad_v = attend_back(
        bounds, q, k, v, seg_q, seg_k, att_heads, lse, grad_att, chunks
    )
    if chunks > 1:
        grad_k = lax.psum_scatter(
            grad_k.astype(BF), "ctx", axis_index_groups=same_place, tiled=True
        )
        grad_v = lax.psum_scatter(
            grad_v.astype(BF), "ctx", axis_index_groups=same_place, tiled=True
        )
    grad_three = jnp.concatenate([grad_q, grad_k, grad_v], axis=1)
    sums3 = jnp.sum(grad_three.astype(F32), axis=0)
    grad_query_b = lax.dynamic_update_slice_in_dim(jnp.zeros_like(query_b), sums3[:PAIR], here, 0)
    grad_value_b = lax.dynamic_update_slice_in_dim(jnp.zeros_like(value_b), sums3[2 * PAIR :], here, 0)
    part_three = dense_in(x_all, grad_three).astype(BF)
    back = dense_back(grad_three, w_three).astype(BF)
    back = back.reshape(laps, GROUP, stripe, width).transpose(1, 0, 2, 3).reshape(n_f, 2, mine, width)
    back = lax.psum_scatter(order(back), "fsdp", scatter_dimension=0)
    back = lax.psum_scatter(back, "ctx", scatter_dimension=0, axis_index_groups=pairs)
    grad_inputs = relocate(back.astype(F32) + grad_mid1).reshape(tok_shape)

    got = order(rows_back(part_three)).reshape(n_f, -1, 3, PAIR)
    got = got.transpose(2, 1, 0, 3)[:, :, :, None, :]
    mask = (jnp.arange(2) == b)[None, None, None, :, None]
    share_three = jnp.where(mask, got, BF(0)).reshape(3, got.shape[1], width)
    share_up = rows_back(part_up).transpose(1, 0, 2).reshape(-1, n_f * units)
    share_three, share_out, share_up, share_down = lax.psum(
        (share_three, part_out, share_up, part_down), "ctx"
    )
    share_three = share_three.astype(F32)
    (
        grad_query_b, grad_value_b, grad_output_b, grad_attn_gain, grad_attn_shift, grad_expand_b,
        grad_reduce_b, grad_ffn_gain, grad_ffn_shift,
    ) = lax.psum(
        (
            grad_query_b, grad_value_b, grad_output_b, grad_attn_gain, grad_attn_shift, grad_expand_b,
            grad_reduce_b, grad_ffn_gain, grad_ffn_shift,
        ),
        ("ctx", "fsdp"),
    )
    return (
        layer_out,
        grad_inputs,
        share_three[0],
        grad_query_b,
        share_three[1],
        share_three[2],
        grad_value_b,
        share_out.astype(F32),
        grad_output_b,
        grad_attn_gain,
        grad_attn_shift,
        share_up.astype(F32),
        grad_expand_b,
        share_down.astype(F32),
        grad_reduce_b,
        grad_ffn_gain,
        grad_ffn_shift,
    )


def solution(mesh):
    acts = P("fsdp", None, "ctx", None)
    rows = P("fsdp", None)
    return jax.shard_map(
        body,
        mesh=mesh,
        in_specs=(
            acts, rows, rows, rows, P(), rows, rows, P(), rows, P(),
            P(), P(), rows, P(), rows, P(), P(), P(), acts,
        ),
        out_specs=(
            acts, acts, rows, P(), rows, rows, P(), rows, P(),
            P(), P(), rows, P(), rows, P(), P(), P(),
        ),
        check_vma=False,
    )
```

```python
import functools
import jax
import jax.numpy as jnp
from jax import lax
from jax.experimental import pallas as pl
from jax.experimental.pallas import tpu as pltpu
from jax.sharding import PartitionSpec as P

H = 16
HD = 64
PAIR = 2 * HD
GROUP = 8
SWAP = (0, 2, 1, 3)
BF = jnp.bfloat16
F32 = jnp.float32


def dense(left, right):
    return jnp.dot(left, right, preferred_element_type=F32)


def dense_back(left, right):
    return lax.dot_general(left, right, (((1,), (1,)), ((), ())), preferred_element_type=F32)


def dense_in(left, right):
    return lax.dot_general(left, right, (((0,), (0,)), ((), ())), preferred_element_type=F32)


def norm_fwd(hidden, gain, shift):
    mean_row = jnp.mean(hidden, axis=-1, keepdims=True)
    centred = hidden - mean_row
    variance = jnp.mean(centred * centred, axis=-1, keepdims=True)
    inv_std = lax.rsqrt(variance + 1e-05)
    x_hat = centred * inv_std
    return (x_hat * gain + shift, x_hat, inv_std)


def norm_back(incoming, x_hat, inv_std, gain):
    scaled = incoming * gain
    grad_in = inv_std * (
        scaled
        - jnp.mean(scaled, axis=-1, keepdims=True)
        - x_hat * jnp.mean(scaled * x_hat, axis=-1, keepdims=True)
    )
    return (grad_in, jnp.sum(incoming * x_hat, axis=0), jnp.sum(incoming, axis=0))


def gelu_slope(pre_act):
    return (
        0.5 * (1.0 + lax.erf(pre_act * 0.7071067811865476))
        + pre_act * jnp.exp(-0.5 * pre_act * pre_act) * 0.3989422804014327
    )


def first_half(shape):
    return lax.broadcasted_iota(jnp.int32, shape, 1) < HD


def both_heads(block):
    left = first_half(block.shape)
    zero = jnp.zeros_like(block)
    return jnp.concatenate([jnp.where(left, block, zero), jnp.where(left, zero, block)], axis=0)


def by_head(stacked):
    rows = stacked.shape[0] // 2
    left = first_half((rows, stacked.shape[1]))
    return jnp.where(left, stacked[:rows], stacked[rows:])


def attend_kernel(bq, bk, chunks, lo_ref, hi_ref, q_ref, k_ref, v_ref, sq_ref, sk_ref, o_ref, lse_ref):
    nq = q_ref.shape[0] // bq
    per_chunk = k_ref.shape[0] // chunks // bk

    def q_step(i, carry):
        rows = pl.ds(pl.multiple_of(i * bq, bq), bq)
        q2 = both_heads(q_ref[rows, :] * BF(0.125))
        seg = sq_ref[rows, :]
        seg2 = jnp.concatenate([seg, seg], axis=0)

        def k_step(j, state):
            accum, run_max, run_sum = state
            keys = pl.ds(pl.multiple_of(j * bk, bk), bk)
            scores = dense_back(q2, k_ref[keys, :])
            same = seg2 == sk_ref[:, keys]
            scores = jnp.where(same, scores, -1e30)
            new_max = jnp.maximum(run_max, jnp.max(scores, axis=1, keepdims=True))
            probs = jnp.where(same, jnp.exp(scores - new_max), 0.0)
            scale = jnp.exp(run_max - new_max)
            run_sum = run_sum * scale + jnp.sum(probs, axis=1, keepdims=True)
            accum = accum * scale + dense(probs.astype(BF), v_ref[keys, :])
            return accum, new_max, run_sum

        state = (
            jnp.zeros((2 * bq, PAIR), F32),
            jnp.full((2 * bq, 1), -1e30, F32),
            jnp.zeros((2 * bq, 1), F32),
        )
        for s in range(chunks):
            base = s * per_chunk
            state = lax.fori_loop(base + lo_ref[i, s], base + hi_ref[i, s], k_step, state)
        accum, run_max, run_sum = state
        o_ref[rows, :] = by_head(accum / run_sum).astype(BF)
        lse_ref[pl.ds(pl.multiple_of(2 * i * bq, 2 * bq), 2 * bq), :] = run_max + jnp.log(run_sum)
        return carry

    lax.fori_loop(0, nq, q_step, 0)


def attend_back_kernel(
    bq, bk, chunks, lo_ref, hi_ref, q_ref, k_ref, v_ref, sq_ref, sk_ref, o_ref, lse_ref, g_ref,
    dq_ref, dk_ref, dv_ref, dk_sum, dv_sum,
):
    nq = q_ref.shape[0] // bq
    per_chunk = k_ref.shape[0] // chunks // bk
    dk_sum[...] = jnp.zeros_like(dk_sum)
    dv_sum[...] = jnp.zeros_like(dv_sum)

    def q_step(i, carry):
        rows = pl.ds(pl.multiple_of(i * bq, bq), bq)
        q2 = both_heads(q_ref[rows, :] * BF(0.125))
        grad = g_ref[rows, :]
        g2 = both_heads(grad)
        prod = grad.astype(F32) * o_ref[rows, :].astype(F32)
        left = first_half(prod.shape)
        delta = jnp.concatenate(
            [
                jnp.sum(jnp.where(left, prod, 0.0), axis=1, keepdims=True),
                jnp.sum(jnp.where(left, 0.0, prod), axis=1, keepdims=True),
            ],
            axis=0,
        )
        lse = lse_ref[pl.ds(pl.multiple_of(2 * i * bq, 2 * bq), 2 * bq), :]
        seg = sq_ref[rows, :]
        seg2 = jnp.concatenate([seg, seg], axis=0)

        def k_step(j, dq2):
            keys = pl.ds(pl.multiple_of(j * bk, bk), bk)
            key_rows = k_ref[keys, :]
            scores = dense_back(q2, key_rows)
            same = seg2 == sk_ref[:, keys]
            probs = jnp.where(same, jnp.exp(jnp.where(same, scores, -1e30) - lse), 0.0)
            grad_prob = dense_back(g2, v_ref[keys, :])
            grad_score = (probs * (grad_prob - delta)).astype(BF)
            dv_sum[keys, :] += dense_in(probs.astype(BF), g2)
            dk_sum[keys, :] += dense_in(grad_score, q2)
            return dq2 + dense(grad_score, key_rows)

        dq2 = jnp.zeros((2 * bq, PAIR), F32)
        for s in range(chunks):
            base = s * per_chunk
            dq2 = lax.fori_loop(base + lo_ref[i, s], base + hi_ref[i, s], k_step, dq2)
        dq_ref[rows, :] = (0.125 * by_head(dq2)).astype(BF)
        return carry

    lax.fori_loop(0, nq, q_step, 0)
    dk_ref[...] = dk_sum[...].astype(dk_ref.dtype)
    dv_ref[...] = dv_sum[...].astype(dv_ref.dtype)


SMEM = pl.BlockSpec(memory_space=pltpu.SMEM)
VMEM = pl.BlockSpec(memory_space=pltpu.VMEM)
BQ = 256
BK = 256


def attend(bounds, q, k, v, seg_q, seg_k, chunks):
    n = q.shape[0]
    return pl.pallas_call(
        functools.partial(attend_kernel, BQ, BK, chunks),
        out_shape=(jax.ShapeDtypeStruct((n, PAIR), BF), jax.ShapeDtypeStruct((2 * n, 1), F32)),
        in_specs=[SMEM, SMEM] + [VMEM] * 5,
        out_specs=(VMEM, VMEM),
        compiler_params=pltpu.CompilerParams(vmem_limit_bytes=48 * 2**20),
    )(*bounds, q, k, v, seg_q, seg_k)


def attend_back(bounds, q, k, v, seg_q, seg_k, out, lse, grad, chunks):
    n, m = q.shape[0], k.shape[0]
    kept = BF if chunks == 1 else F32
    return pl.pallas_call(
        functools.partial(attend_back_kernel, BQ, BK, chunks),
        out_shape=(
            jax.ShapeDtypeStruct((n, PAIR), BF),
            jax.ShapeDtypeStruct((m, PAIR), kept),
            jax.ShapeDtypeStruct((m, PAIR), kept),
        ),
        in_specs=[SMEM, SMEM] + [VMEM] * 8,
        out_specs=(VMEM, VMEM, VMEM),
        scratch_shapes=[pltpu.VMEM((m, PAIR), F32), pltpu.VMEM((m, PAIR), F32)],
        compiler_params=pltpu.CompilerParams(vmem_limit_bytes=56 * 2**20),
    )(*bounds, q, k, v, seg_q, seg_k, out, lse, grad)


def mesh_id(ctx, f):
    return {"ctx": ctx, "fsdp": f}


def swapped(i):
    return i % 2 * 2 + i // 2


class Place:
    def __init__(self):
        self.ctx = lax.axis_index("ctx")
        self.f = lax.axis_index("fsdp")
        self.per_group = lax.axis_size("ctx") // 4
        self.g = self.ctx // self.per_group
        self.b = self.ctx % 2
        self.rest = self.ctx % self.per_group
        self.core = self.f % 2
        self.x = self.f // 2

    def at(self, g=None, b=None, f=None):
        ctx = self.ctx
        if g is not None:
            ctx = ctx + (g - self.g) * self.per_group
        if b is not None:
            ctx = ctx + (b - self.b)
        return mesh_id(ctx, self.f if f is None else f)

    def sibling(self):
        return self.at(f=self.f + 1 - 2 * self.core)

    def beside(self):
        return self.at(f=(self.f + 2) % 4)

    def across(self):
        return self.at(b=1 - self.b)

    def fsdp(self, k):
        return self.at(f=(self.f + k) % 4)

    def moved(self):
        return mesh_id(swapped(self.f) * self.per_group + self.rest, swapped(self.g))

    def stays(self):
        return swapped(self.f) == self.g


def remote(src, dst, send, recv, where):
    return pltpu.make_async_remote_copy(
        src_ref=src, dst_ref=dst, send_sem=send, recv_sem=recv,
        device_id=where, device_id_type=pl.DeviceIdType.MESH,
    )


def meet(me, targets, moves):
    barrier = pltpu.get_barrier_semaphore()
    for t in targets:
        pl.semaphore_signal(barrier, 1, device_id=t, device_id_type=pl.DeviceIdType.MESH)
    if not moves:
        pl.semaphore_wait(barrier, len(targets))
        return

    @pl.when(jnp.logical_not(me.stays()))
    def _():
        pl.semaphore_signal(barrier, 1, device_id=me.moved(), device_id_type=pl.DeviceIdType.MESH)

    pl.semaphore_wait(barrier, len(targets) + jnp.where(me.stays(), 0, 1))


def tail_kernel(
    x_ref, g3_ref, w3_ref, down_ref, up_ref, out_ref, mid_ref, vec_ref,
    down_out, up_out, o_out, three_out, dx_ref, sums_ref,
    dxp, dx1, t1, xa, yb, t2a, t2b, ra, rb, moved_buf,
    yr_down, yr_up, zl, zr, zs, up_send, up_got,
    o_got, o_sum, yr_o, ol, orr, os_,
    gq, ql, qr, qs, q_send,
    vs, vr,
    s_dx, r_dx, s_y, r_y, s_z, r_zl, r_zr, s_u, r_u, s_o, r_o, s_oz, r_ol, r_or, s_q, r_ql, r_qr,
    s_qf, r_qf, s_v, r_v, s_ag, r_ag, s_ay, r_ay, loc,
):
    me = Place()
    g, b, f = me.g, me.b, me.f
    z_others = [me.at(g=(g + k) % 4) for k in (1, 2, 3)]
    meet(me, [me.across()] + [me.fsdp(k) for k in (1, 2, 3)] + z_others, True)

    y_copies = {}
    for p in (3, 0, 2, 1):
        y_copies[p] = (
            remote(down_ref.at[1 - b, p], yr_down.at[p], s_y.at[0, p], r_y.at[0, p], me.across()),
            remote(up_ref.at[:, 1 - b, p], yr_up.at[p], s_y.at[1, p], r_y.at[1, p], me.across()),
        )
        for c in y_copies[p]:
            c.start()
    o_copies = []
    for k in (1, 2, 3):
        c = remote(out_ref.at[(f + k) % 4], o_got.at[k - 1], s_o.at[k - 1], r_o.at[k - 1], me.fsdp(k))
        c.start()
        o_copies.append(c)

    def dx_step(i, carry):
        rows = pl.ds(pl.multiple_of(i * 256, 256), 256)
        part = dense_back(g3_ref[rows, :], w3_ref[...]).astype(BF)
        dxp[pl.ds(2 * i, 2)] = part.reshape(2, 2, 2, 2, 16, 1024)
        return carry

    lax.fori_loop(0, 8, dx_step, 0)
    c_core = remote(dxp.at[:, 1 - me.core], dx1, s_dx.at[0], r_dx.at[0], me.sibling())
    c_core.start()

    hops = [me.sibling(), me.beside(), me.across(), me.at(g=g + 1 - 2 * (g % 2)), me.at(g=(g + 2) % 4)]
    vec = vec_ref[...]

    def hop(i, vec):
        vs[i] = vec
        c = remote(vs.at[i], vr.at[i], s_v.at[i], r_v.at[i], hops[i])
        c.start()
        return c

    v_copies = [hop(0, vec)]

    def hop_end(i, vec):
        v_copies[i].wait()
        return vec + vr[i]

    def q_step(i, carry):
        cols = pl.ds(pl.multiple_of(i * 256, 256), 256)
        part = dense_in(x_ref[:, cols], g3_ref[...]).astype(BF)
        for j in range(3):
            gq[i, j] = part[:, j * 128 : (j + 1) * 128].reshape(4, 64, 128)
        return carry

    lax.fori_loop(0, 4, q_step, 0)

    vec = hop_end(0, vec)
    v_copies.append(hop(1, vec))

    c_core.wait()

    def t1_step(i, carry):
        t1[i] = (dxp[i, me.core].astype(F32) + dx1[i].astype(F32)).astype(BF)
        return carry

    lax.fori_loop(0, 16, t1_step, 0)
    lo, hi = pl.ds(0, 8), pl.ds(8, 8)
    c_xa = remote(t1.at[lo, 1 - me.x], xa, s_dx.at[1], r_dx.at[1], me.beside())
    c_yb = remote(t1.at[hi, :, 1 - b], yb, s_dx.at[2], r_dx.at[2], me.across())
    c_xa.start()
    c_yb.start()

    vec = hop_end(1, vec)
    v_copies.append(hop(2, vec))

    def flow(p, own, left, right, send, s_sem, l_sem, r_sem):
        @pl.when(g < p)
        def _():
            @pl.when(g > 0)
            def _():
                remote(send.at[p], left.at[p], s_sem.at[p], l_sem.at[p], me.across()).wait_recv()
                send[p] = (own(p) + left[p].astype(F32)).astype(BF)

            @pl.when(g == 0)
            def _():
                send[p] = own(p).astype(BF)

            remote(send.at[p], left.at[p], s_sem.at[p], l_sem.at[p], me.at(g=g + 1)).start()

        @pl.when(g > p)
        def _():
            @pl.when(g < 3)
            def _():
                remote(send.at[p], right.at[p], s_sem.at[p], r_sem.at[p], me.across()).wait_recv()
                send[p] = (own(p) + right[p].astype(F32)).astype(BF)

            @pl.when(g == 3)
            def _():
                send[p] = own(p).astype(BF)

            remote(send.at[p], right.at[p], s_sem.at[p], r_sem.at[p], me.at(g=g - 1)).start()

    def flow_end(own, left, right, send, s_sem, l_sem, r_sem):
        send[g] = own(g).astype(BF)

        @pl.when(g > 0)
        def _():
            remote(send.at[g], left.at[g], s_sem.at[g], l_sem.at[g], me.across()).wait_recv()
            send[g] = (send[g].astype(F32) + left[g].astype(F32)).astype(BF)

        @pl.when(g < 3)
        def _():
            remote(send.at[g], right.at[g], s_sem.at[g], r_sem.at[g], me.across()).wait_recv()
            send[g] = (send[g].astype(F32) + right[g].astype(F32)).astype(BF)

        for p in range(4):
            @pl.when(g != p)
            def _():
                remote(send.at[p], left.at[p], s_sem.at[p], l_sem.at[p], me.across()).wait_send()

    def own_q(p):
        return gq[:, :, p].astype(F32)

    q_bufs = (ql, qr, qs, s_q, r_ql, r_qr)
    for p in (3, 0, 2, 1):
        flow(p, own_q, *q_bufs)

    for c in o_copies:
        c.wait()
    o_sum[...] = (
        out_ref[f].astype(F32) + o_got[0].astype(F32) + o_got[1].astype(F32) + o_got[2].astype(F32)
    ).astype(BF)
    c_oy = remote(o_sum.at[1 - b], yr_o, s_y.at[0, 4], r_y.at[0, 4], me.across())
    c_oy.start()

    vec = hop_end(2, vec)
    v_copies.append(hop(3, vec))

    def own_big(p):
        return jnp.concatenate(
            [
                down_ref[b, p].astype(F32) + yr_down[p].astype(F32),
                (up_ref[:, b, p].astype(F32) + yr_up[p].astype(F32)).reshape(128, 1024),
            ],
            axis=0,
        )

    big_bufs = (zl, zr, zs, s_z, r_zl, r_zr)
    for p in (3, 0, 2, 1):
        for c in y_copies[p]:
            c.wait()
        flow(p, own_big, *big_bufs)

    c_xa.wait()
    t2a[...] = (t1[lo, me.x].astype(F32) + xa[...].astype(F32)).astype(BF)
    c_ra = remote(t2a.at[:, 1 - b], ra, s_dx.at[3], r_dx.at[3], me.across())
    c_ra.start()
    c_yb.wait()
    t2b[...] = (t1[hi, :, b].astype(F32) + yb[...].astype(F32)).astype(BF)
    c_rb = remote(t2b.at[:, 1 - me.x], rb, s_dx.at[4], r_dx.at[4], me.beside())
    c_rb.start()

    vec = hop_end(3, vec)
    v_copies.append(hop(4, vec))

    c_oy.wait()

    def own_o(p):
        return o_sum[b, p].astype(F32) + yr_o[p].astype(F32)

    o_bufs = (ol, orr, os_, s_oz, r_ol, r_or)
    for p in (3, 0, 2, 1):
        flow(p, own_o, *o_bufs)

    c_ra.wait()
    c_rb.wait()
    moved_buf[lo] = (t2a[:, b].astype(F32) + ra[...].astype(F32) + mid_ref[lo]).astype(BF)
    moved_buf[hi] = (t2b[:, me.x].astype(F32) + rb[...].astype(F32) + mid_ref[hi]).astype(BF)

    @pl.when(me.stays())
    def _():
        c = pltpu.make_async_copy(moved_buf, dx_ref, loc.at[0])
        c.start()
        c.wait()

    @pl.when(jnp.logical_not(me.stays()))
    def _():
        remote(moved_buf, dx_ref, s_dx.at[5], r_dx.at[5], me.moved()).start()

    def rows(size, q, other=False):
        half = 1 - b if other else b
        return pl.ds(pl.multiple_of((half * 4 + q) * size, size), size)

    def unit_cols(src):
        return pl.ds(pl.multiple_of(src * 1024, 1024), 1024)

    def head_cols(src):
        return pl.ds(pl.multiple_of((b * 4 + swapped(src)) * 128, 128), 128)

    def q_rows(q):
        return pl.ds(pl.multiple_of(q * 64, 64), 64)

    flow_end(own_q, *q_bufs)
    q_send[...] = qs[g]
    three_out[:, q_rows(g), head_cols(f)] = q_send[f]
    q_out = []
    for k in (1, 2, 3):
        c = remote(q_send.at[(f + k) % 4], three_out.at[:, q_rows(g), head_cols(f)], s_qf.at[k - 1], r_qf.at[f], me.fsdp(k))
        c.start()
        q_out.append(c)

    flow_end(own_big, *big_bufs)
    up_send[...] = zs[g, pl.ds(128, 128)].reshape(4, 32, 1024)
    down_out[rows(128, g), :] = zs[g, pl.ds(0, 128)]
    up_out[rows(32, g), unit_cols(f)] = up_send[f]
    u_out = []
    for k in (1, 2, 3):
        c = remote(up_send.at[(f + k) % 4], up_out.at[rows(32, g), unit_cols(f)], s_u.at[k - 1], r_u.at[f], me.fsdp(k))
        c.start()
        u_out.append(c)
    flow_end(own_o, *o_bufs)
    o_out[rows(32, g), :] = os_[g]

    for k in (1, 2, 3):
        src = (f + k) % 4
        remote(q_send.at[0], three_out.at[:, q_rows(g), head_cols(src)], s_qf.at[k - 1], r_qf.at[src], me.fsdp(k)).wait_recv()
        remote(up_send.at[0], up_out.at[rows(32, g), unit_cols(src)], s_u.at[k - 1], r_u.at[src], me.fsdp(k)).wait_recv()
        q_out[k - 1].wait_send()
        u_out[k - 1].wait_send()

    def pieces(q, send, recv, where, other=False):
        half = 1 - b if other else b
        parts = (
            down_out.at[rows(128, q, other), :],
            up_out.at[rows(32, q, other), :],
            o_out.at[rows(32, q, other), :],
            three_out.at[:, q_rows(q), pl.ds(pl.multiple_of(half * 512, 512), 512)],
        )
        return [remote(part, part, send.at[i, q], recv.at[i, q], where) for i, part in enumerate(parts)]

    def spread(q, to_right, to_left):
        for c in pieces(q, s_ay, r_ay, me.across()):
            c.start()
        if to_right:
            @pl.when(g < 3)
            def _():
                for c in pieces(q, s_ag.at[0], r_ag, me.at(g=g + 1)):
                    c.start()
        if to_left:
            @pl.when(g > 0)
            def _():
                for c in pieces(q, s_ag.at[1], r_ag, me.at(g=g - 1)):
                    c.start()

    spread(g, True, True)
    for d in (1, 2, 3):
        @pl.when(g >= d)
        def _():
            for c in pieces(g - d, s_ag.at[0], r_ag, me.across()):
                c.wait_recv()
            spread(g - d, True, False)

        @pl.when(g + d <= 3)
        def _():
            for c in pieces(g + d, s_ag.at[1], r_ag, me.across()):
                c.wait_recv()
            spread(g + d, False, True)

    vec = hop_end(4, vec)
    sums_ref[...] = vec

    @pl.when(jnp.logical_not(me.stays()))
    def _():
        remote(moved_buf, dx_ref, s_dx.at[5], r_dx.at[5], me.moved()).wait()

    for q in range(4):
        for c in pieces(q, s_ay, r_ay, me.across()):
            c.wait_send()

        @pl.when((g >= q) & (g < 3))
        def _():
            for c in pieces(q, s_ag.at[0], r_ag, me.across()):
                c.wait_send()

        @pl.when((g <= q) & (g > 0))
        def _():
            for c in pieces(q, s_ag.at[1], r_ag, me.across()):
                c.wait_send()

        for c in pieces(q, s_ay, r_ay, me.across(), other=True):
            c.wait_recv()


def tail(x_all, g3, w3, down, up, out, mid, vec):
    dma = pltpu.SemaphoreType.DMA
    v = pltpu.VMEM
    scratch = [
        v((16, 2, 2, 2, 16, 1024), BF), v((16, 2, 2, 16, 1024), BF), v((16, 2, 2, 16, 1024), BF),
        v((8, 2, 16, 1024), BF), v((8, 2, 16, 1024), BF), v((8, 2, 16, 1024), BF), v((8, 2, 16, 1024), BF),
        v((8, 16, 1024), BF), v((8, 16, 1024), BF), v((16, 16, 1024), BF),
        v((4, 128, 1024), BF), v((4, 4, 32, 1024), BF), v((4, 256, 1024), BF), v((4, 256, 1024), BF),
        v((4, 256, 1024), BF), v((4, 32, 1024), BF), v((4, 32, 1024), BF),
        v((3, 2, 4, 32, 1024), BF), v((2, 4, 32, 1024), BF), v((4, 32, 1024), BF),
        v((4, 32, 1024), BF), v((4, 32, 1024), BF), v((4, 32, 1024), BF),
        v((4, 3, 4, 64, 128), BF), v((4, 4, 3, 64, 128), BF), v((4, 4, 3, 64, 128), BF), v((4, 4, 3, 64, 128), BF),
        v((4, 3, 64, 128), BF),
        v((5, 16, 1024), F32), v((5, 16, 1024), F32),
        dma((6,)), dma((6,)), dma((2, 5)), dma((2, 5)), dma((4,)), dma((4,)), dma((4,)),
        dma((3,)), dma((4,)), dma((3,)), dma((3,)), dma((4,)), dma((4,)), dma((4,)), dma((4,)), dma((4,)), dma((4,)),
        dma((3,)), dma((4,)), dma((5,)), dma((5,)), dma((2, 4, 4)), dma((4, 4)), dma((4, 4)), dma((4, 4)), dma((1,)),
    ]
    return pl.pallas_call(
        tail_kernel,
        out_shape=(
            jax.ShapeDtypeStruct((1024, 1024), BF),
            jax.ShapeDtypeStruct((256, 4096), BF),
            jax.ShapeDtypeStruct((256, 1024), BF),
            jax.ShapeDtypeStruct((3, 256, 1024), BF),
            jax.ShapeDtypeStruct((16, 16, 1024), BF),
            jax.ShapeDtypeStruct((16, 1024), F32),
        ),
        in_specs=[VMEM] * 8,
        out_specs=(VMEM,) * 6,
        scratch_shapes=scratch,
        compiler_params=pltpu.CompilerParams(collective_id=1, has_side_effects=True, vmem_limit_bytes=60 * 2**20),
        cost_estimate=pl.CostEstimate(flops=4 * 10**9, bytes_accessed=40 * 2**20, transcendentals=0),
    )(x_all, g3, w3, down.reshape(2, 4, 128, 1024), up.reshape(4, 2, 4, 32, 1024), out.reshape(4, 2, 4, 32, 1024), mid.reshape(16, 16, 1024), vec)


def body(
    tokens, lengths, packing, query_w, query_b, key_w, value_w, value_b, output_w, output_b,
    attn_gain, attn_shift, expand_w, expand_b, reduce_w, reduce_b, ffn_gain, ffn_shift, cotangent,
):
    tok_shape = tokens.shape
    laps, stripe, width = tok_shape[1], tok_shape[2], tok_shape[3]
    mine = laps * stripe
    n_ctx = lax.axis_size("ctx")
    n_f = lax.axis_size("fsdp")
    per_group = n_ctx // n_f
    chunks = per_group // 2
    ctx = lax.axis_index("ctx")
    f = lax.axis_index("fsdp")
    g = ctx // per_group
    chunk = ctx % per_group // 2
    b = ctx % 2
    swap = jnp.array(SWAP, jnp.int32)
    u = swap[f] * 2 + b
    pairs = [[2 * j, 2 * j + 1] for j in range(n_ctx // 2)]

    route = []
    for c0 in range(n_ctx):
        for f0 in range(n_f):
            g0, b0 = divmod(c0, per_group)
            route.append((c0 * n_f + f0, (SWAP[f0] * per_group + b0) * n_f + SWAP[g0]))

    def relocate(block):
        return lax.ppermute(block, ("ctx", "fsdp"), route)

    def order(block):
        return jnp.stack([block[SWAP[i]] for i in range(n_f)])

    def gather_group(block):
        both = lax.all_gather(block, "ctx", axis_index_groups=pairs)
        everyone = order(lax.all_gather(both, "fsdp"))
        everyone = everyone.reshape(GROUP, laps, stripe, -1)
        return everyone.transpose(1, 0, 2, 3).reshape(GROUP * mine, -1)

    def swap_group(block):
        block = order(block.reshape(n_f, 2, mine, -1))
        block = lax.all_to_all(block, "fsdp", 0, 0)
        block = lax.all_to_all(block, "ctx", 1, 1, axis_index_groups=pairs)
        return order(block).reshape(GROUP, mine, -1)

    def to_tokens(block):
        parts = block.reshape(laps, GROUP, stripe, PAIR).transpose(1, 0, 2, 3).reshape(GROUP, mine, PAIR)
        got = swap_group(parts).reshape(n_f, 2, mine, PAIR)
        return got.transpose(2, 1, 0, 3).reshape(mine, width)

    def to_heads(block):
        parts = block.reshape(mine, 2, n_f, PAIR).transpose(2, 1, 0, 3)
        got = swap_group(parts).reshape(GROUP, laps, stripe, PAIR)
        return got.transpose(1, 0, 2, 3).reshape(GROUP * mine, PAIR)

    def columns(w):
        return lax.all_to_all(w.reshape(w.shape[0], n_f, -1).transpose(1, 0, 2), "fsdp", 0, 0).reshape(
            n_f * w.shape[0], -1
        )

    row_id = swap[g]
    ordered_all = jnp.sum(
        jnp.where(
            packing[0][:, None] == jnp.arange(lengths.shape[1], dtype=jnp.int32)[None, :],
            lengths[0][None, :],
            0,
        ),
        axis=1,
    )
    ordered = lax.all_gather(ordered_all, "fsdp")[row_id]
    slots = jnp.arange(ordered.shape[0], dtype=jnp.int32)
    slot_ends = jnp.sum(jnp.where(slots[None, :] <= slots[:, None], ordered[None, :], 0), axis=1)
    span = GROUP * mine
    index = jnp.arange(span, dtype=jnp.int32)

    def segments(which):
        lap, rest = index // (GROUP * stripe), index % (GROUP * stripe)
        unit, place = rest // stripe, rest % stripe
        owner = unit // 2 * per_group + which * 2 + unit % 2
        position = lap * (n_ctx * stripe) + owner * stripe + place
        return jnp.sum((position[:, None] >= slot_ends[None, :]).astype(jnp.int32), axis=1)

    seg_q = segments(chunk)
    seg_k = jnp.concatenate([segments(s) for s in range(chunks)])
    q_first, q_last = seg_q[::BQ], seg_q[BQ - 1 :: BQ]
    k_first = seg_k[::BK].reshape(chunks, -1)
    k_last = seg_k[BK - 1 :: BK].reshape(chunks, -1)
    lo = jnp.sum((k_last[None] < q_first[:, None, None]).astype(jnp.int32), axis=2)
    hi = jnp.sum((k_first[None] <= q_last[:, None, None]).astype(jnp.int32), axis=2)
    bounds = (lo, hi)
    seg_q = seg_q[:, None]
    seg_k = seg_k[None, :]

    inputs = relocate(tokens.reshape(mine, width))
    upstream = relocate(cotangent.reshape(mine, width)).astype(F32)
    x_all = gather_group(inputs)
    w_three = jnp.stack([query_w, key_w, value_w]).reshape(3, -1, 2, n_f, PAIR)
    w_three = lax.dynamic_index_in_dim(w_three, b, 2, keepdims=False)
    w_three = order(w_three.transpose(2, 1, 0, 3).reshape(n_f, -1, 3 * PAIR))
    w_three = lax.all_to_all(w_three, "fsdp", 0, 0).reshape(width, 3 * PAIR)
    here = (b * n_f + swap[f]) * PAIR
    bias3 = jnp.concatenate(
        [
            lax.dynamic_slice_in_dim(query_b, here, PAIR),
            jnp.zeros((PAIR,), F32),
            lax.dynamic_slice_in_dim(value_b, here, PAIR),
        ]
    )
    three = (dense(x_all, w_three) + bias3).astype(BF)
    q, k_own, v_own = three[:, :PAIR], three[:, PAIR : 2 * PAIR], three[:, 2 * PAIR :]
    same_place = [
        [(gg * chunks + s) * 2 + bb for s in range(chunks)] for gg in range(n_f) for bb in range(2)
    ]
    if chunks == 1:
        k, v = k_own, v_own
    else:
        k = lax.all_gather(k_own, "ctx", axis_index_groups=same_place, tiled=True)
        v = lax.all_gather(v_own, "ctx", axis_index_groups=same_place, tiled=True)
    att_heads, lse = attend(bounds, q, k, v, seg_q, seg_k, chunks)

    w_output = lax.all_gather(output_w, "fsdp", axis=0, tiled=True)
    attended = to_tokens(att_heads)
    branch = dense(attended, w_output) + output_b
    normed, x_hat1, inv_std1 = norm_fwd(inputs.astype(F32) + branch, attn_gain, attn_shift)
    normed_low = lax.all_gather(normed.astype(BF), "fsdp", axis=0, tiled=True)

    w_up = columns(expand_w)
    units = w_up.shape[1]
    pre_act = dense(normed_low, w_up) + lax.dynamic_slice_in_dim(expand_b, f * units, units)
    hidden = jax.nn.gelu(pre_act, approximate=False).astype(BF)
    ffn_out = lax.psum_scatter(dense(hidden, reduce_w).astype(BF), "fsdp", tiled=True).astype(F32) + reduce_b
    outputs, x_hat2, inv_std2 = norm_fwd(normed + ffn_out, ffn_gain, ffn_shift)
    layer_out = relocate(outputs.astype(BF)).reshape(tok_shape)
    grad_mid2, grad_ffn_gain, grad_ffn_shift = norm_back(upstream, x_hat2, inv_std2, ffn_gain)
    grad_ffn_own = grad_mid2.astype(BF)
    grad_reduce_b = jnp.sum(grad_ffn_own.astype(F32), axis=0)
    grad_ffn = lax.all_gather(grad_ffn_own, "fsdp", axis=0, tiled=True)
    part_down = dense_in(hidden, grad_ffn).astype(BF)
    grad_pre = (dense_back(grad_ffn, reduce_w) * gelu_slope(pre_act)).astype(BF)
    grad_expand_b = jnp.sum(grad_pre.astype(F32), axis=0)
    part_up = dense_in(normed_low, grad_pre).astype(BF)
    grad_normed = lax.psum_scatter(dense_back(grad_pre, w_up).astype(BF), "fsdp", tiled=True).astype(F32) + grad_mid2
    grad_mid1, grad_attn_gain, grad_attn_shift = norm_back(grad_normed, x_hat1, inv_std1, attn_gain)
    grad_branch = grad_mid1.astype(BF)
    grad_output_b = jnp.sum(grad_branch.astype(F32), axis=0)
    part_out = dense_in(attended, grad_branch).astype(BF)
    grad_att = to_heads(dense_back(grad_branch, w_output).astype(BF))

    grad_q, grad_k, grad_v = attend_back(
        bounds, q, k, v, seg_q, seg_k, att_heads, lse, grad_att, chunks
    )
    if chunks > 1:
        grad_k = lax.psum_scatter(
            grad_k.astype(BF), "ctx", axis_index_groups=same_place, tiled=True
        )
        grad_v = lax.psum_scatter(
            grad_v.astype(BF), "ctx", axis_index_groups=same_place, tiled=True
        )
    grad_three = jnp.concatenate([grad_q, grad_k, grad_v], axis=1)
    sums3 = jnp.sum(grad_three.astype(F32), axis=0)
    grad_query_b = lax.dynamic_update_slice_in_dim(jnp.zeros_like(query_b), sums3[:PAIR], here, 0)
    grad_value_b = lax.dynamic_update_slice_in_dim(jnp.zeros_like(value_b), sums3[2 * PAIR :], here, 0)
    here_rows = jnp.zeros((n_f, units), F32)
    sums = jnp.concatenate(
        [
            jnp.stack(
                [grad_query_b, grad_value_b, grad_output_b, grad_attn_gain, grad_attn_shift, grad_reduce_b, grad_ffn_gain, grad_ffn_shift]
            ),
            lax.dynamic_update_slice_in_dim(here_rows, grad_expand_b[None], f, 0),
            here_rows,
        ]
    )
    share_down, share_up, share_out, share_three, moved, sums = tail(
        x_all, grad_three, w_three, part_down, part_up, part_out, grad_mid1, sums
    )
    grad_inputs = moved.reshape(tok_shape).astype(F32)
    shares = tuple(part.astype(F32) for part in (share_three, share_out, share_up, share_down)) + (sums,)
    if chunks > 1:
        shares = lax.psum(shares, "ctx", axis_index_groups=same_place)
    share_three, share_out, share_up, share_down, sums = shares
    (
        grad_query_b, grad_value_b, grad_output_b, grad_attn_gain, grad_attn_shift, grad_reduce_b,
        grad_ffn_gain, grad_ffn_shift,
    ) = (sums[i] for i in range(8))
    grad_expand_b = sums[8 : 8 + n_f].reshape(-1)
    return (
        layer_out,
        grad_inputs,
        share_three[0],
        grad_query_b,
        share_three[1],
        share_three[2],
        grad_value_b,
        share_out,
        grad_output_b,
        grad_attn_gain,
        grad_attn_shift,
        share_up,
        grad_expand_b,
        share_down,
        grad_reduce_b,
        grad_ffn_gain,
        grad_ffn_shift,
    )


def solution(mesh):
    acts = P("fsdp", None, "ctx", None)
    rows = P("fsdp", None)
    return jax.shard_map(
        body,
        mesh=mesh,
        in_specs=(
            acts, rows, rows, rows, P(), rows, rows, P(), rows, P(),
            P(), P(), rows, P(), rows, P(), P(), P(), acts,
        ),
        out_specs=(
            acts, acts, rows, P(), rows, rows, P(), rows, P(),
            P(), P(), rows, P(), rows, P(), P(), P(),
        ),
        check_vma=False,
    )
```

```python
import functools
import jax
import jax.numpy as jnp
from jax import lax
from jax.experimental import pallas as pl
from jax.experimental.pallas import tpu as pltpu
from jax.sharding import PartitionSpec as P

H = 16
HD = 64
PAIR = 2 * HD
GROUP = 8
SWAP = (0, 2, 1, 3)
BF = jnp.bfloat16
F32 = jnp.float32


def dense(left, right):
    return jnp.dot(left, right, preferred_element_type=F32)


def dense_back(left, right):
    return lax.dot_general(left, right, (((1,), (1,)), ((), ())), preferred_element_type=F32)


def dense_in(left, right):
    return lax.dot_general(left, right, (((0,), (0,)), ((), ())), preferred_element_type=F32)


def norm_fwd(hidden, gain, shift):
    mean_row = jnp.mean(hidden, axis=-1, keepdims=True)
    centred = hidden - mean_row
    variance = jnp.mean(centred * centred, axis=-1, keepdims=True)
    inv_std = lax.rsqrt(variance + 1e-05)
    x_hat = centred * inv_std
    return (x_hat * gain + shift, x_hat, inv_std)


def norm_back(incoming, x_hat, inv_std, gain):
    scaled = incoming * gain
    grad_in = inv_std * (
        scaled
        - jnp.mean(scaled, axis=-1, keepdims=True)
        - x_hat * jnp.mean(scaled * x_hat, axis=-1, keepdims=True)
    )
    return (grad_in, jnp.sum(incoming * x_hat, axis=0), jnp.sum(incoming, axis=0))


def gelu_slope(pre_act):
    return (
        0.5 * (1.0 + lax.erf(pre_act * 0.7071067811865476))
        + pre_act * jnp.exp(-0.5 * pre_act * pre_act) * 0.3989422804014327
    )


def first_half(shape):
    return lax.broadcasted_iota(jnp.int32, shape, 1) < HD


def both_heads(block):
    left = first_half(block.shape)
    zero = jnp.zeros_like(block)
    return jnp.concatenate([jnp.where(left, block, zero), jnp.where(left, zero, block)], axis=0)


def by_head(stacked):
    rows = stacked.shape[0] // 2
    left = first_half((rows, stacked.shape[1]))
    return jnp.where(left, stacked[:rows], stacked[rows:])


def attend_kernel(bq, bk, chunks, lo_ref, hi_ref, q_ref, k_ref, v_ref, sq_ref, sk_ref, o_ref, lse_ref):
    nq = q_ref.shape[0] // bq
    per_chunk = k_ref.shape[0] // chunks // bk

    def q_step(i, carry):
        rows = pl.ds(pl.multiple_of(i * bq, bq), bq)
        q2 = both_heads(q_ref[rows, :] * BF(0.125))
        seg = sq_ref[rows, :]
        seg2 = jnp.concatenate([seg, seg], axis=0)

        def k_step(j, state):
            accum, run_max, run_sum = state
            keys = pl.ds(pl.multiple_of(j * bk, bk), bk)
            scores = dense_back(q2, k_ref[keys, :])
            same = seg2 == sk_ref[:, keys]
            scores = jnp.where(same, scores, -1e30)
            new_max = jnp.maximum(run_max, jnp.max(scores, axis=1, keepdims=True))
            probs = jnp.where(same, jnp.exp(scores - new_max), 0.0)
            scale = jnp.exp(run_max - new_max)
            run_sum = run_sum * scale + jnp.sum(probs, axis=1, keepdims=True)
            accum = accum * scale + dense(probs.astype(BF), v_ref[keys, :])
            return accum, new_max, run_sum

        state = (
            jnp.zeros((2 * bq, PAIR), F32),
            jnp.full((2 * bq, 1), -1e30, F32),
            jnp.zeros((2 * bq, 1), F32),
        )
        for s in range(chunks):
            base = s * per_chunk
            state = lax.fori_loop(base + lo_ref[i, s], base + hi_ref[i, s], k_step, state)
        accum, run_max, run_sum = state
        o_ref[rows, :] = by_head(accum / run_sum).astype(BF)
        lse_ref[pl.ds(pl.multiple_of(2 * i * bq, 2 * bq), 2 * bq), :] = run_max + jnp.log(run_sum)
        return carry

    lax.fori_loop(0, nq, q_step, 0)


def attend_back_kernel(
    bq, bk, chunks, lo_ref, hi_ref, q_ref, k_ref, v_ref, sq_ref, sk_ref, o_ref, lse_ref, g_ref,
    dq_ref, dk_ref, dv_ref, dk_sum, dv_sum,
):
    nq = q_ref.shape[0] // bq
    per_chunk = k_ref.shape[0] // chunks // bk
    dk_sum[...] = jnp.zeros_like(dk_sum)
    dv_sum[...] = jnp.zeros_like(dv_sum)

    def q_step(i, carry):
        rows = pl.ds(pl.multiple_of(i * bq, bq), bq)
        q2 = both_heads(q_ref[rows, :] * BF(0.125))
        grad = g_ref[rows, :]
        g2 = both_heads(grad)
        prod = grad.astype(F32) * o_ref[rows, :].astype(F32)
        left = first_half(prod.shape)
        delta = jnp.concatenate(
            [
                jnp.sum(jnp.where(left, prod, 0.0), axis=1, keepdims=True),
                jnp.sum(jnp.where(left, 0.0, prod), axis=1, keepdims=True),
            ],
            axis=0,
        )
        lse = lse_ref[pl.ds(pl.multiple_of(2 * i * bq, 2 * bq), 2 * bq), :]
        seg = sq_ref[rows, :]
        seg2 = jnp.concatenate([seg, seg], axis=0)

        def k_step(j, dq2):
            keys = pl.ds(pl.multiple_of(j * bk, bk), bk)
            key_rows = k_ref[keys, :]
            scores = dense_back(q2, key_rows)
            same = seg2 == sk_ref[:, keys]
            probs = jnp.where(same, jnp.exp(jnp.where(same, scores, -1e30) - lse), 0.0)
            grad_prob = dense_back(g2, v_ref[keys, :])
            grad_score = (probs * (grad_prob - delta)).astype(BF)
            dv_sum[keys, :] += dense_in(probs.astype(BF), g2)
            dk_sum[keys, :] += dense_in(grad_score, q2)
            return dq2 + dense(grad_score, key_rows)

        dq2 = jnp.zeros((2 * bq, PAIR), F32)
        for s in range(chunks):
            base = s * per_chunk
            dq2 = lax.fori_loop(base + lo_ref[i, s], base + hi_ref[i, s], k_step, dq2)
        dq_ref[rows, :] = (0.125 * by_head(dq2)).astype(BF)
        return carry

    lax.fori_loop(0, nq, q_step, 0)
    dk_ref[...] = dk_sum[...].astype(dk_ref.dtype)
    dv_ref[...] = dv_sum[...].astype(dv_ref.dtype)


SMEM = pl.BlockSpec(memory_space=pltpu.SMEM)
VMEM = pl.BlockSpec(memory_space=pltpu.VMEM)
BQ = 256
BK = 256


def attend(bounds, q, k, v, seg_q, seg_k, chunks):
    n = q.shape[0]
    return pl.pallas_call(
        functools.partial(attend_kernel, BQ, BK, chunks),
        out_shape=(jax.ShapeDtypeStruct((n, PAIR), BF), jax.ShapeDtypeStruct((2 * n, 1), F32)),
        in_specs=[SMEM, SMEM] + [VMEM] * 5,
        out_specs=(VMEM, VMEM),
        compiler_params=pltpu.CompilerParams(vmem_limit_bytes=48 * 2**20),
    )(*bounds, q, k, v, seg_q, seg_k)


def attend_back(bounds, q, k, v, seg_q, seg_k, out, lse, grad, chunks):
    n, m = q.shape[0], k.shape[0]
    kept = BF if chunks == 1 else F32
    return pl.pallas_call(
        functools.partial(attend_back_kernel, BQ, BK, chunks),
        out_shape=(
            jax.ShapeDtypeStruct((n, PAIR), BF),
            jax.ShapeDtypeStruct((m, PAIR), kept),
            jax.ShapeDtypeStruct((m, PAIR), kept),
        ),
        in_specs=[SMEM, SMEM] + [VMEM] * 8,
        out_specs=(VMEM, VMEM, VMEM),
        scratch_shapes=[pltpu.VMEM((m, PAIR), F32), pltpu.VMEM((m, PAIR), F32)],
        compiler_params=pltpu.CompilerParams(vmem_limit_bytes=56 * 2**20),
    )(*bounds, q, k, v, seg_q, seg_k, out, lse, grad)


def mesh_id(ctx, f):
    return {"ctx": ctx, "fsdp": f}


def swapped(i):
    return i % 2 * 2 + i // 2


class Place:
    def __init__(self):
        self.ctx = lax.axis_index("ctx")
        self.f = lax.axis_index("fsdp")
        self.per_group = lax.axis_size("ctx") // 4
        self.g = self.ctx // self.per_group
        self.b = self.ctx % 2
        self.rest = self.ctx % self.per_group
        self.core = self.f % 2
        self.x = self.f // 2

    def at(self, g=None, b=None, f=None):
        ctx = self.ctx
        if g is not None:
            ctx = ctx + (g - self.g) * self.per_group
        if b is not None:
            ctx = ctx + (b - self.b)
        return mesh_id(ctx, self.f if f is None else f)

    def sibling(self):
        return self.at(f=self.f + 1 - 2 * self.core)

    def beside(self):
        return self.at(f=(self.f + 2) % 4)

    def across(self):
        return self.at(b=1 - self.b)

    def fsdp(self, k):
        return self.at(f=(self.f + k) % 4)

    def moved(self):
        return mesh_id(swapped(self.f) * self.per_group + self.rest, swapped(self.g))

    def stays(self):
        return swapped(self.f) == self.g


def remote(src, dst, send, recv, where):
    return pltpu.make_async_remote_copy(
        src_ref=src, dst_ref=dst, send_sem=send, recv_sem=recv,
        device_id=where, device_id_type=pl.DeviceIdType.MESH,
    )


def meet(me, targets, moves):
    barrier = pltpu.get_barrier_semaphore()
    for t in targets:
        pl.semaphore_signal(barrier, 1, device_id=t, device_id_type=pl.DeviceIdType.MESH)
    if not moves:
        pl.semaphore_wait(barrier, len(targets))
        return

    @pl.when(jnp.logical_not(me.stays()))
    def _():
        pl.semaphore_signal(barrier, 1, device_id=me.moved(), device_id_type=pl.DeviceIdType.MESH)

    pl.semaphore_wait(barrier, len(targets) + jnp.where(me.stays(), 0, 1))


def tail_kernel(
    x_ref, g3_ref, w3_ref, down_ref, up_ref, out_ref, mid_ref, vec_ref,
    down_out, up_out, o_out, three_out, dx_ref, sums_ref,
    dxp, dx1, t1, xa, yb, t2a, t2b, ra, rb, moved_buf,
    yr_down, yr_up, zl, zr, zs, up_send, up_got,
    o_got, o_sum, yr_o, ol, orr, os_,
    gq, ql, qr, qs, q_send,
    vs, vr,
    s_dx, r_dx, s_y, r_y, s_z, r_zl, r_zr, s_u, r_u, s_o, r_o, s_oz, r_ol, r_or, s_q, r_ql, r_qr,
    s_qf, r_qf, s_v, r_v, s_ag, r_ag, s_ay, r_ay, loc,
):
    me = Place()
    g, b, f = me.g, me.b, me.f
    z_others = [me.at(g=(g + k) % 4) for k in (1, 2, 3)]
    meet(me, [me.across()] + [me.fsdp(k) for k in (1, 2, 3)] + z_others, True)

    y_copies = {}
    for p in (3, 0, 2, 1):
        y_copies[p] = (
            remote(down_ref.at[1 - b, p], yr_down.at[p], s_y.at[0, p], r_y.at[0, p], me.across()),
            remote(up_ref.at[:, 1 - b, p], yr_up.at[p], s_y.at[1, p], r_y.at[1, p], me.across()),
        )
        for c in y_copies[p]:
            c.start()
    o_copies = []
    for k in (1, 2, 3):
        c = remote(out_ref.at[(f + k) % 4], o_got.at[k - 1], s_o.at[k - 1], r_o.at[k - 1], me.fsdp(k))
        c.start()
        o_copies.append(c)

    def dx_step(i, carry):
        rows = pl.ds(pl.multiple_of(i * 256, 256), 256)
        part = dense_back(g3_ref[rows, :], w3_ref[...]).astype(BF)
        dxp[pl.ds(2 * i, 2)] = part.reshape(2, 2, 2, 2, 16, 1024)
        return carry

    lax.fori_loop(0, 8, dx_step, 0)
    c_core = remote(dxp.at[:, 1 - me.core], dx1, s_dx.at[0], r_dx.at[0], me.sibling())
    c_core.start()

    hops = [me.sibling(), me.beside(), me.across(), me.at(g=g + 1 - 2 * (g % 2)), me.at(g=(g + 2) % 4)]
    vec = vec_ref[...]

    def hop(i, vec):
        vs[i] = vec
        c = remote(vs.at[i], vr.at[i], s_v.at[i], r_v.at[i], hops[i])
        c.start()
        return c

    v_copies = [hop(0, vec)]

    def hop_end(i, vec):
        v_copies[i].wait()
        return vec + vr[i]

    def q_step(i, carry):
        cols = pl.ds(pl.multiple_of(i * 256, 256), 256)
        part = dense_in(x_ref[:, cols], g3_ref[...]).astype(BF)
        for j in range(3):
            gq[i, j] = part[:, j * 128 : (j + 1) * 128].reshape(4, 64, 128)
        return carry

    lax.fori_loop(0, 4, q_step, 0)

    vec = hop_end(0, vec)
    v_copies.append(hop(1, vec))

    c_core.wait()

    def t1_step(i, carry):
        t1[i] = (dxp[i, me.core].astype(F32) + dx1[i].astype(F32)).astype(BF)
        return carry

    lax.fori_loop(0, 16, t1_step, 0)
    lo, hi = pl.ds(0, 8), pl.ds(8, 8)
    c_xa = remote(t1.at[lo, 1 - me.x], xa, s_dx.at[1], r_dx.at[1], me.beside())
    c_yb = remote(t1.at[hi, :, 1 - b], yb, s_dx.at[2], r_dx.at[2], me.across())
    c_xa.start()
    c_yb.start()

    vec = hop_end(1, vec)
    v_copies.append(hop(2, vec))

    def flow(p, own, left, right, send, s_sem, l_sem, r_sem):
        @pl.when(g < p)
        def _():
            @pl.when(g > 0)
            def _():
                remote(send.at[p], left.at[p], s_sem.at[p], l_sem.at[p], me.across()).wait_recv()
                send[p] = (own(p) + left[p].astype(F32)).astype(BF)

            @pl.when(g == 0)
            def _():
                send[p] = own(p).astype(BF)

            remote(send.at[p], left.at[p], s_sem.at[p], l_sem.at[p], me.at(g=g + 1)).start()

        @pl.when(g > p)
        def _():
            @pl.when(g < 3)
            def _():
                remote(send.at[p], right.at[p], s_sem.at[p], r_sem.at[p], me.across()).wait_recv()
                send[p] = (own(p) + right[p].astype(F32)).astype(BF)

            @pl.when(g == 3)
            def _():
                send[p] = own(p).astype(BF)

            remote(send.at[p], right.at[p], s_sem.at[p], r_sem.at[p], me.at(g=g - 1)).start()

    def flow_end(own, left, right, send, s_sem, l_sem, r_sem):
        send[g] = own(g).astype(BF)

        @pl.when(g > 0)
        def _():
            remote(send.at[g], left.at[g], s_sem.at[g], l_sem.at[g], me.across()).wait_recv()
            send[g] = (send[g].astype(F32) + left[g].astype(F32)).astype(BF)

        @pl.when(g < 3)
        def _():
            remote(send.at[g], right.at[g], s_sem.at[g], r_sem.at[g], me.across()).wait_recv()
            send[g] = (send[g].astype(F32) + right[g].astype(F32)).astype(BF)

        for p in range(4):
            @pl.when(g != p)
            def _():
                remote(send.at[p], left.at[p], s_sem.at[p], l_sem.at[p], me.across()).wait_send()

    def own_q(p):
        return gq[:, :, p].astype(F32)

    q_bufs = (ql, qr, qs, s_q, r_ql, r_qr)
    for p in (3, 0, 2, 1):
        flow(p, own_q, *q_bufs)

    for c in o_copies:
        c.wait()
    o_sum[...] = (
        out_ref[f].astype(F32) + o_got[0].astype(F32) + o_got[1].astype(F32) + o_got[2].astype(F32)
    ).astype(BF)
    c_oy = remote(o_sum.at[1 - b], yr_o, s_y.at[0, 4], r_y.at[0, 4], me.across())
    c_oy.start()

    vec = hop_end(2, vec)
    v_copies.append(hop(3, vec))

    def own_big(p):
        return jnp.concatenate(
            [
                down_ref[b, p].astype(F32) + yr_down[p].astype(F32),
                (up_ref[:, b, p].astype(F32) + yr_up[p].astype(F32)).reshape(128, 1024),
            ],
            axis=0,
        )

    big_bufs = (zl, zr, zs, s_z, r_zl, r_zr)
    for p in (3, 0, 2, 1):
        for c in y_copies[p]:
            c.wait()
        flow(p, own_big, *big_bufs)

    c_xa.wait()
    t2a[...] = (t1[lo, me.x].astype(F32) + xa[...].astype(F32)).astype(BF)
    c_ra = remote(t2a.at[:, 1 - b], ra, s_dx.at[3], r_dx.at[3], me.across())
    c_ra.start()
    c_yb.wait()
    t2b[...] = (t1[hi, :, b].astype(F32) + yb[...].astype(F32)).astype(BF)
    c_rb = remote(t2b.at[:, 1 - me.x], rb, s_dx.at[4], r_dx.at[4], me.beside())
    c_rb.start()

    vec = hop_end(3, vec)
    v_copies.append(hop(4, vec))

    c_oy.wait()

    def own_o(p):
        return o_sum[b, p].astype(F32) + yr_o[p].astype(F32)

    o_bufs = (ol, orr, os_, s_oz, r_ol, r_or)
    for p in (3, 0, 2, 1):
        flow(p, own_o, *o_bufs)

    c_ra.wait()
    c_rb.wait()
    moved_buf[lo] = (t2a[:, b].astype(F32) + ra[...].astype(F32) + mid_ref[lo]).astype(BF)
    moved_buf[hi] = (t2b[:, me.x].astype(F32) + rb[...].astype(F32) + mid_ref[hi]).astype(BF)

    @pl.when(me.stays())
    def _():
        c = pltpu.make_async_copy(moved_buf, dx_ref, loc.at[0])
        c.start()
        c.wait()

    @pl.when(jnp.logical_not(me.stays()))
    def _():
        remote(moved_buf, dx_ref, s_dx.at[5], r_dx.at[5], me.moved()).start()

    def rows(size, q, other=False):
        half = 1 - b if other else b
        return pl.ds(pl.multiple_of((half * 4 + q) * size, size), size)

    def unit_cols(src):
        return pl.ds(pl.multiple_of(src * 1024, 1024), 1024)

    def head_cols(src):
        return pl.ds(pl.multiple_of((b * 4 + swapped(src)) * 128, 128), 128)

    def q_rows(q):
        return pl.ds(pl.multiple_of(q * 64, 64), 64)

    flow_end(own_q, *q_bufs)
    q_send[...] = qs[g]
    three_out[:, q_rows(g), head_cols(f)] = q_send[f]
    q_out = []
    for k in (1, 2, 3):
        c = remote(q_send.at[(f + k) % 4], three_out.at[:, q_rows(g), head_cols(f)], s_qf.at[k - 1], r_qf.at[f], me.fsdp(k))
        c.start()
        q_out.append(c)

    flow_end(own_big, *big_bufs)
    up_send[...] = zs[g, pl.ds(128, 128)].reshape(4, 32, 1024)
    down_out[rows(128, g), :] = zs[g, pl.ds(0, 128)]
    up_out[rows(32, g), unit_cols(f)] = up_send[f]
    u_out = []
    for k in (1, 2, 3):
        c = remote(up_send.at[(f + k) % 4], up_out.at[rows(32, g), unit_cols(f)], s_u.at[k - 1], r_u.at[f], me.fsdp(k))
        c.start()
        u_out.append(c)
    flow_end(own_o, *o_bufs)
    o_out[rows(32, g), :] = os_[g]

    for k in (1, 2, 3):
        src = (f + k) % 4
        remote(q_send.at[0], three_out.at[:, q_rows(g), head_cols(src)], s_qf.at[k - 1], r_qf.at[src], me.fsdp(k)).wait_recv()
        remote(up_send.at[0], up_out.at[rows(32, g), unit_cols(src)], s_u.at[k - 1], r_u.at[src], me.fsdp(k)).wait_recv()
        q_out[k - 1].wait_send()
        u_out[k - 1].wait_send()

    def pieces(q, send, recv, where, other=False):
        half = 1 - b if other else b
        parts = (
            down_out.at[rows(128, q, other), :],
            up_out.at[rows(32, q, other), :],
            o_out.at[rows(32, q, other), :],
            three_out.at[:, q_rows(q), pl.ds(pl.multiple_of(half * 512, 512), 512)],
        )
        return [remote(part, part, send.at[i, q], recv.at[i, q], where) for i, part in enumerate(parts)]

    def spread(q, to_right, to_left):
        for c in pieces(q, s_ay, r_ay, me.across()):
            c.start()
        if to_right:
            @pl.when(g < 3)
            def _():
                for c in pieces(q, s_ag.at[0], r_ag, me.at(g=g + 1)):
                    c.start()
        if to_left:
            @pl.when(g > 0)
            def _():
                for c in pieces(q, s_ag.at[1], r_ag, me.at(g=g - 1)):
                    c.start()

    spread(g, True, True)
    for d in (1, 2, 3):
        @pl.when(g >= d)
        def _():
            for c in pieces(g - d, s_ag.at[0], r_ag, me.across()):
                c.wait_recv()
            spread(g - d, True, False)

        @pl.when(g + d <= 3)
        def _():
            for c in pieces(g + d, s_ag.at[1], r_ag, me.across()):
                c.wait_recv()
            spread(g + d, False, True)

    vec = hop_end(4, vec)
    sums_ref[...] = vec

    @pl.when(jnp.logical_not(me.stays()))
    def _():
        remote(moved_buf, dx_ref, s_dx.at[5], r_dx.at[5], me.moved()).wait()

    for q in range(4):
        for c in pieces(q, s_ay, r_ay, me.across()):
            c.wait_send()

        @pl.when((g >= q) & (g < 3))
        def _():
            for c in pieces(q, s_ag.at[0], r_ag, me.across()):
                c.wait_send()

        @pl.when((g <= q) & (g > 0))
        def _():
            for c in pieces(q, s_ag.at[1], r_ag, me.across()):
                c.wait_send()

        for c in pieces(q, s_ay, r_ay, me.across(), other=True):
            c.wait_recv()


def tail(x_all, g3, w3, down, up, out, mid, vec):
    dma = pltpu.SemaphoreType.DMA
    v = pltpu.VMEM
    scratch = [
        v((16, 2, 2, 2, 16, 1024), BF), v((16, 2, 2, 16, 1024), BF), v((16, 2, 2, 16, 1024), BF),
        v((8, 2, 16, 1024), BF), v((8, 2, 16, 1024), BF), v((8, 2, 16, 1024), BF), v((8, 2, 16, 1024), BF),
        v((8, 16, 1024), BF), v((8, 16, 1024), BF), v((16, 16, 1024), BF),
        v((4, 128, 1024), BF), v((4, 4, 32, 1024), BF), v((4, 256, 1024), BF), v((4, 256, 1024), BF),
        v((4, 256, 1024), BF), v((4, 32, 1024), BF), v((4, 32, 1024), BF),
        v((3, 2, 4, 32, 1024), BF), v((2, 4, 32, 1024), BF), v((4, 32, 1024), BF),
        v((4, 32, 1024), BF), v((4, 32, 1024), BF), v((4, 32, 1024), BF),
        v((4, 3, 4, 64, 128), BF), v((4, 4, 3, 64, 128), BF), v((4, 4, 3, 64, 128), BF), v((4, 4, 3, 64, 128), BF),
        v((4, 3, 64, 128), BF),
        v((5, 16, 1024), F32), v((5, 16, 1024), F32),
        dma((6,)), dma((6,)), dma((2, 5)), dma((2, 5)), dma((4,)), dma((4,)), dma((4,)),
        dma((3,)), dma((4,)), dma((3,)), dma((3,)), dma((4,)), dma((4,)), dma((4,)), dma((4,)), dma((4,)), dma((4,)),
        dma((3,)), dma((4,)), dma((5,)), dma((5,)), dma((2, 4, 4)), dma((4, 4)), dma((4, 4)), dma((4, 4)), dma((1,)),
    ]
    return pl.pallas_call(
        tail_kernel,
        out_shape=(
            jax.ShapeDtypeStruct((1024, 1024), BF),
            jax.ShapeDtypeStruct((256, 4096), BF),
            jax.ShapeDtypeStruct((256, 1024), BF),
            jax.ShapeDtypeStruct((3, 256, 1024), BF),
            jax.ShapeDtypeStruct((16, 16, 1024), BF),
            jax.ShapeDtypeStruct((16, 1024), F32),
        ),
        in_specs=[VMEM] * 8,
        out_specs=(VMEM,) * 6,
        scratch_shapes=scratch,
        compiler_params=pltpu.CompilerParams(collective_id=1, has_side_effects=True, vmem_limit_bytes=60 * 2**20),
        cost_estimate=pl.CostEstimate(flops=4 * 10**9, bytes_accessed=40 * 2**20, transcendentals=0),
    )(x_all, g3, w3, down.reshape(2, 4, 128, 1024), up.reshape(4, 2, 4, 32, 1024), out.reshape(4, 2, 4, 32, 1024), mid.reshape(16, 16, 1024), vec)


def tile_cols(i, size):
    return pl.ds(pl.multiple_of(i * size, size), size)


def middle_kernel(
    heads_ref, x_ref, up_ref, wo_ref, wu_ref, wd_ref, par_ref,
    layer_ref, down_out, upg_out, og_out, gatt_ref, mid1_ref, vec_ref,
    att, nl, gff, slope, hid, gpre, normed, xhat, rstd, work, moved_buf, gbr, gas, ps, pr,
    s_a, r_a, s_b, r_b, s_g, r_g, s_p, r_p, s_m, r_m, loc,
):
    me = Place()
    f, b = me.f, me.b
    sib = f + 1 - 2 * me.core
    xs = (f + 2) % 4
    xo = xs + 1 - 2 * me.core
    peers = [me.at(f=(f + k % 4) % 4, b=(b + k // 4) % 2) for k in range(1, 8)]
    meet(me, peers, True)
    slot = swapped(f) * 2 + b
    unit = b * 4 + swapped(f)

    def peer_slot(k, sign):
        pf, pb = (f + sign * (k % 4) + 4) % 4, (b + k // 4) % 2
        return swapped(pf) * 2 + pb, pb * 4 + swapped(pf)

    def lanes(index):
        return pl.ds(pl.multiple_of(index * PAIR, PAIR), PAIR)

    for k in range(1, 8):
        where, _ = peer_slot(k, 1)
        remote(heads_ref.at[:, where], att.at[:, :, lanes(unit)], s_a.at[k - 1], r_a.at[k - 1], peers[k - 1]).start()
    att[:, :, lanes(unit)] = heads_ref[:, slot]
    for k in range(1, 8):
        _, theirs = peer_slot(k, -1)
        remote(heads_ref.at[:, slot], att.at[:, :, lanes(theirs)], s_a.at[k - 1], r_a.at[k - 1], peers[k - 1]).wait()

    def row(i):
        return par_ref[pl.ds(i, 1), :]

    def att_rows():
        return att[...].reshape(256, 1024)

    def proj(i, carry):
        cols = tile_cols(i, 512)
        work[:, cols] = dense(att_rows(), wo_ref[:, cols])
        return carry

    lax.fori_loop(0, 2, proj, 0)
    value, x_hat, inv = norm_fwd(x_ref[...].astype(F32) + work[...] + row(0), row(1), row(2))
    normed[...] = value
    xhat[...] = x_hat
    rstd[...] = inv
    nl[f] = value.astype(BF)

    def share(buf, t):
        to_sib = remote(buf.at[f], buf.at[f], s_g.at[t, 0], r_g.at[t, 0], me.sibling())
        to_x = remote(buf.at[f], buf.at[f], s_g.at[t, 1], r_g.at[t, 1], me.beside())
        to_x.start()
        to_sib.start()

        def from_sib():
            to_sib.wait_send()
            remote(buf.at[sib], buf.at[sib], s_g.at[t, 0], r_g.at[t, 0], me.sibling()).wait_recv()

        def from_x():
            to_x.wait_send()
            remote(buf.at[xs], buf.at[xs], s_g.at[t, 1], r_g.at[t, 1], me.beside()).wait_recv()
            remote(buf.at[xs], buf.at[xs], s_g.at[t, 2], r_g.at[t, 2], me.sibling()).start()

        def from_other():
            remote(buf.at[xs], buf.at[xs], s_g.at[t, 2], r_g.at[t, 2], me.sibling()).wait_send()
            remote(buf.at[xo], buf.at[xo], s_g.at[t, 2], r_g.at[t, 2], me.sibling()).wait_recv()

        return from_sib, from_x, from_other

    def scatter(t, i, where):
        return remote(ps.at[t, i], pr.at[t, i], s_p.at[t, i], r_p.at[t, i], where)

    def run(t, block, buf, beside_x):
        from_sib, from_x, from_other = share(buf, t)
        block(f, 3)
        from_sib()
        block(sib, 0)
        scatter(t, 0, me.sibling()).start()
        from_x()
        block(xs, 2)
        from_other()
        block(xo, 1)
        scatter(t, 1, me.sibling()).start()
        scatter(t, 1, me.sibling()).wait()
        ps[t, 2] = (ps[t, 2].astype(F32) + pr[t, 1].astype(F32)).astype(BF)
        scatter(t, 2, me.beside()).start()
        beside_x()
        scatter(t, 0, me.sibling()).wait()
        scatter(t, 2, me.beside()).wait()
        return ps[t, 3].astype(F32) + pr[t, 0].astype(F32) + pr[t, 2].astype(F32)

    def forward(index, into):
        def up_tile(i, carry):
            cols = tile_cols(i, 256)
            pre = dense(nl[index], wu_ref[:, cols]) + par_ref[pl.ds(6, 1), cols]
            cdf = 0.5 * (1.0 + lax.erf(pre * 0.7071067811865476))
            hid[index, :, cols] = (pre * cdf).astype(BF)
            slope[index, :, cols] = cdf + pre * jnp.exp(-0.5 * pre * pre) * 0.3989422804014327
            return carry

        def down_tile(i, carry):
            cols = tile_cols(i, 512)
            ps[0, into, :, cols] = dense(hid[index], wd_ref[:, cols]).astype(BF)
            return carry

        lax.fori_loop(0, 4, up_tile, 0)
        lax.fori_loop(0, 2, down_tile, 0)

    ffn = run(0, forward, nl, lambda: None)
    value, x_hat, inv = norm_fwd(normed[...] + ffn + row(3), row(4), row(5))
    moved_buf[...] = value.astype(BF)

    @pl.when(me.stays())
    def _():
        pltpu.make_async_copy(moved_buf, layer_ref, loc.at[0]).start()

    @pl.when(jnp.logical_not(me.stays()))
    def _():
        remote(moved_buf, layer_ref, s_m.at[0], r_m.at[0], me.moved()).start()

    grad2, gain2, shift2 = norm_back(up_ref[...].astype(F32), x_hat, inv, row(4))
    work[...] = grad2
    low2 = grad2.astype(BF)
    gff[f] = low2
    vec_ref[pl.ds(4, 1), :] = jnp.sum(low2.astype(F32), axis=0, keepdims=True)
    vec_ref[pl.ds(5, 1), :] = gain2[None]
    vec_ref[pl.ds(6, 1), :] = shift2[None]

    def backward(index, into):
        def pre_tile(i, carry):
            cols = tile_cols(i, 512)
            part = dense_back(gff[index], wd_ref[cols, :])
            gpre[index, :, cols] = (part * slope[index, :, cols]).astype(BF)
            return carry

        def in_tile(i, carry):
            cols = tile_cols(i, 512)
            ps[1, into, :, cols] = dense_back(gpre[index], wu_ref[cols, :]).astype(BF)
            return carry

        lax.fori_loop(0, 2, pre_tile, 0)
        lax.fori_loop(0, 2, in_tile, 0)

    def weight_grads():
        def tile(i, carry):
            cols = tile_cols(i, 256)
            down_out[cols, :] = dense_in(hid[:, :, cols].reshape(1024, 256), gff[...].reshape(1024, 1024)).astype(BF)
            upg_out[cols, :] = dense_in(nl[:, :, cols].reshape(1024, 256), gpre[...].reshape(1024, 1024)).astype(BF)
            return carry

        lax.fori_loop(0, 4, tile, 0)
        vec_ref[pl.ds(3, 1), :] = jnp.sum(gpre[...].reshape(1024, 1024).astype(F32), axis=0, keepdims=True)

    back = run(1, backward, gff, weight_grads)
    grad1, gain1, shift1 = norm_back(back + work[...], xhat[...], rstd[...], row(1))
    mid1_ref[...] = grad1
    low1 = grad1.astype(BF)
    gbr[...] = low1
    vec_ref[pl.ds(0, 1), :] = jnp.sum(low1.astype(F32), axis=0, keepdims=True)
    vec_ref[pl.ds(1, 1), :] = gain1[None]
    vec_ref[pl.ds(2, 1), :] = shift1[None]
    vec_ref[pl.ds(7, 1), :] = jnp.zeros((1, 1024), F32)

    def att_tile(i, carry):
        part = dense_back(gbr[...], wo_ref[tile_cols(i, 256), :]).astype(BF)
        for j in range(2):
            gas[2 * i + j] = part[:, j * PAIR : (j + 1) * PAIR].reshape(16, 16, PAIR)
        return carry

    lax.fori_loop(0, 4, att_tile, 0)
    for k in range(1, 8):
        _, theirs = peer_slot(k, 1)
        remote(gas.at[theirs], gatt_ref.at[:, slot], s_b.at[k - 1], r_b.at[k - 1], peers[k - 1]).start()
    gatt_ref[:, slot] = gas[unit]

    def o_tile(i, carry):
        cols = tile_cols(i, 256)
        og_out[cols, :] = dense_in(att[:, :, cols].reshape(256, 256), gbr[...]).astype(BF)
        return carry

    lax.fori_loop(0, 4, o_tile, 0)
    for k in range(1, 8):
        where, _ = peer_slot(k, -1)
        remote(gas.at[0], gatt_ref.at[:, where], s_b.at[k - 1], r_b.at[k - 1], peers[k - 1]).wait()

    @pl.when(me.stays())
    def _():
        pltpu.make_async_copy(moved_buf, layer_ref, loc.at[0]).wait()

    @pl.when(jnp.logical_not(me.stays()))
    def _():
        remote(moved_buf, layer_ref, s_m.at[0], r_m.at[0], me.moved()).wait()


def middle(heads, x, upstream, w_output, w_up, w_down, params):
    dma = pltpu.SemaphoreType.DMA
    v = pltpu.VMEM
    block = (4, 256, 1024)
    scratch = [
        v((16, 16, 1024), BF), v(block, BF), v(block, BF), v(block, F32), v(block, BF), v(block, BF),
        v((256, 1024), F32), v((256, 1024), F32), v((256, 1), F32), v((256, 1024), F32), v((256, 1024), BF),
        v((256, 1024), BF), v((8, 16, 16, PAIR), BF), v((2, 4, 256, 1024), BF), v((2, 3, 256, 1024), BF),
        dma((7,)), dma((7,)), dma((7,)), dma((7,)), dma((2, 3)), dma((2, 3)), dma((2, 3)), dma((2, 3)),
        dma((1,)), dma((1,)), dma((1,)),
    ]
    square = jax.ShapeDtypeStruct((1024, 1024), BF)
    return pl.pallas_call(
        middle_kernel,
        out_shape=(
            jax.ShapeDtypeStruct((256, 1024), BF), square, square, square,
            jax.ShapeDtypeStruct((16, 8, 16, PAIR), BF),
            jax.ShapeDtypeStruct((256, 1024), F32),
            jax.ShapeDtypeStruct((8, 1024), F32),
        ),
        in_specs=[VMEM] * 7,
        out_specs=(VMEM,) * 7,
        scratch_shapes=scratch,
        compiler_params=pltpu.CompilerParams(collective_id=2, has_side_effects=True, vmem_limit_bytes=60 * 2**20),
        cost_estimate=pl.CostEstimate(flops=14 * 10**9, bytes_accessed=20 * 2**20, transcendentals=2**21),
    )(heads.reshape(16, 8, 16, PAIR), x, upstream, w_output, w_up, w_down, params)


def body(
    tokens, lengths, packing, query_w, query_b, key_w, value_w, value_b, output_w, output_b,
    attn_gain, attn_shift, expand_w, expand_b, reduce_w, reduce_b, ffn_gain, ffn_shift, cotangent,
):
    tok_shape = tokens.shape
    laps, stripe, width = tok_shape[1], tok_shape[2], tok_shape[3]
    mine = laps * stripe
    n_ctx = lax.axis_size("ctx")
    n_f = lax.axis_size("fsdp")
    per_group = n_ctx // n_f
    chunks = per_group // 2
    ctx = lax.axis_index("ctx")
    f = lax.axis_index("fsdp")
    g = ctx // per_group
    chunk = ctx % per_group // 2
    b = ctx % 2
    swap = jnp.array(SWAP, jnp.int32)
    u = swap[f] * 2 + b
    pairs = [[2 * j, 2 * j + 1] for j in range(n_ctx // 2)]

    route = []
    for c0 in range(n_ctx):
        for f0 in range(n_f):
            g0, b0 = divmod(c0, per_group)
            route.append((c0 * n_f + f0, (SWAP[f0] * per_group + b0) * n_f + SWAP[g0]))

    def relocate(block):
        return lax.ppermute(block, ("ctx", "fsdp"), route)

    def order(block):
        return jnp.stack([block[SWAP[i]] for i in range(n_f)])

    def gather_group(block):
        both = lax.all_gather(block, "ctx", axis_index_groups=pairs)
        everyone = order(lax.all_gather(both, "fsdp"))
        everyone = everyone.reshape(GROUP, laps, stripe, -1)
        return everyone.transpose(1, 0, 2, 3).reshape(GROUP * mine, -1)

    def columns(w):
        return lax.all_to_all(w.reshape(w.shape[0], n_f, -1).transpose(1, 0, 2), "fsdp", 0, 0).reshape(
            n_f * w.shape[0], -1
        )

    row_id = swap[g]
    ordered_all = jnp.sum(
        jnp.where(
            packing[0][:, None] == jnp.arange(lengths.shape[1], dtype=jnp.int32)[None, :],
            lengths[0][None, :],
            0,
        ),
        axis=1,
    )
    ordered = lax.all_gather(ordered_all, "fsdp")[row_id]
    slots = jnp.arange(ordered.shape[0], dtype=jnp.int32)
    slot_ends = jnp.sum(jnp.where(slots[None, :] <= slots[:, None], ordered[None, :], 0), axis=1)
    span = GROUP * mine
    index = jnp.arange(span, dtype=jnp.int32)

    def segments(which):
        lap, rest = index // (GROUP * stripe), index % (GROUP * stripe)
        unit, place = rest // stripe, rest % stripe
        owner = unit // 2 * per_group + which * 2 + unit % 2
        position = lap * (n_ctx * stripe) + owner * stripe + place
        return jnp.sum((position[:, None] >= slot_ends[None, :]).astype(jnp.int32), axis=1)

    seg_q = segments(chunk)
    seg_k = jnp.concatenate([segments(s) for s in range(chunks)])
    q_first, q_last = seg_q[::BQ], seg_q[BQ - 1 :: BQ]
    k_first = seg_k[::BK].reshape(chunks, -1)
    k_last = seg_k[BK - 1 :: BK].reshape(chunks, -1)
    lo = jnp.sum((k_last[None] < q_first[:, None, None]).astype(jnp.int32), axis=2)
    hi = jnp.sum((k_first[None] <= q_last[:, None, None]).astype(jnp.int32), axis=2)
    bounds = (lo, hi)
    seg_q = seg_q[:, None]
    seg_k = seg_k[None, :]

    inputs = relocate(tokens.reshape(mine, width))
    upstream = relocate(cotangent.reshape(mine, width))
    x_all = gather_group(inputs)
    w_three = jnp.stack([query_w, key_w, value_w]).reshape(3, -1, 2, n_f, PAIR)
    w_three = lax.dynamic_index_in_dim(w_three, b, 2, keepdims=False)
    w_three = order(w_three.transpose(2, 1, 0, 3).reshape(n_f, -1, 3 * PAIR))
    w_three = lax.all_to_all(w_three, "fsdp", 0, 0).reshape(width, 3 * PAIR)
    here = (b * n_f + swap[f]) * PAIR
    bias3 = jnp.concatenate(
        [
            lax.dynamic_slice_in_dim(query_b, here, PAIR),
            jnp.zeros((PAIR,), F32),
            lax.dynamic_slice_in_dim(value_b, here, PAIR),
        ]
    )
    three = (dense(x_all, w_three) + bias3).astype(BF)
    q, k_own, v_own = three[:, :PAIR], three[:, PAIR : 2 * PAIR], three[:, 2 * PAIR :]
    same_place = [
        [(gg * chunks + s) * 2 + bb for s in range(chunks)] for gg in range(n_f) for bb in range(2)
    ]
    if chunks == 1:
        k, v = k_own, v_own
    else:
        k = lax.all_gather(k_own, "ctx", axis_index_groups=same_place, tiled=True)
        v = lax.all_gather(v_own, "ctx", axis_index_groups=same_place, tiled=True)
    att_heads, lse = attend(bounds, q, k, v, seg_q, seg_k, chunks)

    w_output = lax.all_gather(output_w, "fsdp", axis=0, tiled=True)
    w_up = columns(expand_w)
    units = w_up.shape[1]
    params = jnp.stack(
        [
            output_b, attn_gain, attn_shift, reduce_b, ffn_gain, ffn_shift,
            lax.dynamic_slice_in_dim(expand_b, f * units, units), jnp.zeros_like(output_b),
        ]
    )
    layer_out, part_down, part_up, part_out, grad_att, grad_mid1, vec = middle(
        att_heads, inputs, upstream, w_output, w_up, reduce_w, params
    )
    layer_out = layer_out.reshape(tok_shape)
    grad_att = grad_att.reshape(GROUP * mine, PAIR)

    grad_q, grad_k, grad_v = attend_back(
        bounds, q, k, v, seg_q, seg_k, att_heads, lse, grad_att, chunks
    )
    if chunks > 1:
        grad_k = lax.psum_scatter(
            grad_k.astype(BF), "ctx", axis_index_groups=same_place, tiled=True
        )
        grad_v = lax.psum_scatter(
            grad_v.astype(BF), "ctx", axis_index_groups=same_place, tiled=True
        )
    grad_three = jnp.concatenate([grad_q, grad_k, grad_v], axis=1)
    sums3 = jnp.sum(grad_three.astype(F32), axis=0)
    grad_query_b = lax.dynamic_update_slice_in_dim(jnp.zeros_like(query_b), sums3[:PAIR], here, 0)
    grad_value_b = lax.dynamic_update_slice_in_dim(jnp.zeros_like(value_b), sums3[2 * PAIR :], here, 0)
    here_rows = jnp.zeros((n_f, units), F32)
    sums = jnp.concatenate(
        [
            jnp.stack([grad_query_b, grad_value_b]),
            vec[:3],
            vec[4:7],
            lax.dynamic_update_slice_in_dim(here_rows, vec[3:4], f, 0),
            here_rows,
        ]
    )
    share_down, share_up, share_out, share_three, moved, sums = tail(
        x_all, grad_three, w_three, part_down, part_up, part_out, grad_mid1, sums
    )
    grad_inputs = moved.reshape(tok_shape).astype(F32)
    shares = tuple(part.astype(F32) for part in (share_three, share_out, share_up, share_down)) + (sums,)
    if chunks > 1:
        shares = lax.psum(shares, "ctx", axis_index_groups=same_place)
    share_three, share_out, share_up, share_down, sums = shares
    (
        grad_query_b, grad_value_b, grad_output_b, grad_attn_gain, grad_attn_shift, grad_reduce_b,
        grad_ffn_gain, grad_ffn_shift,
    ) = (sums[i] for i in range(8))
    grad_expand_b = sums[8 : 8 + n_f].reshape(-1)
    return (
        layer_out,
        grad_inputs,
        share_three[0],
        grad_query_b,
        share_three[1],
        share_three[2],
        grad_value_b,
        share_out,
        grad_output_b,
        grad_attn_gain,
        grad_attn_shift,
        share_up,
        grad_expand_b,
        share_down,
        grad_reduce_b,
        grad_ffn_gain,
        grad_ffn_shift,
    )


def solution(mesh):
    acts = P("fsdp", None, "ctx", None)
    rows = P("fsdp", None)
    return jax.shard_map(
        body,
        mesh=mesh,
        in_specs=(
            acts, rows, rows, rows, P(), rows, rows, P(), rows, P(),
            P(), P(), rows, P(), rows, P(), P(), P(), acts,
        ),
        out_specs=(
            acts, acts, rows, P(), rows, rows, P(), rows, P(),
            P(), P(), rows, P(), rows, P(), P(), P(),
        ),
        check_vma=False,
    )
```

```python
import functools
import jax
import jax.numpy as jnp
from jax import lax
from jax.experimental import pallas as pl
from jax.experimental.pallas import tpu as pltpu
from jax.sharding import PartitionSpec as P

H = 16
HD = 64
PAIR = 2 * HD
GROUP = 8
SWAP = (0, 2, 1, 3)
BF = jnp.bfloat16
F32 = jnp.float32


def dense(left, right):
    return jnp.dot(left, right, preferred_element_type=F32)


def dense_back(left, right):
    return lax.dot_general(left, right, (((1,), (1,)), ((), ())), preferred_element_type=F32)


def dense_in(left, right):
    return lax.dot_general(left, right, (((0,), (0,)), ((), ())), preferred_element_type=F32)


def norm_fwd(hidden, gain, shift):
    mean_row = jnp.mean(hidden, axis=-1, keepdims=True)
    centred = hidden - mean_row
    variance = jnp.mean(centred * centred, axis=-1, keepdims=True)
    inv_std = lax.rsqrt(variance + 1e-05)
    x_hat = centred * inv_std
    return (x_hat * gain + shift, x_hat, inv_std)


def norm_back(incoming, x_hat, inv_std, gain):
    scaled = incoming * gain
    grad_in = inv_std * (
        scaled
        - jnp.mean(scaled, axis=-1, keepdims=True)
        - x_hat * jnp.mean(scaled * x_hat, axis=-1, keepdims=True)
    )
    return (grad_in, jnp.sum(incoming * x_hat, axis=0), jnp.sum(incoming, axis=0))


def gelu_slope(pre_act):
    return (
        0.5 * (1.0 + lax.erf(pre_act * 0.7071067811865476))
        + pre_act * jnp.exp(-0.5 * pre_act * pre_act) * 0.3989422804014327
    )


def first_half(shape):
    return lax.broadcasted_iota(jnp.int32, shape, 1) < HD


def both_heads(block):
    left = first_half(block.shape)
    zero = jnp.zeros_like(block)
    return jnp.concatenate([jnp.where(left, block, zero), jnp.where(left, zero, block)], axis=0)


def by_head(stacked):
    rows = stacked.shape[0] // 2
    left = first_half((rows, stacked.shape[1]))
    return jnp.where(left, stacked[:rows], stacked[rows:])


def attend_kernel(bq, bk, chunks, lo_ref, hi_ref, q_ref, k_ref, v_ref, sq_ref, sk_ref, o_ref, lse_ref):
    nq = q_ref.shape[0] // bq
    per_chunk = k_ref.shape[0] // chunks // bk

    def q_step(i, carry):
        rows = pl.ds(pl.multiple_of(i * bq, bq), bq)
        q2 = both_heads(q_ref[rows, :] * BF(0.125))
        seg = sq_ref[rows, :]
        seg2 = jnp.concatenate([seg, seg], axis=0)

        def k_step(j, state):
            accum, run_max, run_sum = state
            keys = pl.ds(pl.multiple_of(j * bk, bk), bk)
            scores = dense_back(q2, k_ref[keys, :])
            same = seg2 == sk_ref[:, keys]
            scores = jnp.where(same, scores, -1e30)
            new_max = jnp.maximum(run_max, jnp.max(scores, axis=1, keepdims=True))
            probs = jnp.where(same, jnp.exp(scores - new_max), 0.0)
            scale = jnp.exp(run_max - new_max)
            run_sum = run_sum * scale + jnp.sum(probs, axis=1, keepdims=True)
            accum = accum * scale + dense(probs.astype(BF), v_ref[keys, :])
            return accum, new_max, run_sum

        state = (
            jnp.zeros((2 * bq, PAIR), F32),
            jnp.full((2 * bq, 1), -1e30, F32),
            jnp.zeros((2 * bq, 1), F32),
        )
        for s in range(chunks):
            base = s * per_chunk
            state = lax.fori_loop(base + lo_ref[i, s], base + hi_ref[i, s], k_step, state)
        accum, run_max, run_sum = state
        o_ref[rows, :] = by_head(accum / run_sum).astype(BF)
        lse_ref[pl.ds(pl.multiple_of(2 * i * bq, 2 * bq), 2 * bq), :] = run_max + jnp.log(run_sum)
        return carry

    lax.fori_loop(0, nq, q_step, 0)


def attend_back_kernel(
    bq, bk, chunks, lo_ref, hi_ref, q_ref, k_ref, v_ref, sq_ref, sk_ref, o_ref, lse_ref, g_ref,
    dq_ref, dk_ref, dv_ref, dk_sum, dv_sum,
):
    nq = q_ref.shape[0] // bq
    per_chunk = k_ref.shape[0] // chunks // bk
    dk_sum[...] = jnp.zeros_like(dk_sum)
    dv_sum[...] = jnp.zeros_like(dv_sum)

    def q_step(i, carry):
        rows = pl.ds(pl.multiple_of(i * bq, bq), bq)
        q2 = both_heads(q_ref[rows, :] * BF(0.125))
        grad = g_ref[rows, :]
        g2 = both_heads(grad)
        prod = grad.astype(F32) * o_ref[rows, :].astype(F32)
        left = first_half(prod.shape)
        delta = jnp.concatenate(
            [
                jnp.sum(jnp.where(left, prod, 0.0), axis=1, keepdims=True),
                jnp.sum(jnp.where(left, 0.0, prod), axis=1, keepdims=True),
            ],
            axis=0,
        )
        lse = lse_ref[pl.ds(pl.multiple_of(2 * i * bq, 2 * bq), 2 * bq), :]
        seg = sq_ref[rows, :]
        seg2 = jnp.concatenate([seg, seg], axis=0)

        def k_step(j, dq2):
            keys = pl.ds(pl.multiple_of(j * bk, bk), bk)
            key_rows = k_ref[keys, :]
            scores = dense_back(q2, key_rows)
            same = seg2 == sk_ref[:, keys]
            probs = jnp.where(same, jnp.exp(jnp.where(same, scores, -1e30) - lse), 0.0)
            grad_prob = dense_back(g2, v_ref[keys, :])
            grad_score = (probs * (grad_prob - delta)).astype(BF)
            dv_sum[keys, :] += dense_in(probs.astype(BF), g2)
            dk_sum[keys, :] += dense_in(grad_score, q2)
            return dq2 + dense(grad_score, key_rows)

        dq2 = jnp.zeros((2 * bq, PAIR), F32)
        for s in range(chunks):
            base = s * per_chunk
            dq2 = lax.fori_loop(base + lo_ref[i, s], base + hi_ref[i, s], k_step, dq2)
        dq_ref[rows, :] = (0.125 * by_head(dq2)).astype(BF)
        return carry

    lax.fori_loop(0, nq, q_step, 0)
    dk_ref[...] = dk_sum[...].astype(dk_ref.dtype)
    dv_ref[...] = dv_sum[...].astype(dv_ref.dtype)


SMEM = pl.BlockSpec(memory_space=pltpu.SMEM)
VMEM = pl.BlockSpec(memory_space=pltpu.VMEM)
BQ = 256
BK = 256


def attend(bounds, q, k, v, seg_q, seg_k, chunks):
    n = q.shape[0]
    return pl.pallas_call(
        functools.partial(attend_kernel, BQ, BK, chunks),
        out_shape=(jax.ShapeDtypeStruct((n, PAIR), BF), jax.ShapeDtypeStruct((2 * n, 1), F32)),
        in_specs=[SMEM, SMEM] + [VMEM] * 5,
        out_specs=(VMEM, VMEM),
        compiler_params=pltpu.CompilerParams(vmem_limit_bytes=48 * 2**20),
    )(*bounds, q, k, v, seg_q, seg_k)


def attend_back(bounds, q, k, v, seg_q, seg_k, out, lse, grad, chunks):
    n, m = q.shape[0], k.shape[0]
    kept = BF if chunks == 1 else F32
    return pl.pallas_call(
        functools.partial(attend_back_kernel, BQ, BK, chunks),
        out_shape=(
            jax.ShapeDtypeStruct((n, PAIR), BF),
            jax.ShapeDtypeStruct((m, PAIR), kept),
            jax.ShapeDtypeStruct((m, PAIR), kept),
        ),
        in_specs=[SMEM, SMEM] + [VMEM] * 8,
        out_specs=(VMEM, VMEM, VMEM),
        scratch_shapes=[pltpu.VMEM((m, PAIR), F32), pltpu.VMEM((m, PAIR), F32)],
        compiler_params=pltpu.CompilerParams(vmem_limit_bytes=56 * 2**20),
    )(*bounds, q, k, v, seg_q, seg_k, out, lse, grad)


def mesh_id(ctx, f):
    return {"ctx": ctx, "fsdp": f}


def swapped(i):
    return i % 2 * 2 + i // 2


class Place:
    def __init__(self):
        self.ctx = lax.axis_index("ctx")
        self.f = lax.axis_index("fsdp")
        self.per_group = lax.axis_size("ctx") // 4
        self.g = self.ctx // self.per_group
        self.b = self.ctx % 2
        self.rest = self.ctx % self.per_group
        self.core = self.f % 2
        self.x = self.f // 2

    def at(self, g=None, b=None, f=None):
        ctx = self.ctx
        if g is not None:
            ctx = ctx + (g - self.g) * self.per_group
        if b is not None:
            ctx = ctx + (b - self.b)
        return mesh_id(ctx, self.f if f is None else f)

    def sibling(self):
        return self.at(f=self.f + 1 - 2 * self.core)

    def beside(self):
        return self.at(f=(self.f + 2) % 4)

    def across(self):
        return self.at(b=1 - self.b)

    def fsdp(self, k):
        return self.at(f=(self.f + k) % 4)

    def moved(self):
        return mesh_id(swapped(self.f) * self.per_group + self.rest, swapped(self.g))

    def stays(self):
        return swapped(self.f) == self.g


def remote(src, dst, send, recv, where):
    return pltpu.make_async_remote_copy(
        src_ref=src, dst_ref=dst, send_sem=send, recv_sem=recv,
        device_id=where, device_id_type=pl.DeviceIdType.MESH,
    )


def meet(me, targets, moves):
    barrier = pltpu.get_barrier_semaphore()
    for t in targets:
        pl.semaphore_signal(barrier, 1, device_id=t, device_id_type=pl.DeviceIdType.MESH)
    if not moves:
        pl.semaphore_wait(barrier, len(targets))
        return

    @pl.when(jnp.logical_not(me.stays()))
    def _():
        pl.semaphore_signal(barrier, 1, device_id=me.moved(), device_id_type=pl.DeviceIdType.MESH)

    pl.semaphore_wait(barrier, len(targets) + jnp.where(me.stays(), 0, 1))


class Flow:
    def __init__(self, me, own, buf, got, sent, came):
        self.me, self.own, self.buf, self.got, self.sent, self.came = me, own, buf, got, sent, came
        self.low = me.g < 2
        self.inner = jnp.where((me.g == 1) | (me.g == 2), 1, 0)
        step = jnp.where(self.low, 1, -1)
        self.ahead = me.at(g=me.g + step)
        self.back_to = me.at(g=me.g - step)

    def piece(self, i):
        return jnp.where(self.low, 3 - i, i)

    def copy(self, p, side, where):
        return remote(self.buf.at[p], self.got.at[side, p], self.sent.at[p], self.came.at[side, p], where)

    def forward(self, i):
        p = self.piece(i)

        @pl.when(self.inner == 0)
        def _():
            self.buf[p] = self.own(p).astype(BF)
            self.copy(p, 0, self.ahead).start()

        if i < 2:
            @pl.when(self.inner == 1)
            def _():
                self.copy(p, 0, self.back_to).wait_recv()
                self.buf[p] = (self.own(p) + self.got[0, p].astype(F32)).astype(BF)
                self.copy(p, 1, self.ahead).start()

    def back(self):
        p = self.piece(3)

        @pl.when(self.inner == 1)
        def _():
            self.copy(p, 1, self.ahead).wait_recv()
            self.buf[p] = (self.own(p) + self.got[1, p].astype(F32)).astype(BF)
            self.copy(p, 1, self.back_to).start()

    def end(self):
        g = self.me.g

        @pl.when(self.inner == 0)
        def _():
            self.copy(g, 1, self.ahead).wait_recv()
            self.buf[g] = (self.own(g) + self.got[1, g].astype(F32)).astype(BF)

        @pl.when(self.inner == 1)
        def _():
            self.copy(g, 0, self.back_to).wait_recv()
            self.copy(g, 1, self.ahead).wait_recv()
            self.buf[g] = (self.own(g) + self.got[0, g].astype(F32) + self.got[1, g].astype(F32)).astype(BF)

        for p in range(4):
            @pl.when(g != p)
            def _():
                self.copy(p, 0, self.ahead).wait_send()


def tail_kernel(
    x_ref, g3_ref, w3_ref, down_ref, up_ref, out_ref, mid_ref, vec_ref,
    down_out, up_out, o_out, three_out, dx_ref, sums_ref,
    dxp, dx1, t1, xa, yb, t2a, t2b, ra, rb, moved_buf,
    yr_down, yr_up, dbuf, dgot, ubuf, ugot,
    o_got, o_sum, yr_o, obuf, ogot,
    gq, qbuf, qgot, vs, vr,
    s_dx, r_dx, s_y, r_y, s_d, r_d, s_z, r_z, s_u, r_u, s_o, r_o, s_oz, r_oz, s_q, r_q,
    s_qf, r_qf, s_v, r_v, s_ag, r_ag, s_ay, r_ay, loc,
):
    me = Place()
    g, b, f = me.g, me.b, me.f
    z_others = [me.at(g=(g + k) % 4) for k in (1, 2, 3)]
    meet(me, [me.across()] + [me.fsdp(k) for k in (1, 2, 3)] + z_others, True)

    def own_down(p):
        return down_ref[b, p].astype(F32) + yr_down[p].astype(F32)

    def own_up(p):
        return up_ref[:, b, p].astype(F32) + yr_up[p].astype(F32)

    def own_q(p):
        return gq[:, :, p].astype(F32)

    def own_o(p):
        return o_sum[b, p].astype(F32) + yr_o[p].astype(F32)

    flow_d = Flow(me, own_down, dbuf, dgot, s_d, r_d)
    flow_u = Flow(me, own_up, ubuf, ugot, s_z, r_z)
    flow_q = Flow(me, own_q, qbuf, qgot, s_q, r_q)
    flow_o = Flow(me, own_o, obuf, ogot, s_oz, r_oz)

    y_copies = []
    for i in range(4):
        p = flow_d.piece(i)
        pair = (
            remote(down_ref.at[1 - b, p], yr_down.at[p], s_y.at[0, i], r_y.at[0, i], me.across()),
            remote(up_ref.at[:, 1 - b, p], yr_up.at[p], s_y.at[1, i], r_y.at[1, i], me.across()),
        )
        for c in pair:
            c.start()
        y_copies.append(pair)

    hops = [me.sibling(), me.beside(), me.across(), me.at(g=g + 1 - 2 * (g % 2)), me.at(g=(g + 2) % 4)]
    vec = vec_ref[...]

    def hop(i, vec):
        vs[i] = vec
        c = remote(vs.at[i], vr.at[i], s_v.at[i], r_v.at[i], hops[i])
        c.start()
        return c

    v_copies = [hop(0, vec)]

    def hop_end(i, vec):
        v_copies[i].wait()
        return vec + vr[i]

    o_copies = []
    for k in (1, 2, 3):
        c = remote(out_ref.at[(f + k) % 4], o_got.at[k - 1], s_o.at[k - 1], r_o.at[k - 1], me.fsdp(k))
        c.start()
        o_copies.append(c)

    def q_step(i, carry):
        cols = pl.ds(pl.multiple_of(i * 256, 256), 256)
        part = dense_in(x_ref[:, cols], g3_ref[...]).astype(BF)
        for j in range(3):
            gq[i, j] = part[:, j * 128 : (j + 1) * 128].reshape(4, 64, 128)
        return carry

    lax.fori_loop(0, 4, q_step, 0)
    vec = hop_end(0, vec)
    v_copies.append(hop(1, vec))
    for i in range(3):
        @pl.when(flow_q.inner == 0)
        def _():
            flow_q.forward(i)

    def dx_step(i, carry):
        rows = pl.ds(pl.multiple_of(i * 256, 256), 256)
        part = dense_back(g3_ref[rows, :], w3_ref[...]).astype(BF)
        dxp[pl.ds(2 * i, 2)] = part.reshape(2, 2, 2, 2, 16, 1024)
        return carry

    lax.fori_loop(0, 8, dx_step, 0)
    c_core = remote(dxp.at[:, 1 - me.core], dx1, s_dx.at[0], r_dx.at[0], me.sibling())
    c_core.start()
    vec = hop_end(1, vec)
    v_copies.append(hop(2, vec))

    @pl.when(flow_q.inner == 1)
    def _():
        flow_q.forward(0)
        flow_q.forward(1)

    def large(i):
        for c in y_copies[i]:
            c.wait()
        flow_d.forward(i)
        flow_u.forward(i)

    c_core.wait()

    def t1_step(i, carry):
        t1[i] = (dxp[i, me.core].astype(F32) + dx1[i].astype(F32)).astype(BF)
        return carry

    lax.fori_loop(0, 16, t1_step, 0)
    lo, hi = pl.ds(0, 8), pl.ds(8, 8)
    c_xa = remote(t1.at[lo, 1 - me.x], xa, s_dx.at[1], r_dx.at[1], me.beside())
    c_yb = remote(t1.at[hi, :, 1 - b], yb, s_dx.at[2], r_dx.at[2], me.across())
    c_xa.start()
    c_yb.start()

    large(0)
    flow_q.back()
    large(1)

    for c in o_copies:
        c.wait()
    o_sum[...] = (
        out_ref[f].astype(F32) + o_got[0].astype(F32) + o_got[1].astype(F32) + o_got[2].astype(F32)
    ).astype(BF)
    c_oy = remote(o_sum.at[1 - b], yr_o, s_y.at[0, 4], r_y.at[0, 4], me.across())
    c_oy.start()

    large(2)
    c_xa.wait()
    t2a[...] = (t1[lo, me.x].astype(F32) + xa[...].astype(F32)).astype(BF)
    c_ra = remote(t2a.at[:, 1 - b], ra, s_dx.at[3], r_dx.at[3], me.across())
    c_ra.start()
    for c in y_copies[3]:
        c.wait()
    flow_d.back()
    flow_u.back()
    vec = hop_end(2, vec)
    v_copies.append(hop(3, vec))
    c_oy.wait()
    for i in range(3):
        flow_o.forward(i)
    c_yb.wait()
    t2b[...] = (t1[hi, :, b].astype(F32) + yb[...].astype(F32)).astype(BF)
    c_rb = remote(t2b.at[:, 1 - me.x], rb, s_dx.at[4], r_dx.at[4], me.beside())
    c_rb.start()
    flow_o.back()

    def rows(size, q, other=False):
        half = 1 - b if other else b
        return pl.ds(pl.multiple_of((half * 4 + q) * size, size), size)

    def unit_cols(src):
        return pl.ds(pl.multiple_of(src * 1024, 1024), 1024)

    def head_cols(src):
        return pl.ds(pl.multiple_of((b * 4 + swapped(src)) * 128, 128), 128)

    def q_rows(q):
        return pl.ds(pl.multiple_of(q * 64, 64), 64)

    flow_q.end()
    three_out[:, q_rows(g), head_cols(f)] = qbuf[g, f]
    q_out = []
    for k in (1, 2, 3):
        c = remote(qbuf.at[g, (f + k) % 4], three_out.at[:, q_rows(g), head_cols(f)], s_qf.at[k - 1], r_qf.at[f], me.fsdp(k))
        c.start()
        q_out.append(c)

    flow_u.end()
    up_out[rows(32, g), unit_cols(f)] = ubuf[g, f]
    u_out = []
    for k in (1, 2, 3):
        c = remote(ubuf.at[g, (f + k) % 4], up_out.at[rows(32, g), unit_cols(f)], s_u.at[k - 1], r_u.at[f], me.fsdp(k))
        c.start()
        u_out.append(c)
    flow_d.end()
    down_out[rows(128, g), :] = dbuf[g]
    flow_o.end()
    o_out[rows(32, g), :] = obuf[g]

    for k in (1, 2, 3):
        src = (f + k) % 4
        remote(qbuf.at[g, 0], three_out.at[:, q_rows(g), head_cols(src)], s_qf.at[k - 1], r_qf.at[src], me.fsdp(k)).wait_recv()
        remote(ubuf.at[g, 0], up_out.at[rows(32, g), unit_cols(src)], s_u.at[k - 1], r_u.at[src], me.fsdp(k)).wait_recv()
        q_out[k - 1].wait_send()
        u_out[k - 1].wait_send()

    def pieces(q, send, recv, where, other=False):
        half = 1 - b if other else b
        parts = (
            down_out.at[rows(128, q, other), :],
            up_out.at[rows(32, q, other), :],
            o_out.at[rows(32, q, other), :],
            three_out.at[:, q_rows(q), pl.ds(pl.multiple_of(half * 512, 512), 512)],
        )
        return [remote(part, part, send.at[i, q], recv.at[i, q], where) for i, part in enumerate(parts)]

    def spread(q, to_right, to_left):
        for c in pieces(q, s_ay, r_ay, me.across()):
            c.start()
        if to_right:
            @pl.when(g < 3)
            def _():
                for c in pieces(q, s_ag.at[0], r_ag, me.at(g=g + 1)):
                    c.start()
        if to_left:
            @pl.when(g > 0)
            def _():
                for c in pieces(q, s_ag.at[1], r_ag, me.at(g=g - 1)):
                    c.start()

    spread(g, True, True)
    c_ra.wait()
    c_rb.wait()
    moved_buf[lo] = (t2a[:, b].astype(F32) + ra[...].astype(F32) + mid_ref[lo]).astype(BF)
    moved_buf[hi] = (t2b[:, me.x].astype(F32) + rb[...].astype(F32) + mid_ref[hi]).astype(BF)

    @pl.when(me.stays())
    def _():
        c = pltpu.make_async_copy(moved_buf, dx_ref, loc.at[0])
        c.start()
        c.wait()

    @pl.when(jnp.logical_not(me.stays()))
    def _():
        remote(moved_buf, dx_ref, s_dx.at[5], r_dx.at[5], me.moved()).start()

    vec = hop_end(3, vec)
    v_copies.append(hop(4, vec))
    for d in (1, 2, 3):
        @pl.when(g >= d)
        def _():
            for c in pieces(g - d, s_ag.at[0], r_ag, me.across()):
                c.wait_recv()
            spread(g - d, True, False)

        @pl.when(g + d <= 3)
        def _():
            for c in pieces(g + d, s_ag.at[1], r_ag, me.across()):
                c.wait_recv()
            spread(g + d, False, True)

    vec = hop_end(4, vec)
    sums_ref[...] = vec

    @pl.when(jnp.logical_not(me.stays()))
    def _():
        remote(moved_buf, dx_ref, s_dx.at[5], r_dx.at[5], me.moved()).wait()

    for q in range(4):
        for c in pieces(q, s_ay, r_ay, me.across()):
            c.wait_send()

        @pl.when((g >= q) & (g < 3))
        def _():
            for c in pieces(q, s_ag.at[0], r_ag, me.across()):
                c.wait_send()

        @pl.when((g <= q) & (g > 0))
        def _():
            for c in pieces(q, s_ag.at[1], r_ag, me.across()):
                c.wait_send()

        for c in pieces(q, s_ay, r_ay, me.across(), other=True):
            c.wait_recv()


def tail(x_all, g3, w3, down, up, out, mid, vec):
    dma = pltpu.SemaphoreType.DMA
    v = pltpu.VMEM
    scratch = [
        v((16, 2, 2, 2, 16, 1024), BF), v((16, 2, 2, 16, 1024), BF), v((16, 2, 2, 16, 1024), BF),
        v((8, 2, 16, 1024), BF), v((8, 2, 16, 1024), BF), v((8, 2, 16, 1024), BF), v((8, 2, 16, 1024), BF),
        v((8, 16, 1024), BF), v((8, 16, 1024), BF), v((16, 16, 1024), BF),
        v((4, 128, 1024), BF), v((4, 4, 32, 1024), BF), v((4, 128, 1024), BF), v((2, 4, 128, 1024), BF),
        v((4, 4, 32, 1024), BF), v((2, 4, 4, 32, 1024), BF),
        v((3, 2, 4, 32, 1024), BF), v((2, 4, 32, 1024), BF), v((4, 32, 1024), BF),
        v((4, 32, 1024), BF), v((2, 4, 32, 1024), BF),
        v((4, 3, 4, 64, 128), BF), v((4, 4, 3, 64, 128), BF), v((2, 4, 4, 3, 64, 128), BF),
        v((5, 16, 1024), F32), v((5, 16, 1024), F32),
        dma((6,)), dma((6,)), dma((2, 5)), dma((2, 5)), dma((4,)), dma((2, 4)), dma((4,)), dma((2, 4)),
        dma((3,)), dma((4,)), dma((3,)), dma((3,)), dma((4,)), dma((2, 4)), dma((4,)), dma((2, 4)),
        dma((3,)), dma((4,)), dma((5,)), dma((5,)), dma((2, 4, 4)), dma((4, 4)), dma((4, 4)), dma((4, 4)), dma((1,)),
    ]
    return pl.pallas_call(
        tail_kernel,
        out_shape=(
            jax.ShapeDtypeStruct((1024, 1024), BF),
            jax.ShapeDtypeStruct((256, 4096), BF),
            jax.ShapeDtypeStruct((256, 1024), BF),
            jax.ShapeDtypeStruct((3, 256, 1024), BF),
            jax.ShapeDtypeStruct((16, 16, 1024), BF),
            jax.ShapeDtypeStruct((16, 1024), F32),
        ),
        in_specs=[VMEM] * 8,
        out_specs=(VMEM,) * 6,
        scratch_shapes=scratch,
        compiler_params=pltpu.CompilerParams(collective_id=1, has_side_effects=True, vmem_limit_bytes=60 * 2**20),
        cost_estimate=pl.CostEstimate(flops=4 * 10**9, bytes_accessed=40 * 2**20, transcendentals=0),
    )(x_all, g3, w3, down.reshape(2, 4, 128, 1024), up.reshape(4, 2, 4, 32, 1024), out.reshape(4, 2, 4, 32, 1024), mid.reshape(16, 16, 1024), vec)


def tile_cols(i, size):
    return pl.ds(pl.multiple_of(i * size, size), size)


def middle_kernel(
    heads_ref, x_ref, up_ref, wo_ref, wu_ref, wd_ref, par_ref,
    layer_ref, down_out, upg_out, og_out, gatt_ref, mid1_ref, vec_ref,
    att, nl, gff, slope, hid, gpre, normed, xhat, rstd, work, moved_buf, gbr, gas, ps, pr,
    s_a, r_a, s_b, r_b, s_g, r_g, s_p, r_p, s_m, r_m, loc,
):
    me = Place()
    f, b = me.f, me.b
    sib = f + 1 - 2 * me.core
    xs = (f + 2) % 4
    xo = xs + 1 - 2 * me.core
    peers = [me.at(f=(f + k % 4) % 4, b=(b + k // 4) % 2) for k in range(1, 8)]
    meet(me, peers, True)
    slot = swapped(f) * 2 + b
    unit = b * 4 + swapped(f)

    def peer_slot(k, sign):
        pf, pb = (f + sign * (k % 4) + 4) % 4, (b + k // 4) % 2
        return swapped(pf) * 2 + pb, pb * 4 + swapped(pf)

    def lanes(index):
        return pl.ds(pl.multiple_of(index * PAIR, PAIR), PAIR)

    for k in range(1, 8):
        where, _ = peer_slot(k, 1)
        remote(heads_ref.at[:, where], att.at[:, :, lanes(unit)], s_a.at[k - 1], r_a.at[k - 1], peers[k - 1]).start()
    att[:, :, lanes(unit)] = heads_ref[:, slot]
    for k in range(1, 8):
        _, theirs = peer_slot(k, -1)
        remote(heads_ref.at[:, slot], att.at[:, :, lanes(theirs)], s_a.at[k - 1], r_a.at[k - 1], peers[k - 1]).wait()

    def row(i):
        return par_ref[pl.ds(i, 1), :]

    def att_rows():
        return att[...].reshape(256, 1024)

    def proj(i, carry):
        cols = tile_cols(i, 512)
        work[:, cols] = dense(att_rows(), wo_ref[:, cols])
        return carry

    lax.fori_loop(0, 2, proj, 0)
    value, x_hat, inv = norm_fwd(x_ref[...].astype(F32) + work[...] + row(0), row(1), row(2))
    normed[...] = value
    xhat[...] = x_hat
    rstd[...] = inv
    nl[f] = value.astype(BF)

    def share(buf, t):
        to_sib = remote(buf.at[f], buf.at[f], s_g.at[t, 0], r_g.at[t, 0], me.sibling())
        to_x = remote(buf.at[f], buf.at[f], s_g.at[t, 1], r_g.at[t, 1], me.beside())
        to_x.start()
        to_sib.start()

        def from_sib():
            to_sib.wait_send()
            remote(buf.at[sib], buf.at[sib], s_g.at[t, 0], r_g.at[t, 0], me.sibling()).wait_recv()

        def from_x():
            to_x.wait_send()
            remote(buf.at[xs], buf.at[xs], s_g.at[t, 1], r_g.at[t, 1], me.beside()).wait_recv()
            remote(buf.at[xs], buf.at[xs], s_g.at[t, 2], r_g.at[t, 2], me.sibling()).start()

        def from_other():
            remote(buf.at[xs], buf.at[xs], s_g.at[t, 2], r_g.at[t, 2], me.sibling()).wait_send()
            remote(buf.at[xo], buf.at[xo], s_g.at[t, 2], r_g.at[t, 2], me.sibling()).wait_recv()

        return from_sib, from_x, from_other

    def scatter(t, i, where):
        return remote(ps.at[t, i], pr.at[t, i], s_p.at[t, i], r_p.at[t, i], where)

    def run(t, block, buf, beside_x):
        from_sib, from_x, from_other = share(buf, t)
        block(f, 3)
        from_sib()
        block(sib, 0)
        scatter(t, 0, me.sibling()).start()
        from_x()
        block(xs, 2)
        from_other()
        block(xo, 1)
        scatter(t, 1, me.sibling()).start()
        scatter(t, 1, me.sibling()).wait()
        ps[t, 2] = (ps[t, 2].astype(F32) + pr[t, 1].astype(F32)).astype(BF)
        scatter(t, 2, me.beside()).start()
        beside_x()
        scatter(t, 0, me.sibling()).wait()
        scatter(t, 2, me.beside()).wait()
        return ps[t, 3].astype(F32) + pr[t, 0].astype(F32) + pr[t, 2].astype(F32)

    def forward(index, into):
        def up_tile(i, carry):
            cols = tile_cols(i, 256)
            pre = dense(nl[index], wu_ref[:, cols]) + par_ref[pl.ds(6, 1), cols]
            cdf = 0.5 * (1.0 + lax.erf(pre * 0.7071067811865476))
            hid[index, :, cols] = (pre * cdf).astype(BF)
            slope[index, :, cols] = cdf + pre * jnp.exp(-0.5 * pre * pre) * 0.3989422804014327
            return carry

        def down_tile(i, carry):
            cols = tile_cols(i, 512)
            ps[0, into, :, cols] = dense(hid[index], wd_ref[:, cols]).astype(BF)
            return carry

        lax.fori_loop(0, 4, up_tile, 0)
        lax.fori_loop(0, 2, down_tile, 0)

    ffn = run(0, forward, nl, lambda: None)
    value, x_hat, inv = norm_fwd(normed[...] + ffn + row(3), row(4), row(5))
    moved_buf[...] = value.astype(BF)

    @pl.when(me.stays())
    def _():
        pltpu.make_async_copy(moved_buf, layer_ref, loc.at[0]).start()

    @pl.when(jnp.logical_not(me.stays()))
    def _():
        remote(moved_buf, layer_ref, s_m.at[0], r_m.at[0], me.moved()).start()

    grad2, gain2, shift2 = norm_back(up_ref[...].astype(F32), x_hat, inv, row(4))
    work[...] = grad2
    low2 = grad2.astype(BF)
    gff[f] = low2
    vec_ref[pl.ds(4, 1), :] = jnp.sum(low2.astype(F32), axis=0, keepdims=True)
    vec_ref[pl.ds(5, 1), :] = gain2[None]
    vec_ref[pl.ds(6, 1), :] = shift2[None]

    def backward(index, into):
        def pre_tile(i, carry):
            cols = tile_cols(i, 512)
            part = dense_back(gff[index], wd_ref[cols, :])
            gpre[index, :, cols] = (part * slope[index, :, cols]).astype(BF)
            return carry

        def in_tile(i, carry):
            cols = tile_cols(i, 512)
            ps[1, into, :, cols] = dense_back(gpre[index], wu_ref[cols, :]).astype(BF)
            return carry

        lax.fori_loop(0, 2, pre_tile, 0)
        lax.fori_loop(0, 2, in_tile, 0)

    def weight_grads():
        def tile(i, carry):
            cols = tile_cols(i, 256)
            down_out[cols, :] = dense_in(hid[:, :, cols].reshape(1024, 256), gff[...].reshape(1024, 1024)).astype(BF)
            upg_out[cols, :] = dense_in(nl[:, :, cols].reshape(1024, 256), gpre[...].reshape(1024, 1024)).astype(BF)
            return carry

        lax.fori_loop(0, 4, tile, 0)
        vec_ref[pl.ds(3, 1), :] = jnp.sum(gpre[...].reshape(1024, 1024).astype(F32), axis=0, keepdims=True)

    back = run(1, backward, gff, weight_grads)
    grad1, gain1, shift1 = norm_back(back + work[...], xhat[...], rstd[...], row(1))
    mid1_ref[...] = grad1
    low1 = grad1.astype(BF)
    gbr[...] = low1
    vec_ref[pl.ds(0, 1), :] = jnp.sum(low1.astype(F32), axis=0, keepdims=True)
    vec_ref[pl.ds(1, 1), :] = gain1[None]
    vec_ref[pl.ds(2, 1), :] = shift1[None]
    vec_ref[pl.ds(7, 1), :] = jnp.zeros((1, 1024), F32)

    def att_tile(i, carry):
        part = dense_back(gbr[...], wo_ref[tile_cols(i, 256), :]).astype(BF)
        for j in range(2):
            gas[2 * i + j] = part[:, j * PAIR : (j + 1) * PAIR].reshape(16, 16, PAIR)
        return carry

    lax.fori_loop(0, 4, att_tile, 0)
    for k in range(1, 8):
        _, theirs = peer_slot(k, 1)
        remote(gas.at[theirs], gatt_ref.at[:, slot], s_b.at[k - 1], r_b.at[k - 1], peers[k - 1]).start()
    gatt_ref[:, slot] = gas[unit]

    def o_tile(i, carry):
        cols = tile_cols(i, 256)
        og_out[cols, :] = dense_in(att[:, :, cols].reshape(256, 256), gbr[...]).astype(BF)
        return carry

    lax.fori_loop(0, 4, o_tile, 0)
    for k in range(1, 8):
        where, _ = peer_slot(k, -1)
        remote(gas.at[0], gatt_ref.at[:, where], s_b.at[k - 1], r_b.at[k - 1], peers[k - 1]).wait()

    @pl.when(me.stays())
    def _():
        pltpu.make_async_copy(moved_buf, layer_ref, loc.at[0]).wait()

    @pl.when(jnp.logical_not(me.stays()))
    def _():
        remote(moved_buf, layer_ref, s_m.at[0], r_m.at[0], me.moved()).wait()


def middle(heads, x, upstream, w_output, w_up, w_down, params):
    dma = pltpu.SemaphoreType.DMA
    v = pltpu.VMEM
    block = (4, 256, 1024)
    scratch = [
        v((16, 16, 1024), BF), v(block, BF), v(block, BF), v(block, F32), v(block, BF), v(block, BF),
        v((256, 1024), F32), v((256, 1024), F32), v((256, 1), F32), v((256, 1024), F32), v((256, 1024), BF),
        v((256, 1024), BF), v((8, 16, 16, PAIR), BF), v((2, 4, 256, 1024), BF), v((2, 3, 256, 1024), BF),
        dma((7,)), dma((7,)), dma((7,)), dma((7,)), dma((2, 3)), dma((2, 3)), dma((2, 3)), dma((2, 3)),
        dma((1,)), dma((1,)), dma((1,)),
    ]
    square = jax.ShapeDtypeStruct((1024, 1024), BF)
    return pl.pallas_call(
        middle_kernel,
        out_shape=(
            jax.ShapeDtypeStruct((256, 1024), BF), square, square, square,
            jax.ShapeDtypeStruct((16, 8, 16, PAIR), BF),
            jax.ShapeDtypeStruct((256, 1024), F32),
            jax.ShapeDtypeStruct((8, 1024), F32),
        ),
        in_specs=[VMEM] * 7,
        out_specs=(VMEM,) * 7,
        scratch_shapes=scratch,
        compiler_params=pltpu.CompilerParams(collective_id=2, has_side_effects=True, vmem_limit_bytes=60 * 2**20),
        cost_estimate=pl.CostEstimate(flops=14 * 10**9, bytes_accessed=20 * 2**20, transcendentals=2**21),
    )(heads.reshape(16, 8, 16, PAIR), x, upstream, w_output, w_up, w_down, params)


def start_kernel(
    tok_ref, cot_ref, ends_ref, qw_ref, kw_ref, vw_ref, ow_ref, ew_ref, bias_ref,
    x_ref, up_ref, ends_out, q_ref, k_ref, v_ref, w3_ref, wo_ref, wu_ref,
    s_m, r_m, s_w, r_w, s_u, r_u, s_o, r_o, s_x, r_x, loc,
):
    me = Place()
    g, b, f = me.g, me.b, me.f
    sib = f + 1 - 2 * me.core
    xs = (f + 2) % 4
    xo = xs + 1 - 2 * me.core
    meet(me, [me.across()] + [me.fsdp(k) for k in (1, 2, 3)], True)
    slot = me.core * 4 + me.x * 2 + b
    slot_x = me.core * 4 + (1 - me.x) * 2 + b
    slot_y = slot + 1 - 2 * b
    slot_d = slot_x + 1 - 2 * b
    other = 4 - 8 * me.core
    lo, hi = pl.ds(0, 8), pl.ds(8, 8)

    def moves(i, src, dst):
        return remote(src, dst, s_m.at[i], r_m.at[i], me.moved())

    def relocate(i, src, dst):
        @pl.when(me.stays())
        def _():
            pltpu.make_async_copy(src, dst, loc.at[i]).start()

        @pl.when(jnp.logical_not(me.stays()))
        def _():
            moves(i, src, dst).start()

    def relocated(i, src, dst):
        @pl.when(me.stays())
        def _():
            pltpu.make_async_copy(src, dst, loc.at[i]).wait()

        @pl.when(jnp.logical_not(me.stays()))
        def _():
            moves(i, src, dst).wait()

    theirs = x_ref.at[:, g * 2 + b]
    relocate(0, tok_ref, theirs)
    relocate(1, ends_ref, ends_out)

    def cols(index, size):
        return pl.ds(pl.multiple_of(index * size, size), size)

    def w3_rows(src):
        return cols(src, 256)

    weights = (qw_ref, kw_ref, vw_ref)
    for k in (2, 3, 1):
        dest = b * 4 + swapped((f + k) % 4)
        for j in range(3):
            remote(
                weights[j].at[:, cols(dest, 128)], w3_ref.at[w3_rows(f), pl.ds(128 * j, 128)],
                s_w.at[j, k - 1], r_w.at[j, k - 1], me.fsdp(k),
            ).start()
    for j in range(3):
        pltpu.make_async_copy(
            weights[j].at[:, cols(b * 4 + swapped(f), 128)], w3_ref.at[w3_rows(f), pl.ds(128 * j, 128)], loc.at[2 + j]
        ).start()

    half = cols(b, 128)

    def wo_rows(src, which):
        return pl.ds(pl.multiple_of(src * 256 + which * 128, 128), 128)

    o_own = pltpu.make_async_copy(ow_ref, wo_ref.at[w3_rows(f)], loc.at[5])
    o_own.start()
    o_sib = remote(ow_ref, wo_ref.at[w3_rows(f)], s_o.at[0], r_o.at[0], me.sibling())
    o_x = remote(ow_ref.at[half], wo_ref.at[wo_rows(f, b)], s_o.at[1], r_o.at[1], me.beside())
    o_x.start()
    o_sib.start()

    u_own = pltpu.make_async_copy(ew_ref.at[:, cols(f, 1024)], wu_ref.at[w3_rows(f)], loc.at[6])
    u_own.start()
    u_sib = remote(ew_ref.at[:, cols(sib, 1024)], wu_ref.at[w3_rows(f)], s_u.at[0], r_u.at[0], me.sibling())
    u_sib.start()
    u_x = [
        remote(ew_ref.at[half, cols(xs, 1024)], wu_ref.at[wo_rows(f, b)], s_u.at[1], r_u.at[1], me.beside()),
        remote(ew_ref.at[half, cols(xo, 1024)], wu_ref.at[wo_rows(f, b)], s_u.at[2], r_u.at[2], me.at(f=xo)),
    ]

    def piece(i, ref, where):
        return remote(ref, ref, s_x.at[i], r_x.at[i], where)

    relocated(0, tok_ref, theirs)
    relocate(7, cot_ref, up_ref)
    own = x_ref.at[:, slot]
    sends = [piece(1, own, me.beside()), piece(2, own, me.across()), piece(0, own, me.sibling())]
    for c in sends:
        c.start()
    piece(1, x_ref.at[:, slot_x], me.beside()).wait_recv()
    more = [piece(4, x_ref.at[hi, slot_x], me.across()), piece(3, x_ref.at[:, slot_x], me.sibling())]
    for c in more:
        c.start()
    sends += more
    piece(2, x_ref.at[:, slot_y], me.across()).wait_recv()
    more = [piece(6, x_ref.at[lo, slot_y], me.beside()), piece(5, x_ref.at[:, slot_y], me.sibling())]
    for c in more:
        c.start()
    sends += more
    for c in u_x:
        c.start()
    o_x.wait()
    o_fwd = [
        remote(wo_ref.at[wo_rows(xs, b)], wo_ref.at[wo_rows(xs, b)], s_o.at[2], r_o.at[2], me.sibling()),
        remote(wo_ref.at[wo_rows(xs, b)], wo_ref.at[wo_rows(xs, b)], s_o.at[3], r_o.at[3], me.across()),
    ]
    for c in o_fwd:
        c.start()
    piece(4, x_ref.at[hi, slot_d], me.across()).wait_recv()
    more = [piece(8, x_ref.at[hi, slot_d], me.sibling())]
    more[0].start()
    piece(6, x_ref.at[lo, slot_d], me.beside()).wait_recv()
    more.append(piece(7, x_ref.at[lo, slot_d], me.sibling()))
    more[1].start()
    sends += more
    for k in (1, 2, 3):
        src = (f + 4 - k) % 4
        for j in range(3):
            remote(
                weights[j].at[:, cols(0, 128)], w3_ref.at[w3_rows(src), pl.ds(128 * j, 128)],
                s_w.at[j, k - 1], r_w.at[j, k - 1], me.fsdp(k),
            ).wait()
    for j in range(3):
        pltpu.make_async_copy(
            weights[j].at[:, cols(b * 4 + swapped(f), 128)], w3_ref.at[w3_rows(f), pl.ds(128 * j, 128)], loc.at[2 + j]
        ).wait()
    o_fwd[0].wait()
    o_fwd[1].wait()
    late = remote(wo_ref.at[wo_rows(xs, 1 - b)], wo_ref.at[wo_rows(xs, 1 - b)], s_o.at[4], r_o.at[4], me.sibling())
    late.start()
    for i, where, part in (
        (0, own, slot + other), (3, own, slot_x + other), (5, own, slot_y + other),
    ):
        piece(i, x_ref.at[:, part], me.sibling()).wait_recv()
    piece(8, x_ref.at[hi, slot_d + other], me.sibling()).wait_recv()
    piece(7, x_ref.at[lo, slot_d + other], me.sibling()).wait_recv()

    def project(i, carry):
        part = dense(x_ref[pl.ds(2 * i, 2)].reshape(256, 1024), w3_ref[...]) + bias_ref[...]
        part = part.astype(BF)
        rows = cols(i, 256)
        q_ref[rows, :] = part[:, :PAIR]
        k_ref[rows, :] = part[:, PAIR : 2 * PAIR]
        v_ref[rows, :] = part[:, 2 * PAIR :]
        return carry

    lax.fori_loop(0, 8, project, 0)

    for i, c in enumerate(u_x):
        c.wait()
    u_fwd = [
        remote(wu_ref.at[wo_rows(src, b)], wu_ref.at[wo_rows(src, b)], s_u.at[3 + i], r_u.at[3 + i], me.across())
        for i, src in enumerate((xs, xo))
    ]
    for c in u_fwd:
        c.start()
    for c in sends:
        c.wait_send()
    late.wait()
    o_own.wait()
    o_sib.wait()
    u_own.wait()
    u_sib.wait()
    relocated(1, ends_ref, ends_out)
    relocated(7, cot_ref, up_ref)
    for c in u_fwd:
        c.wait()


def start(tokens, cotangent, ends, query_w, key_w, value_w, output_w, expand_w, bias3):
    dma = pltpu.SemaphoreType.DMA
    hbm = pl.BlockSpec(memory_space=pl.ANY)
    heads = jax.ShapeDtypeStruct((2048, PAIR), BF)
    square = jax.ShapeDtypeStruct((1024, 1024), BF)
    return pl.pallas_call(
        start_kernel,
        out_shape=(
            jax.ShapeDtypeStruct((16, GROUP, 16, 1024), BF), jax.ShapeDtypeStruct((16, 16, 1024), BF),
            jax.ShapeDtypeStruct((8, 128), jnp.int32), heads, heads, heads,
            jax.ShapeDtypeStruct((1024, 3 * PAIR), BF), square, square,
        ),
        in_specs=[hbm, hbm, VMEM] + [hbm] * 5 + [VMEM],
        out_specs=(VMEM,) * 9,
        scratch_shapes=[
            dma((8,)), dma((8,)), dma((3, 3)), dma((3, 3)), dma((5,)), dma((5,)), dma((5,)), dma((5,)),
            dma((9,)), dma((9,)), dma((8,)),
        ],
        compiler_params=pltpu.CompilerParams(collective_id=3, has_side_effects=True, vmem_limit_bytes=40 * 2**20),
        cost_estimate=pl.CostEstimate(flops=2 * 10**9, bytes_accessed=20 * 2**20, transcendentals=0),
    )(tokens, cotangent, ends, query_w, key_w, value_w, output_w, expand_w, bias3)


def body(
    tokens, lengths, packing, query_w, query_b, key_w, value_w, value_b, output_w, output_b,
    attn_gain, attn_shift, expand_w, expand_b, reduce_w, reduce_b, ffn_gain, ffn_shift, cotangent,
):
    tok_shape = tokens.shape
    laps, stripe, width = tok_shape[1], tok_shape[2], tok_shape[3]
    mine = laps * stripe
    n_ctx = lax.axis_size("ctx")
    n_f = lax.axis_size("fsdp")
    per_group = n_ctx // n_f
    chunks = per_group // 2
    ctx = lax.axis_index("ctx")
    f = lax.axis_index("fsdp")
    g = ctx // per_group
    chunk = ctx % per_group // 2
    b = ctx % 2
    same_place = [
        [(gg * chunks + s) * 2 + bb for s in range(chunks)] for gg in range(n_f) for bb in range(2)
    ]
    units = expand_w.shape[1] // n_f

    ordered = jnp.sum(
        jnp.where(
            packing[0][:, None] == jnp.arange(lengths.shape[1], dtype=jnp.int32)[None, :],
            lengths[0][None, :],
            0,
        ),
        axis=1,
    )
    slots = jnp.arange(ordered.shape[0], dtype=jnp.int32)
    own_ends = jnp.sum(jnp.where(slots[None, :] <= slots[:, None], ordered[None, :], 0), axis=1)
    own_ends = jnp.pad(own_ends[None], ((0, 7), (0, 128 - own_ends.shape[0])))

    here = (b * n_f + swapped(f)) * PAIR
    bias3 = jnp.concatenate(
        [
            lax.dynamic_slice_in_dim(query_b, here, PAIR),
            jnp.zeros((PAIR,), F32),
            lax.dynamic_slice_in_dim(value_b, here, PAIR),
        ]
    )[None]
    acts = (laps, stripe, width)
    x_all, upstream, ends, q, k_own, v_own, w_three, w_output, w_up = start(
        tokens.reshape(acts), cotangent.reshape(acts), own_ends, query_w, key_w, value_w, output_w, expand_w, bias3
    )
    inputs = lax.dynamic_index_in_dim(x_all, swapped(f) * 2 + b, 1, keepdims=False).reshape(mine, width)
    x_all = x_all.reshape(GROUP * mine, width)
    upstream = upstream.reshape(mine, width)
    slot_ends = ends[0, : ordered.shape[0]]

    span = GROUP * mine
    index = jnp.arange(span, dtype=jnp.int32)

    def segments(which):
        lap, rest = index // (GROUP * stripe), index % (GROUP * stripe)
        unit, place = rest // stripe, rest % stripe
        owner = unit // 2 * per_group + which * 2 + unit % 2
        position = lap * (n_ctx * stripe) + owner * stripe + place
        return jnp.sum((position[:, None] >= slot_ends[None, :]).astype(jnp.int32), axis=1)

    seg_q = segments(chunk)
    seg_k = jnp.concatenate([segments(s) for s in range(chunks)])
    q_first, q_last = seg_q[::BQ], seg_q[BQ - 1 :: BQ]
    k_first = seg_k[::BK].reshape(chunks, -1)
    k_last = seg_k[BK - 1 :: BK].reshape(chunks, -1)
    lo = jnp.sum((k_last[None] < q_first[:, None, None]).astype(jnp.int32), axis=2)
    hi = jnp.sum((k_first[None] <= q_last[:, None, None]).astype(jnp.int32), axis=2)
    bounds = (lo, hi)
    seg_q = seg_q[:, None]
    seg_k = seg_k[None, :]

    if chunks == 1:
        k, v = k_own, v_own
    else:
        k = lax.all_gather(k_own, "ctx", axis_index_groups=same_place, tiled=True)
        v = lax.all_gather(v_own, "ctx", axis_index_groups=same_place, tiled=True)
    att_heads, lse = attend(bounds, q, k, v, seg_q, seg_k, chunks)

    params = jnp.stack(
        [
            output_b, attn_gain, attn_shift, reduce_b, ffn_gain, ffn_shift,
            lax.dynamic_slice_in_dim(expand_b, f * units, units), jnp.zeros_like(output_b),
        ]
    )
    layer_out, part_down, part_up, part_out, grad_att, grad_mid1, vec = middle(
        att_heads, inputs, upstream, w_output, w_up, reduce_w, params
    )
    layer_out = layer_out.reshape(tok_shape)
    grad_att = grad_att.reshape(GROUP * mine, PAIR)

    grad_q, grad_k, grad_v = attend_back(
        bounds, q, k, v, seg_q, seg_k, att_heads, lse, grad_att, chunks
    )
    if chunks > 1:
        grad_k = lax.psum_scatter(
            grad_k.astype(BF), "ctx", axis_index_groups=same_place, tiled=True
        )
        grad_v = lax.psum_scatter(
            grad_v.astype(BF), "ctx", axis_index_groups=same_place, tiled=True
        )
    grad_three = jnp.concatenate([grad_q, grad_k, grad_v], axis=1)
    sums3 = jnp.sum(grad_three.astype(F32), axis=0)
    grad_query_b = lax.dynamic_update_slice_in_dim(jnp.zeros_like(query_b), sums3[:PAIR], here, 0)
    grad_value_b = lax.dynamic_update_slice_in_dim(jnp.zeros_like(value_b), sums3[2 * PAIR :], here, 0)
    here_rows = jnp.zeros((n_f, units), F32)
    sums = jnp.concatenate(
        [
            jnp.stack([grad_query_b, grad_value_b]),
            vec[:3],
            vec[4:7],
            lax.dynamic_update_slice_in_dim(here_rows, vec[3:4], f, 0),
            here_rows,
        ]
    )
    share_down, share_up, share_out, share_three, moved, sums = tail(
        x_all, grad_three, w_three, part_down, part_up, part_out, grad_mid1, sums
    )
    grad_inputs = moved.reshape(tok_shape).astype(F32)
    shares = tuple(part.astype(F32) for part in (share_three, share_out, share_up, share_down)) + (sums,)
    if chunks > 1:
        shares = lax.psum(shares, "ctx", axis_index_groups=same_place)
    share_three, share_out, share_up, share_down, sums = shares
    (
        grad_query_b, grad_value_b, grad_output_b, grad_attn_gain, grad_attn_shift, grad_reduce_b,
        grad_ffn_gain, grad_ffn_shift,
    ) = (sums[i] for i in range(8))
    grad_expand_b = sums[8 : 8 + n_f].reshape(-1)
    return (
        layer_out,
        grad_inputs,
        share_three[0],
        grad_query_b,
        share_three[1],
        share_three[2],
        grad_value_b,
        share_out,
        grad_output_b,
        grad_attn_gain,
        grad_attn_shift,
        share_up,
        grad_expand_b,
        share_down,
        grad_reduce_b,
        grad_ffn_gain,
        grad_ffn_shift,
    )


def solution(mesh):
    acts = P("fsdp", None, "ctx", None)
    rows = P("fsdp", None)
    return jax.shard_map(
        body,
        mesh=mesh,
        in_specs=(
            acts, rows, rows, rows, P(), rows, rows, P(), rows, P(),
            P(), P(), rows, P(), rows, P(), P(), P(), acts,
        ),
        out_specs=(
            acts, acts, rows, P(), rows, rows, P(), rows, P(),
            P(), P(), rows, P(), rows, P(), P(), P(),
        ),
        check_vma=False,
    )
```

```python
import functools
import jax
import jax.numpy as jnp
from jax import lax
from jax.experimental import pallas as pl
from jax.experimental.pallas import tpu as pltpu
from jax.sharding import PartitionSpec as P

H = 16
HD = 64
PAIR = 2 * HD
GROUP = 8
SWAP = (0, 2, 1, 3)
BF = jnp.bfloat16
F32 = jnp.float32


def dense(left, right):
    return jnp.dot(left, right, preferred_element_type=F32)


def dense_back(left, right):
    return lax.dot_general(left, right, (((1,), (1,)), ((), ())), preferred_element_type=F32)


def dense_in(left, right):
    return lax.dot_general(left, right, (((0,), (0,)), ((), ())), preferred_element_type=F32)


def norm_fwd(hidden, gain, shift):
    mean_row = jnp.mean(hidden, axis=-1, keepdims=True)
    centred = hidden - mean_row
    variance = jnp.mean(centred * centred, axis=-1, keepdims=True)
    inv_std = lax.rsqrt(variance + 1e-05)
    x_hat = centred * inv_std
    return (x_hat * gain + shift, x_hat, inv_std)


def norm_back(incoming, x_hat, inv_std, gain):
    scaled = incoming * gain
    grad_in = inv_std * (
        scaled
        - jnp.mean(scaled, axis=-1, keepdims=True)
        - x_hat * jnp.mean(scaled * x_hat, axis=-1, keepdims=True)
    )
    return (grad_in, jnp.sum(incoming * x_hat, axis=0), jnp.sum(incoming, axis=0))


def gelu_slope(pre_act):
    return (
        0.5 * (1.0 + lax.erf(pre_act * 0.7071067811865476))
        + pre_act * jnp.exp(-0.5 * pre_act * pre_act) * 0.3989422804014327
    )


def first_half(shape):
    return lax.broadcasted_iota(jnp.int32, shape, 1) < HD


def both_heads(block):
    left = first_half(block.shape)
    zero = jnp.zeros_like(block)
    return jnp.concatenate([jnp.where(left, block, zero), jnp.where(left, zero, block)], axis=0)


def by_head(stacked):
    rows = stacked.shape[0] // 2
    left = first_half((rows, stacked.shape[1]))
    return jnp.where(left, stacked[:rows], stacked[rows:])


def attend_kernel(bq, bk, chunks, lo_ref, hi_ref, q_ref, k_ref, v_ref, sq_ref, sk_ref, o_ref, lse_ref):
    nq = q_ref.shape[0] // bq
    per_chunk = k_ref.shape[0] // chunks // bk

    def q_step(i, carry):
        rows = pl.ds(pl.multiple_of(i * bq, bq), bq)
        q2 = both_heads(q_ref[rows, :] * BF(0.125))
        seg = sq_ref[rows, :]
        seg2 = jnp.concatenate([seg, seg], axis=0)

        def k_step(j, state):
            accum, run_max, run_sum = state
            keys = pl.ds(pl.multiple_of(j * bk, bk), bk)
            scores = dense_back(q2, k_ref[keys, :])
            same = seg2 == sk_ref[:, keys]
            scores = jnp.where(same, scores, -1e30)
            new_max = jnp.maximum(run_max, jnp.max(scores, axis=1, keepdims=True))
            probs = jnp.exp(scores - new_max)
            scale = jnp.exp(run_max - new_max)
            run_sum = run_sum * scale + jnp.sum(probs, axis=1, keepdims=True)
            accum = accum * scale + dense(probs.astype(BF), v_ref[keys, :])
            return accum, new_max, run_sum

        state = (
            jnp.zeros((2 * bq, PAIR), F32),
            jnp.full((2 * bq, 1), -1e30, F32),
            jnp.zeros((2 * bq, 1), F32),
        )
        for s in range(chunks):
            base = s * per_chunk
            state = lax.fori_loop(base + lo_ref[i, s], base + hi_ref[i, s], k_step, state)
        accum, run_max, run_sum = state
        o_ref[rows, :] = by_head(accum / run_sum).astype(BF)
        lse_ref[pl.ds(pl.multiple_of(2 * i * bq, 2 * bq), 2 * bq), :] = run_max + jnp.log(run_sum)
        return carry

    lax.fori_loop(0, nq, q_step, 0)


def attend_back_rows(i, bq, bk, ranges, q_ref, k_ref, v_ref, sq_ref, sk_ref, o_ref, lse_ref, g_ref, dk_sum, dv_sum):
    rows = pl.ds(pl.multiple_of(i * bq, bq), bq)
    q2 = both_heads(q_ref[rows, :] * BF(0.125))
    grad = g_ref[rows, :]
    g2 = both_heads(grad)
    prod = grad.astype(F32) * o_ref[rows, :].astype(F32)
    left = first_half(prod.shape)
    delta = jnp.concatenate(
        [
            jnp.sum(jnp.where(left, prod, 0.0), axis=1, keepdims=True),
            jnp.sum(jnp.where(left, 0.0, prod), axis=1, keepdims=True),
        ],
        axis=0,
    )
    lse = lse_ref[pl.ds(pl.multiple_of(2 * i * bq, 2 * bq), 2 * bq), :]
    seg = sq_ref[rows, :]
    seg2 = jnp.concatenate([seg, seg], axis=0)

    def k_step(j, dq2):
        keys = pl.ds(pl.multiple_of(j * bk, bk), bk)
        key_rows = k_ref[keys, :]
        scores = dense_back(q2, key_rows)
        same = seg2 == sk_ref[:, keys]
        probs = jnp.exp(jnp.where(same, scores, -1e30) - lse)
        grad_prob = dense_back(g2, v_ref[keys, :])
        grad_score = (probs * (grad_prob - delta)).astype(BF)
        dv_sum[keys, :] += dense_in(probs.astype(BF), g2)
        dk_sum[keys, :] += dense_in(grad_score, q2)
        return dq2 + dense(grad_score, key_rows)

    dq2 = jnp.zeros((2 * bq, PAIR), F32)
    for first, last in ranges:
        dq2 = lax.fori_loop(first, last, k_step, dq2)
    return (0.125 * by_head(dq2)).astype(BF)


def attend_back_kernel(
    bq, bk, chunks, lo_ref, hi_ref, q_ref, k_ref, v_ref, sq_ref, sk_ref, o_ref, lse_ref, g_ref,
    dq_ref, dk_ref, dv_ref, dk_sum, dv_sum,
):
    nq = q_ref.shape[0] // bq
    per_chunk = k_ref.shape[0] // chunks // bk
    dk_sum[...] = jnp.zeros_like(dk_sum)
    dv_sum[...] = jnp.zeros_like(dv_sum)

    def q_step(i, carry):
        ranges = [(s * per_chunk + lo_ref[i, s], s * per_chunk + hi_ref[i, s]) for s in range(chunks)]
        dq_ref[pl.ds(pl.multiple_of(i * bq, bq), bq), :] = attend_back_rows(
            i, bq, bk, ranges, q_ref, k_ref, v_ref, sq_ref, sk_ref, o_ref, lse_ref, g_ref, dk_sum, dv_sum
        )
        return carry

    lax.fori_loop(0, nq, q_step, 0)
    dk_ref[...] = dk_sum[...].astype(dk_ref.dtype)
    dv_ref[...] = dv_sum[...].astype(dv_ref.dtype)


SMEM = pl.BlockSpec(memory_space=pltpu.SMEM)
VMEM = pl.BlockSpec(memory_space=pltpu.VMEM)
BQ = 256
BK = 256


def attend(bounds, q, k, v, seg_q, seg_k, chunks):
    n = q.shape[0]
    return pl.pallas_call(
        functools.partial(attend_kernel, BQ, BK, chunks),
        out_shape=(jax.ShapeDtypeStruct((n, PAIR), BF), jax.ShapeDtypeStruct((2 * n, 1), F32)),
        in_specs=[SMEM, SMEM] + [VMEM] * 5,
        out_specs=(VMEM, VMEM),
        compiler_params=pltpu.CompilerParams(vmem_limit_bytes=48 * 2**20),
    )(*bounds, q, k, v, seg_q, seg_k)


def attend_back(bounds, q, k, v, seg_q, seg_k, out, lse, grad, chunks):
    n, m = q.shape[0], k.shape[0]
    kept = BF if chunks == 1 else F32
    return pl.pallas_call(
        functools.partial(attend_back_kernel, BQ, BK, chunks),
        out_shape=(
            jax.ShapeDtypeStruct((n, PAIR), BF),
            jax.ShapeDtypeStruct((m, PAIR), kept),
            jax.ShapeDtypeStruct((m, PAIR), kept),
        ),
        in_specs=[SMEM, SMEM] + [VMEM] * 8,
        out_specs=(VMEM, VMEM, VMEM),
        scratch_shapes=[pltpu.VMEM((m, PAIR), F32), pltpu.VMEM((m, PAIR), F32)],
        compiler_params=pltpu.CompilerParams(vmem_limit_bytes=56 * 2**20),
    )(*bounds, q, k, v, seg_q, seg_k, out, lse, grad)


def mesh_id(ctx, f):
    return {"ctx": ctx, "fsdp": f}


def swapped(i):
    return i % 2 * 2 + i // 2


class Place:
    def __init__(self):
        self.ctx = lax.axis_index("ctx")
        self.f = lax.axis_index("fsdp")
        self.per_group = lax.axis_size("ctx") // 4
        self.g = self.ctx // self.per_group
        self.b = self.ctx % 2
        self.rest = self.ctx % self.per_group
        self.core = self.f % 2
        self.x = self.f // 2

    def at(self, g=None, b=None, f=None):
        ctx = self.ctx
        if g is not None:
            ctx = ctx + (g - self.g) * self.per_group
        if b is not None:
            ctx = ctx + (b - self.b)
        return mesh_id(ctx, self.f if f is None else f)

    def sibling(self):
        return self.at(f=self.f + 1 - 2 * self.core)

    def beside(self):
        return self.at(f=(self.f + 2) % 4)

    def across(self):
        return self.at(b=1 - self.b)

    def fsdp(self, k):
        return self.at(f=(self.f + k) % 4)

    def moved(self):
        return mesh_id(swapped(self.f) * self.per_group + self.rest, swapped(self.g))

    def stays(self):
        return swapped(self.f) == self.g


def remote(src, dst, send, recv, where):
    return pltpu.make_async_remote_copy(
        src_ref=src, dst_ref=dst, send_sem=send, recv_sem=recv,
        device_id=where, device_id_type=pl.DeviceIdType.MESH,
    )


def meet(me, targets, moves):
    barrier = pltpu.get_barrier_semaphore()
    for t in targets:
        pl.semaphore_signal(barrier, 1, device_id=t, device_id_type=pl.DeviceIdType.MESH)
    if not moves:
        pl.semaphore_wait(barrier, len(targets))
        return

    @pl.when(jnp.logical_not(me.stays()))
    def _():
        pl.semaphore_signal(barrier, 1, device_id=me.moved(), device_id_type=pl.DeviceIdType.MESH)

    pl.semaphore_wait(barrier, len(targets) + jnp.where(me.stays(), 0, 1))


class Flow:
    def __init__(self, me, own, buf, got, sent, came):
        self.me, self.own, self.buf, self.got, self.sent, self.came = me, own, buf, got, sent, came
        self.low = me.g < 2
        self.inner = jnp.where((me.g == 1) | (me.g == 2), 1, 0)
        step = jnp.where(self.low, 1, -1)
        self.ahead = me.at(g=me.g + step)
        self.back_to = me.at(g=me.g - step)

    def piece(self, i):
        return jnp.where(self.low, 3 - i, i)

    def copy(self, p, side, where):
        return remote(self.buf.at[p], self.got.at[side, p], self.sent.at[p], self.came.at[side, p], where)

    def forward(self, i):
        p = self.piece(i)

        @pl.when(self.inner == 0)
        def _():
            self.buf[p] = self.own(p).astype(BF)
            self.copy(p, 0, self.ahead).start()

        if i < 2:
            @pl.when(self.inner == 1)
            def _():
                self.copy(p, 0, self.back_to).wait_recv()
                self.buf[p] = (self.own(p) + self.got[0, p].astype(F32)).astype(BF)
                self.copy(p, 1, self.ahead).start()

    def back(self):
        p = self.piece(3)

        @pl.when(self.inner == 1)
        def _():
            self.copy(p, 1, self.ahead).wait_recv()
            self.buf[p] = (self.own(p) + self.got[1, p].astype(F32)).astype(BF)
            self.copy(p, 1, self.back_to).start()

    def end(self):
        g = self.me.g

        @pl.when(self.inner == 0)
        def _():
            self.copy(g, 1, self.ahead).wait_recv()
            self.buf[g] = (self.own(g) + self.got[1, g].astype(F32)).astype(BF)

        @pl.when(self.inner == 1)
        def _():
            self.copy(g, 0, self.back_to).wait_recv()
            self.copy(g, 1, self.ahead).wait_recv()
            self.buf[g] = (self.own(g) + self.got[0, g].astype(F32) + self.got[1, g].astype(F32)).astype(BF)

        for p in range(4):
            @pl.when(g != p)
            def _():
                self.copy(p, 0, self.ahead).wait_send()


QUARTERS = ((0, 2), (0, 3), (1, 4), (2, 4))


def tail_kernel(fused, *refs):
    if fused:
        attention, refs, (g3_ref, dk_sum, dv_sum) = refs[:8], refs[8:-3], refs[-3:]
        tail_steps(attention, dk_sum, dv_sum, refs[0], g3_ref, *refs[1:])
    else:
        tail_steps(None, None, None, *refs)


def tail_steps(
    attention, dk_sum, dv_sum,
    x_ref, g3_ref, w3_ref, down_ref, up_ref, out_ref, mid_ref, vec_ref,
    down_out, up_out, o_out, three_out, dx_ref, sums_ref,
    dxp, dx1, t1, xa, yb, t2a, t2b, ra, rb, moved_buf,
    yr_up, dbuf, dgot, ubuf, ugot,
    o_got, o_sum, yr_o, obuf, ogot,
    gq, qbuf, qgot, vs, vr,
    s_dx, r_dx, s_y, r_y, s_d, r_d, s_z, r_z, s_u, r_u, s_o, r_o, s_oz, r_oz, s_q, r_q,
    s_qf, r_qf, s_v, r_v, s_ag, r_ag, s_ay, r_ay, loc,
):
    me = Place()
    g, b, f = me.g, me.b, me.f
    z_others = [me.at(g=(g + k) % 4) for k in (1, 2, 3)]
    meet(me, [me.across()] + [me.fsdp(k) for k in (1, 2, 3)] + z_others, True)

    def own_down(p):
        return down_ref[p].astype(F32)

    def own_up(p):
        return up_ref[:, b, p].astype(F32) + yr_up[p].astype(F32)

    def own_q(p):
        return gq[:, :, p].astype(F32)

    def own_o(p):
        return o_sum[b, p].astype(F32) + yr_o[p].astype(F32)

    flow_d = Flow(me, own_down, dbuf, dgot, s_d, r_d)
    flow_u = Flow(me, own_up, ubuf, ugot, s_z, r_z)
    flow_q = Flow(me, own_q, qbuf, qgot, s_q, r_q)
    flow_o = Flow(me, own_o, obuf, ogot, s_oz, r_oz)

    edge, inner = flow_d.inner == 0, flow_d.inner == 1

    def at(which, *steps):
        @pl.when(which)
        def _():
            for step in steps:
                step()

    y_copies = []
    for i in range(4):
        p = flow_u.piece(i)
        c = remote(up_ref.at[:, 1 - b, p], yr_up.at[p], s_y.at[0, i], r_y.at[0, i], me.across())
        c.start()
        y_copies.append(c)

    o_copies = []
    for k in (1, 2, 3):
        c = remote(out_ref.at[(f + k) % 4], o_got.at[k - 1], s_o.at[k - 1], r_o.at[k - 1], me.fsdp(k))
        c.start()
        o_copies.append(c)
    c_oy = remote(o_sum.at[1 - b], yr_o, s_y.at[1, 0], r_y.at[1, 0], me.across())

    def up_forward(i):
        y_copies[i].wait()
        flow_u.forward(i)

    def up_back():
        y_copies[3].wait()
        flow_u.back()

    def output_rows():
        for c in o_copies:
            c.wait()
        o_sum[...] = (
            out_ref[f].astype(F32) + o_got[0].astype(F32) + o_got[1].astype(F32) + o_got[2].astype(F32)
        ).astype(BF)
        c_oy.start()

    at(edge, *(functools.partial(flow_d.forward, i) for i in range(3)))
    do = functools.partial
    between = (
        ((edge, do(up_forward, 0)), (inner, do(flow_d.forward, 0))),
        ((True, output_rows), (edge, do(up_forward, 1)), (inner, do(flow_d.forward, 1), do(up_forward, 0))),
        ((edge, do(up_forward, 2)), (inner, flow_d.back, do(up_forward, 1))),
        ((edge, y_copies[3].wait), (inner, y_copies[2].wait, up_back)),
    )
    if attention is not None:
        dk_sum[...] = jnp.zeros_like(dk_sum)
        dv_sum[...] = jnp.zeros_like(dv_sum)
    per = 2048 // BQ // 4
    for quarter, (first, last) in enumerate(QUARTERS):
        ranges = [(first * 512 // BK, last * 512 // BK)]

        def rows_step(i, carry):
            g3_ref[pl.ds(pl.multiple_of(i * BQ, BQ), BQ), pl.ds(0, PAIR)] = attend_back_rows(
                i, BQ, BK, ranges, *attention, dk_sum, dv_sum
            )
            return carry

        if attention is not None:
            lax.fori_loop(quarter * per, (quarter + 1) * per, rows_step, 0)
        for which, *steps in between[quarter]:
            if which is True:
                for step in steps:
                    step()
            else:
                at(which, *steps)
    if attention is not None:
        g3_ref[:, pl.ds(PAIR, PAIR)] = dk_sum[...].astype(BF)
        g3_ref[:, pl.ds(2 * PAIR, PAIR)] = dv_sum[...].astype(BF)

    hops = [me.sibling(), me.beside(), me.across(), me.at(g=g + 1 - 2 * (g % 2)), me.at(g=(g + 2) % 4)]
    vs[0] = vec_ref[...]
    here = pl.ds(pl.multiple_of((b * 4 + swapped(f)) * PAIR, PAIR), PAIR)
    sums3 = jnp.sum(g3_ref[...].astype(F32), axis=0, keepdims=True)
    vs[0, pl.ds(0, 1), here] = sums3[:, :PAIR]
    vs[0, pl.ds(1, 1), here] = sums3[:, 2 * PAIR :]

    def hop(i):
        if i > 0:
            hop_copy(i - 1).wait()
            vs[i] = vs[i - 1] + vr[i - 1]
        hop_copy(i).start()

    def hop_copy(i):
        return remote(vs.at[i], vr.at[i], s_v.at[i], r_v.at[i], hops[i])

    hop(0)

    def rows(size, q, other=False):
        half = 1 - b if other else b
        return pl.ds(pl.multiple_of((half * 4 + q) * size, size), size)

    def unit_cols(src):
        return pl.ds(pl.multiple_of(src * 1024, 1024), 1024)

    def head_cols(src):
        return pl.ds(pl.multiple_of((b * 4 + swapped(src)) * 128, 128), 128)

    def q_rows(q):
        return pl.ds(pl.multiple_of(q * 64, 64), 64)

    def pieces(kind, q, send, recv, where, other=False):
        half = 1 - b if other else b
        if kind == 0:
            parts = (down_out.at[rows(128, q, other), :], up_out.at[rows(32, q, other), :])
        else:
            parts = (
                o_out.at[rows(32, q, other), :],
                three_out.at[:, q_rows(q), pl.ds(pl.multiple_of(half * 512, 512), 512)],
            )
        return [remote(part, part, send.at[2 * kind + i, q], recv.at[2 * kind + i, q], where) for i, part in enumerate(parts)]

    def spread(kind, q, to_right, to_left):
        if to_right:
            @pl.when(g < 3)
            def _():
                for c in pieces(kind, q, s_ag.at[0], r_ag, me.at(g=g + 1)):
                    c.start()
        if to_left:
            @pl.when(g > 0)
            def _():
                for c in pieces(kind, q, s_ag.at[1], r_ag, me.at(g=g - 1)):
                    c.start()
        for c in pieces(kind, q, s_ay, r_ay, me.across()):
            c.start()

    def pass_on(kind, d):
        @pl.when(g >= d)
        def _():
            for c in pieces(kind, g - d, s_ag.at[0], r_ag, me.across()):
                c.wait_recv()
            spread(kind, g - d, True, False)

        @pl.when(g + d <= 3)
        def _():
            for c in pieces(kind, g + d, s_ag.at[1], r_ag, me.across()):
                c.wait_recv()
            spread(kind, g + d, False, True)

    flow_u.end()
    up_out[rows(32, g), unit_cols(f)] = ubuf[g, f]
    u_out = []
    for k in (1, 2, 3):
        c = remote(ubuf.at[g, (f + k) % 4], up_out.at[rows(32, g), unit_cols(f)], s_u.at[k - 1], r_u.at[f], me.fsdp(k))
        c.start()
        u_out.append(c)
    flow_d.end()
    down_out[rows(128, g), :] = dbuf[g]

    def q_step(i, carry):
        cols = pl.ds(pl.multiple_of(i * 256, 256), 256)
        part = dense_in(x_ref[:, cols], g3_ref[...]).astype(BF)
        for j in range(3):
            gq[i, j] = part[:, j * 128 : (j + 1) * 128].reshape(4, 64, 128)
        return carry

    lax.fori_loop(0, 4, q_step, 0)
    for k in (1, 2, 3):
        src = (f + k) % 4
        remote(ubuf.at[g, 0], up_out.at[rows(32, g), unit_cols(src)], s_u.at[k - 1], r_u.at[src], me.fsdp(k)).wait_recv()
        u_out[k - 1].wait_send()
    spread(0, g, True, True)
    at(edge, *(do(flow_q.forward, i) for i in range(3)))
    c_oy.wait()
    at(edge, *(do(flow_o.forward, i) for i in range(3)))
    hop(1)

    def dx_step(i, carry):
        rows = pl.ds(pl.multiple_of(i * 256, 256), 256)
        part = dense_back(g3_ref[rows, :], w3_ref[...]).astype(BF)
        dxp[pl.ds(2 * i, 2)] = part.reshape(2, 2, 2, 2, 16, 1024)
        return carry

    lax.fori_loop(0, 8, dx_step, 0)
    c_core = remote(dxp.at[:, 1 - me.core], dx1, s_dx.at[0], r_dx.at[0], me.sibling())
    c_core.start()
    at(inner, do(flow_q.forward, 0), do(flow_q.forward, 1), do(flow_o.forward, 0), do(flow_o.forward, 1))
    hop(2)

    c_core.wait()

    def t1_step(i, carry):
        t1[i] = (dxp[i, me.core].astype(F32) + dx1[i].astype(F32)).astype(BF)
        return carry

    lax.fori_loop(0, 16, t1_step, 0)
    lo, hi = pl.ds(0, 8), pl.ds(8, 8)
    c_xa = remote(t1.at[lo, 1 - me.x], xa, s_dx.at[1], r_dx.at[1], me.beside())
    c_yb = remote(t1.at[hi, :, 1 - b], yb, s_dx.at[2], r_dx.at[2], me.across())
    c_xa.start()
    c_yb.start()
    pass_on(0, 1)
    flow_q.back()
    flow_o.back()

    flow_q.end()
    three_out[:, q_rows(g), head_cols(f)] = qbuf[g, f]
    q_out = []
    for k in (1, 2, 3):
        c = remote(qbuf.at[g, (f + k) % 4], three_out.at[:, q_rows(g), head_cols(f)], s_qf.at[k - 1], r_qf.at[f], me.fsdp(k))
        c.start()
        q_out.append(c)
    flow_o.end()
    o_out[rows(32, g), :] = obuf[g]
    c_xa.wait()
    t2a[...] = (t1[lo, me.x].astype(F32) + xa[...].astype(F32)).astype(BF)
    c_ra = remote(t2a.at[:, 1 - b], ra, s_dx.at[3], r_dx.at[3], me.across())
    c_ra.start()
    for k in (1, 2, 3):
        src = (f + k) % 4
        remote(qbuf.at[g, 0], three_out.at[:, q_rows(g), head_cols(src)], s_qf.at[k - 1], r_qf.at[src], me.fsdp(k)).wait_recv()
        q_out[k - 1].wait_send()
    spread(1, g, True, True)
    pass_on(0, 2)
    pass_on(1, 1)
    c_yb.wait()
    t2b[...] = (t1[hi, :, b].astype(F32) + yb[...].astype(F32)).astype(BF)
    c_rb = remote(t2b.at[:, 1 - me.x], rb, s_dx.at[4], r_dx.at[4], me.beside())
    c_rb.start()
    hop(3)
    pass_on(0, 3)
    c_ra.wait()
    c_rb.wait()
    moved_buf[lo] = (t2a[:, b].astype(F32) + ra[...].astype(F32) + mid_ref[lo]).astype(BF)
    moved_buf[hi] = (t2b[:, me.x].astype(F32) + rb[...].astype(F32) + mid_ref[hi]).astype(BF)

    @pl.when(me.stays())
    def _():
        c = pltpu.make_async_copy(moved_buf, dx_ref, loc.at[0])
        c.start()
        c.wait()

    @pl.when(jnp.logical_not(me.stays()))
    def _():
        remote(moved_buf, dx_ref, s_dx.at[5], r_dx.at[5], me.moved()).start()

    pass_on(1, 2)
    hop(4)
    pass_on(1, 3)
    hop_copy(4).wait()
    sums_ref[...] = vs[4] + vr[4]

    @pl.when(jnp.logical_not(me.stays()))
    def _():
        remote(moved_buf, dx_ref, s_dx.at[5], r_dx.at[5], me.moved()).wait()

    for kind in (0, 1):
        for q in range(4):
            for c in pieces(kind, q, s_ay, r_ay, me.across()):
                c.wait_send()

            @pl.when((g >= q) & (g < 3))
            def _():
                for c in pieces(kind, q, s_ag.at[0], r_ag, me.across()):
                    c.wait_send()

            @pl.when((g <= q) & (g > 0))
            def _():
                for c in pieces(kind, q, s_ag.at[1], r_ag, me.across()):
                    c.wait_send()

            for c in pieces(kind, q, s_ay, r_ay, me.across(), other=True):
                c.wait_recv()


def tail(attention, x_all, g3, w3, down, up, out, mid, vec):
    fused = attention is not None
    dma = pltpu.SemaphoreType.DMA
    v = pltpu.VMEM
    scratch = [
        v((16, 2, 2, 2, 16, 1024), BF), v((16, 2, 2, 16, 1024), BF), v((16, 2, 2, 16, 1024), BF),
        v((8, 2, 16, 1024), BF), v((8, 2, 16, 1024), BF), v((8, 2, 16, 1024), BF), v((8, 2, 16, 1024), BF),
        v((8, 16, 1024), BF), v((8, 16, 1024), BF), v((16, 16, 1024), BF),
        v((4, 4, 32, 1024), BF), v((4, 128, 1024), BF), v((2, 4, 128, 1024), BF),
        v((4, 4, 32, 1024), BF), v((2, 4, 4, 32, 1024), BF),
        v((3, 2, 4, 32, 1024), BF), v((2, 4, 32, 1024), BF), v((4, 32, 1024), BF),
        v((4, 32, 1024), BF), v((2, 4, 32, 1024), BF),
        v((4, 3, 4, 64, 128), BF), v((4, 4, 3, 64, 128), BF), v((2, 4, 4, 3, 64, 128), BF),
        v((5, 16, 1024), F32), v((5, 16, 1024), F32),
        dma((6,)), dma((6,)), dma((2, 5)), dma((2, 5)), dma((4,)), dma((2, 4)), dma((4,)), dma((2, 4)),
        dma((3,)), dma((4,)), dma((3,)), dma((3,)), dma((4,)), dma((2, 4)), dma((4,)), dma((2, 4)),
        dma((3,)), dma((4,)), dma((5,)), dma((5,)), dma((2, 4, 4)), dma((4, 4)), dma((4, 4)), dma((4, 4)), dma((1,)),
    ]
    if fused:
        scratch += [v((2048, 3 * PAIR), BF), v((2048, PAIR), F32), v((2048, PAIR), F32)]
        operands = (*attention, x_all)
    else:
        operands = (x_all, g3)
    operands += (
        w3, down.reshape(4, 128, 1024), up.reshape(4, 2, 4, 32, 1024), out.reshape(4, 2, 4, 32, 1024),
        mid.reshape(16, 16, 1024), vec,
    )
    return pl.pallas_call(
        functools.partial(tail_kernel, fused),
        out_shape=(
            jax.ShapeDtypeStruct((1024, 1024), BF),
            jax.ShapeDtypeStruct((256, 4096), BF),
            jax.ShapeDtypeStruct((256, 1024), BF),
            jax.ShapeDtypeStruct((3, 256, 1024), BF),
            jax.ShapeDtypeStruct((16, 16, 1024), BF),
            jax.ShapeDtypeStruct((16, 1024), F32),
        ),
        in_specs=[VMEM] * len(operands),
        out_specs=(VMEM,) * 6,
        scratch_shapes=scratch,
        compiler_params=pltpu.CompilerParams(collective_id=1, has_side_effects=True, vmem_limit_bytes=60 * 2**20),
        cost_estimate=pl.CostEstimate(flops=4 * 10**9, bytes_accessed=40 * 2**20, transcendentals=0),
    )(*operands)


def tile_cols(i, size):
    return pl.ds(pl.multiple_of(i * size, size), size)


def middle_kernel(
    heads_ref, x_ref, up_ref, wo_ref, wu_ref, wd_ref, par_ref,
    layer_ref, down_out, upg_out, og_out, gatt_ref, mid1_ref, vec_ref,
    att, nl, gff, slope, hid, gpre, normed, xhat, rstd, work, moved_buf, gbr, gas, ps, pr, down, down_y,
    s_a, r_a, s_b, r_b, s_g, r_g, s_p, r_p, s_m, r_m, s_y, r_y, loc,
):
    me = Place()
    f, b = me.f, me.b
    sib = f + 1 - 2 * me.core
    xs = (f + 2) % 4
    xo = xs + 1 - 2 * me.core
    peers = [me.at(f=(f + k % 4) % 4, b=(b + k // 4) % 2) for k in range(1, 8)]
    meet(me, peers, True)
    slot = swapped(f) * 2 + b
    unit = b * 4 + swapped(f)

    def peer_slot(k, sign):
        pf, pb = (f + sign * (k % 4) + 4) % 4, (b + k // 4) % 2
        return swapped(pf) * 2 + pb, pb * 4 + swapped(pf)

    def lanes(index):
        return pl.ds(pl.multiple_of(index * PAIR, PAIR), PAIR)

    for k in range(1, 8):
        where, _ = peer_slot(k, 1)
        remote(heads_ref.at[:, where], att.at[:, :, lanes(unit)], s_a.at[k - 1], r_a.at[k - 1], peers[k - 1]).start()
    att[:, :, lanes(unit)] = heads_ref[:, slot]
    for k in range(1, 8):
        _, theirs = peer_slot(k, -1)
        remote(heads_ref.at[:, slot], att.at[:, :, lanes(theirs)], s_a.at[k - 1], r_a.at[k - 1], peers[k - 1]).wait()

    def row(i):
        return par_ref[pl.ds(i, 1), :]

    def att_rows():
        return att[...].reshape(256, 1024)

    def proj(i, carry):
        cols = tile_cols(i, 512)
        work[:, cols] = dense(att_rows(), wo_ref[:, cols])
        return carry

    lax.fori_loop(0, 2, proj, 0)
    value, x_hat, inv = norm_fwd(x_ref[...].astype(F32) + work[...] + row(0), row(1), row(2))
    normed[...] = value
    xhat[...] = x_hat
    rstd[...] = inv
    nl[f] = value.astype(BF)

    def share(buf, t):
        to_sib = remote(buf.at[f], buf.at[f], s_g.at[t, 0], r_g.at[t, 0], me.sibling())
        to_x = remote(buf.at[f], buf.at[f], s_g.at[t, 1], r_g.at[t, 1], me.beside())
        to_x.start()
        to_sib.start()

        def from_sib():
            to_sib.wait_send()
            remote(buf.at[sib], buf.at[sib], s_g.at[t, 0], r_g.at[t, 0], me.sibling()).wait_recv()

        def from_x():
            to_x.wait_send()
            remote(buf.at[xs], buf.at[xs], s_g.at[t, 1], r_g.at[t, 1], me.beside()).wait_recv()
            remote(buf.at[xs], buf.at[xs], s_g.at[t, 2], r_g.at[t, 2], me.sibling()).start()

        def from_other():
            remote(buf.at[xs], buf.at[xs], s_g.at[t, 2], r_g.at[t, 2], me.sibling()).wait_send()
            remote(buf.at[xo], buf.at[xo], s_g.at[t, 2], r_g.at[t, 2], me.sibling()).wait_recv()

        return from_sib, from_x, from_other

    def scatter(t, i, where):
        return remote(ps.at[t, i], pr.at[t, i], s_p.at[t, i], r_p.at[t, i], where)

    def run(t, block, buf, beside_x):
        from_sib, from_x, from_other = share(buf, t)
        block(f, 3)
        from_sib()
        block(sib, 0)
        scatter(t, 0, me.sibling()).start()
        from_x()
        block(xs, 2)
        from_other()
        block(xo, 1)
        scatter(t, 1, me.sibling()).start()
        scatter(t, 1, me.sibling()).wait()
        ps[t, 2] = (ps[t, 2].astype(F32) + pr[t, 1].astype(F32)).astype(BF)
        scatter(t, 2, me.beside()).start()
        beside_x()
        scatter(t, 0, me.sibling()).wait()
        scatter(t, 2, me.beside()).wait()
        return ps[t, 3].astype(F32) + pr[t, 0].astype(F32) + pr[t, 2].astype(F32)

    def forward(index, into):
        def up_tile(i, carry):
            cols = tile_cols(i, 256)
            pre = dense(nl[index], wu_ref[:, cols]) + par_ref[pl.ds(6, 1), cols]
            cdf = 0.5 * (1.0 + lax.erf(pre * 0.7071067811865476))
            hid[index, :, cols] = (pre * cdf).astype(BF)
            slope[index, :, cols] = cdf + pre * jnp.exp(-0.5 * pre * pre) * 0.3989422804014327
            return carry

        def down_tile(i, carry):
            cols = tile_cols(i, 512)
            ps[0, into, :, cols] = dense(hid[index], wd_ref[:, cols]).astype(BF)
            return carry

        lax.fori_loop(0, 4, up_tile, 0)
        lax.fori_loop(0, 2, down_tile, 0)

    ffn = run(0, forward, nl, lambda: None)
    value, x_hat, inv = norm_fwd(normed[...] + ffn + row(3), row(4), row(5))
    moved_buf[...] = value.astype(BF)

    @pl.when(me.stays())
    def _():
        pltpu.make_async_copy(moved_buf, layer_ref, loc.at[0]).start()

    @pl.when(jnp.logical_not(me.stays()))
    def _():
        remote(moved_buf, layer_ref, s_m.at[0], r_m.at[0], me.moved()).start()

    grad2, gain2, shift2 = norm_back(up_ref[...].astype(F32), x_hat, inv, row(4))
    work[...] = grad2
    low2 = grad2.astype(BF)
    gff[f] = low2
    vec_ref[pl.ds(4, 1), :] = jnp.sum(low2.astype(F32), axis=0, keepdims=True)
    vec_ref[pl.ds(5, 1), :] = gain2[None]
    vec_ref[pl.ds(6, 1), :] = shift2[None]

    def backward(index, into):
        def pre_tile(i, carry):
            cols = tile_cols(i, 512)
            part = dense_back(gff[index], wd_ref[cols, :])
            gpre[index, :, cols] = (part * slope[index, :, cols]).astype(BF)
            return carry

        def in_tile(i, carry):
            cols = tile_cols(i, 512)
            ps[1, into, :, cols] = dense_back(gpre[index], wu_ref[cols, :]).astype(BF)
            return carry

        lax.fori_loop(0, 2, pre_tile, 0)
        lax.fori_loop(0, 2, in_tile, 0)

    c_down = remote(down.at[1 - b], down_y, s_y.at[0], r_y.at[0], me.across())

    def weight_grads():
        def down_tile(i, carry):
            cols = tile_cols(i, 256)
            part = dense_in(hid[:, :, cols].reshape(1024, 256), gff[...].reshape(1024, 1024)).astype(BF)
            down[i // 2, pl.ds(pl.multiple_of(i % 2 * 256, 256), 256)] = part
            return carry

        def up_tile(i, carry):
            cols = tile_cols(i, 256)
            upg_out[cols, :] = dense_in(nl[:, :, cols].reshape(1024, 256), gpre[...].reshape(1024, 1024)).astype(BF)
            return carry

        lax.fori_loop(0, 4, down_tile, 0)
        c_down.start()
        lax.fori_loop(0, 4, up_tile, 0)
        vec_ref[pl.ds(3, 1), :] = jnp.sum(gpre[...].reshape(1024, 1024).astype(F32), axis=0, keepdims=True)

    back = run(1, backward, gff, weight_grads)
    grad1, gain1, shift1 = norm_back(back + work[...], xhat[...], rstd[...], row(1))
    mid1_ref[...] = grad1
    low1 = grad1.astype(BF)
    gbr[...] = low1
    vec_ref[pl.ds(0, 1), :] = jnp.sum(low1.astype(F32), axis=0, keepdims=True)
    vec_ref[pl.ds(1, 1), :] = gain1[None]
    vec_ref[pl.ds(2, 1), :] = shift1[None]
    vec_ref[pl.ds(7, 1), :] = jnp.zeros((1, 1024), F32)

    def att_tile(i, carry):
        part = dense_back(gbr[...], wo_ref[tile_cols(i, 256), :]).astype(BF)
        for j in range(2):
            gas[2 * i + j] = part[:, j * PAIR : (j + 1) * PAIR].reshape(16, 16, PAIR)
        return carry

    lax.fori_loop(0, 4, att_tile, 0)
    for k in range(1, 8):
        _, theirs = peer_slot(k, 1)
        remote(gas.at[theirs], gatt_ref.at[:, slot], s_b.at[k - 1], r_b.at[k - 1], peers[k - 1]).start()
    gatt_ref[:, slot] = gas[unit]

    def o_tile(i, carry):
        cols = tile_cols(i, 256)
        og_out[cols, :] = dense_in(att[:, :, cols].reshape(256, 256), gbr[...]).astype(BF)
        return carry

    lax.fori_loop(0, 4, o_tile, 0)
    for k in range(1, 8):
        where, _ = peer_slot(k, -1)
        remote(gas.at[0], gatt_ref.at[:, where], s_b.at[k - 1], r_b.at[k - 1], peers[k - 1]).wait()
    c_down.wait()
    down_out[...] = (down[b].astype(F32) + down_y[...].astype(F32)).astype(BF)

    @pl.when(me.stays())
    def _():
        pltpu.make_async_copy(moved_buf, layer_ref, loc.at[0]).wait()

    @pl.when(jnp.logical_not(me.stays()))
    def _():
        remote(moved_buf, layer_ref, s_m.at[0], r_m.at[0], me.moved()).wait()


def middle(heads, x, upstream, w_output, w_up, w_down, params):
    dma = pltpu.SemaphoreType.DMA
    v = pltpu.VMEM
    block = (4, 256, 1024)
    scratch = [
        v((16, 16, 1024), BF), v(block, BF), v(block, BF), v(block, F32), v(block, BF), v(block, BF),
        v((256, 1024), F32), v((256, 1024), F32), v((256, 1), F32), v((256, 1024), F32), v((256, 1024), BF),
        v((256, 1024), BF), v((8, 16, 16, PAIR), BF), v((2, 4, 256, 1024), BF), v((2, 3, 256, 1024), BF),
        v((2, 512, 1024), BF), v((512, 1024), BF),
        dma((7,)), dma((7,)), dma((7,)), dma((7,)), dma((2, 3)), dma((2, 3)), dma((2, 3)), dma((2, 3)),
        dma((1,)), dma((1,)), dma((1,)), dma((1,)), dma((1,)),
    ]
    square = jax.ShapeDtypeStruct((1024, 1024), BF)
    return pl.pallas_call(
        middle_kernel,
        out_shape=(
            jax.ShapeDtypeStruct((256, 1024), BF), jax.ShapeDtypeStruct((512, 1024), BF), square, square,
            jax.ShapeDtypeStruct((16, 8, 16, PAIR), BF),
            jax.ShapeDtypeStruct((256, 1024), F32),
            jax.ShapeDtypeStruct((8, 1024), F32),
        ),
        in_specs=[VMEM] * 7,
        out_specs=(VMEM,) * 7,
        scratch_shapes=scratch,
        compiler_params=pltpu.CompilerParams(collective_id=2, has_side_effects=True, vmem_limit_bytes=60 * 2**20),
        cost_estimate=pl.CostEstimate(flops=14 * 10**9, bytes_accessed=20 * 2**20, transcendentals=2**21),
    )(heads.reshape(16, 8, 16, PAIR), x, upstream, w_output, w_up, w_down, params)


def start_kernel(
    tok_ref, cot_ref, ends_ref, qw_ref, kw_ref, vw_ref, ow_ref, ew_ref, bias_ref,
    x_ref, up_ref, ends_out, q_ref, k_ref, v_ref, w3_ref, wo_ref, wu_ref,
    s_m, r_m, s_w, r_w, s_u, r_u, s_o, r_o, s_x, r_x, loc,
):
    me = Place()
    g, b, f = me.g, me.b, me.f
    sib = f + 1 - 2 * me.core
    xs = (f + 2) % 4
    xo = xs + 1 - 2 * me.core
    meet(me, [me.across()] + [me.fsdp(k) for k in (1, 2, 3)], True)
    slot = me.core * 4 + me.x * 2 + b
    slot_x = me.core * 4 + (1 - me.x) * 2 + b
    slot_y = slot + 1 - 2 * b
    slot_d = slot_x + 1 - 2 * b
    other = 4 - 8 * me.core
    lo, hi = pl.ds(0, 8), pl.ds(8, 8)

    def moves(i, src, dst):
        return remote(src, dst, s_m.at[i], r_m.at[i], me.moved())

    def relocate(i, src, dst):
        @pl.when(me.stays())
        def _():
            pltpu.make_async_copy(src, dst, loc.at[i]).start()

        @pl.when(jnp.logical_not(me.stays()))
        def _():
            moves(i, src, dst).start()

    def relocated(i, src, dst):
        @pl.when(me.stays())
        def _():
            pltpu.make_async_copy(src, dst, loc.at[i]).wait()

        @pl.when(jnp.logical_not(me.stays()))
        def _():
            moves(i, src, dst).wait()

    theirs = x_ref.at[:, g * 2 + b]
    relocate(0, tok_ref, theirs)
    relocate(1, ends_ref, ends_out)

    def cols(index, size):
        return pl.ds(pl.multiple_of(index * size, size), size)

    def w3_rows(src):
        return cols(src, 256)

    def wo_rows(src, which):
        return pl.ds(pl.multiple_of(src * 256 + which * 128, 128), 128)

    half = cols(b, 128)
    u_x = [
        remote(ew_ref.at[half, cols(xs, 1024)], wu_ref.at[wo_rows(f, b)], s_u.at[1], r_u.at[1], me.beside()),
        remote(ew_ref.at[half, cols(xo, 1024)], wu_ref.at[wo_rows(f, b)], s_u.at[2], r_u.at[2], me.at(f=xo)),
    ]
    o_x = remote(ow_ref.at[half], wo_ref.at[wo_rows(f, b)], s_o.at[1], r_o.at[1], me.beside())
    u_sib = remote(ew_ref.at[:, cols(sib, 1024)], wu_ref.at[w3_rows(f)], s_u.at[0], r_u.at[0], me.sibling())
    o_sib = remote(ow_ref, wo_ref.at[w3_rows(f)], s_o.at[0], r_o.at[0], me.sibling())
    for c in u_x + [o_x, u_sib, o_sib]:
        c.start()
    o_own = pltpu.make_async_copy(ow_ref, wo_ref.at[w3_rows(f)], loc.at[5])
    u_own = pltpu.make_async_copy(ew_ref.at[:, cols(f, 1024)], wu_ref.at[w3_rows(f)], loc.at[6])
    o_own.start()
    u_own.start()
    weights = (qw_ref, kw_ref, vw_ref)

    def w3_own(j):
        return pltpu.make_async_copy(
            weights[j].at[:, cols(b * 4 + swapped(f), 128)], w3_ref.at[w3_rows(f), pl.ds(128 * j, 128)], loc.at[2 + j]
        )

    for j in range(3):
        w3_own(j).start()
    for c in u_x:
        c.wait()
    u_fwd = [
        remote(wu_ref.at[wo_rows(src, b)], wu_ref.at[wo_rows(src, b)], s_u.at[3 + i], r_u.at[3 + i], me.across())
        for i, src in enumerate((xs, xo))
    ]
    for c in u_fwd:
        c.start()
    o_x.wait()
    o_fwd = [
        remote(wo_ref.at[wo_rows(xs, b)], wo_ref.at[wo_rows(xs, b)], s_o.at[2], r_o.at[2], me.sibling()),
        remote(wo_ref.at[wo_rows(xs, b)], wo_ref.at[wo_rows(xs, b)], s_o.at[3], r_o.at[3], me.across()),
    ]
    for c in o_fwd:
        c.start()

    def piece(i, ref, where):
        return remote(ref, ref, s_x.at[i], r_x.at[i], where)

    relocated(0, tok_ref, theirs)
    own = x_ref.at[:, slot]
    sends = [piece(1, own, me.beside()), piece(2, own, me.across()), piece(0, own, me.sibling())]
    for c in sends:
        c.start()
    relocate(7, cot_ref, up_ref)

    for k in (2, 3, 1):
        dest = b * 4 + swapped((f + k) % 4)
        for j in range(3):
            remote(
                weights[j].at[:, cols(dest, 128)], w3_ref.at[w3_rows(f), pl.ds(128 * j, 128)],
                s_w.at[j, k - 1], r_w.at[j, k - 1], me.fsdp(k),
            ).start()

    def project(which):
        part = dense(x_ref[:, which].reshape(256, 1024), w3_ref[...]) + bias_ref[...]
        part = part.astype(BF).reshape(16, 16, 3 * PAIR)
        q_ref[:, which] = part[:, :, :PAIR]
        k_ref[:, which] = part[:, :, PAIR : 2 * PAIR]
        v_ref[:, which] = part[:, :, 2 * PAIR :]

    piece(1, x_ref.at[:, slot_x], me.beside()).wait_recv()
    more = [piece(4, x_ref.at[hi, slot_x], me.across()), piece(3, x_ref.at[:, slot_x], me.sibling())]
    for c in more:
        c.start()
    sends += more
    piece(2, x_ref.at[:, slot_y], me.across()).wait_recv()
    more = [piece(6, x_ref.at[lo, slot_y], me.beside()), piece(5, x_ref.at[:, slot_y], me.sibling())]
    for c in more:
        c.start()
    sends += more
    o_fwd[0].wait()
    o_fwd[1].wait()
    late = remote(wo_ref.at[wo_rows(xs, 1 - b)], wo_ref.at[wo_rows(xs, 1 - b)], s_o.at[4], r_o.at[4], me.sibling())
    late.start()
    for k in (1, 2, 3):
        src = (f + 4 - k) % 4
        for j in range(3):
            remote(
                weights[j].at[:, cols(0, 128)], w3_ref.at[w3_rows(src), pl.ds(128 * j, 128)],
                s_w.at[j, k - 1], r_w.at[j, k - 1], me.fsdp(k),
            ).wait()
    for j in range(3):
        w3_own(j).wait()
    project(slot)
    project(slot_x)
    piece(4, x_ref.at[hi, slot_d], me.across()).wait_recv()
    more = [piece(8, x_ref.at[hi, slot_d], me.sibling())]
    more[0].start()
    piece(6, x_ref.at[lo, slot_d], me.beside()).wait_recv()
    more.append(piece(7, x_ref.at[lo, slot_d], me.sibling()))
    more[1].start()
    sends += more
    project(slot_y)
    for i, part in ((0, slot + other), (3, slot_x + other), (5, slot_y + other)):
        piece(i, x_ref.at[:, part], me.sibling()).wait_recv()
        project(part)
    project(slot_d)
    piece(8, x_ref.at[hi, slot_d + other], me.sibling()).wait_recv()
    piece(7, x_ref.at[lo, slot_d + other], me.sibling()).wait_recv()
    project(slot_d + other)

    for c in sends:
        c.wait_send()
    late.wait()
    o_own.wait()
    o_sib.wait()
    u_own.wait()
    u_sib.wait()
    relocated(1, ends_ref, ends_out)
    relocated(7, cot_ref, up_ref)
    for c in u_fwd:
        c.wait()


def start(tokens, cotangent, ends, query_w, key_w, value_w, output_w, expand_w, bias3):
    dma = pltpu.SemaphoreType.DMA
    hbm = pl.BlockSpec(memory_space=pl.ANY)
    heads = jax.ShapeDtypeStruct((16, GROUP, 16, PAIR), BF)
    square = jax.ShapeDtypeStruct((1024, 1024), BF)
    return pl.pallas_call(
        start_kernel,
        out_shape=(
            jax.ShapeDtypeStruct((16, GROUP, 16, 1024), BF), jax.ShapeDtypeStruct((16, 16, 1024), BF),
            jax.ShapeDtypeStruct((8, 128), jnp.int32), heads, heads, heads,
            jax.ShapeDtypeStruct((1024, 3 * PAIR), BF), square, square,
        ),
        in_specs=[hbm, hbm, VMEM] + [hbm] * 5 + [VMEM],
        out_specs=(VMEM, hbm, VMEM, VMEM, VMEM, VMEM, VMEM, hbm, hbm),
        scratch_shapes=[
            dma((8,)), dma((8,)), dma((3, 3)), dma((3, 3)), dma((5,)), dma((5,)), dma((5,)), dma((5,)),
            dma((9,)), dma((9,)), dma((8,)),
        ],
        compiler_params=pltpu.CompilerParams(collective_id=3, has_side_effects=True, vmem_limit_bytes=60 * 2**20),
        cost_estimate=pl.CostEstimate(flops=2 * 10**9, bytes_accessed=20 * 2**20, transcendentals=0),
    )(tokens, cotangent, ends, query_w, key_w, value_w, output_w, expand_w, bias3)


def body(
    tokens, lengths, packing, query_w, query_b, key_w, value_w, value_b, output_w, output_b,
    attn_gain, attn_shift, expand_w, expand_b, reduce_w, reduce_b, ffn_gain, ffn_shift, cotangent,
):
    tok_shape = tokens.shape
    laps, stripe, width = tok_shape[1], tok_shape[2], tok_shape[3]
    mine = laps * stripe
    n_ctx = lax.axis_size("ctx")
    n_f = lax.axis_size("fsdp")
    per_group = n_ctx // n_f
    chunks = per_group // 2
    ctx = lax.axis_index("ctx")
    f = lax.axis_index("fsdp")
    g = ctx // per_group
    chunk = ctx % per_group // 2
    b = ctx % 2
    same_place = [
        [(gg * chunks + s) * 2 + bb for s in range(chunks)] for gg in range(n_f) for bb in range(2)
    ]
    units = expand_w.shape[1] // n_f

    ordered = jnp.sum(
        jnp.where(
            packing[0][:, None] == jnp.arange(lengths.shape[1], dtype=jnp.int32)[None, :],
            lengths[0][None, :],
            0,
        ),
        axis=1,
    )
    slots = jnp.arange(ordered.shape[0], dtype=jnp.int32)
    own_ends = jnp.sum(jnp.where(slots[None, :] <= slots[:, None], ordered[None, :], 0), axis=1)
    own_ends = jnp.pad(own_ends[None], ((0, 7), (0, 128 - own_ends.shape[0])))

    here = (b * n_f + swapped(f)) * PAIR
    bias3 = jnp.concatenate(
        [
            lax.dynamic_slice_in_dim(query_b, here, PAIR),
            jnp.zeros((PAIR,), F32),
            lax.dynamic_slice_in_dim(value_b, here, PAIR),
        ]
    )[None]
    acts = (laps, stripe, width)
    x_all, upstream, ends, q, k_own, v_own, w_three, w_output, w_up = start(
        tokens.reshape(acts), cotangent.reshape(acts), own_ends, query_w, key_w, value_w, output_w, expand_w, bias3
    )
    q, k_own, v_own = (part.reshape(GROUP * mine, PAIR) for part in (q, k_own, v_own))
    inputs = lax.dynamic_index_in_dim(x_all, swapped(f) * 2 + b, 1, keepdims=False).reshape(mine, width)
    x_all = x_all.reshape(GROUP * mine, width)
    upstream = upstream.reshape(mine, width)
    slot_ends = ends[0, : ordered.shape[0]]

    span = GROUP * mine
    index = jnp.arange(span, dtype=jnp.int32)

    def segments(which):
        lap, rest = index // (GROUP * stripe), index % (GROUP * stripe)
        unit, place = rest // stripe, rest % stripe
        owner = unit // 2 * per_group + which * 2 + unit % 2
        position = lap * (n_ctx * stripe) + owner * stripe + place
        return jnp.sum((position[:, None] >= slot_ends[None, :]).astype(jnp.int32), axis=1)

    seg_q = segments(chunk)
    seg_k = jnp.concatenate([segments(s) for s in range(chunks)])
    q_first, q_last = seg_q[::BQ], seg_q[BQ - 1 :: BQ]
    k_first = seg_k[::BK].reshape(chunks, -1)
    k_last = seg_k[BK - 1 :: BK].reshape(chunks, -1)
    lo = jnp.sum((k_last[None] < q_first[:, None, None]).astype(jnp.int32), axis=2)
    hi = jnp.sum((k_first[None] <= q_last[:, None, None]).astype(jnp.int32), axis=2)
    bounds = (lo, hi)
    seg_q = seg_q[:, None]
    seg_k = seg_k[None, :]

    if chunks == 1:
        k, v = k_own, v_own
    else:
        k = lax.all_gather(k_own, "ctx", axis_index_groups=same_place, tiled=True)
        v = lax.all_gather(v_own, "ctx", axis_index_groups=same_place, tiled=True)
    att_heads, lse = attend(bounds, q, k, v, seg_q, seg_k, chunks)

    params = jnp.stack(
        [
            output_b, attn_gain, attn_shift, reduce_b, ffn_gain, ffn_shift,
            lax.dynamic_slice_in_dim(expand_b, f * units, units), jnp.zeros_like(output_b),
        ]
    )
    layer_out, part_down, part_up, part_out, grad_att, grad_mid1, vec = middle(
        att_heads, inputs, upstream, w_output, w_up, reduce_w, params
    )
    layer_out = layer_out.reshape(tok_shape)
    grad_att = grad_att.reshape(GROUP * mine, PAIR)

    attention = (q, k, v, seg_q, seg_k, att_heads, lse, grad_att)
    grad_three = None
    if chunks > 1:
        grad_q, grad_k, grad_v = attend_back(bounds, *attention, chunks)
        attention = None
        grad_k = lax.psum_scatter(
            grad_k.astype(BF), "ctx", axis_index_groups=same_place, tiled=True
        )
        grad_v = lax.psum_scatter(
            grad_v.astype(BF), "ctx", axis_index_groups=same_place, tiled=True
        )
        grad_three = jnp.concatenate([grad_q, grad_k, grad_v], axis=1)
    here_rows = jnp.zeros((n_f, units), F32)
    sums = jnp.concatenate(
        [
            jnp.zeros((2, width), F32),
            vec[:3],
            vec[4:7],
            lax.dynamic_update_slice_in_dim(here_rows, vec[3:4], f, 0),
            here_rows,
        ]
    )
    share_down, share_up, share_out, share_three, moved, sums = tail(
        attention, x_all, grad_three, w_three, part_down, part_up, part_out, grad_mid1, sums
    )
    grad_inputs = moved.reshape(tok_shape).astype(F32)
    shares = tuple(part.astype(F32) for part in (share_three, share_out, share_up, share_down)) + (sums,)
    if chunks > 1:
        shares = lax.psum(shares, "ctx", axis_index_groups=same_place)
    share_three, share_out, share_up, share_down, sums = shares
    (
        grad_query_b, grad_value_b, grad_output_b, grad_attn_gain, grad_attn_shift, grad_reduce_b,
        grad_ffn_gain, grad_ffn_shift,
    ) = (sums[i] for i in range(8))
    grad_expand_b = sums[8 : 8 + n_f].reshape(-1)
    return (
        layer_out,
        grad_inputs,
        share_three[0],
        grad_query_b,
        share_three[1],
        share_three[2],
        grad_value_b,
        share_out,
        grad_output_b,
        grad_attn_gain,
        grad_attn_shift,
        share_up,
        grad_expand_b,
        share_down,
        grad_reduce_b,
        grad_ffn_gain,
        grad_ffn_shift,
    )


def solution(mesh):
    acts = P("fsdp", None, "ctx", None)
    rows = P("fsdp", None)
    return jax.shard_map(
        body,
        mesh=mesh,
        in_specs=(
            acts, rows, rows, rows, P(), rows, rows, P(), rows, P(),
            P(), P(), rows, P(), rows, P(), P(), P(), acts,
        ),
        out_specs=(
            acts, acts, rows, P(), rows, rows, P(), rows, P(),
            P(), P(), rows, P(), rows, P(), P(), P(),
        ),
        check_vma=False,
    )
```

```python
import functools
import jax
import jax.numpy as jnp
from jax import lax
from jax.experimental import pallas as pl
from jax.experimental.pallas import tpu as pltpu
from jax.sharding import PartitionSpec as P

H = 16
HD = 64
PAIR = 2 * HD
GROUP = 8
SWAP = (0, 2, 1, 3)
BQ = 512
BK = 512
WIDE = 512
QUARTERS = ((0, 2), (0, 3), (1, 4), (2, 4))
BF = jnp.bfloat16
F32 = jnp.float32


def dense(left, right):
    return jnp.dot(left, right, preferred_element_type=F32)


def dense_back(left, right):
    return lax.dot_general(left, right, (((1,), (1,)), ((), ())), preferred_element_type=F32)


def dense_in(left, right):
    return lax.dot_general(left, right, (((0,), (0,)), ((), ())), preferred_element_type=F32)


def norm_fwd(hidden, gain, shift):
    mean_row = jnp.mean(hidden, axis=-1, keepdims=True)
    centred = hidden - mean_row
    variance = jnp.mean(centred * centred, axis=-1, keepdims=True)
    inv_std = lax.rsqrt(variance + 1e-05)
    x_hat = centred * inv_std
    return (x_hat * gain + shift, x_hat, inv_std)


def norm_back(incoming, x_hat, inv_std, gain):
    scaled = incoming * gain
    grad_in = inv_std * (
        scaled
        - jnp.mean(scaled, axis=-1, keepdims=True)
        - x_hat * jnp.mean(scaled * x_hat, axis=-1, keepdims=True)
    )
    return (grad_in, jnp.sum(incoming * x_hat, axis=0), jnp.sum(incoming, axis=0))


def gelu_slope(pre_act):
    return (
        0.5 * (1.0 + lax.erf(pre_act * 0.7071067811865476))
        + pre_act * jnp.exp(-0.5 * pre_act * pre_act) * 0.3989422804014327
    )


def first_half(shape):
    return lax.broadcasted_iota(jnp.int32, shape, 1) < HD


def both_heads(block):
    left = first_half(block.shape)
    zero = jnp.zeros_like(block)
    return jnp.concatenate([jnp.where(left, block, zero), jnp.where(left, zero, block)], axis=0)


def by_head(stacked):
    rows = stacked.shape[0] // 2
    left = first_half((rows, stacked.shape[1]))
    return jnp.where(left, stacked[:rows], stacked[rows:])


def row_block(ref, i, size):
    if len(ref.shape) == 2:
        return ref[pl.ds(pl.multiple_of(i * size, size), size), :]
    laps = size // (ref.shape[1] * ref.shape[2])
    return ref[pl.ds(i * laps, laps)].reshape(size, ref.shape[3])


def attend_rows(i, bq, bk, ranges, q_ref, k_ref, v_ref, query_seg, key_seg):
    q2 = both_heads(row_block(q_ref, i, bq) * BF(0.125))
    seg = query_seg(i)
    seg2 = jnp.concatenate([seg, seg], axis=0)

    def k_step(j, state):
        accum, run_max, run_sum = state
        scores = dense_back(q2, row_block(k_ref, j, bk))
        scores = jnp.where(seg2 == key_seg(j), scores, -1e30)
        new_max = jnp.maximum(run_max, jnp.max(scores, axis=1, keepdims=True))
        probs = jnp.exp(scores - new_max)
        scale = jnp.exp(run_max - new_max)
        run_sum = run_sum * scale + jnp.sum(probs, axis=1, keepdims=True)
        accum = accum * scale + dense(probs.astype(BF), row_block(v_ref, j, bk))
        return accum, new_max, run_sum

    state = (
        jnp.zeros((2 * bq, PAIR), F32),
        jnp.full((2 * bq, 1), -1e30, F32),
        jnp.zeros((2 * bq, 1), F32),
    )
    for first, last in ranges:
        state = lax.fori_loop(first, last, k_step, state)
    accum, run_max, run_sum = state
    return by_head(accum / run_sum), run_max + jnp.log(run_sum)


def attend_wide(i, bq, first, size, q_ref, k_ref, v_ref, query_seg, key_seg):
    q2 = both_heads(row_block(q_ref, i, bq) * BF(0.125))
    seg = query_seg(i, bq)
    keys = pl.ds(first // 128, size // 128)
    scores = dense_back(q2, k_ref[keys].reshape(size, PAIR))
    scores = jnp.where(jnp.concatenate([seg, seg], axis=0) == key_seg(first, size), scores, -1e30)
    row_max = jnp.max(scores, axis=1, keepdims=True)
    probs = jnp.exp(scores - row_max)
    row_sum = jnp.sum(probs, axis=1, keepdims=True)
    accum = dense(probs.astype(BF), v_ref[keys].reshape(size, PAIR))
    return by_head(accum / row_sum), row_max + jnp.log(row_sum)


def attend_kernel(bq, bk, chunks, lo_ref, hi_ref, q_ref, k_ref, v_ref, sq_ref, sk_ref, o_ref, lse_ref):
    nq = q_ref.shape[0] // bq
    per_chunk = k_ref.shape[0] // chunks // bk

    def q_step(i, carry):
        ranges = [(s * per_chunk + lo_ref[i, s], s * per_chunk + hi_ref[i, s]) for s in range(chunks)]
        rows, lse = attend_rows(
            i, bq, bk, ranges, q_ref, k_ref, v_ref, lambda i: row_block(sq_ref, i, bq),
            lambda j: sk_ref[:, pl.ds(pl.multiple_of(j * bk, bk), bk)],
        )
        o_ref[pl.ds(pl.multiple_of(i * bq, bq), bq), :] = rows.astype(BF)
        lse_ref[pl.ds(pl.multiple_of(2 * i * bq, 2 * bq), 2 * bq), :] = lse
        return carry

    lax.fori_loop(0, nq, q_step, 0)


def segments_from(ends_ref, slots):
    def count(position):
        total = jnp.zeros(position.shape, jnp.int32)
        for j in range(slots):
            total += jnp.where(position >= ends_ref[pl.ds(0, 1), pl.ds(j, 1)], 1, 0)
        return total

    return (
        lambda i, size=BQ: count(i * size + lax.broadcasted_iota(jnp.int32, (size, 1), 0)),
        lambda first, size: count(first + lax.broadcasted_iota(jnp.int32, (1, size), 1)),
    )


def attend_back_rows(i, bq, bk, ranges, q_ref, k_ref, v_ref, query_seg, key_seg, o_ref, lse_ref, g_ref, dk_sum, dv_sum):
    rows = pl.ds(pl.multiple_of(i * bq, bq), bq)
    q2 = both_heads(q_ref[rows, :] * BF(0.125))
    grad = g_ref[rows, :]
    g2 = both_heads(grad)
    prod = grad.astype(F32) * o_ref[rows, :].astype(F32)
    left = first_half(prod.shape)
    delta = jnp.concatenate(
        [
            jnp.sum(jnp.where(left, prod, 0.0), axis=1, keepdims=True),
            jnp.sum(jnp.where(left, 0.0, prod), axis=1, keepdims=True),
        ],
        axis=0,
    )
    lse = lse_ref[pl.ds(pl.multiple_of(2 * i * bq, 2 * bq), 2 * bq), :]
    seg = query_seg(i)
    seg2 = jnp.concatenate([seg, seg], axis=0)

    def k_step(j, dq2):
        keys = pl.ds(pl.multiple_of(j * bk, bk), bk)
        key_rows = k_ref[keys, :]
        scores = dense_back(q2, key_rows)
        probs = jnp.exp(jnp.where(seg2 == key_seg(j), scores, -1e30) - lse)
        grad_prob = dense_back(g2, v_ref[keys, :])
        grad_score = (probs * (grad_prob - delta)).astype(BF)
        dv_sum[keys, :] += dense_in(probs.astype(BF), g2)
        dk_sum[keys, :] += dense_in(grad_score, q2)
        return dq2 + dense(grad_score, key_rows)

    dq2 = jnp.zeros((2 * bq, PAIR), F32)
    for first, last in ranges:
        dq2 = lax.fori_loop(first, last, k_step, dq2)
    return (0.125 * by_head(dq2)).astype(BF)


def attend_back_kernel(
    bq, bk, chunks, lo_ref, hi_ref, q_ref, k_ref, v_ref, sq_ref, sk_ref, o_ref, lse_ref, g_ref,
    dq_ref, dk_ref, dv_ref, dk_sum, dv_sum,
):
    nq = q_ref.shape[0] // bq
    per_chunk = k_ref.shape[0] // chunks // bk
    dk_sum[...] = jnp.zeros_like(dk_sum)
    dv_sum[...] = jnp.zeros_like(dv_sum)

    def q_step(i, carry):
        ranges = [(s * per_chunk + lo_ref[i, s], s * per_chunk + hi_ref[i, s]) for s in range(chunks)]
        dq_ref[pl.ds(pl.multiple_of(i * bq, bq), bq), :] = attend_back_rows(
            i, bq, bk, ranges, q_ref, k_ref, v_ref, lambda i: row_block(sq_ref, i, bq),
            lambda j: sk_ref[:, pl.ds(pl.multiple_of(j * bk, bk), bk)], o_ref, lse_ref, g_ref, dk_sum, dv_sum,
        )
        return carry

    lax.fori_loop(0, nq, q_step, 0)
    dk_ref[...] = dk_sum[...].astype(dk_ref.dtype)
    dv_ref[...] = dv_sum[...].astype(dv_ref.dtype)


SMEM = pl.BlockSpec(memory_space=pltpu.SMEM)
VMEM = pl.BlockSpec(memory_space=pltpu.VMEM)


def attend(bounds, q, k, v, seg_q, seg_k, chunks):
    n = q.shape[0]
    return pl.pallas_call(
        functools.partial(attend_kernel, BQ, BK, chunks),
        out_shape=(jax.ShapeDtypeStruct((n, PAIR), BF), jax.ShapeDtypeStruct((2 * n, 1), F32)),
        in_specs=[SMEM, SMEM] + [VMEM] * 5,
        out_specs=(VMEM, VMEM),
        compiler_params=pltpu.CompilerParams(vmem_limit_bytes=48 * 2**20),
    )(*bounds, q, k, v, seg_q, seg_k)


def attend_back(bounds, q, k, v, seg_q, seg_k, out, lse, grad, chunks):
    n, m = q.shape[0], k.shape[0]
    kept = BF if chunks == 1 else F32
    return pl.pallas_call(
        functools.partial(attend_back_kernel, BQ, BK, chunks),
        out_shape=(
            jax.ShapeDtypeStruct((n, PAIR), BF),
            jax.ShapeDtypeStruct((m, PAIR), kept),
            jax.ShapeDtypeStruct((m, PAIR), kept),
        ),
        in_specs=[SMEM, SMEM] + [VMEM] * 8,
        out_specs=(VMEM, VMEM, VMEM),
        scratch_shapes=[pltpu.VMEM((m, PAIR), F32), pltpu.VMEM((m, PAIR), F32)],
        compiler_params=pltpu.CompilerParams(vmem_limit_bytes=56 * 2**20),
    )(*bounds, q, k, v, seg_q, seg_k, out, lse, grad)


def mesh_id(ctx, f):
    return {"ctx": ctx, "fsdp": f}


def swapped(i):
    return i % 2 * 2 + i // 2


class Place:
    def __init__(self):
        self.ctx = lax.axis_index("ctx")
        self.f = lax.axis_index("fsdp")
        self.per_group = lax.axis_size("ctx") // 4
        self.g = self.ctx // self.per_group
        self.b = self.ctx % 2
        self.rest = self.ctx % self.per_group
        self.core = self.f % 2
        self.x = self.f // 2

    def at(self, g=None, b=None, f=None):
        ctx = self.ctx
        if g is not None:
            ctx = ctx + (g - self.g) * self.per_group
        if b is not None:
            ctx = ctx + (b - self.b)
        return mesh_id(ctx, self.f if f is None else f)

    def sibling(self):
        return self.at(f=self.f + 1 - 2 * self.core)

    def beside(self):
        return self.at(f=(self.f + 2) % 4)

    def across(self):
        return self.at(b=1 - self.b)

    def fsdp(self, k):
        return self.at(f=(self.f + k) % 4)

    def moved(self):
        return mesh_id(swapped(self.f) * self.per_group + self.rest, swapped(self.g))

    def stays(self):
        return swapped(self.f) == self.g


def remote(src, dst, send, recv, where):
    return pltpu.make_async_remote_copy(
        src_ref=src, dst_ref=dst, send_sem=send, recv_sem=recv,
        device_id=where, device_id_type=pl.DeviceIdType.MESH,
    )


def meet(me, targets, moves):
    barrier = pltpu.get_barrier_semaphore()
    for t in targets:
        pl.semaphore_signal(barrier, 1, device_id=t, device_id_type=pl.DeviceIdType.MESH)
    if not moves:
        pl.semaphore_wait(barrier, len(targets))
        return

    @pl.when(jnp.logical_not(me.stays()))
    def _():
        pl.semaphore_signal(barrier, 1, device_id=me.moved(), device_id_type=pl.DeviceIdType.MESH)

    pl.semaphore_wait(barrier, len(targets) + jnp.where(me.stays(), 0, 1))


class Flow:
    def __init__(self, me, own, buf, got, sent, came):
        self.me, self.own, self.buf, self.got, self.sent, self.came = me, own, buf, got, sent, came
        self.low = me.g < 2
        self.inner = jnp.where((me.g == 1) | (me.g == 2), 1, 0)
        step = jnp.where(self.low, 1, -1)
        self.ahead = me.at(g=me.g + step)
        self.back_to = me.at(g=me.g - step)

    def piece(self, i):
        return jnp.where(self.low, 3 - i, i)

    def copy(self, p, side, where):
        return remote(self.buf.at[p], self.got.at[side, p], self.sent.at[p], self.came.at[side, p], where)

    def forward(self, i):
        p = self.piece(i)

        @pl.when(self.inner == 0)
        def _():
            self.buf[p] = self.own(p).astype(BF)
            self.copy(p, 0, self.ahead).start()

        if i < 2:
            @pl.when(self.inner == 1)
            def _():
                self.copy(p, 0, self.back_to).wait_recv()
                self.buf[p] = (self.own(p) + self.got[0, p].astype(F32)).astype(BF)
                self.copy(p, 1, self.ahead).start()

    def back(self):
        p = self.piece(3)

        @pl.when(self.inner == 1)
        def _():
            self.copy(p, 1, self.ahead).wait_recv()
            self.buf[p] = (self.own(p) + self.got[1, p].astype(F32)).astype(BF)
            self.copy(p, 1, self.back_to).start()

    def end(self):
        g = self.me.g

        @pl.when(self.inner == 0)
        def _():
            self.copy(g, 1, self.ahead).wait_recv()
            self.buf[g] = (self.own(g) + self.got[1, g].astype(F32)).astype(BF)

        @pl.when(self.inner == 1)
        def _():
            self.copy(g, 0, self.back_to).wait_recv()
            self.copy(g, 1, self.ahead).wait_recv()
            self.buf[g] = (self.own(g) + self.got[0, g].astype(F32) + self.got[1, g].astype(F32)).astype(BF)

        for p in range(4):
            @pl.when(g != p)
            def _():
                self.copy(p, 0, self.ahead).wait_send()


def tail_kernel(slots, *refs):
    if slots:
        q_ref, k_ref, v_ref, ends_ref, o_ref, lse_ref, grad_ref, x_ref = refs[:8]
        g3_ref, dk_sum, dv_sum = refs[-3:]
        query_seg, key_seg = segments_from(ends_ref, slots)
        attention = (
            q_ref, k_ref, v_ref, query_seg, lambda j: key_seg(j * BK, BK), o_ref, lse_ref, grad_ref,
        )
        tail_steps(attention, dk_sum, dv_sum, x_ref, g3_ref, *refs[8:-3])
    else:
        tail_steps(None, None, None, *refs)


def tail_steps(
    attention, dk_sum, dv_sum,
    x_ref, g3_ref, w3_ref, down_ref, up_ref, out_ref, mid_ref, vec_ref,
    down_out, up_out, o_out, three_out, dx_ref, sums_ref,
    dxp, dx1, t1, xa, yb, t2a, t2b, ra, rb, moved_buf,
    yr_up, dbuf, dgot, ubuf, ugot,
    o_got, o_sum, yr_o, obuf, ogot,
    gq, qbuf, qgot, vs, vr,
    s_dx, r_dx, s_y, r_y, s_d, r_d, s_z, r_z, s_u, r_u, s_o, r_o, s_oz, r_oz, s_q, r_q,
    s_qf, r_qf, s_v, r_v, s_ag, r_ag, s_ay, r_ay, loc, x_rows,
):
    me = Place()
    g, b, f = me.g, me.b, me.f
    z_others = [me.at(g=(g + k) % 4) for k in (1, 2, 3)]
    meet(me, [me.across()] + [me.fsdp(k) for k in (1, 2, 3)] + z_others, True)

    def own_down(p):
        return down_ref[p].astype(F32)

    def own_up(p):
        return up_ref[:, b, p].astype(F32) + yr_up[p].astype(F32)

    def own_q(p):
        return gq[:, :, p].astype(F32)

    def own_o(p):
        return o_sum[b, p].astype(F32) + yr_o[p].astype(F32)

    flow_d = Flow(me, own_down, dbuf, dgot, s_d, r_d)
    flow_u = Flow(me, own_up, ubuf, ugot, s_z, r_z)
    flow_q = Flow(me, own_q, qbuf, qgot, s_q, r_q)
    flow_o = Flow(me, own_o, obuf, ogot, s_oz, r_oz)

    edge, inner = flow_d.inner == 0, flow_d.inner == 1
    x_copy = pltpu.make_async_copy(x_ref, x_rows, loc.at[1])
    x_copy.start()

    def at(which, *steps):
        @pl.when(which)
        def _():
            for step in steps:
                step()

    y_copies = []
    for i in range(4):
        p = flow_u.piece(i)
        c = remote(up_ref.at[:, 1 - b, p], yr_up.at[p], s_y.at[0, i], r_y.at[0, i], me.across())
        c.start()
        y_copies.append(c)

    o_copies = []
    for k in (1, 2, 3):
        c = remote(out_ref.at[(f + k) % 4], o_got.at[k - 1], s_o.at[k - 1], r_o.at[k - 1], me.fsdp(k))
        c.start()
        o_copies.append(c)
    c_oy = remote(o_sum.at[1 - b], yr_o, s_y.at[1, 0], r_y.at[1, 0], me.across())

    def up_forward(i):
        y_copies[i].wait()
        flow_u.forward(i)

    def up_back():
        y_copies[3].wait()
        flow_u.back()

    def output_rows():
        for c in o_copies:
            c.wait()
        o_sum[...] = (
            out_ref[f].astype(F32) + o_got[0].astype(F32) + o_got[1].astype(F32) + o_got[2].astype(F32)
        ).astype(BF)
        c_oy.start()

    at(edge, *(functools.partial(flow_d.forward, i) for i in range(3)))
    do = functools.partial
    between = (
        ((edge, do(up_forward, 0)), (inner, do(flow_d.forward, 0))),
        ((True, output_rows), (edge, do(up_forward, 1)), (inner, do(flow_d.forward, 1), do(up_forward, 0))),
        ((edge, do(up_forward, 2)), (inner, flow_d.back, do(up_forward, 1))),
        ((edge, y_copies[3].wait), (inner, y_copies[2].wait, up_back)),
    )
    if attention is not None:
        dk_sum[...] = jnp.zeros_like(dk_sum)
        dv_sum[...] = jnp.zeros_like(dv_sum)
    per = 2048 // BQ // 4
    for quarter, (first, last) in enumerate(QUARTERS):
        ranges = [(first * 512 // BK, last * 512 // BK)]

        def rows_step(i, carry):
            g3_ref[pl.ds(pl.multiple_of(i * BQ, BQ), BQ), pl.ds(0, PAIR)] = attend_back_rows(
                i, BQ, BK, ranges, *attention, dk_sum, dv_sum
            )
            return carry

        if attention is not None:
            lax.fori_loop(quarter * per, (quarter + 1) * per, rows_step, 0)
        for which, *steps in between[quarter]:
            if which is True:
                for step in steps:
                    step()
            else:
                at(which, *steps)
    if attention is not None:
        g3_ref[:, pl.ds(PAIR, PAIR)] = dk_sum[...].astype(BF)
        g3_ref[:, pl.ds(2 * PAIR, PAIR)] = dv_sum[...].astype(BF)

    hops = [me.sibling(), me.beside(), me.across(), me.at(g=g + 1 - 2 * (g % 2)), me.at(g=(g + 2) % 4)]
    vs[0] = vec_ref[...]
    here = pl.ds(pl.multiple_of((b * 4 + swapped(f)) * PAIR, PAIR), PAIR)
    sums3 = jnp.sum(g3_ref[...].astype(F32), axis=0, keepdims=True)
    vs[0, pl.ds(0, 1), here] = sums3[:, :PAIR]
    vs[0, pl.ds(1, 1), here] = sums3[:, 2 * PAIR :]

    def hop(i):
        if i > 0:
            hop_copy(i - 1).wait()
            vs[i] = vs[i - 1] + vr[i - 1]
        hop_copy(i).start()

    def hop_copy(i):
        return remote(vs.at[i], vr.at[i], s_v.at[i], r_v.at[i], hops[i])

    hop(0)

    def rows(size, q, other=False):
        half = 1 - b if other else b
        return pl.ds(pl.multiple_of((half * 4 + q) * size, size), size)

    def unit_cols(src):
        return pl.ds(pl.multiple_of(src * 1024, 1024), 1024)

    def head_cols(src):
        return pl.ds(pl.multiple_of((b * 4 + swapped(src)) * 128, 128), 128)

    def q_rows(q):
        return pl.ds(pl.multiple_of(q * 64, 64), 64)

    def pieces(kind, q, send, recv, where, other=False):
        half = 1 - b if other else b
        if kind == 0:
            parts = (down_out.at[rows(128, q, other), :], up_out.at[rows(32, q, other), :])
        else:
            parts = (
                o_out.at[rows(32, q, other), :],
                three_out.at[:, q_rows(q), pl.ds(pl.multiple_of(half * 512, 512), 512)],
            )
        return [remote(part, part, send.at[2 * kind + i, q], recv.at[2 * kind + i, q], where) for i, part in enumerate(parts)]

    def spread(kind, q, to_right, to_left):
        if to_right:
            @pl.when(g < 3)
            def _():
                for c in pieces(kind, q, s_ag.at[0], r_ag, me.at(g=g + 1)):
                    c.start()
        if to_left:
            @pl.when(g > 0)
            def _():
                for c in pieces(kind, q, s_ag.at[1], r_ag, me.at(g=g - 1)):
                    c.start()
        for c in pieces(kind, q, s_ay, r_ay, me.across()):
            c.start()

    def pass_on(kind, d):
        @pl.when(g >= d)
        def _():
            for c in pieces(kind, g - d, s_ag.at[0], r_ag, me.across()):
                c.wait_recv()
            spread(kind, g - d, True, False)

        @pl.when(g + d <= 3)
        def _():
            for c in pieces(kind, g + d, s_ag.at[1], r_ag, me.across()):
                c.wait_recv()
            spread(kind, g + d, False, True)

    def dx_step(i, carry):
        rows = pl.ds(pl.multiple_of(i * 256, 256), 256)
        part = dense_back(g3_ref[rows, :], w3_ref[...]).astype(BF)
        dxp[pl.ds(2 * i, 2)] = part.reshape(2, 2, 2, 2, 16, 1024)
        return carry

    lax.fori_loop(0, 8, dx_step, 0)
    c_core = remote(dxp.at[:, 1 - me.core], dx1, s_dx.at[0], r_dx.at[0], me.sibling())
    c_core.start()

    flow_u.end()
    up_out[rows(32, g), unit_cols(f)] = ubuf[g, f]
    u_out = []
    for k in (1, 2, 3):
        c = remote(ubuf.at[g, (f + k) % 4], up_out.at[rows(32, g), unit_cols(f)], s_u.at[k - 1], r_u.at[f], me.fsdp(k))
        c.start()
        u_out.append(c)
    flow_d.end()
    down_out[rows(128, g), :] = dbuf[g]

    c_core.wait()

    def t1_step(i, carry):
        t1[i] = (dxp[i, me.core].astype(F32) + dx1[i].astype(F32)).astype(BF)
        return carry

    lax.fori_loop(0, 16, t1_step, 0)
    lo, hi = pl.ds(0, 8), pl.ds(8, 8)
    c_xa = remote(t1.at[lo, 1 - me.x], xa, s_dx.at[1], r_dx.at[1], me.beside())
    c_yb = remote(t1.at[hi, :, 1 - b], yb, s_dx.at[2], r_dx.at[2], me.across())
    c_xa.start()
    c_yb.start()
    hop(1)

    x_copy.wait()

    def q_step(i, carry):
        cols = pl.ds(pl.multiple_of(i * 256, 256), 256)
        part = dense_in(x_rows[:, cols], g3_ref[...]).astype(BF)
        for j in range(3):
            gq[i, j] = part[:, j * 128 : (j + 1) * 128].reshape(4, 64, 128)
        return carry

    lax.fori_loop(0, 4, q_step, 0)
    at(edge, *(do(flow_q.forward, i) for i in range(3)))
    c_oy.wait()
    at(edge, *(do(flow_o.forward, i) for i in range(3)))
    for k in (1, 2, 3):
        src = (f + k) % 4
        remote(ubuf.at[g, 0], up_out.at[rows(32, g), unit_cols(src)], s_u.at[k - 1], r_u.at[src], me.fsdp(k)).wait_recv()
        u_out[k - 1].wait_send()
    c_xa.wait()
    t2a[...] = (t1[lo, me.x].astype(F32) + xa[...].astype(F32)).astype(BF)
    c_ra = remote(t2a.at[:, 1 - b], ra, s_dx.at[3], r_dx.at[3], me.across())
    c_ra.start()
    c_yb.wait()
    t2b[...] = (t1[hi, :, b].astype(F32) + yb[...].astype(F32)).astype(BF)
    c_rb = remote(t2b.at[:, 1 - me.x], rb, s_dx.at[4], r_dx.at[4], me.beside())
    c_rb.start()
    spread(0, g, True, True)
    at(inner, do(flow_q.forward, 0), do(flow_q.forward, 1), do(flow_o.forward, 0), do(flow_o.forward, 1))
    hop(2)
    c_ra.wait()
    c_rb.wait()
    moved_buf[lo] = (t2a[:, b].astype(F32) + ra[...].astype(F32) + mid_ref[lo]).astype(BF)
    moved_buf[hi] = (t2b[:, me.x].astype(F32) + rb[...].astype(F32) + mid_ref[hi]).astype(BF)

    @pl.when(me.stays())
    def _():
        c = pltpu.make_async_copy(moved_buf, dx_ref, loc.at[0])
        c.start()
        c.wait()

    @pl.when(jnp.logical_not(me.stays()))
    def _():
        remote(moved_buf, dx_ref, s_dx.at[5], r_dx.at[5], me.moved()).start()

    flow_q.back()
    flow_o.back()
    pass_on(0, 1)
    hop(3)

    flow_q.end()
    three_out[:, q_rows(g), head_cols(f)] = qbuf[g, f]
    q_out = []
    for k in (1, 2, 3):
        c = remote(qbuf.at[g, (f + k) % 4], three_out.at[:, q_rows(g), head_cols(f)], s_qf.at[k - 1], r_qf.at[f], me.fsdp(k))
        c.start()
        q_out.append(c)
    flow_o.end()
    o_out[rows(32, g), :] = obuf[g]
    for k in (1, 2, 3):
        src = (f + k) % 4
        remote(qbuf.at[g, 0], three_out.at[:, q_rows(g), head_cols(src)], s_qf.at[k - 1], r_qf.at[src], me.fsdp(k)).wait_recv()
        q_out[k - 1].wait_send()
    spread(1, g, True, True)
    pass_on(0, 2)
    pass_on(1, 1)
    pass_on(0, 3)
    hop(4)
    pass_on(1, 2)
    pass_on(1, 3)
    hop_copy(4).wait()
    sums_ref[...] = vs[4] + vr[4]

    @pl.when(jnp.logical_not(me.stays()))
    def _():
        remote(moved_buf, dx_ref, s_dx.at[5], r_dx.at[5], me.moved()).wait()

    for kind in (0, 1):
        for q in range(4):
            for c in pieces(kind, q, s_ay, r_ay, me.across()):
                c.wait_send()

            @pl.when((g >= q) & (g < 3))
            def _():
                for c in pieces(kind, q, s_ag.at[0], r_ag, me.across()):
                    c.wait_send()

            @pl.when((g <= q) & (g > 0))
            def _():
                for c in pieces(kind, q, s_ag.at[1], r_ag, me.across()):
                    c.wait_send()

            for c in pieces(kind, q, s_ay, r_ay, me.across(), other=True):
                c.wait_recv()


def tail(slots, attention, x_all, g3, w3, down, up, out, mid, vec):
    dma = pltpu.SemaphoreType.DMA
    v = pltpu.VMEM
    scratch = [
        v((16, 2, 2, 2, 16, 1024), BF), v((16, 2, 2, 16, 1024), BF), v((16, 2, 2, 16, 1024), BF),
        v((8, 2, 16, 1024), BF), v((8, 2, 16, 1024), BF), v((8, 2, 16, 1024), BF), v((8, 2, 16, 1024), BF),
        v((8, 16, 1024), BF), v((8, 16, 1024), BF), v((16, 16, 1024), BF),
        v((4, 4, 32, 1024), BF), v((4, 128, 1024), BF), v((2, 4, 128, 1024), BF),
        v((4, 4, 32, 1024), BF), v((2, 4, 4, 32, 1024), BF),
        v((3, 2, 4, 32, 1024), BF), v((2, 4, 32, 1024), BF), v((4, 32, 1024), BF),
        v((4, 32, 1024), BF), v((2, 4, 32, 1024), BF),
        v((4, 3, 4, 64, 128), BF), v((4, 4, 3, 64, 128), BF), v((2, 4, 4, 3, 64, 128), BF),
        v((5, 16, 1024), F32), v((5, 16, 1024), F32),
        dma((6,)), dma((6,)), dma((2, 5)), dma((2, 5)), dma((4,)), dma((2, 4)), dma((4,)), dma((2, 4)),
        dma((3,)), dma((4,)), dma((3,)), dma((3,)), dma((4,)), dma((2, 4)), dma((4,)), dma((2, 4)),
        dma((3,)), dma((4,)), dma((5,)), dma((5,)), dma((2, 4, 4)), dma((4, 4)), dma((4, 4)), dma((4, 4)), dma((2,)),
        v((2048, 1024), BF),
    ]
    if slots:
        scratch += [v((2048, 3 * PAIR), BF), v((2048, PAIR), F32), v((2048, PAIR), F32)]
        operands = (*attention, x_all)
    else:
        operands = (x_all, g3)
    operands += (
        w3, down.reshape(4, 128, 1024), up.reshape(4, 2, 4, 32, 1024), out.reshape(4, 2, 4, 32, 1024),
        mid.reshape(16, 16, 1024), vec,
    )
    return pl.pallas_call(
        functools.partial(tail_kernel, slots),
        out_shape=(
            jax.ShapeDtypeStruct((1024, 1024), BF),
            jax.ShapeDtypeStruct((256, 4096), BF),
            jax.ShapeDtypeStruct((256, 1024), BF),
            jax.ShapeDtypeStruct((3, 256, 1024), BF),
            jax.ShapeDtypeStruct((16, 16, 1024), BF),
            jax.ShapeDtypeStruct((16, 1024), F32),
        ),
        in_specs=[pl.BlockSpec(memory_space=pl.ANY) if ref is x_all else VMEM for ref in operands],
        out_specs=(VMEM,) * 6,
        scratch_shapes=scratch,
        compiler_params=pltpu.CompilerParams(collective_id=1, has_side_effects=True, vmem_limit_bytes=60 * 2**20),
        cost_estimate=pl.CostEstimate(flops=4 * 10**9, bytes_accessed=40 * 2**20, transcendentals=0),
    )(*operands)


def tile_cols(i, size):
    return pl.ds(pl.multiple_of(i * size, size), size)


def middle_kernel(
    heads_ref, x_ref, up_ref, wo_ref, wu_ref, wd_ref, par_ref,
    layer_ref, down_out, upg_out, og_out, gatt_ref, mid1_ref, vec_ref,
    att, nl, gff, slope, hid, gpre, normed, xhat, rstd, work, moved_buf, gbr, gas, ps, pr, down, down_y,
    s_a, r_a, s_b, r_b, s_g, r_g, s_p, r_p, s_m, r_m, s_y, r_y, loc,
):
    me = Place()
    f, b = me.f, me.b
    sib = f + 1 - 2 * me.core
    xs = (f + 2) % 4
    xo = xs + 1 - 2 * me.core
    peers = [me.at(f=(f + k % 4) % 4, b=(b + k // 4) % 2) for k in range(1, 8)]
    meet(me, peers, True)
    slot = swapped(f) * 2 + b
    unit = b * 4 + swapped(f)

    def peer_slot(k, sign):
        pf, pb = (f + sign * (k % 4) + 4) % 4, (b + k // 4) % 2
        return swapped(pf) * 2 + pb, pb * 4 + swapped(pf)

    def lanes(index):
        return pl.ds(pl.multiple_of(index * PAIR, PAIR), PAIR)

    for k in range(1, 8):
        where, _ = peer_slot(k, 1)
        remote(heads_ref.at[:, where], att.at[:, :, lanes(unit)], s_a.at[k - 1], r_a.at[k - 1], peers[k - 1]).start()
    att[:, :, lanes(unit)] = heads_ref[:, slot]
    for k in range(1, 8):
        _, theirs = peer_slot(k, -1)
        remote(heads_ref.at[:, slot], att.at[:, :, lanes(theirs)], s_a.at[k - 1], r_a.at[k - 1], peers[k - 1]).wait()

    def row(i):
        return par_ref[pl.ds(i, 1), :]

    def att_rows():
        return att[...].reshape(256, 1024)

    def proj(i, carry):
        cols = tile_cols(i, 512)
        work[:, cols] = dense(att_rows(), wo_ref[:, cols])
        return carry

    lax.fori_loop(0, 2, proj, 0)
    value, x_hat, inv = norm_fwd(x_ref[...].astype(F32) + work[...] + row(0), row(1), row(2))
    normed[...] = value
    xhat[...] = x_hat
    rstd[...] = inv
    nl[f] = value.astype(BF)

    def share(buf, t):
        to_sib = remote(buf.at[f], buf.at[f], s_g.at[t, 0], r_g.at[t, 0], me.sibling())
        to_x = remote(buf.at[f], buf.at[f], s_g.at[t, 1], r_g.at[t, 1], me.beside())
        to_x.start()
        to_sib.start()

        def from_sib():
            to_sib.wait_send()
            remote(buf.at[sib], buf.at[sib], s_g.at[t, 0], r_g.at[t, 0], me.sibling()).wait_recv()

        def from_x():
            to_x.wait_send()
            remote(buf.at[xs], buf.at[xs], s_g.at[t, 1], r_g.at[t, 1], me.beside()).wait_recv()
            remote(buf.at[xs], buf.at[xs], s_g.at[t, 2], r_g.at[t, 2], me.sibling()).start()

        def from_other():
            remote(buf.at[xs], buf.at[xs], s_g.at[t, 2], r_g.at[t, 2], me.sibling()).wait_send()
            remote(buf.at[xo], buf.at[xo], s_g.at[t, 2], r_g.at[t, 2], me.sibling()).wait_recv()

        return from_sib, from_x, from_other

    def scatter(t, i, where):
        return remote(ps.at[t, i], pr.at[t, i], s_p.at[t, i], r_p.at[t, i], where)

    def run(t, block, buf, beside_x):
        from_sib, from_x, from_other = share(buf, t)
        block(f, 3)
        from_sib()
        block(sib, 0)
        scatter(t, 0, me.sibling()).start()
        from_x()
        block(xs, 2)
        from_other()
        block(xo, 1)
        scatter(t, 1, me.sibling()).start()
        scatter(t, 1, me.sibling()).wait()
        ps[t, 2] = (ps[t, 2].astype(F32) + pr[t, 1].astype(F32)).astype(BF)
        scatter(t, 2, me.beside()).start()
        beside_x()
        scatter(t, 0, me.sibling()).wait()
        scatter(t, 2, me.beside()).wait()
        return ps[t, 3].astype(F32) + pr[t, 0].astype(F32) + pr[t, 2].astype(F32)

    def forward(index, into):
        def up_tile(i, carry):
            cols = tile_cols(i, 256)
            pre = dense(nl[index], wu_ref[:, cols]) + par_ref[pl.ds(6, 1), cols]
            cdf = 0.5 * (1.0 + lax.erf(pre * 0.7071067811865476))
            hid[index, :, cols] = (pre * cdf).astype(BF)
            slope[index, :, cols] = cdf + pre * jnp.exp(-0.5 * pre * pre) * 0.3989422804014327
            return carry

        def down_tile(i, carry):
            cols = tile_cols(i, 512)
            ps[0, into, :, cols] = dense(hid[index], wd_ref[:, cols]).astype(BF)
            return carry

        lax.fori_loop(0, 4, up_tile, 0)
        lax.fori_loop(0, 2, down_tile, 0)

    ffn = run(0, forward, nl, lambda: None)
    value, x_hat, inv = norm_fwd(normed[...] + ffn + row(3), row(4), row(5))
    moved_buf[...] = value.astype(BF)

    @pl.when(me.stays())
    def _():
        pltpu.make_async_copy(moved_buf, layer_ref, loc.at[0]).start()

    @pl.when(jnp.logical_not(me.stays()))
    def _():
        remote(moved_buf, layer_ref, s_m.at[0], r_m.at[0], me.moved()).start()

    grad2, gain2, shift2 = norm_back(up_ref[...].astype(F32), x_hat, inv, row(4))
    work[...] = grad2
    low2 = grad2.astype(BF)
    gff[f] = low2
    vec_ref[pl.ds(4, 1), :] = jnp.sum(low2.astype(F32), axis=0, keepdims=True)
    vec_ref[pl.ds(5, 1), :] = gain2[None]
    vec_ref[pl.ds(6, 1), :] = shift2[None]

    def backward(index, into):
        def pre_tile(i, carry):
            cols = tile_cols(i, 512)
            part = dense_back(gff[index], wd_ref[cols, :])
            gpre[index, :, cols] = (part * slope[index, :, cols]).astype(BF)
            return carry

        def in_tile(i, carry):
            cols = tile_cols(i, 512)
            ps[1, into, :, cols] = dense_back(gpre[index], wu_ref[cols, :]).astype(BF)
            return carry

        lax.fori_loop(0, 2, pre_tile, 0)
        lax.fori_loop(0, 2, in_tile, 0)

    c_down = remote(down.at[1 - b], down_y, s_y.at[0], r_y.at[0], me.across())

    def weight_grads():
        def down_tile(i, carry):
            cols = tile_cols(i, 256)
            part = dense_in(hid[:, :, cols].reshape(1024, 256), gff[...].reshape(1024, 1024)).astype(BF)
            down[i // 2, pl.ds(pl.multiple_of(i % 2 * 256, 256), 256)] = part
            return carry

        def up_tile(i, carry):
            cols = tile_cols(i, 256)
            upg_out[cols, :] = dense_in(nl[:, :, cols].reshape(1024, 256), gpre[...].reshape(1024, 1024)).astype(BF)
            return carry

        lax.fori_loop(0, 4, down_tile, 0)
        c_down.start()
        lax.fori_loop(0, 4, up_tile, 0)
        vec_ref[pl.ds(3, 1), :] = jnp.sum(gpre[...].reshape(1024, 1024).astype(F32), axis=0, keepdims=True)

    back = run(1, backward, gff, weight_grads)
    grad1, gain1, shift1 = norm_back(back + work[...], xhat[...], rstd[...], row(1))
    mid1_ref[...] = grad1
    low1 = grad1.astype(BF)
    gbr[...] = low1
    vec_ref[pl.ds(0, 1), :] = jnp.sum(low1.astype(F32), axis=0, keepdims=True)
    vec_ref[pl.ds(1, 1), :] = gain1[None]
    vec_ref[pl.ds(2, 1), :] = shift1[None]
    vec_ref[pl.ds(7, 1), :] = jnp.zeros((1, 1024), F32)

    def att_tile(i, carry):
        part = dense_back(gbr[...], wo_ref[tile_cols(i, 256), :]).astype(BF)
        for j in range(2):
            gas[2 * i + j] = part[:, j * PAIR : (j + 1) * PAIR].reshape(16, 16, PAIR)
        return carry

    lax.fori_loop(0, 4, att_tile, 0)
    for k in range(1, 8):
        _, theirs = peer_slot(k, 1)
        remote(gas.at[theirs], gatt_ref.at[:, slot], s_b.at[k - 1], r_b.at[k - 1], peers[k - 1]).start()
    gatt_ref[:, slot] = gas[unit]

    def o_tile(i, carry):
        cols = tile_cols(i, 256)
        og_out[cols, :] = dense_in(att[:, :, cols].reshape(256, 256), gbr[...]).astype(BF)
        return carry

    lax.fori_loop(0, 4, o_tile, 0)
    for k in range(1, 8):
        where, _ = peer_slot(k, -1)
        remote(gas.at[0], gatt_ref.at[:, where], s_b.at[k - 1], r_b.at[k - 1], peers[k - 1]).wait()
    c_down.wait()
    down_out[...] = (down[b].astype(F32) + down_y[...].astype(F32)).astype(BF)

    @pl.when(me.stays())
    def _():
        pltpu.make_async_copy(moved_buf, layer_ref, loc.at[0]).wait()

    @pl.when(jnp.logical_not(me.stays()))
    def _():
        remote(moved_buf, layer_ref, s_m.at[0], r_m.at[0], me.moved()).wait()


def middle(heads, x, upstream, w_output, w_up, w_down, params):
    dma = pltpu.SemaphoreType.DMA
    v = pltpu.VMEM
    block = (4, 256, 1024)
    scratch = [
        v((16, 16, 1024), BF), v(block, BF), v(block, BF), v(block, F32), v(block, BF), v(block, BF),
        v((256, 1024), F32), v((256, 1024), F32), v((256, 1), F32), v((256, 1024), F32), v((256, 1024), BF),
        v((256, 1024), BF), v((8, 16, 16, PAIR), BF), v((2, 4, 256, 1024), BF), v((2, 3, 256, 1024), BF),
        v((2, 512, 1024), BF), v((512, 1024), BF),
        dma((7,)), dma((7,)), dma((7,)), dma((7,)), dma((2, 3)), dma((2, 3)), dma((2, 3)), dma((2, 3)),
        dma((1,)), dma((1,)), dma((1,)), dma((1,)), dma((1,)),
    ]
    square = jax.ShapeDtypeStruct((1024, 1024), BF)
    return pl.pallas_call(
        middle_kernel,
        out_shape=(
            jax.ShapeDtypeStruct((256, 1024), BF), jax.ShapeDtypeStruct((512, 1024), BF), square, square,
            jax.ShapeDtypeStruct((16, 8, 16, PAIR), BF),
            jax.ShapeDtypeStruct((256, 1024), F32),
            jax.ShapeDtypeStruct((8, 1024), F32),
        ),
        in_specs=[VMEM] * 7,
        out_specs=(VMEM,) * 7,
        scratch_shapes=scratch,
        compiler_params=pltpu.CompilerParams(collective_id=2, has_side_effects=True, vmem_limit_bytes=60 * 2**20),
        cost_estimate=pl.CostEstimate(flops=14 * 10**9, bytes_accessed=20 * 2**20, transcendentals=2**21),
    )(heads.reshape(16, 8, 16, PAIR), x, upstream, w_output, w_up, w_down, params)


def start_kernel(
    slots, tok_ref, cot_ref, ends_ref, qw_ref, kw_ref, vw_ref, ow_ref, ew_ref, bias_ref,
    x_ref, up_ref, ends_out, q_ref, k_ref, v_ref, w3_ref, wo_ref, wu_ref, att_ref, lse_ref,
    s_m, r_m, s_w, r_w, s_u, r_u, s_o, r_o, s_x, r_x, loc,
):
    me = Place()
    g, b, f = me.g, me.b, me.f
    sib = f + 1 - 2 * me.core
    xs = (f + 2) % 4
    xo = xs + 1 - 2 * me.core
    meet(me, [me.across()] + [me.fsdp(k) for k in (1, 2, 3)], True)
    slot = me.core * 4 + me.x * 2 + b
    slot_x = me.core * 4 + (1 - me.x) * 2 + b
    slot_y = slot + 1 - 2 * b
    slot_d = slot_x + 1 - 2 * b
    other = 4 - 8 * me.core
    lo, hi = pl.ds(0, 8), pl.ds(8, 8)

    def moves(i, src, dst):
        return remote(src, dst, s_m.at[i], r_m.at[i], me.moved())

    def relocate(i, src, dst):
        @pl.when(me.stays())
        def _():
            pltpu.make_async_copy(src, dst, loc.at[i]).start()

        @pl.when(jnp.logical_not(me.stays()))
        def _():
            moves(i, src, dst).start()

    def relocated(i, src, dst):
        @pl.when(me.stays())
        def _():
            pltpu.make_async_copy(src, dst, loc.at[i]).wait()

        @pl.when(jnp.logical_not(me.stays()))
        def _():
            moves(i, src, dst).wait()

    theirs = x_ref.at[:, g * 2 + b]
    relocate(0, tok_ref, theirs)
    relocate(1, ends_ref, ends_out)

    def cols(index, size):
        return pl.ds(pl.multiple_of(index * size, size), size)

    def w3_rows(src):
        return cols(src, 256)

    def wo_rows(src, which):
        return pl.ds(pl.multiple_of(src * 256 + which * 128, 128), 128)

    half = cols(b, 128)
    u_x = [
        remote(ew_ref.at[half, cols(xs, 1024)], wu_ref.at[wo_rows(f, b)], s_u.at[1], r_u.at[1], me.beside()),
        remote(ew_ref.at[half, cols(xo, 1024)], wu_ref.at[wo_rows(f, b)], s_u.at[2], r_u.at[2], me.at(f=xo)),
    ]
    o_x = remote(ow_ref.at[half], wo_ref.at[wo_rows(f, b)], s_o.at[1], r_o.at[1], me.beside())
    u_sib = remote(ew_ref.at[:, cols(sib, 1024)], wu_ref.at[w3_rows(f)], s_u.at[0], r_u.at[0], me.sibling())
    o_sib = remote(ow_ref, wo_ref.at[w3_rows(f)], s_o.at[0], r_o.at[0], me.sibling())
    for c in (u_x[0], u_sib, o_sib):
        c.start()
    o_own = pltpu.make_async_copy(ow_ref, wo_ref.at[w3_rows(f)], loc.at[5])
    u_own = pltpu.make_async_copy(ew_ref.at[:, cols(f, 1024)], wu_ref.at[w3_rows(f)], loc.at[6])
    o_own.start()
    u_own.start()
    weights = (qw_ref, kw_ref, vw_ref)

    def w3_own(j):
        return pltpu.make_async_copy(
            weights[j].at[:, cols(b * 4 + swapped(f), 128)], w3_ref.at[w3_rows(f), pl.ds(128 * j, 128)], loc.at[2 + j]
        )

    for j in range(3):
        w3_own(j).start()
    for k in (2, 3, 1):
        dest = b * 4 + swapped((f + k) % 4)
        for j in range(3):
            remote(
                weights[j].at[:, cols(dest, 128)], w3_ref.at[w3_rows(f), pl.ds(128 * j, 128)],
                s_w.at[j, k - 1], r_w.at[j, k - 1], me.fsdp(k),
            ).start()

    def piece(i, ref, where):
        return remote(ref, ref, s_x.at[i], r_x.at[i], where)

    relocated(0, tok_ref, theirs)
    own = x_ref.at[:, slot]
    sends = [piece(1, own, me.beside()), piece(2, own, me.across()), piece(0, own, me.sibling())]
    for c in sends:
        c.start()

    def project(which):
        part = dense(x_ref[:, which].reshape(256, 1024), w3_ref[...]) + bias_ref[...]
        part = part.astype(BF).reshape(16, 16, 3 * PAIR)
        q_ref[:, which] = part[:, :, :PAIR]
        k_ref[:, which] = part[:, :, PAIR : 2 * PAIR]
        v_ref[:, which] = part[:, :, 2 * PAIR :]

    piece(1, x_ref.at[:, slot_x], me.beside()).wait_recv()
    more = [piece(4, x_ref.at[hi, slot_x], me.across()), piece(3, x_ref.at[:, slot_x], me.sibling())]
    for c in more:
        c.start()
    sends += more
    piece(2, x_ref.at[:, slot_y], me.across()).wait_recv()
    more = [piece(6, x_ref.at[lo, slot_y], me.beside()), piece(5, x_ref.at[:, slot_y], me.sibling())]
    for c in more:
        c.start()
    sends += more
    for c in (u_x[1], o_x):
        c.start()
    relocate(7, cot_ref, up_ref)
    u_fwd = [
        remote(wu_ref.at[wo_rows(src, b)], wu_ref.at[wo_rows(src, b)], s_u.at[3 + i], r_u.at[3 + i], me.across())
        for i, src in enumerate((xs, xo))
    ]
    u_x[0].wait()
    u_fwd[0].start()
    for k in (1, 2, 3):
        src = (f + 4 - k) % 4
        for j in range(3):
            remote(
                weights[j].at[:, cols(0, 128)], w3_ref.at[w3_rows(src), pl.ds(128 * j, 128)],
                s_w.at[j, k - 1], r_w.at[j, k - 1], me.fsdp(k),
            ).wait()
    for j in range(3):
        w3_own(j).wait()
    project(slot)
    project(slot_x)
    piece(4, x_ref.at[hi, slot_d], me.across()).wait_recv()
    more = [piece(8, x_ref.at[hi, slot_d], me.sibling())]
    more[0].start()
    piece(6, x_ref.at[lo, slot_d], me.beside()).wait_recv()
    more.append(piece(7, x_ref.at[lo, slot_d], me.sibling()))
    more[1].start()
    sends += more
    project(slot_y)
    for i, part in ((0, slot + other), (3, slot_x + other), (5, slot_y + other)):
        piece(i, x_ref.at[:, part], me.sibling()).wait_recv()
        project(part)
    project(slot_d)
    piece(8, x_ref.at[hi, slot_d + other], me.sibling()).wait_recv()
    piece(7, x_ref.at[lo, slot_d + other], me.sibling()).wait_recv()
    project(slot_d + other)
    for c in sends:
        c.wait_send()
    relocated(1, ends_ref, ends_out)

    segments = segments_from(ends_out, slots)

    def attend_quarter(quarter):
        first, last = QUARTERS[quarter]

        rows, lse = attend_wide(quarter, WIDE, first * 512, (last - first) * 512, q_ref, k_ref, v_ref, *segments)
        att_ref[pl.ds(quarter * 4, 4)] = rows.astype(BF).reshape(4, GROUP, 16, PAIR)
        for part in range(WIDE // BQ):
            for head in range(2):
                to = 2 * (quarter * WIDE + part * BQ) + head * BQ
                lse_ref[pl.ds(to, BQ), :] = lse[head * WIDE + part * BQ : head * WIDE + (part + 1) * BQ]

    if slots:
        attend_quarter(0)
    u_x[1].wait()
    u_fwd[1].start()
    o_x.wait()
    o_fwd = [
        remote(wo_ref.at[wo_rows(xs, b)], wo_ref.at[wo_rows(xs, b)], s_o.at[2], r_o.at[2], me.sibling()),
        remote(wo_ref.at[wo_rows(xs, b)], wo_ref.at[wo_rows(xs, b)], s_o.at[3], r_o.at[3], me.across()),
    ]
    for c in o_fwd:
        c.start()
    if slots:
        attend_quarter(1)
        attend_quarter(2)
    o_fwd[0].wait()
    o_fwd[1].wait()
    late = remote(wo_ref.at[wo_rows(xs, 1 - b)], wo_ref.at[wo_rows(xs, 1 - b)], s_o.at[4], r_o.at[4], me.sibling())
    late.start()
    if slots:
        attend_quarter(3)
    late.wait()
    o_own.wait()
    o_sib.wait()
    u_own.wait()
    u_sib.wait()
    relocated(7, cot_ref, up_ref)
    for c in u_fwd:
        c.wait()


def start(slots, tokens, cotangent, ends, query_w, key_w, value_w, output_w, expand_w, bias3):
    dma = pltpu.SemaphoreType.DMA
    hbm = pl.BlockSpec(memory_space=pl.ANY)
    heads = jax.ShapeDtypeStruct((16, GROUP, 16, PAIR), BF)
    square = jax.ShapeDtypeStruct((1024, 1024), BF)
    return pl.pallas_call(
        functools.partial(start_kernel, slots),
        out_shape=(
            jax.ShapeDtypeStruct((16, GROUP, 16, 1024), BF), jax.ShapeDtypeStruct((16, 16, 1024), BF),
            jax.ShapeDtypeStruct((8, 128), jnp.int32), heads, heads, heads,
            jax.ShapeDtypeStruct((1024, 3 * PAIR), BF), square, square,
            heads, jax.ShapeDtypeStruct((4096, 1), F32),
        ),
        in_specs=[hbm, hbm, VMEM] + [hbm] * 5 + [VMEM],
        out_specs=(VMEM, hbm, VMEM, VMEM, VMEM, VMEM, VMEM, hbm, hbm, VMEM, VMEM),
        scratch_shapes=[
            dma((8,)), dma((8,)), dma((3, 3)), dma((3, 3)), dma((5,)), dma((5,)), dma((5,)), dma((5,)),
            dma((9,)), dma((9,)), dma((8,)),
        ],
        compiler_params=pltpu.CompilerParams(collective_id=3, has_side_effects=True, vmem_limit_bytes=60 * 2**20),
        cost_estimate=pl.CostEstimate(flops=2 * 10**9, bytes_accessed=20 * 2**20, transcendentals=0),
    )(tokens, cotangent, ends, query_w, key_w, value_w, output_w, expand_w, bias3)


def body(
    tokens, lengths, packing, query_w, query_b, key_w, value_w, value_b, output_w, output_b,
    attn_gain, attn_shift, expand_w, expand_b, reduce_w, reduce_b, ffn_gain, ffn_shift, cotangent,
):
    tok_shape = tokens.shape
    laps, stripe, width = tok_shape[1], tok_shape[2], tok_shape[3]
    mine = laps * stripe
    n_ctx = lax.axis_size("ctx")
    n_f = lax.axis_size("fsdp")
    per_group = n_ctx // n_f
    chunks = per_group // 2
    ctx = lax.axis_index("ctx")
    f = lax.axis_index("fsdp")
    g = ctx // per_group
    chunk = ctx % per_group // 2
    b = ctx % 2
    same_place = [
        [(gg * chunks + s) * 2 + bb for s in range(chunks)] for gg in range(n_f) for bb in range(2)
    ]
    units = expand_w.shape[1] // n_f

    ordered = jnp.sum(
        jnp.where(
            packing[0][:, None] == jnp.arange(lengths.shape[1], dtype=jnp.int32)[None, :],
            lengths[0][None, :],
            0,
        ),
        axis=1,
    )
    slots = jnp.arange(ordered.shape[0], dtype=jnp.int32)
    own_ends = jnp.sum(jnp.where(slots[None, :] <= slots[:, None], ordered[None, :], 0), axis=1)
    own_ends = jnp.pad(own_ends[None], ((0, 7), (0, 128 - own_ends.shape[0])))

    here = (b * n_f + swapped(f)) * PAIR
    bias3 = jnp.concatenate(
        [
            lax.dynamic_slice_in_dim(query_b, here, PAIR),
            jnp.zeros((PAIR,), F32),
            lax.dynamic_slice_in_dim(value_b, here, PAIR),
        ]
    )[None]
    acts = (laps, stripe, width)
    n_slots = lengths.shape[1] if chunks == 1 else 0
    x_all, upstream, ends, q, k_own, v_own, w_three, w_output, w_up, att_heads, lse = start(
        n_slots, tokens.reshape(acts), cotangent.reshape(acts), own_ends, query_w, key_w, value_w, output_w, expand_w, bias3
    )
    q, k_own, v_own = (part.reshape(GROUP * mine, PAIR) for part in (q, k_own, v_own))
    inputs = lax.dynamic_index_in_dim(x_all, swapped(f) * 2 + b, 1, keepdims=False).reshape(mine, width)
    x_all = x_all.reshape(GROUP * mine, width)
    upstream = upstream.reshape(mine, width)
    slot_ends = ends[0, : ordered.shape[0]]

    span = GROUP * mine
    index = jnp.arange(span, dtype=jnp.int32)

    def segments(which):
        lap, rest = index // (GROUP * stripe), index % (GROUP * stripe)
        unit, place = rest // stripe, rest % stripe
        owner = unit // 2 * per_group + which * 2 + unit % 2
        position = lap * (n_ctx * stripe) + owner * stripe + place
        return jnp.sum((position[:, None] >= slot_ends[None, :]).astype(jnp.int32), axis=1)

    attention = (q, k_own, v_own, ends, att_heads.reshape(span, PAIR), lse)
    if chunks > 1:
        seg_q = segments(chunk)
        seg_k = jnp.concatenate([segments(s) for s in range(chunks)])
        q_first, q_last = seg_q[::BQ], seg_q[BQ - 1 :: BQ]
        k_first = seg_k[::BK].reshape(chunks, -1)
        k_last = seg_k[BK - 1 :: BK].reshape(chunks, -1)
        lo = jnp.sum((k_last[None] < q_first[:, None, None]).astype(jnp.int32), axis=2)
        hi = jnp.sum((k_first[None] <= q_last[:, None, None]).astype(jnp.int32), axis=2)
        bounds = (lo, hi)
        k = lax.all_gather(k_own, "ctx", axis_index_groups=same_place, tiled=True)
        v = lax.all_gather(v_own, "ctx", axis_index_groups=same_place, tiled=True)
        keyed = (q, k, v, seg_q[:, None], seg_k[None, :])
        att_heads, lse = attend(bounds, *keyed, chunks)

    params = jnp.stack(
        [
            output_b, attn_gain, attn_shift, reduce_b, ffn_gain, ffn_shift,
            lax.dynamic_slice_in_dim(expand_b, f * units, units), jnp.zeros_like(output_b),
        ]
    )
    layer_out, part_down, part_up, part_out, grad_att, grad_mid1, vec = middle(
        att_heads, inputs, upstream, w_output, w_up, reduce_w, params
    )
    layer_out = layer_out.reshape(tok_shape)
    grad_att = grad_att.reshape(GROUP * mine, PAIR)

    attention += (grad_att,)
    grad_three = None
    if chunks > 1:
        grad_q, grad_k, grad_v = attend_back(bounds, *keyed, att_heads, lse, grad_att, chunks)
        attention = None
        grad_k = lax.psum_scatter(
            grad_k.astype(BF), "ctx", axis_index_groups=same_place, tiled=True
        )
        grad_v = lax.psum_scatter(
            grad_v.astype(BF), "ctx", axis_index_groups=same_place, tiled=True
        )
        grad_three = jnp.concatenate([grad_q, grad_k, grad_v], axis=1)
    here_rows = jnp.zeros((n_f, units), F32)
    sums = jnp.concatenate(
        [
            jnp.zeros((2, width), F32),
            vec[:3],
            vec[4:7],
            lax.dynamic_update_slice_in_dim(here_rows, vec[3:4], f, 0),
            here_rows,
        ]
    )
    share_down, share_up, share_out, share_three, moved, sums = tail(
        n_slots, attention, x_all, grad_three, w_three, part_down, part_up, part_out, grad_mid1, sums
    )
    grad_inputs = moved.reshape(tok_shape).astype(F32)
    shares = tuple(part.astype(F32) for part in (share_three, share_out, share_up, share_down)) + (sums,)
    if chunks > 1:
        shares = lax.psum(shares, "ctx", axis_index_groups=same_place)
    share_three, share_out, share_up, share_down, sums = shares
    (
        grad_query_b, grad_value_b, grad_output_b, grad_attn_gain, grad_attn_shift, grad_reduce_b,
        grad_ffn_gain, grad_ffn_shift,
    ) = (sums[i] for i in range(8))
    grad_expand_b = sums[8 : 8 + n_f].reshape(-1)
    return (
        layer_out,
        grad_inputs,
        share_three[0],
        grad_query_b,
        share_three[1],
        share_three[2],
        grad_value_b,
        share_out,
        grad_output_b,
        grad_attn_gain,
        grad_attn_shift,
        share_up,
        grad_expand_b,
        share_down,
        grad_reduce_b,
        grad_ffn_gain,
        grad_ffn_shift,
    )


def solution(mesh):
    acts = P("fsdp", None, "ctx", None)
    rows = P("fsdp", None)
    return jax.shard_map(
        body,
        mesh=mesh,
        in_specs=(
            acts, rows, rows, rows, P(), rows, rows, P(), rows, P(),
            P(), P(), rows, P(), rows, P(), P(), P(), acts,
        ),
        out_specs=(
            acts, acts, rows, P(), rows, rows, P(), rows, P(),
            P(), P(), rows, P(), rows, P(), P(), P(),
        ),
        check_vma=False,
    )
```

```python
import functools
import jax
import jax.numpy as jnp
from jax import lax
from jax.experimental import pallas as pl
from jax.experimental.pallas import tpu as pltpu
from jax.sharding import PartitionSpec as P

H = 16
HD = 64
PAIR = 2 * HD
GROUP = 8
SWAP = (0, 2, 1, 3)
BQ = 512
BK = 512
WIDE = 512
QUARTERS = ((0, 2), (0, 3), (1, 4), (2, 4))
BF = jnp.bfloat16
F32 = jnp.float32


def dense(left, right):
    return jnp.dot(left, right, preferred_element_type=F32)


def dense_back(left, right):
    return lax.dot_general(left, right, (((1,), (1,)), ((), ())), preferred_element_type=F32)


def dense_in(left, right):
    return lax.dot_general(left, right, (((0,), (0,)), ((), ())), preferred_element_type=F32)


def norm_fwd(hidden, gain, shift):
    mean_row = jnp.mean(hidden, axis=-1, keepdims=True)
    centred = hidden - mean_row
    variance = jnp.mean(centred * centred, axis=-1, keepdims=True)
    inv_std = lax.rsqrt(variance + 1e-05)
    x_hat = centred * inv_std
    return (x_hat * gain + shift, x_hat, inv_std)


def norm_back(incoming, x_hat, inv_std, gain):
    scaled = incoming * gain
    grad_in = inv_std * (
        scaled
        - jnp.mean(scaled, axis=-1, keepdims=True)
        - x_hat * jnp.mean(scaled * x_hat, axis=-1, keepdims=True)
    )
    return (grad_in, jnp.sum(incoming * x_hat, axis=0), jnp.sum(incoming, axis=0))


def gelu_slope(pre_act):
    return (
        0.5 * (1.0 + lax.erf(pre_act * 0.7071067811865476))
        + pre_act * jnp.exp(-0.5 * pre_act * pre_act) * 0.3989422804014327
    )


def first_half(shape):
    return lax.broadcasted_iota(jnp.int32, shape, 1) < HD


def both_heads(block):
    left = first_half(block.shape)
    zero = jnp.zeros_like(block)
    return jnp.concatenate([jnp.where(left, block, zero), jnp.where(left, zero, block)], axis=0)


def by_head(stacked):
    rows = stacked.shape[0] // 2
    left = first_half((rows, stacked.shape[1]))
    return jnp.where(left, stacked[:rows], stacked[rows:])


def row_block(ref, i, size):
    if len(ref.shape) == 2:
        return ref[pl.ds(pl.multiple_of(i * size, size), size), :]
    laps = size // (ref.shape[1] * ref.shape[2])
    return ref[pl.ds(i * laps, laps)].reshape(size, ref.shape[3])


def attend_rows(i, bq, bk, ranges, q_ref, k_ref, v_ref, query_seg, key_seg):
    q2 = both_heads(row_block(q_ref, i, bq) * BF(0.125))
    seg = query_seg(i)
    seg2 = jnp.concatenate([seg, seg], axis=0)

    def k_step(j, state):
        accum, run_max, run_sum = state
        scores = dense_back(q2, row_block(k_ref, j, bk))
        scores = jnp.where(seg2 == key_seg(j), scores, -1e30)
        new_max = jnp.maximum(run_max, jnp.max(scores, axis=1, keepdims=True))
        probs = jnp.exp(scores - new_max)
        scale = jnp.exp(run_max - new_max)
        run_sum = run_sum * scale + jnp.sum(probs, axis=1, keepdims=True)
        accum = accum * scale + dense(probs.astype(BF), row_block(v_ref, j, bk))
        return accum, new_max, run_sum

    state = (
        jnp.zeros((2 * bq, PAIR), F32),
        jnp.full((2 * bq, 1), -1e30, F32),
        jnp.zeros((2 * bq, 1), F32),
    )
    for first, last in ranges:
        state = lax.fori_loop(first, last, k_step, state)
    accum, run_max, run_sum = state
    return by_head(accum / run_sum), run_max + jnp.log(run_sum)


def attend_wide(i, bq, first, size, q_ref, k_ref, v_ref, query_seg, key_seg):
    q2 = both_heads(row_block(q_ref, i, bq) * BF(0.125))
    seg = query_seg(i, bq)
    keys = pl.ds(first // 128, size // 128)
    scores = dense_back(q2, k_ref[keys].reshape(size, PAIR))
    scores = jnp.where(jnp.concatenate([seg, seg], axis=0) == key_seg(first, size), scores, -1e30)
    row_max = jnp.max(scores, axis=1, keepdims=True)
    probs = jnp.exp(scores - row_max)
    row_sum = jnp.sum(probs, axis=1, keepdims=True)
    accum = dense(probs.astype(BF), v_ref[keys].reshape(size, PAIR))
    return by_head(accum / row_sum), row_max + jnp.log(row_sum)


def attend_kernel(bq, bk, chunks, lo_ref, hi_ref, q_ref, k_ref, v_ref, sq_ref, sk_ref, o_ref, lse_ref):
    nq = q_ref.shape[0] // bq
    per_chunk = k_ref.shape[0] // chunks // bk

    def q_step(i, carry):
        ranges = [(s * per_chunk + lo_ref[i, s], s * per_chunk + hi_ref[i, s]) for s in range(chunks)]
        rows, lse = attend_rows(
            i, bq, bk, ranges, q_ref, k_ref, v_ref, lambda i: row_block(sq_ref, i, bq),
            lambda j: sk_ref[:, pl.ds(pl.multiple_of(j * bk, bk), bk)],
        )
        o_ref[pl.ds(pl.multiple_of(i * bq, bq), bq), :] = rows.astype(BF)
        lse_ref[pl.ds(pl.multiple_of(2 * i * bq, 2 * bq), 2 * bq), :] = lse
        return carry

    lax.fori_loop(0, nq, q_step, 0)


def segments_from(ends_ref, slots):
    def count(position):
        total = jnp.zeros(position.shape, jnp.int32)
        for j in range(slots):
            total += jnp.where(position >= ends_ref[pl.ds(0, 1), pl.ds(j, 1)], 1, 0)
        return total

    return (
        lambda i, size=BQ: count(i * size + lax.broadcasted_iota(jnp.int32, (size, 1), 0)),
        lambda first, size: count(first + lax.broadcasted_iota(jnp.int32, (1, size), 1)),
    )


def attend_back_rows(i, bq, bk, ranges, q_ref, k_ref, v_ref, query_seg, key_seg, o_ref, lse_ref, g_ref, dk_sum, dv_sum):
    rows = pl.ds(pl.multiple_of(i * bq, bq), bq)
    q2 = both_heads(q_ref[rows, :] * BF(0.125))
    grad = g_ref[rows, :]
    g2 = both_heads(grad)
    prod = grad.astype(F32) * o_ref[rows, :].astype(F32)
    left = first_half(prod.shape)
    delta = jnp.concatenate(
        [
            jnp.sum(jnp.where(left, prod, 0.0), axis=1, keepdims=True),
            jnp.sum(jnp.where(left, 0.0, prod), axis=1, keepdims=True),
        ],
        axis=0,
    )
    lse = lse_ref[pl.ds(pl.multiple_of(2 * i * bq, 2 * bq), 2 * bq), :]
    seg = query_seg(i)
    seg2 = jnp.concatenate([seg, seg], axis=0)

    def k_step(j, dq2):
        keys = pl.ds(pl.multiple_of(j * bk, bk), bk)
        key_rows = k_ref[keys, :]
        scores = dense_back(q2, key_rows)
        probs = jnp.exp(jnp.where(seg2 == key_seg(j), scores, -1e30) - lse)
        grad_prob = dense_back(g2, v_ref[keys, :])
        grad_score = (probs * (grad_prob - delta)).astype(BF)
        dv_sum[keys, :] += dense_in(probs.astype(BF), g2)
        dk_sum[keys, :] += dense_in(grad_score, q2)
        return dq2 + dense(grad_score, key_rows)

    dq2 = jnp.zeros((2 * bq, PAIR), F32)
    for first, last in ranges:
        dq2 = lax.fori_loop(first, last, k_step, dq2)
    return (0.125 * by_head(dq2)).astype(BF)


def attend_back_kernel(
    bq, bk, chunks, lo_ref, hi_ref, q_ref, k_ref, v_ref, sq_ref, sk_ref, o_ref, lse_ref, g_ref,
    dq_ref, dk_ref, dv_ref, dk_sum, dv_sum,
):
    nq = q_ref.shape[0] // bq
    per_chunk = k_ref.shape[0] // chunks // bk
    dk_sum[...] = jnp.zeros_like(dk_sum)
    dv_sum[...] = jnp.zeros_like(dv_sum)

    def q_step(i, carry):
        ranges = [(s * per_chunk + lo_ref[i, s], s * per_chunk + hi_ref[i, s]) for s in range(chunks)]
        dq_ref[pl.ds(pl.multiple_of(i * bq, bq), bq), :] = attend_back_rows(
            i, bq, bk, ranges, q_ref, k_ref, v_ref, lambda i: row_block(sq_ref, i, bq),
            lambda j: sk_ref[:, pl.ds(pl.multiple_of(j * bk, bk), bk)], o_ref, lse_ref, g_ref, dk_sum, dv_sum,
        )
        return carry

    lax.fori_loop(0, nq, q_step, 0)
    dk_ref[...] = dk_sum[...].astype(dk_ref.dtype)
    dv_ref[...] = dv_sum[...].astype(dv_ref.dtype)


SMEM = pl.BlockSpec(memory_space=pltpu.SMEM)
VMEM = pl.BlockSpec(memory_space=pltpu.VMEM)


def attend(bounds, q, k, v, seg_q, seg_k, chunks):
    n = q.shape[0]
    return pl.pallas_call(
        functools.partial(attend_kernel, BQ, BK, chunks),
        out_shape=(jax.ShapeDtypeStruct((n, PAIR), BF), jax.ShapeDtypeStruct((2 * n, 1), F32)),
        in_specs=[SMEM, SMEM] + [VMEM] * 5,
        out_specs=(VMEM, VMEM),
        compiler_params=pltpu.CompilerParams(vmem_limit_bytes=48 * 2**20),
    )(*bounds, q, k, v, seg_q, seg_k)


def attend_back(bounds, q, k, v, seg_q, seg_k, out, lse, grad, chunks):
    n, m = q.shape[0], k.shape[0]
    kept = BF if chunks == 1 else F32
    return pl.pallas_call(
        functools.partial(attend_back_kernel, BQ, BK, chunks),
        out_shape=(
            jax.ShapeDtypeStruct((n, PAIR), BF),
            jax.ShapeDtypeStruct((m, PAIR), kept),
            jax.ShapeDtypeStruct((m, PAIR), kept),
        ),
        in_specs=[SMEM, SMEM] + [VMEM] * 8,
        out_specs=(VMEM, VMEM, VMEM),
        scratch_shapes=[pltpu.VMEM((m, PAIR), F32), pltpu.VMEM((m, PAIR), F32)],
        compiler_params=pltpu.CompilerParams(vmem_limit_bytes=56 * 2**20),
    )(*bounds, q, k, v, seg_q, seg_k, out, lse, grad)


def mesh_id(ctx, f):
    return {"ctx": ctx, "fsdp": f}


def swapped(i):
    return i % 2 * 2 + i // 2


class Place:
    def __init__(self):
        self.ctx = lax.axis_index("ctx")
        self.f = lax.axis_index("fsdp")
        self.per_group = lax.axis_size("ctx") // 4
        self.g = self.ctx // self.per_group
        self.b = self.ctx % 2
        self.rest = self.ctx % self.per_group
        self.core = self.f % 2
        self.x = self.f // 2

    def at(self, g=None, b=None, f=None):
        ctx = self.ctx
        if g is not None:
            ctx = ctx + (g - self.g) * self.per_group
        if b is not None:
            ctx = ctx + (b - self.b)
        return mesh_id(ctx, self.f if f is None else f)

    def sibling(self):
        return self.at(f=self.f + 1 - 2 * self.core)

    def beside(self):
        return self.at(f=(self.f + 2) % 4)

    def across(self):
        return self.at(b=1 - self.b)

    def fsdp(self, k):
        return self.at(f=(self.f + k) % 4)

    def moved(self):
        return mesh_id(swapped(self.f) * self.per_group + self.rest, swapped(self.g))

    def stays(self):
        return swapped(self.f) == self.g


def remote(src, dst, send, recv, where):
    return pltpu.make_async_remote_copy(
        src_ref=src, dst_ref=dst, send_sem=send, recv_sem=recv,
        device_id=where, device_id_type=pl.DeviceIdType.MESH,
    )


def meet(me, targets, moves):
    barrier = pltpu.get_barrier_semaphore()
    for t in targets:
        pl.semaphore_signal(barrier, 1, device_id=t, device_id_type=pl.DeviceIdType.MESH)
    if not moves:
        pl.semaphore_wait(barrier, len(targets))
        return

    @pl.when(jnp.logical_not(me.stays()))
    def _():
        pl.semaphore_signal(barrier, 1, device_id=me.moved(), device_id_type=pl.DeviceIdType.MESH)

    pl.semaphore_wait(barrier, len(targets) + jnp.where(me.stays(), 0, 1))


class Flow:
    def __init__(self, me, own, buf, got, sent, came):
        self.me, self.own, self.buf, self.got, self.sent, self.came = me, own, buf, got, sent, came
        self.low = me.g < 2
        self.inner = jnp.where((me.g == 1) | (me.g == 2), 1, 0)
        step = jnp.where(self.low, 1, -1)
        self.ahead = me.at(g=me.g + step)
        self.back_to = me.at(g=me.g - step)

    def piece(self, i):
        return jnp.where(self.low, 3 - i, i)

    def copy(self, p, side, where):
        return remote(self.buf.at[p], self.got.at[side, p], self.sent.at[p], self.came.at[side, p], where)

    def forward(self, i):
        p = self.piece(i)

        @pl.when(self.inner == 0)
        def _():
            self.buf[p] = self.own(p, i).astype(BF)
            self.copy(p, 0, self.ahead).start()

        if i < 2:
            @pl.when(self.inner == 1)
            def _():
                self.copy(p, 0, self.back_to).wait_recv()
                self.buf[p] = (self.own(p, i) + self.got[0, p].astype(F32)).astype(BF)
                self.copy(p, 1, self.ahead).start()

    def back(self):
        p = self.piece(3)

        @pl.when(self.inner == 1)
        def _():
            self.copy(p, 1, self.ahead).wait_recv()
            self.buf[p] = (self.own(p, 3) + self.got[1, p].astype(F32)).astype(BF)
            self.copy(p, 1, self.back_to).start()

    def end(self):
        g = self.me.g

        @pl.when(self.inner == 0)
        def _():
            self.copy(g, 1, self.ahead).wait_recv()
            self.buf[g] = (self.own(g, 3) + self.got[1, g].astype(F32)).astype(BF)

        @pl.when(self.inner == 1)
        def _():
            self.copy(g, 0, self.back_to).wait_recv()
            self.copy(g, 1, self.ahead).wait_recv()
            self.buf[g] = (self.own(g, 3) + self.got[0, g].astype(F32) + self.got[1, g].astype(F32)).astype(BF)

        for p in range(4):
            @pl.when(g != p)
            def _():
                self.copy(p, 0, self.ahead).wait_send()


def tail_kernel(slots, *refs):
    if slots:
        q_ref, k_ref, v_ref, ends_ref, o_ref, lse_ref, grad_ref, x_ref = refs[:8]
        g3_ref, dk_sum, dv_sum = refs[-3:]
        query_seg, key_seg = segments_from(ends_ref, slots)
        attention = (
            q_ref, k_ref, v_ref, query_seg, lambda j: key_seg(j * BK, BK), o_ref, lse_ref, grad_ref,
        )
        tail_steps(attention, dk_sum, dv_sum, x_ref, g3_ref, *refs[8:-3])
    else:
        tail_steps(None, None, None, *refs)


def tail_steps(
    attention, dk_sum, dv_sum,
    x_ref, g3_ref, w3_ref, down_ref, rest_ref, up_ref, out_ref, mid_ref, vec_ref,
    down_out, up_out, o_out, three_out, dx_ref, sums_ref,
    dxp, dx1, t1, xa, yb, t2a, t2b, ra, rb, moved_buf,
    yr_down, yr_up, dbuf, dgot, ubuf, ugot,
    o_got, o_sum, yr_o, obuf, ogot,
    gq, qbuf, qgot, vs, vr,
    s_dx, r_dx, s_y, r_y, s_d, r_d, s_z, r_z, s_u, r_u, s_o, r_o, s_oz, r_oz, s_q, r_q,
    s_qf, r_qf, s_v, r_v, s_ag, r_ag, s_ay, r_ay, loc, x_rows,
):
    me = Place()
    g, b, f = me.g, me.b, me.f
    z_others = [me.at(g=(g + k) % 4) for k in (1, 2, 3)]
    meet(me, [me.across()] + [me.fsdp(k) for k in (1, 2, 3)] + z_others, True)

    rest = jnp.where(g < 2, 0, 2)

    def own_down(p, i):
        if i < 2:
            return down_ref[p].astype(F32)
        return down_ref[p].astype(F32) + yr_down[p - rest].astype(F32)

    def own_up(p, i):
        return up_ref[:, b, p].astype(F32) + yr_up[p].astype(F32)

    def own_q(p, i):
        return gq[:, :, p].astype(F32)

    def own_o(p, i):
        return o_sum[b, p].astype(F32) + yr_o[p].astype(F32)

    flow_d = Flow(me, own_down, dbuf, dgot, s_d, r_d)
    flow_u = Flow(me, own_up, ubuf, ugot, s_z, r_z)
    flow_q = Flow(me, own_q, qbuf, qgot, s_q, r_q)
    flow_o = Flow(me, own_o, obuf, ogot, s_oz, r_oz)

    edge, inner = flow_d.inner == 0, flow_d.inner == 1
    x_copy = pltpu.make_async_copy(x_ref, x_rows, loc.at[1])
    x_copy.start()

    def at(which, *steps):
        @pl.when(which)
        def _():
            for step in steps:
                step()

    y_copies = []
    for i in range(4):
        p = flow_u.piece(i)
        c = remote(up_ref.at[:, 1 - b, p], yr_up.at[p], s_y.at[0, i], r_y.at[0, i], me.across())
        c.start()
        y_copies.append(c)
    y_down = []
    for i in (2, 3):
        p = flow_d.piece(i) - rest
        c = remote(rest_ref.at[p], yr_down.at[p], s_y.at[1, i], r_y.at[1, i], me.across())
        c.start()
        y_down.append(c)

    o_copies = []
    for k in (1, 2, 3):
        c = remote(out_ref.at[(f + k) % 4], o_got.at[k - 1], s_o.at[k - 1], r_o.at[k - 1], me.fsdp(k))
        c.start()
        o_copies.append(c)
    c_oy = remote(o_sum.at[1 - b], yr_o, s_y.at[1, 0], r_y.at[1, 0], me.across())

    def up_forward(i):
        y_copies[i].wait()
        flow_u.forward(i)

    def up_back():
        y_copies[3].wait()
        flow_u.back()

    def output_rows():
        for c in o_copies:
            c.wait()
        o_sum[...] = (
            out_ref[f].astype(F32) + o_got[0].astype(F32) + o_got[1].astype(F32) + o_got[2].astype(F32)
        ).astype(BF)
        c_oy.start()

    do = functools.partial
    at(edge, do(flow_d.forward, 0), do(flow_d.forward, 1))

    def down_forward():
        y_down[0].wait()
        flow_d.forward(2)

    def down_back():
        for c in y_down:
            c.wait()
        flow_d.back()

    between = (
        ((edge, do(up_forward, 0)), (inner, do(flow_d.forward, 0))),
        ((True, output_rows), (edge, do(up_forward, 1)), (inner, do(flow_d.forward, 1), do(up_forward, 0))),
        ((edge, do(up_forward, 2), down_forward), (inner, do(up_forward, 1))),
        ((edge, y_down[1].wait, y_copies[3].wait), (inner, down_back, y_copies[2].wait, up_back)),
    )
    if attention is not None:
        dk_sum[...] = jnp.zeros_like(dk_sum)
        dv_sum[...] = jnp.zeros_like(dv_sum)
    per = 2048 // BQ // 4
    for quarter, (first, last) in enumerate(QUARTERS):
        ranges = [(first * 512 // BK, last * 512 // BK)]

        def rows_step(i, carry):
            g3_ref[pl.ds(pl.multiple_of(i * BQ, BQ), BQ), pl.ds(0, PAIR)] = attend_back_rows(
                i, BQ, BK, ranges, *attention, dk_sum, dv_sum
            )
            return carry

        if attention is not None:
            lax.fori_loop(quarter * per, (quarter + 1) * per, rows_step, 0)
        for which, *steps in between[quarter]:
            if which is True:
                for step in steps:
                    step()
            else:
                at(which, *steps)
    if attention is not None:
        g3_ref[:, pl.ds(PAIR, PAIR)] = dk_sum[...].astype(BF)
        g3_ref[:, pl.ds(2 * PAIR, PAIR)] = dv_sum[...].astype(BF)

    hops = [me.sibling(), me.beside(), me.across(), me.at(g=g + 1 - 2 * (g % 2)), me.at(g=(g + 2) % 4)]
    vs[0] = vec_ref[...]
    here = pl.ds(pl.multiple_of((b * 4 + swapped(f)) * PAIR, PAIR), PAIR)
    sums3 = jnp.sum(g3_ref[...].astype(F32), axis=0, keepdims=True)
    vs[0, pl.ds(0, 1), here] = sums3[:, :PAIR]
    vs[0, pl.ds(1, 1), here] = sums3[:, 2 * PAIR :]

    def hop(i):
        if i > 0:
            hop_copy(i - 1).wait()
            vs[i] = vs[i - 1] + vr[i - 1]
        hop_copy(i).start()

    def hop_copy(i):
        return remote(vs.at[i], vr.at[i], s_v.at[i], r_v.at[i], hops[i])

    hop(0)

    def rows(size, q, other=False):
        half = 1 - b if other else b
        return pl.ds(pl.multiple_of((half * 4 + q) * size, size), size)

    def unit_cols(src):
        return pl.ds(pl.multiple_of(src * 1024, 1024), 1024)

    def head_cols(src):
        return pl.ds(pl.multiple_of((b * 4 + swapped(src)) * 128, 128), 128)

    def q_rows(q):
        return pl.ds(pl.multiple_of(q * 64, 64), 64)

    def pieces(kind, q, send, recv, where, other=False):
        half = 1 - b if other else b
        if kind == 0:
            parts = (down_out.at[rows(128, q, other), :], up_out.at[rows(32, q, other), :])
        else:
            parts = (
                o_out.at[rows(32, q, other), :],
                three_out.at[:, q_rows(q), pl.ds(pl.multiple_of(half * 512, 512), 512)],
            )
        return [remote(part, part, send.at[2 * kind + i, q], recv.at[2 * kind + i, q], where) for i, part in enumerate(parts)]

    def spread(kind, q, to_right, to_left):
        if to_right:
            @pl.when(g < 3)
            def _():
                for c in pieces(kind, q, s_ag.at[0], r_ag, me.at(g=g + 1)):
                    c.start()
        if to_left:
            @pl.when(g > 0)
            def _():
                for c in pieces(kind, q, s_ag.at[1], r_ag, me.at(g=g - 1)):
                    c.start()
        for c in pieces(kind, q, s_ay, r_ay, me.across()):
            c.start()

    def pass_on(kind, d):
        @pl.when(g >= d)
        def _():
            for c in pieces(kind, g - d, s_ag.at[0], r_ag, me.across()):
                c.wait_recv()
            spread(kind, g - d, True, False)

        @pl.when(g + d <= 3)
        def _():
            for c in pieces(kind, g + d, s_ag.at[1], r_ag, me.across()):
                c.wait_recv()
            spread(kind, g + d, False, True)

    def dx_step(i, carry):
        rows = pl.ds(pl.multiple_of(i * 256, 256), 256)
        part = dense_back(g3_ref[rows, :], w3_ref[...]).astype(BF)
        dxp[pl.ds(2 * i, 2)] = part.reshape(2, 2, 2, 2, 16, 1024)
        return carry

    lax.fori_loop(0, 8, dx_step, 0)
    c_core = remote(dxp.at[:, 1 - me.core], dx1, s_dx.at[0], r_dx.at[0], me.sibling())
    c_core.start()

    flow_u.end()
    up_out[rows(32, g), unit_cols(f)] = ubuf[g, f]
    u_out = []
    for k in (1, 2, 3):
        c = remote(ubuf.at[g, (f + k) % 4], up_out.at[rows(32, g), unit_cols(f)], s_u.at[k - 1], r_u.at[f], me.fsdp(k))
        c.start()
        u_out.append(c)
    flow_d.end()
    down_out[rows(128, g), :] = dbuf[g]

    c_core.wait()

    def t1_step(i, carry):
        t1[i] = (dxp[i, me.core].astype(F32) + dx1[i].astype(F32)).astype(BF)
        return carry

    lax.fori_loop(0, 16, t1_step, 0)
    lo, hi = pl.ds(0, 8), pl.ds(8, 8)
    c_xa = remote(t1.at[lo, 1 - me.x], xa, s_dx.at[1], r_dx.at[1], me.beside())
    c_yb = remote(t1.at[hi, :, 1 - b], yb, s_dx.at[2], r_dx.at[2], me.across())
    c_xa.start()
    c_yb.start()
    hop(1)

    x_copy.wait()

    def q_step(i, carry):
        cols = pl.ds(pl.multiple_of(i * 256, 256), 256)
        part = dense_in(x_rows[:, cols], g3_ref[...]).astype(BF)
        for j in range(3):
            gq[i, j] = part[:, j * 128 : (j + 1) * 128].reshape(4, 64, 128)
        return carry

    lax.fori_loop(0, 4, q_step, 0)
    at(edge, *(do(flow_q.forward, i) for i in range(3)))
    c_oy.wait()
    at(edge, *(do(flow_o.forward, i) for i in range(3)))
    for k in (1, 2, 3):
        src = (f + k) % 4
        remote(ubuf.at[g, 0], up_out.at[rows(32, g), unit_cols(src)], s_u.at[k - 1], r_u.at[src], me.fsdp(k)).wait_recv()
        u_out[k - 1].wait_send()
    c_xa.wait()
    t2a[...] = (t1[lo, me.x].astype(F32) + xa[...].astype(F32)).astype(BF)
    c_ra = remote(t2a.at[:, 1 - b], ra, s_dx.at[3], r_dx.at[3], me.across())
    c_ra.start()
    c_yb.wait()
    t2b[...] = (t1[hi, :, b].astype(F32) + yb[...].astype(F32)).astype(BF)
    c_rb = remote(t2b.at[:, 1 - me.x], rb, s_dx.at[4], r_dx.at[4], me.beside())
    c_rb.start()
    spread(0, g, True, True)
    at(inner, do(flow_q.forward, 0), do(flow_q.forward, 1), do(flow_o.forward, 0), do(flow_o.forward, 1))
    hop(2)
    c_ra.wait()
    c_rb.wait()
    moved_buf[lo] = (t2a[:, b].astype(F32) + ra[...].astype(F32) + mid_ref[lo]).astype(BF)
    moved_buf[hi] = (t2b[:, me.x].astype(F32) + rb[...].astype(F32) + mid_ref[hi]).astype(BF)

    @pl.when(me.stays())
    def _():
        c = pltpu.make_async_copy(moved_buf, dx_ref, loc.at[0])
        c.start()
        c.wait()

    @pl.when(jnp.logical_not(me.stays()))
    def _():
        remote(moved_buf, dx_ref, s_dx.at[5], r_dx.at[5], me.moved()).start()

    flow_q.back()
    flow_o.back()
    pass_on(0, 1)
    hop(3)

    flow_q.end()
    three_out[:, q_rows(g), head_cols(f)] = qbuf[g, f]
    q_out = []
    for k in (1, 2, 3):
        c = remote(qbuf.at[g, (f + k) % 4], three_out.at[:, q_rows(g), head_cols(f)], s_qf.at[k - 1], r_qf.at[f], me.fsdp(k))
        c.start()
        q_out.append(c)
    flow_o.end()
    o_out[rows(32, g), :] = obuf[g]
    for k in (1, 2, 3):
        src = (f + k) % 4
        remote(qbuf.at[g, 0], three_out.at[:, q_rows(g), head_cols(src)], s_qf.at[k - 1], r_qf.at[src], me.fsdp(k)).wait_recv()
        q_out[k - 1].wait_send()
    spread(1, g, True, True)
    pass_on(0, 2)
    pass_on(1, 1)
    pass_on(0, 3)
    hop(4)
    pass_on(1, 2)
    pass_on(1, 3)
    hop_copy(4).wait()
    sums_ref[...] = vs[4] + vr[4]

    @pl.when(jnp.logical_not(me.stays()))
    def _():
        remote(moved_buf, dx_ref, s_dx.at[5], r_dx.at[5], me.moved()).wait()

    for kind in (0, 1):
        for q in range(4):
            for c in pieces(kind, q, s_ay, r_ay, me.across()):
                c.wait_send()

            @pl.when((g >= q) & (g < 3))
            def _():
                for c in pieces(kind, q, s_ag.at[0], r_ag, me.across()):
                    c.wait_send()

            @pl.when((g <= q) & (g > 0))
            def _():
                for c in pieces(kind, q, s_ag.at[1], r_ag, me.across()):
                    c.wait_send()

            for c in pieces(kind, q, s_ay, r_ay, me.across(), other=True):
                c.wait_recv()


def tail(slots, attention, x_all, g3, w3, down, rest, up, out, mid, vec):
    dma = pltpu.SemaphoreType.DMA
    v = pltpu.VMEM
    scratch = [
        v((16, 2, 2, 2, 16, 1024), BF), v((16, 2, 2, 16, 1024), BF), v((16, 2, 2, 16, 1024), BF),
        v((8, 2, 16, 1024), BF), v((8, 2, 16, 1024), BF), v((8, 2, 16, 1024), BF), v((8, 2, 16, 1024), BF),
        v((8, 16, 1024), BF), v((8, 16, 1024), BF), v((16, 16, 1024), BF),
        v((2, 128, 1024), BF), v((4, 4, 32, 1024), BF), v((4, 128, 1024), BF), v((2, 4, 128, 1024), BF),
        v((4, 4, 32, 1024), BF), v((2, 4, 4, 32, 1024), BF),
        v((3, 2, 4, 32, 1024), BF), v((2, 4, 32, 1024), BF), v((4, 32, 1024), BF),
        v((4, 32, 1024), BF), v((2, 4, 32, 1024), BF),
        v((4, 3, 4, 64, 128), BF), v((4, 4, 3, 64, 128), BF), v((2, 4, 4, 3, 64, 128), BF),
        v((5, 16, 1024), F32), v((5, 16, 1024), F32),
        dma((6,)), dma((6,)), dma((2, 5)), dma((2, 5)), dma((4,)), dma((2, 4)), dma((4,)), dma((2, 4)),
        dma((3,)), dma((4,)), dma((3,)), dma((3,)), dma((4,)), dma((2, 4)), dma((4,)), dma((2, 4)),
        dma((3,)), dma((4,)), dma((5,)), dma((5,)), dma((2, 4, 4)), dma((4, 4)), dma((4, 4)), dma((4, 4)), dma((2,)),
        v((2048, 1024), BF),
    ]
    if slots:
        scratch += [v((2048, 3 * PAIR), BF), v((2048, PAIR), F32), v((2048, PAIR), F32)]
        operands = (*attention, x_all)
    else:
        operands = (x_all, g3)
    operands += (
        w3, down.reshape(4, 128, 1024), rest.reshape(2, 128, 1024), up.reshape(4, 2, 4, 32, 1024), out.reshape(4, 2, 4, 32, 1024),
        mid.reshape(16, 16, 1024), vec,
    )
    return pl.pallas_call(
        functools.partial(tail_kernel, slots),
        out_shape=(
            jax.ShapeDtypeStruct((1024, 1024), BF),
            jax.ShapeDtypeStruct((256, 4096), BF),
            jax.ShapeDtypeStruct((256, 1024), BF),
            jax.ShapeDtypeStruct((3, 256, 1024), BF),
            jax.ShapeDtypeStruct((16, 16, 1024), BF),
            jax.ShapeDtypeStruct((16, 1024), F32),
        ),
        in_specs=[pl.BlockSpec(memory_space=pl.ANY) if ref is x_all else VMEM for ref in operands],
        out_specs=(VMEM,) * 6,
        scratch_shapes=scratch,
        compiler_params=pltpu.CompilerParams(collective_id=1, has_side_effects=True, vmem_limit_bytes=60 * 2**20),
        cost_estimate=pl.CostEstimate(flops=4 * 10**9, bytes_accessed=40 * 2**20, transcendentals=0),
    )(*operands)


def tile_cols(i, size):
    return pl.ds(pl.multiple_of(i * size, size), size)


def middle_kernel(
    heads_ref, x_ref, cot_ref, wo_ref, wu_in, wd_ref, par_ref,
    layer_ref, down_out, rest_out, upg_out, og_out, gatt_ref, mid1_ref, vec_ref,
    att, nl, gff, slope, hid, gpre, normed, xhat, rstd, work, moved_buf, gbr, gas, ps, pr, down, down_y, wu_ref, up_ref,
    s_a, r_a, s_b, r_b, s_g, r_g, s_p, r_p, s_m, r_m, s_y, r_y, loc, s_u, r_u, s_l,
):
    me = Place()
    f, b = me.f, me.b
    sib = f + 1 - 2 * me.core
    xs = (f + 2) % 4
    xo = xs + 1 - 2 * me.core
    peers = [me.at(f=(f + k % 4) % 4, b=(b + k // 4) % 2) for k in range(1, 8)]
    meet(me, peers, True)
    slot = swapped(f) * 2 + b
    unit = b * 4 + swapped(f)

    def peer_slot(k, sign):
        pf, pb = (f + sign * (k % 4) + 4) % 4, (b + k // 4) % 2
        return swapped(pf) * 2 + pb, pb * 4 + swapped(pf)

    def lanes(index):
        return pl.ds(pl.multiple_of(index * PAIR, PAIR), PAIR)

    for k in range(1, 8):
        where, _ = peer_slot(k, 1)
        remote(heads_ref.at[:, where], att.at[:, :, lanes(unit)], s_a.at[k - 1], r_a.at[k - 1], peers[k - 1]).start()
    att[:, :, lanes(unit)] = heads_ref[:, slot]

    def unit_rows(src, half):
        return pl.ds(pl.multiple_of(src * 256 + half * 128, 128), 128)

    u_out = [
        remote(wu_in.at[unit_rows(src, b)], wu_ref.at[unit_rows(src, b)], s_u.at[i], r_u.at[i], me.across())
        for i, src in enumerate((xs, xo))
    ]
    for c in u_out:
        c.start()
    cot_there = remote(cot_ref, up_ref, s_m.at[1], r_m.at[1], me.moved())
    cot_here = pltpu.make_async_copy(cot_ref, up_ref, loc.at[1])

    @pl.when(me.stays())
    def _():
        cot_here.start()

    @pl.when(jnp.logical_not(me.stays()))
    def _():
        cot_there.start()

    kept = [unit_rows(f, 0), unit_rows(f, 1), unit_rows(sib, 0), unit_rows(sib, 1), unit_rows(xs, b), unit_rows(xo, b)]
    u_kept = [pltpu.make_async_copy(wu_in.at[rows], wu_ref.at[rows], s_l.at[i]) for i, rows in enumerate(kept)]
    for c in u_kept:
        c.start()
    for k in range(1, 8):
        _, theirs = peer_slot(k, -1)
        remote(heads_ref.at[:, slot], att.at[:, :, lanes(theirs)], s_a.at[k - 1], r_a.at[k - 1], peers[k - 1]).wait()

    def row(i):
        return par_ref[pl.ds(i, 1), :]

    def att_rows():
        return att[...].reshape(256, 1024)

    def proj(i, carry):
        cols = tile_cols(i, 512)
        work[:, cols] = dense(att_rows(), wo_ref[:, cols])
        return carry

    lax.fori_loop(0, 2, proj, 0)
    value, x_hat, inv = norm_fwd(x_ref[...].astype(F32) + work[...] + row(0), row(1), row(2))
    normed[...] = value
    xhat[...] = x_hat
    rstd[...] = inv
    nl[f] = value.astype(BF)

    whole, halves = pl.ds(0, 256), (pl.ds(0, 128), pl.ds(128, 128))

    def passed(buf, t, i, src, rows, where):
        return remote(buf.at[src, rows], buf.at[src, rows], s_g.at[t, i], r_g.at[t, i], where)

    def scatter(t, i, part, rows, where):
        return remote(ps.at[t, part, rows], pr.at[t, part, rows], s_p.at[t, i], r_p.at[t, i], where)

    def run(t, block, buf, beside_x):
        for i, rows in enumerate(halves):
            passed(buf, t, 1 + i, f, rows, me.beside()).start()
        passed(buf, t, 0, f, whole, me.sibling()).start()
        block(f, 3, whole)
        passed(buf, t, 0, f, whole, me.sibling()).wait_send()
        passed(buf, t, 0, sib, whole, me.sibling()).wait_recv()
        block(sib, 0, whole)
        scatter(t, 0, 0, whole, me.sibling()).start()

        def from_x(i):
            passed(buf, t, 1 + i, f, halves[i], me.beside()).wait_send()
            passed(buf, t, 1 + i, xs, halves[i], me.beside()).wait_recv()
            passed(buf, t, 3 + i, xs, halves[i], me.sibling()).start()

        def from_other(i):
            passed(buf, t, 3 + i, xs, halves[i], me.sibling()).wait_send()
            passed(buf, t, 3 + i, xo, halves[i], me.sibling()).wait_recv()

        def chip_sum(i):
            rows = halves[i]
            scatter(t, 1 + i, 1, rows, me.sibling()).wait()
            ps[t, 2, rows] = (ps[t, 2, rows].astype(F32) + pr[t, 1, rows].astype(F32)).astype(BF)
            scatter(t, 3 + i, 2, rows, me.beside()).start()

        from_x(0)
        block(xs, 2, halves[0])
        from_other(0)
        block(xo, 1, halves[0])
        scatter(t, 1, 1, halves[0], me.sibling()).start()
        from_x(1)
        chip_sum(0)
        block(xs, 2, halves[1])
        from_other(1)
        block(xo, 1, halves[1])
        scatter(t, 2, 1, halves[1], me.sibling()).start()
        chip_sum(1)
        beside_x()
        scatter(t, 0, 0, whole, me.sibling()).wait()
        for i, rows in enumerate(halves):
            scatter(t, 3 + i, 2, rows, me.beside()).wait()
        return ps[t, 3].astype(F32) + pr[t, 0].astype(F32) + pr[t, 2].astype(F32)

    def forward(index, into, rows):
        def up_tile(i, carry):
            cols = tile_cols(i, 256)
            pre = dense(nl[index, rows], wu_ref[:, cols]) + par_ref[pl.ds(6, 1), cols]
            cdf = 0.5 * (1.0 + lax.erf(pre * 0.7071067811865476))
            hid[index, rows, cols] = (pre * cdf).astype(BF)
            slope[index, rows, cols] = cdf + pre * jnp.exp(-0.5 * pre * pre) * 0.3989422804014327
            return carry

        def down_tile(i, carry):
            cols = tile_cols(i, 512)
            ps[0, into, rows, cols] = dense(hid[index, rows], wd_ref[:, cols]).astype(BF)
            return carry

        lax.fori_loop(0, 4, up_tile, 0)
        lax.fori_loop(0, 2, down_tile, 0)

    for c in u_out + u_kept:
        c.wait()
    ffn = run(0, forward, nl, lambda: None)

    @pl.when(me.stays())
    def _():
        cot_here.wait()

    @pl.when(jnp.logical_not(me.stays()))
    def _():
        cot_there.wait()

    value, x_hat, inv = norm_fwd(normed[...] + ffn + row(3), row(4), row(5))
    moved_buf[...] = value.astype(BF)

    @pl.when(me.stays())
    def _():
        pltpu.make_async_copy(moved_buf, layer_ref, loc.at[0]).start()

    @pl.when(jnp.logical_not(me.stays()))
    def _():
        remote(moved_buf, layer_ref, s_m.at[0], r_m.at[0], me.moved()).start()

    grad2, gain2, shift2 = norm_back(up_ref[...].astype(F32), x_hat, inv, row(4))
    work[...] = grad2
    low2 = grad2.astype(BF)
    gff[f] = low2
    vec_ref[pl.ds(4, 1), :] = jnp.sum(low2.astype(F32), axis=0, keepdims=True)
    vec_ref[pl.ds(5, 1), :] = gain2[None]
    vec_ref[pl.ds(6, 1), :] = shift2[None]

    def backward(index, into, rows):
        def pre_tile(i, carry):
            cols = tile_cols(i, 512)
            part = dense_back(gff[index, rows], wd_ref[cols, :])
            gpre[index, rows, cols] = (part * slope[index, rows, cols]).astype(BF)
            return carry

        def in_tile(i, carry):
            cols = tile_cols(i, 512)
            ps[1, into, rows, cols] = dense_back(gpre[index, rows], wu_ref[cols, :]).astype(BF)
            return carry

        lax.fori_loop(0, 2, pre_tile, 0)
        lax.fori_loop(0, 2, in_tile, 0)

    first = pl.ds(pl.multiple_of(jnp.where(me.g < 2, 256, 0), 256), 256)
    later = pl.ds(pl.multiple_of(jnp.where(me.g < 2, 0, 256), 256), 256)
    c_down = remote(down.at[1 - b, first], down_y, s_y.at[0], r_y.at[0], me.across())

    def weight_grads():
        def down_tile(i, carry):
            cols = tile_cols(i, 256)
            part = dense_in(hid[:, :, cols].reshape(1024, 256), gff[...].reshape(1024, 1024)).astype(BF)
            down[i // 2, pl.ds(pl.multiple_of(i % 2 * 256, 256), 256)] = part
            return carry

        def up_tile(i, carry):
            cols = tile_cols(i, 256)
            upg_out[cols, :] = dense_in(nl[:, :, cols].reshape(1024, 256), gpre[...].reshape(1024, 1024)).astype(BF)
            return carry

        lax.fori_loop(0, 4, down_tile, 0)
        c_down.start()
        lax.fori_loop(0, 4, up_tile, 0)
        vec_ref[pl.ds(3, 1), :] = jnp.sum(gpre[...].reshape(1024, 1024).astype(F32), axis=0, keepdims=True)

    back = run(1, backward, gff, weight_grads)
    grad1, gain1, shift1 = norm_back(back + work[...], xhat[...], rstd[...], row(1))
    mid1_ref[...] = grad1
    low1 = grad1.astype(BF)
    gbr[...] = low1
    vec_ref[pl.ds(0, 1), :] = jnp.sum(low1.astype(F32), axis=0, keepdims=True)
    vec_ref[pl.ds(1, 1), :] = gain1[None]
    vec_ref[pl.ds(2, 1), :] = shift1[None]
    vec_ref[pl.ds(7, 1), :] = jnp.zeros((1, 1024), F32)

    def att_tile(i, carry):
        part = dense_back(gbr[...], wo_ref[tile_cols(i, 256), :]).astype(BF)
        for j in range(2):
            gas[2 * i + j] = part[:, j * PAIR : (j + 1) * PAIR].reshape(16, 16, PAIR)
        return carry

    lax.fori_loop(0, 4, att_tile, 0)
    for k in range(1, 8):
        _, theirs = peer_slot(k, 1)
        remote(gas.at[theirs], gatt_ref.at[:, slot], s_b.at[k - 1], r_b.at[k - 1], peers[k - 1]).start()
    gatt_ref[:, slot] = gas[unit]

    def o_tile(i, carry):
        cols = tile_cols(i, 256)
        og_out[cols, :] = dense_in(att[:, :, cols].reshape(256, 256), gbr[...]).astype(BF)
        return carry

    lax.fori_loop(0, 4, o_tile, 0)
    for k in range(1, 8):
        where, _ = peer_slot(k, -1)
        remote(gas.at[0], gatt_ref.at[:, where], s_b.at[k - 1], r_b.at[k - 1], peers[k - 1]).wait()
    c_down.wait()
    down_out[first, :] = (down[b, first].astype(F32) + down_y[...].astype(F32)).astype(BF)
    down_out[later, :] = down[b, later]
    rest_out[...] = down[1 - b, later]

    @pl.when(me.stays())
    def _():
        pltpu.make_async_copy(moved_buf, layer_ref, loc.at[0]).wait()

    @pl.when(jnp.logical_not(me.stays()))
    def _():
        remote(moved_buf, layer_ref, s_m.at[0], r_m.at[0], me.moved()).wait()


def middle(heads, x, upstream, w_output, w_up, w_down, params):
    dma = pltpu.SemaphoreType.DMA
    v = pltpu.VMEM
    block = (4, 256, 1024)
    scratch = [
        v((16, 16, 1024), BF), v(block, BF), v(block, BF), v(block, F32), v(block, BF), v(block, BF),
        v((256, 1024), F32), v((256, 1024), F32), v((256, 1), F32), v((256, 1024), F32), v((256, 1024), BF),
        v((256, 1024), BF), v((8, 16, 16, PAIR), BF), v((2, 4, 256, 1024), BF), v((2, 3, 256, 1024), BF),
        v((2, 512, 1024), BF), v((256, 1024), BF), v((1024, 1024), BF), v((256, 1024), BF),
        dma((7,)), dma((7,)), dma((7,)), dma((7,)), dma((2, 5)), dma((2, 5)), dma((2, 5)), dma((2, 5)),
        dma((2,)), dma((2,)), dma((1,)), dma((1,)), dma((2,)), dma((2,)), dma((2,)), dma((6,)),
    ]
    hbm = pl.BlockSpec(memory_space=pl.ANY)
    square = jax.ShapeDtypeStruct((1024, 1024), BF)
    return pl.pallas_call(
        middle_kernel,
        out_shape=(
            jax.ShapeDtypeStruct((256, 1024), BF), jax.ShapeDtypeStruct((512, 1024), BF),
            jax.ShapeDtypeStruct((256, 1024), BF), square, square,
            jax.ShapeDtypeStruct((16, 8, 16, PAIR), BF),
            jax.ShapeDtypeStruct((256, 1024), F32),
            jax.ShapeDtypeStruct((8, 1024), F32),
        ),
        in_specs=[VMEM, VMEM, hbm, VMEM, hbm, VMEM, VMEM],
        out_specs=(VMEM,) * 8,
        scratch_shapes=scratch,
        compiler_params=pltpu.CompilerParams(collective_id=2, has_side_effects=True, vmem_limit_bytes=60 * 2**20),
        cost_estimate=pl.CostEstimate(flops=14 * 10**9, bytes_accessed=20 * 2**20, transcendentals=2**21),
    )(heads.reshape(16, 8, 16, PAIR), x, upstream, w_output, w_up, w_down, params)


def start_kernel(
    slots, tok_ref, ends_ref, qw_ref, kw_ref, vw_ref, ow_ref, ew_ref, bias_ref,
    x_ref, ends_out, q_ref, k_ref, v_ref, w3_ref, wo_ref, wu_ref, att_ref, lse_ref,
    s_m, r_m, s_w, r_w, s_u, r_u, s_o, r_o, s_x, r_x, loc,
):
    me = Place()
    g, b, f = me.g, me.b, me.f
    sib = f + 1 - 2 * me.core
    xs = (f + 2) % 4
    xo = xs + 1 - 2 * me.core
    meet(me, [me.across()] + [me.fsdp(k) for k in (1, 2, 3)], True)
    slot = me.core * 4 + me.x * 2 + b
    slot_x = me.core * 4 + (1 - me.x) * 2 + b
    slot_y = slot + 1 - 2 * b
    slot_d = slot_x + 1 - 2 * b
    other = 4 - 8 * me.core
    lo, hi = pl.ds(0, 8), pl.ds(8, 8)

    def moves(i, src, dst):
        return remote(src, dst, s_m.at[i], r_m.at[i], me.moved())

    def relocate(i, src, dst):
        @pl.when(me.stays())
        def _():
            pltpu.make_async_copy(src, dst, loc.at[i]).start()

        @pl.when(jnp.logical_not(me.stays()))
        def _():
            moves(i, src, dst).start()

    def relocated(i, src, dst):
        @pl.when(me.stays())
        def _():
            pltpu.make_async_copy(src, dst, loc.at[i]).wait()

        @pl.when(jnp.logical_not(me.stays()))
        def _():
            moves(i, src, dst).wait()

    theirs = x_ref.at[:, g * 2 + b]
    relocate(0, tok_ref, theirs)
    relocate(1, ends_ref, ends_out)

    def cols(index, size):
        return pl.ds(pl.multiple_of(index * size, size), size)

    def w3_rows(src):
        return cols(src, 256)

    def wo_rows(src, which):
        return pl.ds(pl.multiple_of(src * 256 + which * 128, 128), 128)

    half = cols(b, 128)
    u_x = [
        remote(ew_ref.at[half, cols(xs, 1024)], wu_ref.at[wo_rows(f, b)], s_u.at[1], r_u.at[1], me.beside()),
        remote(ew_ref.at[half, cols(xo, 1024)], wu_ref.at[wo_rows(f, b)], s_u.at[2], r_u.at[2], me.at(f=xo)),
    ]
    o_x = remote(ow_ref.at[half], wo_ref.at[wo_rows(f, b)], s_o.at[1], r_o.at[1], me.beside())
    u_sib = remote(ew_ref.at[:, cols(sib, 1024)], wu_ref.at[w3_rows(f)], s_u.at[0], r_u.at[0], me.sibling())
    o_sib = remote(ow_ref, wo_ref.at[w3_rows(f)], s_o.at[0], r_o.at[0], me.sibling())
    for c in (o_x, u_sib, o_sib):
        c.start()
    o_own = pltpu.make_async_copy(ow_ref, wo_ref.at[w3_rows(f)], loc.at[5])
    u_own = pltpu.make_async_copy(ew_ref.at[:, cols(f, 1024)], wu_ref.at[w3_rows(f)], loc.at[6])
    o_own.start()
    u_own.start()
    weights = (qw_ref, kw_ref, vw_ref)

    def w3_own(j):
        return pltpu.make_async_copy(
            weights[j].at[:, cols(b * 4 + swapped(f), 128)], w3_ref.at[w3_rows(f), pl.ds(128 * j, 128)], loc.at[2 + j]
        )

    for j in range(3):
        w3_own(j).start()
    for k in (2, 3, 1):
        dest = b * 4 + swapped((f + k) % 4)
        for j in range(3):
            remote(
                weights[j].at[:, cols(dest, 128)], w3_ref.at[w3_rows(f), pl.ds(128 * j, 128)],
                s_w.at[j, k - 1], r_w.at[j, k - 1], me.fsdp(k),
            ).start()

    def piece(i, ref, where):
        return remote(ref, ref, s_x.at[i], r_x.at[i], where)

    relocated(0, tok_ref, theirs)
    own = x_ref.at[:, slot]
    sends = [piece(1, own, me.beside()), piece(2, own, me.across()), piece(0, own, me.sibling())]
    for c in sends:
        c.start()

    def project(which):
        part = dense(x_ref[:, which].reshape(256, 1024), w3_ref[...]) + bias_ref[...]
        part = part.astype(BF).reshape(16, 16, 3 * PAIR)
        q_ref[:, which] = part[:, :, :PAIR]
        k_ref[:, which] = part[:, :, PAIR : 2 * PAIR]
        v_ref[:, which] = part[:, :, 2 * PAIR :]

    piece(1, x_ref.at[:, slot_x], me.beside()).wait_recv()
    more = [piece(4, x_ref.at[hi, slot_x], me.across()), piece(3, x_ref.at[:, slot_x], me.sibling())]
    for c in more:
        c.start()
    sends += more
    piece(2, x_ref.at[:, slot_y], me.across()).wait_recv()
    more = [piece(6, x_ref.at[lo, slot_y], me.beside()), piece(5, x_ref.at[:, slot_y], me.sibling())]
    for c in more:
        c.start()
    sends += more
    for c in u_x:
        c.start()
    o_x.wait()
    o_fwd = [
        remote(wo_ref.at[wo_rows(xs, b)], wo_ref.at[wo_rows(xs, b)], s_o.at[2], r_o.at[2], me.sibling()),
        remote(wo_ref.at[wo_rows(xs, b)], wo_ref.at[wo_rows(xs, b)], s_o.at[3], r_o.at[3], me.across()),
    ]
    for c in o_fwd:
        c.start()
    for k in (1, 2, 3):
        src = (f + 4 - k) % 4
        for j in range(3):
            remote(
                weights[j].at[:, cols(0, 128)], w3_ref.at[w3_rows(src), pl.ds(128 * j, 128)],
                s_w.at[j, k - 1], r_w.at[j, k - 1], me.fsdp(k),
            ).wait()
    for j in range(3):
        w3_own(j).wait()
    project(slot)
    project(slot_x)
    piece(4, x_ref.at[hi, slot_d], me.across()).wait_recv()
    more = [piece(8, x_ref.at[hi, slot_d], me.sibling())]
    more[0].start()
    piece(6, x_ref.at[lo, slot_d], me.beside()).wait_recv()
    more.append(piece(7, x_ref.at[lo, slot_d], me.sibling()))
    more[1].start()
    sends += more
    project(slot_y)
    for i, part in ((0, slot + other), (3, slot_x + other), (5, slot_y + other)):
        piece(i, x_ref.at[:, part], me.sibling()).wait_recv()
        project(part)
    project(slot_d)
    piece(8, x_ref.at[hi, slot_d + other], me.sibling()).wait_recv()
    piece(7, x_ref.at[lo, slot_d + other], me.sibling()).wait_recv()
    project(slot_d + other)
    for c in sends:
        c.wait_send()
    relocated(1, ends_ref, ends_out)

    segments = segments_from(ends_out, slots)

    def attend_quarter(quarter):
        first, last = QUARTERS[quarter]

        rows, lse = attend_wide(quarter, WIDE, first * 512, (last - first) * 512, q_ref, k_ref, v_ref, *segments)
        att_ref[pl.ds(quarter * 4, 4)] = rows.astype(BF).reshape(4, GROUP, 16, PAIR)
        for part in range(WIDE // BQ):
            for head in range(2):
                to = 2 * (quarter * WIDE + part * BQ) + head * BQ
                lse_ref[pl.ds(to, BQ), :] = lse[head * WIDE + part * BQ : head * WIDE + (part + 1) * BQ]

    if slots:
        attend_quarter(0)
    if slots:
        attend_quarter(1)
        attend_quarter(2)
    o_fwd[0].wait()
    o_fwd[1].wait()
    late = remote(wo_ref.at[wo_rows(xs, 1 - b)], wo_ref.at[wo_rows(xs, 1 - b)], s_o.at[4], r_o.at[4], me.sibling())
    late.start()
    if slots:
        attend_quarter(3)
    late.wait()
    o_own.wait()
    o_sib.wait()
    u_own.wait()
    u_sib.wait()
    for c in u_x:
        c.wait()


def start(slots, tokens, ends, query_w, key_w, value_w, output_w, expand_w, bias3):
    dma = pltpu.SemaphoreType.DMA
    hbm = pl.BlockSpec(memory_space=pl.ANY)
    heads = jax.ShapeDtypeStruct((16, GROUP, 16, PAIR), BF)
    square = jax.ShapeDtypeStruct((1024, 1024), BF)
    return pl.pallas_call(
        functools.partial(start_kernel, slots),
        out_shape=(
            jax.ShapeDtypeStruct((16, GROUP, 16, 1024), BF), jax.ShapeDtypeStruct((8, 128), jnp.int32), heads, heads, heads,
            jax.ShapeDtypeStruct((1024, 3 * PAIR), BF), square, square,
            heads, jax.ShapeDtypeStruct((4096, 1), F32),
        ),
        in_specs=[hbm, VMEM] + [hbm] * 5 + [VMEM],
        out_specs=(VMEM, VMEM, VMEM, VMEM, VMEM, VMEM, hbm, hbm, VMEM, VMEM),
        scratch_shapes=[
            dma((2,)), dma((2,)), dma((3, 3)), dma((3, 3)), dma((3,)), dma((3,)), dma((5,)), dma((5,)),
            dma((9,)), dma((9,)), dma((7,)),
        ],
        compiler_params=pltpu.CompilerParams(collective_id=3, has_side_effects=True, vmem_limit_bytes=60 * 2**20),
        cost_estimate=pl.CostEstimate(flops=2 * 10**9, bytes_accessed=20 * 2**20, transcendentals=0),
    )(tokens, ends, query_w, key_w, value_w, output_w, expand_w, bias3)


def body(
    tokens, lengths, packing, query_w, query_b, key_w, value_w, value_b, output_w, output_b,
    attn_gain, attn_shift, expand_w, expand_b, reduce_w, reduce_b, ffn_gain, ffn_shift, cotangent,
):
    tok_shape = tokens.shape
    laps, stripe, width = tok_shape[1], tok_shape[2], tok_shape[3]
    mine = laps * stripe
    n_ctx = lax.axis_size("ctx")
    n_f = lax.axis_size("fsdp")
    per_group = n_ctx // n_f
    chunks = per_group // 2
    ctx = lax.axis_index("ctx")
    f = lax.axis_index("fsdp")
    g = ctx // per_group
    chunk = ctx % per_group // 2
    b = ctx % 2
    same_place = [
        [(gg * chunks + s) * 2 + bb for s in range(chunks)] for gg in range(n_f) for bb in range(2)
    ]
    units = expand_w.shape[1] // n_f

    ordered = jnp.sum(
        jnp.where(
            packing[0][:, None] == jnp.arange(lengths.shape[1], dtype=jnp.int32)[None, :],
            lengths[0][None, :],
            0,
        ),
        axis=1,
    )
    slots = jnp.arange(ordered.shape[0], dtype=jnp.int32)
    own_ends = jnp.sum(jnp.where(slots[None, :] <= slots[:, None], ordered[None, :], 0), axis=1)
    own_ends = jnp.pad(own_ends[None], ((0, 7), (0, 128 - own_ends.shape[0])))

    here = (b * n_f + swapped(f)) * PAIR
    bias3 = jnp.concatenate(
        [
            lax.dynamic_slice_in_dim(query_b, here, PAIR),
            jnp.zeros((PAIR,), F32),
            lax.dynamic_slice_in_dim(value_b, here, PAIR),
        ]
    )[None]
    acts = (laps, stripe, width)
    n_slots = lengths.shape[1] if chunks == 1 else 0
    x_all, ends, q, k_own, v_own, w_three, w_output, w_up, att_heads, lse = start(
        n_slots, tokens.reshape(acts), own_ends, query_w, key_w, value_w, output_w, expand_w, bias3
    )
    q, k_own, v_own = (part.reshape(GROUP * mine, PAIR) for part in (q, k_own, v_own))
    inputs = lax.dynamic_index_in_dim(x_all, swapped(f) * 2 + b, 1, keepdims=False).reshape(mine, width)
    x_all = x_all.reshape(GROUP * mine, width)
    upstream = cotangent.reshape(mine, width)
    slot_ends = ends[0, : ordered.shape[0]]

    span = GROUP * mine
    index = jnp.arange(span, dtype=jnp.int32)

    def segments(which):
        lap, rest = index // (GROUP * stripe), index % (GROUP * stripe)
        unit, place = rest // stripe, rest % stripe
        owner = unit // 2 * per_group + which * 2 + unit % 2
        position = lap * (n_ctx * stripe) + owner * stripe + place
        return jnp.sum((position[:, None] >= slot_ends[None, :]).astype(jnp.int32), axis=1)

    attention = (q, k_own, v_own, ends, att_heads.reshape(span, PAIR), lse)
    if chunks > 1:
        seg_q = segments(chunk)
        seg_k = jnp.concatenate([segments(s) for s in range(chunks)])
        q_first, q_last = seg_q[::BQ], seg_q[BQ - 1 :: BQ]
        k_first = seg_k[::BK].reshape(chunks, -1)
        k_last = seg_k[BK - 1 :: BK].reshape(chunks, -1)
        lo = jnp.sum((k_last[None] < q_first[:, None, None]).astype(jnp.int32), axis=2)
        hi = jnp.sum((k_first[None] <= q_last[:, None, None]).astype(jnp.int32), axis=2)
        bounds = (lo, hi)
        k = lax.all_gather(k_own, "ctx", axis_index_groups=same_place, tiled=True)
        v = lax.all_gather(v_own, "ctx", axis_index_groups=same_place, tiled=True)
        keyed = (q, k, v, seg_q[:, None], seg_k[None, :])
        att_heads, lse = attend(bounds, *keyed, chunks)

    params = jnp.stack(
        [
            output_b, attn_gain, attn_shift, reduce_b, ffn_gain, ffn_shift,
            lax.dynamic_slice_in_dim(expand_b, f * units, units), jnp.zeros_like(output_b),
        ]
    )
    layer_out, part_down, rest_down, part_up, part_out, grad_att, grad_mid1, vec = middle(
        att_heads, inputs, upstream, w_output, w_up, reduce_w, params
    )
    layer_out = layer_out.reshape(tok_shape)
    grad_att = grad_att.reshape(GROUP * mine, PAIR)

    attention += (grad_att,)
    grad_three = None
    if chunks > 1:
        grad_q, grad_k, grad_v = attend_back(bounds, *keyed, att_heads, lse, grad_att, chunks)
        attention = None
        grad_k = lax.psum_scatter(
            grad_k.astype(BF), "ctx", axis_index_groups=same_place, tiled=True
        )
        grad_v = lax.psum_scatter(
            grad_v.astype(BF), "ctx", axis_index_groups=same_place, tiled=True
        )
        grad_three = jnp.concatenate([grad_q, grad_k, grad_v], axis=1)
    here_rows = jnp.zeros((n_f, units), F32)
    sums = jnp.concatenate(
        [
            jnp.zeros((2, width), F32),
            vec[:3],
            vec[4:7],
            lax.dynamic_update_slice_in_dim(here_rows, vec[3:4], f, 0),
            here_rows,
        ]
    )
    share_down, share_up, share_out, share_three, moved, sums = tail(
        n_slots, attention, x_all, grad_three, w_three, part_down, rest_down, part_up, part_out, grad_mid1, sums
    )
    grad_inputs = moved.reshape(tok_shape).astype(F32)
    shares = tuple(part.astype(F32) for part in (share_three, share_out, share_up, share_down)) + (sums,)
    if chunks > 1:
        shares = lax.psum(shares, "ctx", axis_index_groups=same_place)
    share_three, share_out, share_up, share_down, sums = shares
    (
        grad_query_b, grad_value_b, grad_output_b, grad_attn_gain, grad_attn_shift, grad_reduce_b,
        grad_ffn_gain, grad_ffn_shift,
    ) = (sums[i] for i in range(8))
    grad_expand_b = sums[8 : 8 + n_f].reshape(-1)
    return (
        layer_out,
        grad_inputs,
        share_three[0],
        grad_query_b,
        share_three[1],
        share_three[2],
        grad_value_b,
        share_out,
        grad_output_b,
        grad_attn_gain,
        grad_attn_shift,
        share_up,
        grad_expand_b,
        share_down,
        grad_reduce_b,
        grad_ffn_gain,
        grad_ffn_shift,
    )


def solution(mesh):
    acts = P("fsdp", None, "ctx", None)
    rows = P("fsdp", None)
    return jax.shard_map(
        body,
        mesh=mesh,
        in_specs=(
            acts, rows, rows, rows, P(), rows, rows, P(), rows, P(),
            P(), P(), rows, P(), rows, P(), P(), P(), acts,
        ),
        out_specs=(
            acts, acts, rows, P(), rows, rows, P(), rows, P(),
            P(), P(), rows, P(), rows, P(), P(), P(),
        ),
        check_vma=False,
    )
```

```python
import functools
import jax
import jax.numpy as jnp
from jax import lax
from jax.experimental import pallas as pl
from jax.experimental.pallas import tpu as pltpu
from jax.sharding import PartitionSpec as P

H = 16
HD = 64
PAIR = 2 * HD
GROUP = 8
SWAP = (0, 2, 1, 3)
BQ = 512
BK = 512
WIDE = 512
QUARTERS = ((0, 2), (0, 3), (1, 4), (2, 4))
BF = jnp.bfloat16
F32 = jnp.float32


def dense(left, right):
    return jnp.dot(left, right, preferred_element_type=F32)


def dense_back(left, right):
    return lax.dot_general(left, right, (((1,), (1,)), ((), ())), preferred_element_type=F32)


def dense_in(left, right):
    return lax.dot_general(left, right, (((0,), (0,)), ((), ())), preferred_element_type=F32)


def norm_fwd(hidden, gain, shift):
    mean_row = jnp.mean(hidden, axis=-1, keepdims=True)
    centred = hidden - mean_row
    variance = jnp.mean(centred * centred, axis=-1, keepdims=True)
    inv_std = lax.rsqrt(variance + 1e-05)
    x_hat = centred * inv_std
    return (x_hat * gain + shift, x_hat, inv_std)


def norm_back(incoming, x_hat, inv_std, gain):
    scaled = incoming * gain
    grad_in = inv_std * (
        scaled
        - jnp.mean(scaled, axis=-1, keepdims=True)
        - x_hat * jnp.mean(scaled * x_hat, axis=-1, keepdims=True)
    )
    return (grad_in, jnp.sum(incoming * x_hat, axis=0), jnp.sum(incoming, axis=0))


def gelu_slope(pre_act):
    return (
        0.5 * (1.0 + lax.erf(pre_act * 0.7071067811865476))
        + pre_act * jnp.exp(-0.5 * pre_act * pre_act) * 0.3989422804014327
    )


def first_half(shape):
    return lax.broadcasted_iota(jnp.int32, shape, 1) < HD


def both_heads(block):
    left = first_half(block.shape)
    zero = jnp.zeros_like(block)
    return jnp.concatenate([jnp.where(left, block, zero), jnp.where(left, zero, block)], axis=0)


def by_head(stacked):
    rows = stacked.shape[0] // 2
    left = first_half((rows, stacked.shape[1]))
    return jnp.where(left, stacked[:rows], stacked[rows:])


def row_block(ref, i, size):
    if len(ref.shape) == 2:
        return ref[pl.ds(pl.multiple_of(i * size, size), size), :]
    laps = size // (ref.shape[1] * ref.shape[2])
    return ref[pl.ds(i * laps, laps)].reshape(size, ref.shape[3])


def attend_rows(i, bq, bk, ranges, q_ref, k_ref, v_ref, query_seg, key_seg):
    q2 = both_heads(row_block(q_ref, i, bq) * BF(0.125))
    seg = query_seg(i)
    seg2 = jnp.concatenate([seg, seg], axis=0)

    def k_step(j, state):
        accum, run_max, run_sum = state
        scores = dense_back(q2, row_block(k_ref, j, bk))
        scores = jnp.where(seg2 == key_seg(j), scores, -1e30)
        new_max = jnp.maximum(run_max, jnp.max(scores, axis=1, keepdims=True))
        probs = jnp.exp(scores - new_max)
        scale = jnp.exp(run_max - new_max)
        run_sum = run_sum * scale + jnp.sum(probs, axis=1, keepdims=True)
        accum = accum * scale + dense(probs.astype(BF), row_block(v_ref, j, bk))
        return accum, new_max, run_sum

    state = (
        jnp.zeros((2 * bq, PAIR), F32),
        jnp.full((2 * bq, 1), -1e30, F32),
        jnp.zeros((2 * bq, 1), F32),
    )
    for first, last in ranges:
        state = lax.fori_loop(first, last, k_step, state)
    accum, run_max, run_sum = state
    return by_head(accum / run_sum), run_max + jnp.log(run_sum)


def attend_wide(i, bq, first, size, q_ref, k_ref, v_ref, query_seg, key_seg):
    q2 = both_heads(row_block(q_ref, i, bq) * BF(0.125))
    seg = query_seg(i, bq)
    keys = pl.ds(first // 128, size // 128)
    scores = dense_back(q2, k_ref[keys].reshape(size, PAIR))
    scores = jnp.where(jnp.concatenate([seg, seg], axis=0) == key_seg(first, size), scores, -1e30)
    row_max = jnp.max(scores, axis=1, keepdims=True)
    probs = jnp.exp(scores - row_max)
    row_sum = jnp.sum(probs, axis=1, keepdims=True)
    accum = dense(probs.astype(BF), v_ref[keys].reshape(size, PAIR))
    return by_head(accum / row_sum), row_max + jnp.log(row_sum)


def attend_kernel(bq, bk, chunks, lo_ref, hi_ref, q_ref, k_ref, v_ref, sq_ref, sk_ref, o_ref, lse_ref):
    nq = q_ref.shape[0] // bq
    per_chunk = k_ref.shape[0] // chunks // bk

    def q_step(i, carry):
        ranges = [(s * per_chunk + lo_ref[i, s], s * per_chunk + hi_ref[i, s]) for s in range(chunks)]
        rows, lse = attend_rows(
            i, bq, bk, ranges, q_ref, k_ref, v_ref, lambda i: row_block(sq_ref, i, bq),
            lambda j: sk_ref[:, pl.ds(pl.multiple_of(j * bk, bk), bk)],
        )
        o_ref[pl.ds(pl.multiple_of(i * bq, bq), bq), :] = rows.astype(BF)
        lse_ref[pl.ds(pl.multiple_of(2 * i * bq, 2 * bq), 2 * bq), :] = lse
        return carry

    lax.fori_loop(0, nq, q_step, 0)


def segments_from(ends_ref, slots):
    def count(position):
        total = jnp.zeros(position.shape, jnp.int32)
        for j in range(slots):
            total += jnp.where(position >= ends_ref[pl.ds(0, 1), pl.ds(j, 1)], 1, 0)
        return total

    return (
        lambda i, size=BQ: count(i * size + lax.broadcasted_iota(jnp.int32, (size, 1), 0)),
        lambda first, size: count(first + lax.broadcasted_iota(jnp.int32, (1, size), 1)),
    )


def attend_back_rows(i, bq, bk, ranges, q_ref, k_ref, v_ref, query_seg, key_seg, o_ref, lse_ref, g_ref, dk_sum, dv_sum):
    rows = pl.ds(pl.multiple_of(i * bq, bq), bq)
    q2 = both_heads(q_ref[rows, :] * BF(0.125))
    grad = g_ref[rows, :]
    g2 = both_heads(grad)
    prod = grad.astype(F32) * o_ref[rows, :].astype(F32)
    left = first_half(prod.shape)
    delta = jnp.concatenate(
        [
            jnp.sum(jnp.where(left, prod, 0.0), axis=1, keepdims=True),
            jnp.sum(jnp.where(left, 0.0, prod), axis=1, keepdims=True),
        ],
        axis=0,
    )
    lse = lse_ref[pl.ds(pl.multiple_of(2 * i * bq, 2 * bq), 2 * bq), :]
    seg = query_seg(i)
    seg2 = jnp.concatenate([seg, seg], axis=0)

    def k_step(j, dq2):
        keys = pl.ds(pl.multiple_of(j * bk, bk), bk)
        key_rows = k_ref[keys, :]
        scores = dense_back(q2, key_rows)
        probs = jnp.exp(jnp.where(seg2 == key_seg(j), scores, -1e30) - lse)
        grad_prob = dense_back(g2, v_ref[keys, :])
        grad_score = (probs * (grad_prob - delta)).astype(BF)
        dv_sum[keys, :] += dense_in(probs.astype(BF), g2)
        dk_sum[keys, :] += dense_in(grad_score, q2)
        return dq2 + dense(grad_score, key_rows)

    dq2 = jnp.zeros((2 * bq, PAIR), F32)
    for first, last in ranges:
        dq2 = lax.fori_loop(first, last, k_step, dq2)
    return (0.125 * by_head(dq2)).astype(BF)


def attend_back_kernel(
    bq, bk, chunks, lo_ref, hi_ref, q_ref, k_ref, v_ref, sq_ref, sk_ref, o_ref, lse_ref, g_ref,
    dq_ref, dk_ref, dv_ref, dk_sum, dv_sum,
):
    nq = q_ref.shape[0] // bq
    per_chunk = k_ref.shape[0] // chunks // bk
    dk_sum[...] = jnp.zeros_like(dk_sum)
    dv_sum[...] = jnp.zeros_like(dv_sum)

    def q_step(i, carry):
        ranges = [(s * per_chunk + lo_ref[i, s], s * per_chunk + hi_ref[i, s]) for s in range(chunks)]
        dq_ref[pl.ds(pl.multiple_of(i * bq, bq), bq), :] = attend_back_rows(
            i, bq, bk, ranges, q_ref, k_ref, v_ref, lambda i: row_block(sq_ref, i, bq),
            lambda j: sk_ref[:, pl.ds(pl.multiple_of(j * bk, bk), bk)], o_ref, lse_ref, g_ref, dk_sum, dv_sum,
        )
        return carry

    lax.fori_loop(0, nq, q_step, 0)
    dk_ref[...] = dk_sum[...].astype(dk_ref.dtype)
    dv_ref[...] = dv_sum[...].astype(dv_ref.dtype)


SMEM = pl.BlockSpec(memory_space=pltpu.SMEM)
VMEM = pl.BlockSpec(memory_space=pltpu.VMEM)


def attend(bounds, q, k, v, seg_q, seg_k, chunks):
    n = q.shape[0]
    return pl.pallas_call(
        functools.partial(attend_kernel, BQ, BK, chunks),
        out_shape=(jax.ShapeDtypeStruct((n, PAIR), BF), jax.ShapeDtypeStruct((2 * n, 1), F32)),
        in_specs=[SMEM, SMEM] + [VMEM] * 5,
        out_specs=(VMEM, VMEM),
        compiler_params=pltpu.CompilerParams(vmem_limit_bytes=48 * 2**20),
    )(*bounds, q, k, v, seg_q, seg_k)


def attend_back(bounds, q, k, v, seg_q, seg_k, out, lse, grad, chunks):
    n, m = q.shape[0], k.shape[0]
    kept = BF if chunks == 1 else F32
    return pl.pallas_call(
        functools.partial(attend_back_kernel, BQ, BK, chunks),
        out_shape=(
            jax.ShapeDtypeStruct((n, PAIR), BF),
            jax.ShapeDtypeStruct((m, PAIR), kept),
            jax.ShapeDtypeStruct((m, PAIR), kept),
        ),
        in_specs=[SMEM, SMEM] + [VMEM] * 8,
        out_specs=(VMEM, VMEM, VMEM),
        scratch_shapes=[pltpu.VMEM((m, PAIR), F32), pltpu.VMEM((m, PAIR), F32)],
        compiler_params=pltpu.CompilerParams(vmem_limit_bytes=56 * 2**20),
    )(*bounds, q, k, v, seg_q, seg_k, out, lse, grad)


def mesh_id(ctx, f):
    return {"ctx": ctx, "fsdp": f}


def swapped(i):
    return i % 2 * 2 + i // 2


class Place:
    def __init__(self):
        self.ctx = lax.axis_index("ctx")
        self.f = lax.axis_index("fsdp")
        self.per_group = lax.axis_size("ctx") // 4
        self.g = self.ctx // self.per_group
        self.b = self.ctx % 2
        self.rest = self.ctx % self.per_group
        self.core = self.f % 2
        self.x = self.f // 2

    def at(self, g=None, b=None, f=None):
        ctx = self.ctx
        if g is not None:
            ctx = ctx + (g - self.g) * self.per_group
        if b is not None:
            ctx = ctx + (b - self.b)
        return mesh_id(ctx, self.f if f is None else f)

    def sibling(self):
        return self.at(f=self.f + 1 - 2 * self.core)

    def beside(self):
        return self.at(f=(self.f + 2) % 4)

    def across(self):
        return self.at(b=1 - self.b)

    def fsdp(self, k):
        return self.at(f=(self.f + k) % 4)

    def moved(self):
        return mesh_id(swapped(self.f) * self.per_group + self.rest, swapped(self.g))

    def stays(self):
        return swapped(self.f) == self.g


def remote(src, dst, send, recv, where):
    return pltpu.make_async_remote_copy(
        src_ref=src, dst_ref=dst, send_sem=send, recv_sem=recv,
        device_id=where, device_id_type=pl.DeviceIdType.MESH,
    )


def meet(me, targets, moves):
    barrier = pltpu.get_barrier_semaphore()
    for t in targets:
        pl.semaphore_signal(barrier, 1, device_id=t, device_id_type=pl.DeviceIdType.MESH)
    if not moves:
        pl.semaphore_wait(barrier, len(targets))
        return

    @pl.when(jnp.logical_not(me.stays()))
    def _():
        pl.semaphore_signal(barrier, 1, device_id=me.moved(), device_id_type=pl.DeviceIdType.MESH)

    pl.semaphore_wait(barrier, len(targets) + jnp.where(me.stays(), 0, 1))


class Flow:
    def __init__(self, me, own, buf, got, sent, came):
        self.me, self.own, self.buf, self.got, self.sent, self.came = me, own, buf, got, sent, came
        self.low = me.g < 2
        self.inner = jnp.where((me.g == 1) | (me.g == 2), 1, 0)
        step = jnp.where(self.low, 1, -1)
        self.ahead = me.at(g=me.g + step)
        self.back_to = me.at(g=me.g - step)

    def piece(self, i):
        return jnp.where(self.low, 3 - i, i)

    def copy(self, p, side, where):
        return remote(self.buf.at[p], self.got.at[side, p], self.sent.at[p], self.came.at[side, p], where)

    def forward(self, i):
        p = self.piece(i)

        @pl.when(self.inner == 0)
        def _():
            self.buf[p] = self.own(p, i).astype(BF)
            self.copy(p, 0, self.ahead).start()

        if i < 2:
            @pl.when(self.inner == 1)
            def _():
                self.copy(p, 0, self.back_to).wait_recv()
                self.buf[p] = (self.own(p, i) + self.got[0, p].astype(F32)).astype(BF)
                self.copy(p, 1, self.ahead).start()

    def back(self):
        p = self.piece(3)

        @pl.when(self.inner == 1)
        def _():
            self.copy(p, 1, self.ahead).wait_recv()
            self.buf[p] = (self.own(p, 3) + self.got[1, p].astype(F32)).astype(BF)
            self.copy(p, 1, self.back_to).start()

    def end(self):
        g = self.me.g

        @pl.when(self.inner == 0)
        def _():
            self.copy(g, 1, self.ahead).wait_recv()
            self.buf[g] = (self.own(g, 3) + self.got[1, g].astype(F32)).astype(BF)

        @pl.when(self.inner == 1)
        def _():
            self.copy(g, 0, self.back_to).wait_recv()
            self.copy(g, 1, self.ahead).wait_recv()
            self.buf[g] = (self.own(g, 3) + self.got[0, g].astype(F32) + self.got[1, g].astype(F32)).astype(BF)

        for p in range(4):
            @pl.when(g != p)
            def _():
                self.copy(p, 0, self.ahead).wait_send()


def tail_kernel(slots, *refs):
    if slots:
        q_ref, k_ref, v_ref, ends_ref, o_ref, lse_ref, grad_ref, x_ref = refs[:8]
        g3_ref, dk_sum, dv_sum = refs[-3:]
        query_seg, key_seg = segments_from(ends_ref, slots)
        attention = (
            q_ref, k_ref, v_ref, query_seg, lambda j: key_seg(j * BK, BK), o_ref, lse_ref, grad_ref,
        )
        tail_steps(attention, dk_sum, dv_sum, x_ref, g3_ref, *refs[8:-3])
    else:
        tail_steps(None, None, None, *refs)


def tail_steps(
    attention, dk_sum, dv_sum,
    x_ref, g3_ref, w3_ref, down_ref, rest_ref, up_ref, out_ref, mid_ref, vec_ref,
    down_out, up_out, o_out, three_out, dx_ref, sums_ref,
    dxp, dx1, t1, xa, yb, t2a, t2b, ra, rb, moved_buf,
    yr_down, yr_up, dbuf, dgot, ubuf, ugot,
    o_got, o_sum, yr_o, obuf, ogot,
    gq, qbuf, qgot, vs, vr,
    s_dx, r_dx, s_y, r_y, s_d, r_d, s_z, r_z, s_u, r_u, s_o, r_o, s_oz, r_oz, s_q, r_q,
    s_qf, r_qf, s_v, r_v, s_ag, r_ag, s_ay, r_ay, loc, x_rows,
):
    me = Place()
    g, b, f = me.g, me.b, me.f
    z_others = [me.at(g=(g + k) % 4) for k in (1, 2, 3)]
    meet(me, [me.across()] + [me.fsdp(k) for k in (1, 2, 3)] + z_others, True)

    rest = jnp.where(g < 2, 0, 2)

    def own_down(p, i):
        if i < 2:
            return down_ref[p].astype(F32)
        return down_ref[p].astype(F32) + yr_down[p - rest].astype(F32)

    def own_up(p, i):
        return up_ref[:, b, p].astype(F32) + yr_up[p].astype(F32)

    def own_q(p, i):
        return gq[:, :, p].astype(F32)

    def own_o(p, i):
        return o_sum[b, p].astype(F32) + yr_o[p].astype(F32)

    flow_d = Flow(me, own_down, dbuf, dgot, s_d, r_d)
    flow_u = Flow(me, own_up, ubuf, ugot, s_z, r_z)
    flow_q = Flow(me, own_q, qbuf, qgot, s_q, r_q)
    flow_o = Flow(me, own_o, obuf, ogot, s_oz, r_oz)

    edge, inner = flow_d.inner == 0, flow_d.inner == 1
    x_copy = pltpu.make_async_copy(x_ref, x_rows, loc.at[1])
    x_copy.start()

    def at(which, *steps):
        @pl.when(which)
        def _():
            for step in steps:
                step()

    y_copies = []
    for i in range(4):
        p = flow_u.piece(i)
        c = remote(up_ref.at[:, 1 - b, p], yr_up.at[p], s_y.at[0, i], r_y.at[0, i], me.across())
        c.start()
        y_copies.append(c)
    y_down = []
    for i in (2, 3):
        p = flow_d.piece(i) - rest
        c = remote(rest_ref.at[p], yr_down.at[p], s_y.at[1, i], r_y.at[1, i], me.across())
        c.start()
        y_down.append(c)

    o_copies = []
    for k in (1, 2, 3):
        c = remote(out_ref.at[(f + k) % 4], o_got.at[k - 1], s_o.at[k - 1], r_o.at[k - 1], me.fsdp(k))
        c.start()
        o_copies.append(c)
    c_oy = remote(o_sum.at[1 - b], yr_o, s_y.at[1, 0], r_y.at[1, 0], me.across())

    def up_forward(i):
        y_copies[i].wait()
        flow_u.forward(i)

    def up_back():
        y_copies[3].wait()
        flow_u.back()

    def output_rows():
        for c in o_copies:
            c.wait()
        o_sum[...] = (
            out_ref[f].astype(F32) + o_got[0].astype(F32) + o_got[1].astype(F32) + o_got[2].astype(F32)
        ).astype(BF)
        c_oy.start()

    do = functools.partial
    at(edge, do(flow_d.forward, 0), do(flow_d.forward, 1))

    def down_forward():
        y_down[0].wait()
        flow_d.forward(2)

    def down_back():
        for c in y_down:
            c.wait()
        flow_d.back()

    between = (
        ((edge, do(up_forward, 0)), (inner, do(flow_d.forward, 0))),
        ((True, output_rows), (edge, do(up_forward, 1)), (inner, do(flow_d.forward, 1), do(up_forward, 0))),
        ((edge, do(up_forward, 2), down_forward), (inner, do(up_forward, 1))),
        ((edge, y_down[1].wait, y_copies[3].wait), (inner, down_back, y_copies[2].wait, up_back)),
    )
    if attention is not None:
        dk_sum[...] = jnp.zeros_like(dk_sum)
        dv_sum[...] = jnp.zeros_like(dv_sum)
    per = 2048 // BQ // 4
    for quarter, (first, last) in enumerate(QUARTERS):
        ranges = [(first * 512 // BK, last * 512 // BK)]

        def rows_step(i, carry):
            g3_ref[pl.ds(pl.multiple_of(i * BQ, BQ), BQ), pl.ds(0, PAIR)] = attend_back_rows(
                i, BQ, BK, ranges, *attention, dk_sum, dv_sum
            )
            return carry

        if attention is not None:
            lax.fori_loop(quarter * per, (quarter + 1) * per, rows_step, 0)
        for which, *steps in between[quarter]:
            if which is True:
                for step in steps:
                    step()
            else:
                at(which, *steps)
    if attention is not None:
        g3_ref[:, pl.ds(PAIR, PAIR)] = dk_sum[...].astype(BF)
        g3_ref[:, pl.ds(2 * PAIR, PAIR)] = dv_sum[...].astype(BF)

    hops = [me.sibling(), me.beside(), me.across(), me.at(g=g + 1 - 2 * (g % 2)), me.at(g=(g + 2) % 4)]
    vs[0] = jnp.zeros((16, 1024), F32)
    vs[0, pl.ds(2, 3)] = vec_ref[pl.ds(0, 3), :]
    vs[0, pl.ds(5, 3)] = vec_ref[pl.ds(4, 3), :]
    vs[0, pl.ds(8 + f, 1)] = vec_ref[pl.ds(3, 1), :]
    here = pl.ds(pl.multiple_of((b * 4 + swapped(f)) * PAIR, PAIR), PAIR)
    sums3 = jnp.sum(g3_ref[...].astype(F32), axis=0, keepdims=True)
    vs[0, pl.ds(0, 1), here] = sums3[:, :PAIR]
    vs[0, pl.ds(1, 1), here] = sums3[:, 2 * PAIR :]

    def hop(i):
        if i > 0:
            hop_copy(i - 1).wait()
            vs[i] = vs[i - 1] + vr[i - 1]
        hop_copy(i).start()

    def hop_copy(i):
        return remote(vs.at[i], vr.at[i], s_v.at[i], r_v.at[i], hops[i])

    hop(0)

    def rows(size, q, other=False):
        half = 1 - b if other else b
        return pl.ds(pl.multiple_of((half * 4 + q) * size, size), size)

    def unit_cols(src):
        return pl.ds(pl.multiple_of(src * 1024, 1024), 1024)

    def head_cols(src):
        return pl.ds(pl.multiple_of((b * 4 + swapped(src)) * 128, 128), 128)

    def q_rows(q):
        return pl.ds(pl.multiple_of(q * 64, 64), 64)

    def pieces(kind, q, send, recv, where, other=False):
        half = 1 - b if other else b
        if kind == 0:
            parts = ((0, down_out.at[rows(128, q, other), :]),)
        elif kind == 1:
            parts = ((1, up_out.at[rows(32, q, other), :]),)
        else:
            parts = (
                (2, o_out.at[rows(32, q, other), :]),
                (3, three_out.at[:, q_rows(q), pl.ds(pl.multiple_of(half * 512, 512), 512)]),
            )
        return [remote(part, part, send.at[i, q], recv.at[i, q], where) for i, part in parts]

    def spread(kind, q, to_right, to_left):
        if to_right:
            @pl.when(g < 3)
            def _():
                for c in pieces(kind, q, s_ag.at[0], r_ag, me.at(g=g + 1)):
                    c.start()
        if to_left:
            @pl.when(g > 0)
            def _():
                for c in pieces(kind, q, s_ag.at[1], r_ag, me.at(g=g - 1)):
                    c.start()
        for c in pieces(kind, q, s_ay, r_ay, me.across()):
            c.start()

    def pass_on(kind, d):
        @pl.when(g >= d)
        def _():
            for c in pieces(kind, g - d, s_ag.at[0], r_ag, me.across()):
                c.wait_recv()
            spread(kind, g - d, True, False)

        @pl.when(g + d <= 3)
        def _():
            for c in pieces(kind, g + d, s_ag.at[1], r_ag, me.across()):
                c.wait_recv()
            spread(kind, g + d, False, True)

    flow_d.end()
    down_out[rows(128, g), :] = dbuf[g]
    spread(0, g, True, True)

    def dx_step(i, carry):
        rows = pl.ds(pl.multiple_of(i * 256, 256), 256)
        part = dense_back(g3_ref[rows, :], w3_ref[...]).astype(BF)
        dxp[pl.ds(2 * i, 2)] = part.reshape(2, 2, 2, 2, 16, 1024)
        return carry

    lax.fori_loop(0, 8, dx_step, 0)
    c_core = remote(dxp.at[:, 1 - me.core], dx1, s_dx.at[0], r_dx.at[0], me.sibling())
    c_core.start()

    flow_u.end()
    up_out[rows(32, g), unit_cols(f)] = ubuf[g, f]
    u_out = []
    for k in (1, 2, 3):
        c = remote(ubuf.at[g, (f + k) % 4], up_out.at[rows(32, g), unit_cols(f)], s_u.at[k - 1], r_u.at[f], me.fsdp(k))
        c.start()
        u_out.append(c)

    c_core.wait()

    def t1_step(i, carry):
        t1[i] = (dxp[i, me.core].astype(F32) + dx1[i].astype(F32)).astype(BF)
        return carry

    lax.fori_loop(0, 16, t1_step, 0)
    lo, hi = pl.ds(0, 8), pl.ds(8, 8)
    c_xa = remote(t1.at[lo, 1 - me.x], xa, s_dx.at[1], r_dx.at[1], me.beside())
    c_yb = remote(t1.at[hi, :, 1 - b], yb, s_dx.at[2], r_dx.at[2], me.across())
    c_xa.start()
    c_yb.start()
    for k in (1, 2, 3):
        src = (f + k) % 4
        remote(ubuf.at[g, 0], up_out.at[rows(32, g), unit_cols(src)], s_u.at[k - 1], r_u.at[src], me.fsdp(k)).wait_recv()
        u_out[k - 1].wait_send()
    spread(1, g, True, True)
    pass_on(0, 1)
    hop(1)

    x_copy.wait()

    def q_step(i, carry):
        cols = pl.ds(pl.multiple_of(i * 256, 256), 256)
        part = dense_in(x_rows[:, cols], g3_ref[...]).astype(BF)
        for j in range(3):
            gq[i, j] = part[:, j * 128 : (j + 1) * 128].reshape(4, 64, 128)
        return carry

    lax.fori_loop(0, 4, q_step, 0)
    at(edge, *(do(flow_q.forward, i) for i in range(3)))
    c_oy.wait()
    at(edge, *(do(flow_o.forward, i) for i in range(3)))
    pass_on(0, 2)
    c_xa.wait()
    t2a[...] = (t1[lo, me.x].astype(F32) + xa[...].astype(F32)).astype(BF)
    c_ra = remote(t2a.at[:, 1 - b], ra, s_dx.at[3], r_dx.at[3], me.across())
    c_ra.start()
    at(inner, do(flow_q.forward, 0), do(flow_q.forward, 1), do(flow_o.forward, 0), do(flow_o.forward, 1))
    pass_on(1, 1)
    c_yb.wait()
    t2b[...] = (t1[hi, :, b].astype(F32) + yb[...].astype(F32)).astype(BF)
    c_rb = remote(t2b.at[:, 1 - me.x], rb, s_dx.at[4], r_dx.at[4], me.beside())
    c_rb.start()
    hop(2)
    flow_q.back()
    flow_o.back()
    pass_on(0, 3)
    pass_on(1, 2)
    c_ra.wait()
    c_rb.wait()
    moved_buf[lo] = (t2a[:, b].astype(F32) + ra[...].astype(F32) + mid_ref[lo]).astype(BF)
    moved_buf[hi] = (t2b[:, me.x].astype(F32) + rb[...].astype(F32) + mid_ref[hi]).astype(BF)

    @pl.when(me.stays())
    def _():
        c = pltpu.make_async_copy(moved_buf, dx_ref, loc.at[0])
        c.start()
        c.wait()

    @pl.when(jnp.logical_not(me.stays()))
    def _():
        remote(moved_buf, dx_ref, s_dx.at[5], r_dx.at[5], me.moved()).start()

    hop(3)

    flow_q.end()
    three_out[:, q_rows(g), head_cols(f)] = qbuf[g, f]
    q_out = []
    for k in (1, 2, 3):
        c = remote(qbuf.at[g, (f + k) % 4], three_out.at[:, q_rows(g), head_cols(f)], s_qf.at[k - 1], r_qf.at[f], me.fsdp(k))
        c.start()
        q_out.append(c)
    flow_o.end()
    o_out[rows(32, g), :] = obuf[g]
    for k in (1, 2, 3):
        src = (f + k) % 4
        remote(qbuf.at[g, 0], three_out.at[:, q_rows(g), head_cols(src)], s_qf.at[k - 1], r_qf.at[src], me.fsdp(k)).wait_recv()
        q_out[k - 1].wait_send()
    spread(2, g, True, True)
    pass_on(1, 3)
    pass_on(2, 1)
    hop(4)
    pass_on(2, 2)
    pass_on(2, 3)
    hop_copy(4).wait()
    sums_ref[...] = vs[4] + vr[4]

    @pl.when(jnp.logical_not(me.stays()))
    def _():
        remote(moved_buf, dx_ref, s_dx.at[5], r_dx.at[5], me.moved()).wait()

    for kind in (0, 1, 2):
        for q in range(4):
            for c in pieces(kind, q, s_ay, r_ay, me.across()):
                c.wait_send()

            @pl.when((g >= q) & (g < 3))
            def _():
                for c in pieces(kind, q, s_ag.at[0], r_ag, me.across()):
                    c.wait_send()

            @pl.when((g <= q) & (g > 0))
            def _():
                for c in pieces(kind, q, s_ag.at[1], r_ag, me.across()):
                    c.wait_send()

            for c in pieces(kind, q, s_ay, r_ay, me.across(), other=True):
                c.wait_recv()


def tail(slots, attention, x_all, g3, w3, down, rest, up, out, mid, vec):
    dma = pltpu.SemaphoreType.DMA
    v = pltpu.VMEM
    scratch = [
        v((16, 2, 2, 2, 16, 1024), BF), v((16, 2, 2, 16, 1024), BF), v((16, 2, 2, 16, 1024), BF),
        v((8, 2, 16, 1024), BF), v((8, 2, 16, 1024), BF), v((8, 2, 16, 1024), BF), v((8, 2, 16, 1024), BF),
        v((8, 16, 1024), BF), v((8, 16, 1024), BF), v((16, 16, 1024), BF),
        v((2, 128, 1024), BF), v((4, 4, 32, 1024), BF), v((4, 128, 1024), BF), v((2, 4, 128, 1024), BF),
        v((4, 4, 32, 1024), BF), v((2, 4, 4, 32, 1024), BF),
        v((3, 2, 4, 32, 1024), BF), v((2, 4, 32, 1024), BF), v((4, 32, 1024), BF),
        v((4, 32, 1024), BF), v((2, 4, 32, 1024), BF),
        v((4, 3, 4, 64, 128), BF), v((4, 4, 3, 64, 128), BF), v((2, 4, 4, 3, 64, 128), BF),
        v((5, 16, 1024), F32), v((5, 16, 1024), F32),
        dma((6,)), dma((6,)), dma((2, 5)), dma((2, 5)), dma((4,)), dma((2, 4)), dma((4,)), dma((2, 4)),
        dma((3,)), dma((4,)), dma((3,)), dma((3,)), dma((4,)), dma((2, 4)), dma((4,)), dma((2, 4)),
        dma((3,)), dma((4,)), dma((5,)), dma((5,)), dma((2, 4, 4)), dma((4, 4)), dma((4, 4)), dma((4, 4)), dma((2,)),
        v((2048, 1024), BF),
    ]
    if slots:
        scratch += [v((2048, 3 * PAIR), BF), v((2048, PAIR), F32), v((2048, PAIR), F32)]
        operands = (*attention, x_all)
    else:
        operands = (x_all, g3)
    operands += (
        w3, down.reshape(4, 128, 1024), rest.reshape(2, 128, 1024), up.reshape(4, 2, 4, 32, 1024), out.reshape(4, 2, 4, 32, 1024),
        mid.reshape(16, 16, 1024), vec,
    )
    return pl.pallas_call(
        functools.partial(tail_kernel, slots),
        out_shape=(
            jax.ShapeDtypeStruct((1024, 1024), BF),
            jax.ShapeDtypeStruct((256, 4096), BF),
            jax.ShapeDtypeStruct((256, 1024), BF),
            jax.ShapeDtypeStruct((3, 256, 1024), BF),
            jax.ShapeDtypeStruct((16, 16, 1024), BF),
            jax.ShapeDtypeStruct((16, 1024), F32),
        ),
        in_specs=[pl.BlockSpec(memory_space=pl.ANY) if ref is x_all else VMEM for ref in operands],
        out_specs=(VMEM,) * 6,
        scratch_shapes=scratch,
        compiler_params=pltpu.CompilerParams(collective_id=1, has_side_effects=True, vmem_limit_bytes=60 * 2**20),
        cost_estimate=pl.CostEstimate(flops=4 * 10**9, bytes_accessed=40 * 2**20, transcendentals=0),
    )(*operands)


def tile_cols(i, size):
    return pl.ds(pl.multiple_of(i * size, size), size)


def middle_kernel(
    heads_ref, x_ref, cot_ref, wo_ref, wu_in, wd_ref, par_ref,
    layer_ref, down_out, rest_out, upg_out, og_out, gatt_ref, mid1_ref, vec_ref,
    att, nl, gff, slope, hid, gpre, normed, xhat, rstd, work, moved_buf, gbr, gas, ps, pr, down, down_y, wu_ref, up_ref,
    s_a, r_a, s_b, r_b, s_g, r_g, s_p, r_p, s_m, r_m, s_y, r_y, loc, s_u, r_u, s_l,
):
    me = Place()
    f, b = me.f, me.b
    sib = f + 1 - 2 * me.core
    xs = (f + 2) % 4
    xo = xs + 1 - 2 * me.core
    peers = [me.at(f=(f + k % 4) % 4, b=(b + k // 4) % 2) for k in range(1, 8)]
    meet(me, peers, True)
    slot = swapped(f) * 2 + b
    unit = b * 4 + swapped(f)

    def peer_slot(k, sign):
        pf, pb = (f + sign * (k % 4) + 4) % 4, (b + k // 4) % 2
        return swapped(pf) * 2 + pb, pb * 4 + swapped(pf)

    def lanes(index):
        return pl.ds(pl.multiple_of(index * PAIR, PAIR), PAIR)

    for k in range(1, 8):
        where, _ = peer_slot(k, 1)
        remote(heads_ref.at[:, where], att.at[:, :, lanes(unit)], s_a.at[k - 1], r_a.at[k - 1], peers[k - 1]).start()
    att[:, :, lanes(unit)] = heads_ref[:, slot]

    def unit_rows(src, half):
        return pl.ds(pl.multiple_of(src * 256 + half * 128, 128), 128)

    u_out = [
        remote(wu_in.at[unit_rows(src, b)], wu_ref.at[unit_rows(src, b)], s_u.at[i], r_u.at[i], me.across())
        for i, src in enumerate((xs, xo))
    ]
    for c in u_out:
        c.start()
    cot_there = remote(cot_ref, up_ref, s_m.at[1], r_m.at[1], me.moved())
    cot_here = pltpu.make_async_copy(cot_ref, up_ref, loc.at[1])

    @pl.when(me.stays())
    def _():
        cot_here.start()

    @pl.when(jnp.logical_not(me.stays()))
    def _():
        cot_there.start()

    kept = [unit_rows(f, 0), unit_rows(f, 1), unit_rows(sib, 0), unit_rows(sib, 1), unit_rows(xs, b), unit_rows(xo, b)]
    u_kept = [pltpu.make_async_copy(wu_in.at[rows], wu_ref.at[rows], s_l.at[i]) for i, rows in enumerate(kept)]
    for c in u_kept:
        c.start()
    for k in range(1, 8):
        _, theirs = peer_slot(k, -1)
        remote(heads_ref.at[:, slot], att.at[:, :, lanes(theirs)], s_a.at[k - 1], r_a.at[k - 1], peers[k - 1]).wait()

    def row(i):
        return par_ref[pl.ds(i, 1), :]

    def att_rows():
        return att[...].reshape(256, 1024)

    def proj(i, carry):
        cols = tile_cols(i, 512)
        work[:, cols] = dense(att_rows(), wo_ref[:, cols])
        return carry

    lax.fori_loop(0, 2, proj, 0)
    value, x_hat, inv = norm_fwd(x_ref[...].astype(F32) + work[...] + row(0), row(1), row(2))
    normed[...] = value
    xhat[...] = x_hat
    rstd[...] = inv
    nl[f] = value.astype(BF)

    whole, halves = pl.ds(0, 256), (pl.ds(0, 128), pl.ds(128, 128))

    def passed(buf, t, i, src, rows, where):
        return remote(buf.at[src, rows], buf.at[src, rows], s_g.at[t, i], r_g.at[t, i], where)

    def scatter(t, i, part, rows, where):
        return remote(ps.at[t, part, rows], pr.at[t, part, rows], s_p.at[t, i], r_p.at[t, i], where)

    def run(t, block, buf, beside_x):
        for i, rows in enumerate(halves):
            passed(buf, t, 1 + i, f, rows, me.beside()).start()
        passed(buf, t, 0, f, whole, me.sibling()).start()
        block(f, 3, whole)
        passed(buf, t, 0, f, whole, me.sibling()).wait_send()
        passed(buf, t, 0, sib, whole, me.sibling()).wait_recv()
        block(sib, 0, whole)
        scatter(t, 0, 0, whole, me.sibling()).start()

        def from_x(i):
            passed(buf, t, 1 + i, f, halves[i], me.beside()).wait_send()
            passed(buf, t, 1 + i, xs, halves[i], me.beside()).wait_recv()
            passed(buf, t, 3 + i, xs, halves[i], me.sibling()).start()

        def from_other(i):
            passed(buf, t, 3 + i, xs, halves[i], me.sibling()).wait_send()
            passed(buf, t, 3 + i, xo, halves[i], me.sibling()).wait_recv()

        def chip_sum(i):
            rows = halves[i]
            scatter(t, 1 + i, 1, rows, me.sibling()).wait()
            ps[t, 2, rows] = (ps[t, 2, rows].astype(F32) + pr[t, 1, rows].astype(F32)).astype(BF)
            scatter(t, 3 + i, 2, rows, me.beside()).start()

        from_x(0)
        block(xs, 2, halves[0])
        from_other(0)
        block(xo, 1, halves[0])
        scatter(t, 1, 1, halves[0], me.sibling()).start()
        from_x(1)
        chip_sum(0)
        block(xs, 2, halves[1])
        from_other(1)
        block(xo, 1, halves[1])
        scatter(t, 2, 1, halves[1], me.sibling()).start()
        chip_sum(1)
        beside_x()
        scatter(t, 0, 0, whole, me.sibling()).wait()
        for i, rows in enumerate(halves):
            scatter(t, 3 + i, 2, rows, me.beside()).wait()
        return ps[t, 3].astype(F32) + pr[t, 0].astype(F32) + pr[t, 2].astype(F32)

    def forward(index, into, rows):
        def up_tile(i, carry):
            cols = tile_cols(i, 256)
            pre = dense(nl[index, rows], wu_ref[:, cols]) + par_ref[pl.ds(6, 1), cols]
            cdf = 0.5 * (1.0 + lax.erf(pre * 0.7071067811865476))
            hid[index, rows, cols] = (pre * cdf).astype(BF)
            slope[index, rows, cols] = cdf + pre * jnp.exp(-0.5 * pre * pre) * 0.3989422804014327
            return carry

        def down_tile(i, carry):
            cols = tile_cols(i, 512)
            ps[0, into, rows, cols] = dense(hid[index, rows], wd_ref[:, cols]).astype(BF)
            return carry

        lax.fori_loop(0, 4, up_tile, 0)
        lax.fori_loop(0, 2, down_tile, 0)

    for c in u_out + u_kept:
        c.wait()
    ffn = run(0, forward, nl, lambda: None)

    @pl.when(me.stays())
    def _():
        cot_here.wait()

    @pl.when(jnp.logical_not(me.stays()))
    def _():
        cot_there.wait()

    value, x_hat, inv = norm_fwd(normed[...] + ffn + row(3), row(4), row(5))
    moved_buf[...] = value.astype(BF)

    @pl.when(me.stays())
    def _():
        pltpu.make_async_copy(moved_buf, layer_ref, loc.at[0]).start()

    @pl.when(jnp.logical_not(me.stays()))
    def _():
        remote(moved_buf, layer_ref, s_m.at[0], r_m.at[0], me.moved()).start()

    grad2, gain2, shift2 = norm_back(up_ref[...].astype(F32), x_hat, inv, row(4))
    work[...] = grad2
    low2 = grad2.astype(BF)
    gff[f] = low2
    vec_ref[pl.ds(4, 1), :] = jnp.sum(low2.astype(F32), axis=0, keepdims=True)
    vec_ref[pl.ds(5, 1), :] = gain2[None]
    vec_ref[pl.ds(6, 1), :] = shift2[None]

    def backward(index, into, rows):
        def pre_tile(i, carry):
            cols = tile_cols(i, 512)
            part = dense_back(gff[index, rows], wd_ref[cols, :])
            gpre[index, rows, cols] = (part * slope[index, rows, cols]).astype(BF)
            return carry

        def in_tile(i, carry):
            cols = tile_cols(i, 512)
            ps[1, into, rows, cols] = dense_back(gpre[index, rows], wu_ref[cols, :]).astype(BF)
            return carry

        lax.fori_loop(0, 2, pre_tile, 0)
        lax.fori_loop(0, 2, in_tile, 0)

    first = pl.ds(pl.multiple_of(jnp.where(me.g < 2, 256, 0), 256), 256)
    later = pl.ds(pl.multiple_of(jnp.where(me.g < 2, 0, 256), 256), 256)
    c_down = remote(down.at[1 - b, first], down_y, s_y.at[0], r_y.at[0], me.across())

    def weight_grads():
        def down_tile(i, carry):
            cols = tile_cols(i, 256)
            part = dense_in(hid[:, :, cols].reshape(1024, 256), gff[...].reshape(1024, 1024)).astype(BF)
            down[i // 2, pl.ds(pl.multiple_of(i % 2 * 256, 256), 256)] = part
            return carry

        def up_tile(i, carry):
            cols = tile_cols(i, 256)
            upg_out[cols, :] = dense_in(nl[:, :, cols].reshape(1024, 256), gpre[...].reshape(1024, 1024)).astype(BF)
            return carry

        lax.fori_loop(0, 4, down_tile, 0)
        c_down.start()
        lax.fori_loop(0, 4, up_tile, 0)
        vec_ref[pl.ds(3, 1), :] = jnp.sum(gpre[...].reshape(1024, 1024).astype(F32), axis=0, keepdims=True)

    back = run(1, backward, gff, weight_grads)
    grad1, gain1, shift1 = norm_back(back + work[...], xhat[...], rstd[...], row(1))
    mid1_ref[...] = grad1
    low1 = grad1.astype(BF)
    gbr[...] = low1
    vec_ref[pl.ds(0, 1), :] = jnp.sum(low1.astype(F32), axis=0, keepdims=True)
    vec_ref[pl.ds(1, 1), :] = gain1[None]
    vec_ref[pl.ds(2, 1), :] = shift1[None]
    vec_ref[pl.ds(7, 1), :] = jnp.zeros((1, 1024), F32)

    def att_tile(i, carry):
        part = dense_back(gbr[...], wo_ref[tile_cols(i, 256), :]).astype(BF)
        for j in range(2):
            gas[2 * i + j] = part[:, j * PAIR : (j + 1) * PAIR].reshape(16, 16, PAIR)
        return carry

    lax.fori_loop(0, 4, att_tile, 0)
    for k in range(1, 8):
        _, theirs = peer_slot(k, 1)
        remote(gas.at[theirs], gatt_ref.at[:, slot], s_b.at[k - 1], r_b.at[k - 1], peers[k - 1]).start()
    gatt_ref[:, slot] = gas[unit]

    def o_tile(i, carry):
        cols = tile_cols(i, 256)
        og_out[cols, :] = dense_in(att[:, :, cols].reshape(256, 256), gbr[...]).astype(BF)
        return carry

    lax.fori_loop(0, 4, o_tile, 0)
    for k in range(1, 8):
        where, _ = peer_slot(k, -1)
        remote(gas.at[0], gatt_ref.at[:, where], s_b.at[k - 1], r_b.at[k - 1], peers[k - 1]).wait()
    c_down.wait()
    down_out[first, :] = (down[b, first].astype(F32) + down_y[...].astype(F32)).astype(BF)
    down_out[later, :] = down[b, later]
    rest_out[...] = down[1 - b, later]

    @pl.when(me.stays())
    def _():
        pltpu.make_async_copy(moved_buf, layer_ref, loc.at[0]).wait()

    @pl.when(jnp.logical_not(me.stays()))
    def _():
        remote(moved_buf, layer_ref, s_m.at[0], r_m.at[0], me.moved()).wait()


def middle(heads, x, upstream, w_output, w_up, w_down, params):
    dma = pltpu.SemaphoreType.DMA
    v = pltpu.VMEM
    block = (4, 256, 1024)
    scratch = [
        v((16, 16, 1024), BF), v(block, BF), v(block, BF), v(block, F32), v(block, BF), v(block, BF),
        v((256, 1024), F32), v((256, 1024), F32), v((256, 1), F32), v((256, 1024), F32), v((256, 1024), BF),
        v((256, 1024), BF), v((8, 16, 16, PAIR), BF), v((2, 4, 256, 1024), BF), v((2, 3, 256, 1024), BF),
        v((2, 512, 1024), BF), v((256, 1024), BF), v((1024, 1024), BF), v((256, 1024), BF),
        dma((7,)), dma((7,)), dma((7,)), dma((7,)), dma((2, 5)), dma((2, 5)), dma((2, 5)), dma((2, 5)),
        dma((2,)), dma((2,)), dma((1,)), dma((1,)), dma((2,)), dma((2,)), dma((2,)), dma((6,)),
    ]
    hbm = pl.BlockSpec(memory_space=pl.ANY)
    square = jax.ShapeDtypeStruct((1024, 1024), BF)
    return pl.pallas_call(
        middle_kernel,
        out_shape=(
            jax.ShapeDtypeStruct((256, 1024), BF), jax.ShapeDtypeStruct((512, 1024), BF),
            jax.ShapeDtypeStruct((256, 1024), BF), square, square,
            jax.ShapeDtypeStruct((16, 8, 16, PAIR), BF),
            jax.ShapeDtypeStruct((256, 1024), F32),
            jax.ShapeDtypeStruct((8, 1024), F32),
        ),
        in_specs=[VMEM, VMEM, hbm, VMEM, hbm, VMEM, VMEM],
        out_specs=(VMEM,) * 8,
        scratch_shapes=scratch,
        compiler_params=pltpu.CompilerParams(collective_id=2, has_side_effects=True, vmem_limit_bytes=60 * 2**20),
        cost_estimate=pl.CostEstimate(flops=14 * 10**9, bytes_accessed=20 * 2**20, transcendentals=2**21),
    )(heads.reshape(16, 8, 16, PAIR), x, upstream, w_output, w_up, w_down, params)


def start_kernel(
    slots, tok_ref, ends_ref, qw_ref, kw_ref, vw_ref, ow_ref, ew_ref, bias_ref,
    x_ref, ends_out, q_ref, k_ref, v_ref, w3_ref, wo_ref, wu_ref, att_ref, lse_ref,
    s_m, r_m, s_w, r_w, s_u, r_u, s_o, r_o, s_x, r_x, loc,
):
    me = Place()
    g, b, f = me.g, me.b, me.f
    sib = f + 1 - 2 * me.core
    xs = (f + 2) % 4
    xo = xs + 1 - 2 * me.core
    meet(me, [me.across()] + [me.fsdp(k) for k in (1, 2, 3)], True)
    slot = me.core * 4 + me.x * 2 + b
    slot_x = me.core * 4 + (1 - me.x) * 2 + b
    slot_y = slot + 1 - 2 * b
    slot_d = slot_x + 1 - 2 * b
    other = 4 - 8 * me.core
    lo, hi = pl.ds(0, 8), pl.ds(8, 8)

    def moves(i, src, dst):
        return remote(src, dst, s_m.at[i], r_m.at[i], me.moved())

    def relocate(i, src, dst):
        @pl.when(me.stays())
        def _():
            pltpu.make_async_copy(src, dst, loc.at[i]).start()

        @pl.when(jnp.logical_not(me.stays()))
        def _():
            moves(i, src, dst).start()

    def relocated(i, src, dst):
        @pl.when(me.stays())
        def _():
            pltpu.make_async_copy(src, dst, loc.at[i]).wait()

        @pl.when(jnp.logical_not(me.stays()))
        def _():
            moves(i, src, dst).wait()

    theirs = x_ref.at[:, g * 2 + b]
    relocate(0, tok_ref, theirs)
    relocate(1, ends_ref, ends_out)

    def cols(index, size):
        return pl.ds(pl.multiple_of(index * size, size), size)

    def w3_rows(src):
        return cols(src, 256)

    def wo_rows(src, which):
        return pl.ds(pl.multiple_of(src * 256 + which * 128, 128), 128)

    half = cols(b, 128)
    u_x = [
        remote(ew_ref.at[half, cols(xs, 1024)], wu_ref.at[wo_rows(f, b)], s_u.at[1], r_u.at[1], me.beside()),
        remote(ew_ref.at[half, cols(xo, 1024)], wu_ref.at[wo_rows(f, b)], s_u.at[2], r_u.at[2], me.at(f=xo)),
    ]
    o_x = remote(ow_ref.at[half], wo_ref.at[wo_rows(f, b)], s_o.at[1], r_o.at[1], me.beside())
    u_sib = remote(ew_ref.at[:, cols(sib, 1024)], wu_ref.at[w3_rows(f)], s_u.at[0], r_u.at[0], me.sibling())
    o_sib = remote(ow_ref, wo_ref.at[w3_rows(f)], s_o.at[0], r_o.at[0], me.sibling())
    for c in (o_x, u_sib, o_sib):
        c.start()
    o_own = pltpu.make_async_copy(ow_ref, wo_ref.at[w3_rows(f)], loc.at[5])
    u_own = pltpu.make_async_copy(ew_ref.at[:, cols(f, 1024)], wu_ref.at[w3_rows(f)], loc.at[6])
    o_own.start()
    u_own.start()
    weights = (qw_ref, kw_ref, vw_ref)

    def w3_own(j):
        return pltpu.make_async_copy(
            weights[j].at[:, cols(b * 4 + swapped(f), 128)], w3_ref.at[w3_rows(f), pl.ds(128 * j, 128)], loc.at[2 + j]
        )

    for j in range(3):
        w3_own(j).start()
    for k in (2, 3, 1):
        dest = b * 4 + swapped((f + k) % 4)
        for j in range(3):
            remote(
                weights[j].at[:, cols(dest, 128)], w3_ref.at[w3_rows(f), pl.ds(128 * j, 128)],
                s_w.at[j, k - 1], r_w.at[j, k - 1], me.fsdp(k),
            ).start()

    def piece(i, ref, where):
        return remote(ref, ref, s_x.at[i], r_x.at[i], where)

    relocated(0, tok_ref, theirs)
    own = x_ref.at[:, slot]
    sends = [piece(1, own, me.beside()), piece(2, own, me.across()), piece(0, own, me.sibling())]
    for c in sends:
        c.start()

    def project(which):
        part = dense(x_ref[:, which].reshape(256, 1024), w3_ref[...]) + bias_ref[...]
        part = part.astype(BF).reshape(16, 16, 3 * PAIR)
        q_ref[:, which] = part[:, :, :PAIR]
        k_ref[:, which] = part[:, :, PAIR : 2 * PAIR]
        v_ref[:, which] = part[:, :, 2 * PAIR :]

    piece(1, x_ref.at[:, slot_x], me.beside()).wait_recv()
    more = [piece(4, x_ref.at[hi, slot_x], me.across()), piece(3, x_ref.at[:, slot_x], me.sibling())]
    for c in more:
        c.start()
    sends += more
    piece(2, x_ref.at[:, slot_y], me.across()).wait_recv()
    more = [piece(6, x_ref.at[lo, slot_y], me.beside()), piece(5, x_ref.at[:, slot_y], me.sibling())]
    for c in more:
        c.start()
    sends += more
    for c in u_x:
        c.start()
    o_x.wait()
    o_fwd = [
        remote(wo_ref.at[wo_rows(xs, b)], wo_ref.at[wo_rows(xs, b)], s_o.at[2], r_o.at[2], me.sibling()),
        remote(wo_ref.at[wo_rows(xs, b)], wo_ref.at[wo_rows(xs, b)], s_o.at[3], r_o.at[3], me.across()),
    ]
    for c in o_fwd:
        c.start()
    for k in (1, 2, 3):
        src = (f + 4 - k) % 4
        for j in range(3):
            remote(
                weights[j].at[:, cols(0, 128)], w3_ref.at[w3_rows(src), pl.ds(128 * j, 128)],
                s_w.at[j, k - 1], r_w.at[j, k - 1], me.fsdp(k),
            ).wait()
    for j in range(3):
        w3_own(j).wait()
    project(slot)
    project(slot_x)
    piece(4, x_ref.at[hi, slot_d], me.across()).wait_recv()
    more = [piece(8, x_ref.at[hi, slot_d], me.sibling())]
    more[0].start()
    piece(6, x_ref.at[lo, slot_d], me.beside()).wait_recv()
    more.append(piece(7, x_ref.at[lo, slot_d], me.sibling()))
    more[1].start()
    sends += more
    project(slot_y)
    for i, part in ((0, slot + other), (3, slot_x + other), (5, slot_y + other)):
        piece(i, x_ref.at[:, part], me.sibling()).wait_recv()
        project(part)
    project(slot_d)
    piece(8, x_ref.at[hi, slot_d + other], me.sibling()).wait_recv()
    piece(7, x_ref.at[lo, slot_d + other], me.sibling()).wait_recv()
    project(slot_d + other)
    for c in sends:
        c.wait_send()
    relocated(1, ends_ref, ends_out)

    segments = segments_from(ends_out, slots)

    def attend_quarter(quarter):
        first, last = QUARTERS[quarter]

        rows, lse = attend_wide(quarter, WIDE, first * 512, (last - first) * 512, q_ref, k_ref, v_ref, *segments)
        att_ref[pl.ds(quarter * 4, 4)] = rows.astype(BF).reshape(4, GROUP, 16, PAIR)
        for part in range(WIDE // BQ):
            for head in range(2):
                to = 2 * (quarter * WIDE + part * BQ) + head * BQ
                lse_ref[pl.ds(to, BQ), :] = lse[head * WIDE + part * BQ : head * WIDE + (part + 1) * BQ]

    if slots:
        attend_quarter(0)
    if slots:
        attend_quarter(1)
        attend_quarter(2)
    o_fwd[0].wait()
    o_fwd[1].wait()
    late = remote(wo_ref.at[wo_rows(xs, 1 - b)], wo_ref.at[wo_rows(xs, 1 - b)], s_o.at[4], r_o.at[4], me.sibling())
    late.start()
    if slots:
        attend_quarter(3)
    late.wait()
    o_own.wait()
    o_sib.wait()
    u_own.wait()
    u_sib.wait()
    for c in u_x:
        c.wait()


def start(slots, tokens, ends, query_w, key_w, value_w, output_w, expand_w, bias3):
    dma = pltpu.SemaphoreType.DMA
    hbm = pl.BlockSpec(memory_space=pl.ANY)
    heads = jax.ShapeDtypeStruct((16, GROUP, 16, PAIR), BF)
    square = jax.ShapeDtypeStruct((1024, 1024), BF)
    return pl.pallas_call(
        functools.partial(start_kernel, slots),
        out_shape=(
            jax.ShapeDtypeStruct((16, GROUP, 16, 1024), BF), jax.ShapeDtypeStruct((8, 128), jnp.int32), heads, heads, heads,
            jax.ShapeDtypeStruct((1024, 3 * PAIR), BF), square, square,
            heads, jax.ShapeDtypeStruct((4096, 1), F32),
        ),
        in_specs=[hbm, VMEM] + [hbm] * 5 + [VMEM],
        out_specs=(VMEM, VMEM, VMEM, VMEM, VMEM, VMEM, hbm, hbm, VMEM, VMEM),
        scratch_shapes=[
            dma((2,)), dma((2,)), dma((3, 3)), dma((3, 3)), dma((3,)), dma((3,)), dma((5,)), dma((5,)),
            dma((9,)), dma((9,)), dma((7,)),
        ],
        compiler_params=pltpu.CompilerParams(collective_id=3, has_side_effects=True, vmem_limit_bytes=60 * 2**20),
        cost_estimate=pl.CostEstimate(flops=2 * 10**9, bytes_accessed=20 * 2**20, transcendentals=0),
    )(tokens, ends, query_w, key_w, value_w, output_w, expand_w, bias3)


def body(
    tokens, lengths, packing, query_w, query_b, key_w, value_w, value_b, output_w, output_b,
    attn_gain, attn_shift, expand_w, expand_b, reduce_w, reduce_b, ffn_gain, ffn_shift, cotangent,
):
    tok_shape = tokens.shape
    laps, stripe, width = tok_shape[1], tok_shape[2], tok_shape[3]
    mine = laps * stripe
    n_ctx = lax.axis_size("ctx")
    n_f = lax.axis_size("fsdp")
    per_group = n_ctx // n_f
    chunks = per_group // 2
    ctx = lax.axis_index("ctx")
    f = lax.axis_index("fsdp")
    g = ctx // per_group
    chunk = ctx % per_group // 2
    b = ctx % 2
    same_place = [
        [(gg * chunks + s) * 2 + bb for s in range(chunks)] for gg in range(n_f) for bb in range(2)
    ]
    units = expand_w.shape[1] // n_f

    ordered = jnp.sum(
        jnp.where(
            packing[0][:, None] == jnp.arange(lengths.shape[1], dtype=jnp.int32)[None, :],
            lengths[0][None, :],
            0,
        ),
        axis=1,
    )
    slots = jnp.arange(ordered.shape[0], dtype=jnp.int32)
    own_ends = jnp.sum(jnp.where(slots[None, :] <= slots[:, None], ordered[None, :], 0), axis=1)
    own_ends = jnp.pad(own_ends[None], ((0, 7), (0, 128 - own_ends.shape[0])))

    here = (b * n_f + swapped(f)) * PAIR
    bias3 = jnp.concatenate(
        [
            lax.dynamic_slice_in_dim(query_b, here, PAIR),
            jnp.zeros((PAIR,), F32),
            lax.dynamic_slice_in_dim(value_b, here, PAIR),
        ]
    )[None]
    acts = (laps, stripe, width)
    n_slots = lengths.shape[1] if chunks == 1 else 0
    x_all, ends, q, k_own, v_own, w_three, w_output, w_up, att_heads, lse = start(
        n_slots, tokens.reshape(acts), own_ends, query_w, key_w, value_w, output_w, expand_w, bias3
    )
    q, k_own, v_own = (part.reshape(GROUP * mine, PAIR) for part in (q, k_own, v_own))
    inputs = lax.dynamic_index_in_dim(x_all, swapped(f) * 2 + b, 1, keepdims=False).reshape(mine, width)
    x_all = x_all.reshape(GROUP * mine, width)
    upstream = cotangent.reshape(mine, width)
    slot_ends = ends[0, : ordered.shape[0]]

    span = GROUP * mine
    index = jnp.arange(span, dtype=jnp.int32)

    def segments(which):
        lap, rest = index // (GROUP * stripe), index % (GROUP * stripe)
        unit, place = rest // stripe, rest % stripe
        owner = unit // 2 * per_group + which * 2 + unit % 2
        position = lap * (n_ctx * stripe) + owner * stripe + place
        return jnp.sum((position[:, None] >= slot_ends[None, :]).astype(jnp.int32), axis=1)

    attention = (q, k_own, v_own, ends, att_heads.reshape(span, PAIR), lse)
    if chunks > 1:
        seg_q = segments(chunk)
        seg_k = jnp.concatenate([segments(s) for s in range(chunks)])
        q_first, q_last = seg_q[::BQ], seg_q[BQ - 1 :: BQ]
        k_first = seg_k[::BK].reshape(chunks, -1)
        k_last = seg_k[BK - 1 :: BK].reshape(chunks, -1)
        lo = jnp.sum((k_last[None] < q_first[:, None, None]).astype(jnp.int32), axis=2)
        hi = jnp.sum((k_first[None] <= q_last[:, None, None]).astype(jnp.int32), axis=2)
        bounds = (lo, hi)
        k = lax.all_gather(k_own, "ctx", axis_index_groups=same_place, tiled=True)
        v = lax.all_gather(v_own, "ctx", axis_index_groups=same_place, tiled=True)
        keyed = (q, k, v, seg_q[:, None], seg_k[None, :])
        att_heads, lse = attend(bounds, *keyed, chunks)

    params = jnp.stack(
        [
            output_b, attn_gain, attn_shift, reduce_b, ffn_gain, ffn_shift,
            lax.dynamic_slice_in_dim(expand_b, f * units, units), jnp.zeros_like(output_b),
        ]
    )
    layer_out, part_down, rest_down, part_up, part_out, grad_att, grad_mid1, vec = middle(
        att_heads, inputs, upstream, w_output, w_up, reduce_w, params
    )
    layer_out = layer_out.reshape(tok_shape)
    grad_att = grad_att.reshape(GROUP * mine, PAIR)

    attention += (grad_att,)
    grad_three = None
    if chunks > 1:
        grad_q, grad_k, grad_v = attend_back(bounds, *keyed, att_heads, lse, grad_att, chunks)
        attention = None
        grad_k = lax.psum_scatter(
            grad_k.astype(BF), "ctx", axis_index_groups=same_place, tiled=True
        )
        grad_v = lax.psum_scatter(
            grad_v.astype(BF), "ctx", axis_index_groups=same_place, tiled=True
        )
        grad_three = jnp.concatenate([grad_q, grad_k, grad_v], axis=1)
    share_down, share_up, share_out, share_three, moved, sums = tail(
        n_slots, attention, x_all, grad_three, w_three, part_down, rest_down, part_up, part_out, grad_mid1, vec
    )
    grad_inputs = moved.reshape(tok_shape).astype(F32)
    shares = tuple(part.astype(F32) for part in (share_three, share_out, share_up, share_down)) + (sums,)
    if chunks > 1:
        shares = lax.psum(shares, "ctx", axis_index_groups=same_place)
    share_three, share_out, share_up, share_down, sums = shares
    (
        grad_query_b, grad_value_b, grad_output_b, grad_attn_gain, grad_attn_shift, grad_reduce_b,
        grad_ffn_gain, grad_ffn_shift,
    ) = (sums[i] for i in range(8))
    grad_expand_b = sums[8 : 8 + n_f].reshape(-1)
    return (
        layer_out,
        grad_inputs,
        share_three[0],
        grad_query_b,
        share_three[1],
        share_three[2],
        grad_value_b,
        share_out,
        grad_output_b,
        grad_attn_gain,
        grad_attn_shift,
        share_up,
        grad_expand_b,
        share_down,
        grad_reduce_b,
        grad_ffn_gain,
        grad_ffn_shift,
    )


def solution(mesh):
    acts = P("fsdp", None, "ctx", None)
    rows = P("fsdp", None)
    return jax.shard_map(
        body,
        mesh=mesh,
        in_specs=(
            acts, rows, rows, rows, P(), rows, rows, P(), rows, P(),
            P(), P(), rows, P(), rows, P(), P(), P(), acts,
        ),
        out_specs=(
            acts, acts, rows, P(), rows, rows, P(), rows, P(),
            P(), P(), rows, P(), rows, P(), P(), P(),
        ),
        check_vma=False,
    )
```

```python
import functools
import jax
import jax.numpy as jnp
from jax import lax
from jax.experimental import pallas as pl
from jax.experimental.pallas import tpu as pltpu
from jax.sharding import PartitionSpec as P

H = 16
HD = 64
PAIR = 2 * HD
GROUP = 8
SWAP = (0, 2, 1, 3)
BQ = 512
BK = 512
WIDE = 512
QUARTERS = ((0, 2), (0, 3), (1, 4), (2, 4))
BF = jnp.bfloat16
F32 = jnp.float32


def dense(left, right):
    return jnp.dot(left, right, preferred_element_type=F32)


def dense_back(left, right):
    return lax.dot_general(left, right, (((1,), (1,)), ((), ())), preferred_element_type=F32)


def dense_in(left, right):
    return lax.dot_general(left, right, (((0,), (0,)), ((), ())), preferred_element_type=F32)


def norm_fwd(hidden, gain, shift):
    mean_row = jnp.mean(hidden, axis=-1, keepdims=True)
    centred = hidden - mean_row
    variance = jnp.mean(centred * centred, axis=-1, keepdims=True)
    inv_std = lax.rsqrt(variance + 1e-05)
    x_hat = centred * inv_std
    return (x_hat * gain + shift, x_hat, inv_std)


def norm_back(incoming, x_hat, inv_std, gain):
    scaled = incoming * gain
    grad_in = inv_std * (
        scaled
        - jnp.mean(scaled, axis=-1, keepdims=True)
        - x_hat * jnp.mean(scaled * x_hat, axis=-1, keepdims=True)
    )
    return (grad_in, jnp.sum(incoming * x_hat, axis=0), jnp.sum(incoming, axis=0))


def gelu_slope(pre_act):
    return (
        0.5 * (1.0 + lax.erf(pre_act * 0.7071067811865476))
        + pre_act * jnp.exp(-0.5 * pre_act * pre_act) * 0.3989422804014327
    )


def first_half(shape):
    return lax.broadcasted_iota(jnp.int32, shape, 1) < HD


def both_heads(block):
    left = first_half(block.shape)
    zero = jnp.zeros_like(block)
    return jnp.concatenate([jnp.where(left, block, zero), jnp.where(left, zero, block)], axis=0)


def by_head(stacked):
    rows = stacked.shape[0] // 2
    left = first_half((rows, stacked.shape[1]))
    return jnp.where(left, stacked[:rows], stacked[rows:])


def row_block(ref, i, size):
    if len(ref.shape) == 2:
        return ref[pl.ds(pl.multiple_of(i * size, size), size), :]
    laps = size // (ref.shape[1] * ref.shape[2])
    return ref[pl.ds(i * laps, laps)].reshape(size, ref.shape[3])


def attend_rows(i, bq, bk, ranges, q_ref, k_ref, v_ref, query_seg, key_seg):
    q2 = both_heads(row_block(q_ref, i, bq) * BF(0.125))
    seg = query_seg(i)
    seg2 = jnp.concatenate([seg, seg], axis=0)

    def k_step(j, state):
        accum, run_max, run_sum = state
        scores = dense_back(q2, row_block(k_ref, j, bk))
        scores = jnp.where(seg2 == key_seg(j), scores, -1e30)
        new_max = jnp.maximum(run_max, jnp.max(scores, axis=1, keepdims=True))
        probs = jnp.exp(scores - new_max)
        scale = jnp.exp(run_max - new_max)
        run_sum = run_sum * scale + jnp.sum(probs, axis=1, keepdims=True)
        accum = accum * scale + dense(probs.astype(BF), row_block(v_ref, j, bk))
        return accum, new_max, run_sum

    state = (
        jnp.zeros((2 * bq, PAIR), F32),
        jnp.full((2 * bq, 1), -1e30, F32),
        jnp.zeros((2 * bq, 1), F32),
    )
    for first, last in ranges:
        state = lax.fori_loop(first, last, k_step, state)
    accum, run_max, run_sum = state
    return by_head(accum / run_sum), run_max + jnp.log(run_sum)


def attend_wide(i, bq, first, size, q_ref, k_ref, v_ref, query_seg, key_seg):
    q2 = both_heads(row_block(q_ref, i, bq) * BF(0.125))
    seg = query_seg(i, bq)
    keys = pl.ds(first // 128, size // 128)
    scores = dense_back(q2, k_ref[keys].reshape(size, PAIR))
    scores = jnp.where(jnp.concatenate([seg, seg], axis=0) == key_seg(first, size), scores, -1e30)
    row_max = jnp.max(scores, axis=1, keepdims=True)
    probs = jnp.exp(scores - row_max)
    row_sum = jnp.sum(probs, axis=1, keepdims=True)
    accum = dense(probs.astype(BF), v_ref[keys].reshape(size, PAIR))
    return by_head(accum / row_sum), row_max + jnp.log(row_sum)


def attend_kernel(bq, bk, chunks, lo_ref, hi_ref, q_ref, k_ref, v_ref, sq_ref, sk_ref, o_ref, lse_ref):
    nq = q_ref.shape[0] // bq
    per_chunk = k_ref.shape[0] // chunks // bk

    def q_step(i, carry):
        ranges = [(s * per_chunk + lo_ref[i, s], s * per_chunk + hi_ref[i, s]) for s in range(chunks)]
        rows, lse = attend_rows(
            i, bq, bk, ranges, q_ref, k_ref, v_ref, lambda i: row_block(sq_ref, i, bq),
            lambda j: sk_ref[:, pl.ds(pl.multiple_of(j * bk, bk), bk)],
        )
        o_ref[pl.ds(pl.multiple_of(i * bq, bq), bq), :] = rows.astype(BF)
        lse_ref[pl.ds(pl.multiple_of(2 * i * bq, 2 * bq), 2 * bq), :] = lse
        return carry

    lax.fori_loop(0, nq, q_step, 0)


def segments_from(ends_ref, slots):
    def count(position):
        total = jnp.zeros(position.shape, jnp.int32)
        for j in range(slots):
            total += jnp.where(position >= ends_ref[pl.ds(0, 1), pl.ds(j, 1)], 1, 0)
        return total

    return (
        lambda i, size=BQ: count(i * size + lax.broadcasted_iota(jnp.int32, (size, 1), 0)),
        lambda first, size: count(first + lax.broadcasted_iota(jnp.int32, (1, size), 1)),
    )


def attend_back_rows(i, bq, bk, ranges, q_ref, k_ref, v_ref, query_seg, key_seg, o_ref, lse_ref, g_ref, dk_sum, dv_sum):
    rows = pl.ds(pl.multiple_of(i * bq, bq), bq)
    q2 = both_heads(q_ref[rows, :] * BF(0.125))
    grad = g_ref[rows, :]
    g2 = both_heads(grad)
    prod = grad.astype(F32) * o_ref[rows, :].astype(F32)
    left = first_half(prod.shape)
    delta = jnp.concatenate(
        [
            jnp.sum(jnp.where(left, prod, 0.0), axis=1, keepdims=True),
            jnp.sum(jnp.where(left, 0.0, prod), axis=1, keepdims=True),
        ],
        axis=0,
    )
    lse = lse_ref[pl.ds(pl.multiple_of(2 * i * bq, 2 * bq), 2 * bq), :]
    seg = query_seg(i)
    seg2 = jnp.concatenate([seg, seg], axis=0)

    def k_step(j, dq2):
        keys = pl.ds(pl.multiple_of(j * bk, bk), bk)
        key_rows = k_ref[keys, :]
        scores = dense_back(q2, key_rows)
        probs = jnp.exp(jnp.where(seg2 == key_seg(j), scores, -1e30) - lse)
        grad_prob = dense_back(g2, v_ref[keys, :])
        grad_score = (probs * (grad_prob - delta)).astype(BF)
        dv_sum[keys, :] += dense_in(probs.astype(BF), g2)
        dk_sum[keys, :] += dense_in(grad_score, q2)
        return dq2 + dense(grad_score, key_rows)

    dq2 = jnp.zeros((2 * bq, PAIR), F32)
    for first, last in ranges:
        dq2 = lax.fori_loop(first, last, k_step, dq2)
    return (0.125 * by_head(dq2)).astype(BF)


def attend_back_kernel(
    bq, bk, chunks, lo_ref, hi_ref, q_ref, k_ref, v_ref, sq_ref, sk_ref, o_ref, lse_ref, g_ref,
    dq_ref, dk_ref, dv_ref, dk_sum, dv_sum,
):
    nq = q_ref.shape[0] // bq
    per_chunk = k_ref.shape[0] // chunks // bk
    dk_sum[...] = jnp.zeros_like(dk_sum)
    dv_sum[...] = jnp.zeros_like(dv_sum)

    def q_step(i, carry):
        ranges = [(s * per_chunk + lo_ref[i, s], s * per_chunk + hi_ref[i, s]) for s in range(chunks)]
        dq_ref[pl.ds(pl.multiple_of(i * bq, bq), bq), :] = attend_back_rows(
            i, bq, bk, ranges, q_ref, k_ref, v_ref, lambda i: row_block(sq_ref, i, bq),
            lambda j: sk_ref[:, pl.ds(pl.multiple_of(j * bk, bk), bk)], o_ref, lse_ref, g_ref, dk_sum, dv_sum,
        )
        return carry

    lax.fori_loop(0, nq, q_step, 0)
    dk_ref[...] = dk_sum[...].astype(dk_ref.dtype)
    dv_ref[...] = dv_sum[...].astype(dv_ref.dtype)


SMEM = pl.BlockSpec(memory_space=pltpu.SMEM)
VMEM = pl.BlockSpec(memory_space=pltpu.VMEM)


def attend(bounds, q, k, v, seg_q, seg_k, chunks):
    n = q.shape[0]
    return pl.pallas_call(
        functools.partial(attend_kernel, BQ, BK, chunks),
        out_shape=(jax.ShapeDtypeStruct((n, PAIR), BF), jax.ShapeDtypeStruct((2 * n, 1), F32)),
        in_specs=[SMEM, SMEM] + [VMEM] * 5,
        out_specs=(VMEM, VMEM),
        compiler_params=pltpu.CompilerParams(vmem_limit_bytes=48 * 2**20),
    )(*bounds, q, k, v, seg_q, seg_k)


def attend_back(bounds, q, k, v, seg_q, seg_k, out, lse, grad, chunks):
    n, m = q.shape[0], k.shape[0]
    kept = BF if chunks == 1 else F32
    return pl.pallas_call(
        functools.partial(attend_back_kernel, BQ, BK, chunks),
        out_shape=(
            jax.ShapeDtypeStruct((n, PAIR), BF),
            jax.ShapeDtypeStruct((m, PAIR), kept),
            jax.ShapeDtypeStruct((m, PAIR), kept),
        ),
        in_specs=[SMEM, SMEM] + [VMEM] * 8,
        out_specs=(VMEM, VMEM, VMEM),
        scratch_shapes=[pltpu.VMEM((m, PAIR), F32), pltpu.VMEM((m, PAIR), F32)],
        compiler_params=pltpu.CompilerParams(vmem_limit_bytes=56 * 2**20),
    )(*bounds, q, k, v, seg_q, seg_k, out, lse, grad)


def mesh_id(ctx, f):
    return {"ctx": ctx, "fsdp": f}


def swapped(i):
    return i % 2 * 2 + i // 2


class Place:
    def __init__(self):
        self.ctx = lax.axis_index("ctx")
        self.f = lax.axis_index("fsdp")
        self.per_group = lax.axis_size("ctx") // 4
        self.g = self.ctx // self.per_group
        self.b = self.ctx % 2
        self.rest = self.ctx % self.per_group
        self.core = self.f % 2
        self.x = self.f // 2

    def at(self, g=None, b=None, f=None):
        ctx = self.ctx
        if g is not None:
            ctx = ctx + (g - self.g) * self.per_group
        if b is not None:
            ctx = ctx + (b - self.b)
        return mesh_id(ctx, self.f if f is None else f)

    def sibling(self):
        return self.at(f=self.f + 1 - 2 * self.core)

    def beside(self):
        return self.at(f=(self.f + 2) % 4)

    def across(self):
        return self.at(b=1 - self.b)

    def fsdp(self, k):
        return self.at(f=(self.f + k) % 4)

    def moved(self):
        return mesh_id(swapped(self.f) * self.per_group + self.rest, swapped(self.g))

    def stays(self):
        return swapped(self.f) == self.g


def remote(src, dst, send, recv, where):
    return pltpu.make_async_remote_copy(
        src_ref=src, dst_ref=dst, send_sem=send, recv_sem=recv,
        device_id=where, device_id_type=pl.DeviceIdType.MESH,
    )


def meet(me, targets, moves):
    barrier = pltpu.get_barrier_semaphore()
    for t in targets:
        pl.semaphore_signal(barrier, 1, device_id=t, device_id_type=pl.DeviceIdType.MESH)
    if not moves:
        pl.semaphore_wait(barrier, len(targets))
        return

    @pl.when(jnp.logical_not(me.stays()))
    def _():
        pl.semaphore_signal(barrier, 1, device_id=me.moved(), device_id_type=pl.DeviceIdType.MESH)

    pl.semaphore_wait(barrier, len(targets) + jnp.where(me.stays(), 0, 1))


class Flow:
    def __init__(self, me, own, buf, got, sent, came):
        self.me, self.own, self.buf, self.got, self.sent, self.came = me, own, buf, got, sent, came
        self.low = me.g < 2
        self.inner = jnp.where((me.g == 1) | (me.g == 2), 1, 0)
        step = jnp.where(self.low, 1, -1)
        self.ahead = me.at(g=me.g + step)
        self.back_to = me.at(g=me.g - step)

    def piece(self, i):
        return jnp.where(self.low, 3 - i, i)

    def copy(self, p, side, where):
        return remote(self.buf.at[p], self.got.at[side, p], self.sent.at[p], self.came.at[side, p], where)

    def forward(self, i):
        p = self.piece(i)

        @pl.when(self.inner == 0)
        def _():
            self.buf[p] = self.own(p, i).astype(BF)
            self.copy(p, 0, self.ahead).start()

        if i < 2:
            @pl.when(self.inner == 1)
            def _():
                self.copy(p, 0, self.back_to).wait_recv()
                self.buf[p] = (self.own(p, i) + self.got[0, p].astype(F32)).astype(BF)
                self.copy(p, 1, self.ahead).start()

    def back(self):
        p = self.piece(3)

        @pl.when(self.inner == 1)
        def _():
            self.copy(p, 1, self.ahead).wait_recv()
            self.buf[p] = (self.own(p, 3) + self.got[1, p].astype(F32)).astype(BF)
            self.copy(p, 1, self.back_to).start()

    def end(self):
        g = self.me.g

        @pl.when(self.inner == 0)
        def _():
            self.copy(g, 1, self.ahead).wait_recv()
            self.buf[g] = (self.own(g, 3) + self.got[1, g].astype(F32)).astype(BF)

        @pl.when(self.inner == 1)
        def _():
            self.copy(g, 0, self.back_to).wait_recv()
            self.copy(g, 1, self.ahead).wait_recv()
            self.buf[g] = (self.own(g, 3) + self.got[0, g].astype(F32) + self.got[1, g].astype(F32)).astype(BF)

        for p in range(4):
            @pl.when(g != p)
            def _():
                self.copy(p, 0, self.ahead).wait_send()


def tail_kernel(slots, *refs):
    if slots:
        q_ref, k_ref, v_ref, ends_ref, o_ref, lse_ref, grad_ref, x_ref = refs[:8]
        g3_ref, dk_sum, dv_sum = refs[-3:]
        query_seg, key_seg = segments_from(ends_ref, slots)
        attention = (
            q_ref, k_ref, v_ref, query_seg, lambda j: key_seg(j * BK, BK), o_ref, lse_ref, grad_ref,
        )
        tail_steps(attention, dk_sum, dv_sum, x_ref, g3_ref, *refs[8:-3])
    else:
        tail_steps(None, None, None, *refs)


def tail_steps(
    attention, dk_sum, dv_sum,
    x_ref, g3_ref, w3_ref, down_ref, rest_ref, up_ref, out_ref, mid_ref, vec_ref,
    down_out, up_out, o_out, three_out, dx_ref, sums_ref,
    dxp, dx1, t1, xa, yb, t2a, t2b, ra, rb, moved_buf,
    yr_down, yr_up, dbuf, dgot, ubuf, ugot,
    o_got, o_sum, yr_o, obuf, ogot,
    gq, qbuf, qgot, vs, vr,
    s_dx, r_dx, s_y, r_y, s_d, r_d, s_z, r_z, s_u, r_u, s_o, r_o, s_oz, r_oz, s_q, r_q,
    s_qf, r_qf, s_v, r_v, s_ag, r_ag, s_ay, r_ay, loc, x_rows,
):
    me = Place()
    g, b, f = me.g, me.b, me.f
    z_others = [me.at(g=(g + k) % 4) for k in (1, 2, 3)]
    meet(me, [me.across()] + [me.fsdp(k) for k in (1, 2, 3)] + z_others, True)

    rest = jnp.where(g < 2, 0, 2)

    def own_down(p, i):
        if i < 2:
            return down_ref[p].astype(F32)
        return down_ref[p].astype(F32) + yr_down[p - rest].astype(F32)

    def own_up(p, i):
        return up_ref[:, b, p].astype(F32) + yr_up[p].astype(F32)

    def own_q(p, i):
        return gq[:, :, p].astype(F32)

    def own_o(p, i):
        return o_sum[b, p].astype(F32) + yr_o[p].astype(F32)

    flow_d = Flow(me, own_down, dbuf, dgot, s_d, r_d)
    flow_u = Flow(me, own_up, ubuf, ugot, s_z, r_z)
    flow_q = Flow(me, own_q, qbuf, qgot, s_q, r_q)
    flow_o = Flow(me, own_o, obuf, ogot, s_oz, r_oz)

    edge, inner = flow_d.inner == 0, flow_d.inner == 1
    x_copy = pltpu.make_async_copy(x_ref, x_rows, loc.at[1])
    x_copy.start()

    def at(which, *steps):
        @pl.when(which)
        def _():
            for step in steps:
                step()

    y_copies = []
    for i in range(4):
        p = flow_u.piece(i)
        c = remote(up_ref.at[:, 1 - b, p], yr_up.at[p], s_y.at[0, i], r_y.at[0, i], me.across())
        c.start()
        y_copies.append(c)
    y_down = []
    for i in (2, 3):
        p = flow_d.piece(i) - rest
        c = remote(rest_ref.at[p], yr_down.at[p], s_y.at[1, i], r_y.at[1, i], me.across())
        c.start()
        y_down.append(c)

    o_copies = []
    for k in (1, 2, 3):
        c = remote(out_ref.at[(f + k) % 4], o_got.at[k - 1], s_o.at[k - 1], r_o.at[k - 1], me.fsdp(k))
        c.start()
        o_copies.append(c)
    c_oy = remote(o_sum.at[1 - b], yr_o, s_y.at[1, 0], r_y.at[1, 0], me.across())

    def up_forward(i):
        y_copies[i].wait()
        flow_u.forward(i)

    def up_back():
        y_copies[3].wait()
        flow_u.back()

    def output_rows():
        for c in o_copies:
            c.wait()
        o_sum[...] = (
            out_ref[f].astype(F32) + o_got[0].astype(F32) + o_got[1].astype(F32) + o_got[2].astype(F32)
        ).astype(BF)
        c_oy.start()

    do = functools.partial
    at(edge, do(flow_d.forward, 0), do(flow_d.forward, 1))

    def down_forward():
        y_down[0].wait()
        flow_d.forward(2)

    def down_back():
        for c in y_down:
            c.wait()
        flow_d.back()

    between = (
        ((edge, do(up_forward, 0)), (inner, do(flow_d.forward, 0))),
        ((True, output_rows), (edge, do(up_forward, 1)), (inner, do(flow_d.forward, 1), do(up_forward, 0))),
        ((edge, do(up_forward, 2), down_forward), (inner, do(up_forward, 1))),
        ((edge, y_down[1].wait, y_copies[3].wait), (inner, down_back, y_copies[2].wait, up_back)),
    )
    if attention is not None:
        dk_sum[...] = jnp.zeros_like(dk_sum)
        dv_sum[...] = jnp.zeros_like(dv_sum)
    per = 2048 // BQ // 4
    for quarter, (first, last) in enumerate(QUARTERS):
        ranges = [(first * 512 // BK, last * 512 // BK)]

        def rows_step(i, carry):
            g3_ref[pl.ds(pl.multiple_of(i * BQ, BQ), BQ), pl.ds(0, PAIR)] = attend_back_rows(
                i, BQ, BK, ranges, *attention, dk_sum, dv_sum
            )
            return carry

        if attention is not None:
            lax.fori_loop(quarter * per, (quarter + 1) * per, rows_step, 0)
        for which, *steps in between[quarter]:
            if which is True:
                for step in steps:
                    step()
            else:
                at(which, *steps)
    if attention is not None:
        g3_ref[:, pl.ds(PAIR, PAIR)] = dk_sum[...].astype(BF)
        g3_ref[:, pl.ds(2 * PAIR, PAIR)] = dv_sum[...].astype(BF)

    hops = [me.sibling(), me.beside(), me.across(), me.at(g=g + 1 - 2 * (g % 2)), me.at(g=(g + 2) % 4)]
    vs[0] = jnp.zeros((16, 1024), F32)
    vs[0, pl.ds(2, 3)] = vec_ref[pl.ds(0, 3), :]
    vs[0, pl.ds(5, 3)] = vec_ref[pl.ds(4, 3), :]
    vs[0, pl.ds(8 + f, 1)] = vec_ref[pl.ds(3, 1), :]
    here = pl.ds(pl.multiple_of((b * 4 + swapped(f)) * PAIR, PAIR), PAIR)
    sums3 = jnp.sum(g3_ref[...].astype(F32), axis=0, keepdims=True)
    vs[0, pl.ds(0, 1), here] = sums3[:, :PAIR]
    vs[0, pl.ds(1, 1), here] = sums3[:, 2 * PAIR :]

    def hop(i):
        if i > 0:
            hop_copy(i - 1).wait()
            vs[i] = vs[i - 1] + vr[i - 1]
        hop_copy(i).start()

    def hop_copy(i):
        return remote(vs.at[i], vr.at[i], s_v.at[i], r_v.at[i], hops[i])

    hop(0)

    def rows(size, q, other=False):
        half = 1 - b if other else b
        return pl.ds(pl.multiple_of((half * 4 + q) * size, size), size)

    def unit_cols(src):
        return pl.ds(pl.multiple_of(src * 1024, 1024), 1024)

    def head_cols(src):
        return pl.ds(pl.multiple_of((b * 4 + swapped(src)) * 128, 128), 128)

    def q_rows(q):
        return pl.ds(pl.multiple_of(q * 64, 64), 64)

    def pieces(kind, q, send, recv, where, other=False):
        half = 1 - b if other else b
        if kind == 0:
            parts = ((0, down_out.at[rows(128, q, other), :]),)
        elif kind == 1:
            parts = ((1, up_out.at[rows(32, q, other), :]),)
        else:
            parts = (
                (2, o_out.at[rows(32, q, other), :]),
                (3, three_out.at[:, q_rows(q), pl.ds(pl.multiple_of(half * 512, 512), 512)]),
            )
        return [remote(part, part, send.at[i, q], recv.at[i, q], where) for i, part in parts]

    def spread(kind, q, to_right, to_left):
        if to_right:
            @pl.when(g < 3)
            def _():
                for c in pieces(kind, q, s_ag.at[0], r_ag, me.at(g=g + 1)):
                    c.start()
        if to_left:
            @pl.when(g > 0)
            def _():
                for c in pieces(kind, q, s_ag.at[1], r_ag, me.at(g=g - 1)):
                    c.start()
        for c in pieces(kind, q, s_ay, r_ay, me.across()):
            c.start()

    def pass_on(kind, d):
        @pl.when(g >= d)
        def _():
            for c in pieces(kind, g - d, s_ag.at[0], r_ag, me.across()):
                c.wait_recv()
            spread(kind, g - d, True, False)

        @pl.when(g + d <= 3)
        def _():
            for c in pieces(kind, g + d, s_ag.at[1], r_ag, me.across()):
                c.wait_recv()
            spread(kind, g + d, False, True)

    flow_d.end()
    down_out[rows(128, g), :] = dbuf[g]
    spread(0, g, True, True)

    x_copy.wait()

    def q_step(i, carry):
        cols = pl.ds(pl.multiple_of(i * 256, 256), 256)
        part = dense_in(x_rows[:, cols], g3_ref[...]).astype(BF)
        for j in range(3):
            gq[i, j] = part[:, j * 128 : (j + 1) * 128].reshape(4, 64, 128)
        return carry

    lax.fori_loop(0, 4, q_step, 0)
    at(edge, *(do(flow_q.forward, i) for i in range(3)))

    def dx_step(i, carry):
        rows = pl.ds(pl.multiple_of(i * 256, 256), 256)
        part = dense_back(g3_ref[rows, :], w3_ref[...]).astype(BF)
        dxp[pl.ds(2 * i, 2)] = part.reshape(2, 2, 2, 2, 16, 1024)
        return carry

    lax.fori_loop(0, 8, dx_step, 0)
    c_core = remote(dxp.at[:, 1 - me.core], dx1, s_dx.at[0], r_dx.at[0], me.sibling())
    c_core.start()

    flow_u.end()
    up_out[rows(32, g), unit_cols(f)] = ubuf[g, f]
    u_out = []
    for k in (1, 2, 3):
        c = remote(ubuf.at[g, (f + k) % 4], up_out.at[rows(32, g), unit_cols(f)], s_u.at[k - 1], r_u.at[f], me.fsdp(k))
        c.start()
        u_out.append(c)

    at(inner, do(flow_q.forward, 0), do(flow_q.forward, 1))

    c_core.wait()

    def t1_step(i, carry):
        t1[i] = (dxp[i, me.core].astype(F32) + dx1[i].astype(F32)).astype(BF)
        return carry

    lax.fori_loop(0, 16, t1_step, 0)
    lo, hi = pl.ds(0, 8), pl.ds(8, 8)
    c_xa = remote(t1.at[lo, 1 - me.x], xa, s_dx.at[1], r_dx.at[1], me.beside())
    c_yb = remote(t1.at[hi, :, 1 - b], yb, s_dx.at[2], r_dx.at[2], me.across())
    c_xa.start()
    c_yb.start()
    for k in (1, 2, 3):
        src = (f + k) % 4
        remote(ubuf.at[g, 0], up_out.at[rows(32, g), unit_cols(src)], s_u.at[k - 1], r_u.at[src], me.fsdp(k)).wait_recv()
        u_out[k - 1].wait_send()
    spread(1, g, True, True)
    c_oy.wait()
    at(edge, *(do(flow_o.forward, i) for i in range(3)))
    pass_on(0, 1)
    at(inner, do(flow_o.forward, 0), do(flow_o.forward, 1))
    hop(1)

    flow_q.back()
    flow_o.back()
    pass_on(0, 2)

    flow_q.end()
    three_out[:, q_rows(g), head_cols(f)] = qbuf[g, f]
    q_out = []
    for k in (1, 2, 3):
        c = remote(qbuf.at[g, (f + k) % 4], three_out.at[:, q_rows(g), head_cols(f)], s_qf.at[k - 1], r_qf.at[f], me.fsdp(k))
        c.start()
        q_out.append(c)
    flow_o.end()
    o_out[rows(32, g), :] = obuf[g]
    c_xa.wait()
    t2a[...] = (t1[lo, me.x].astype(F32) + xa[...].astype(F32)).astype(BF)
    c_ra = remote(t2a.at[:, 1 - b], ra, s_dx.at[3], r_dx.at[3], me.across())
    c_ra.start()
    pass_on(1, 1)
    c_yb.wait()
    t2b[...] = (t1[hi, :, b].astype(F32) + yb[...].astype(F32)).astype(BF)
    c_rb = remote(t2b.at[:, 1 - me.x], rb, s_dx.at[4], r_dx.at[4], me.beside())
    c_rb.start()
    hop(2)
    for k in (1, 2, 3):
        src = (f + k) % 4
        remote(qbuf.at[g, 0], three_out.at[:, q_rows(g), head_cols(src)], s_qf.at[k - 1], r_qf.at[src], me.fsdp(k)).wait_recv()
        q_out[k - 1].wait_send()
    spread(2, g, True, True)
    pass_on(0, 3)
    pass_on(1, 2)
    c_ra.wait()
    c_rb.wait()
    moved_buf[lo] = (t2a[:, b].astype(F32) + ra[...].astype(F32) + mid_ref[lo]).astype(BF)
    moved_buf[hi] = (t2b[:, me.x].astype(F32) + rb[...].astype(F32) + mid_ref[hi]).astype(BF)

    @pl.when(me.stays())
    def _():
        c = pltpu.make_async_copy(moved_buf, dx_ref, loc.at[0])
        c.start()
        c.wait()

    @pl.when(jnp.logical_not(me.stays()))
    def _():
        remote(moved_buf, dx_ref, s_dx.at[5], r_dx.at[5], me.moved()).start()

    hop(3)
    pass_on(2, 1)
    pass_on(1, 3)
    hop(4)
    pass_on(2, 2)
    pass_on(2, 3)
    hop_copy(4).wait()
    sums_ref[...] = vs[4] + vr[4]

    @pl.when(jnp.logical_not(me.stays()))
    def _():
        remote(moved_buf, dx_ref, s_dx.at[5], r_dx.at[5], me.moved()).wait()

    for kind in (0, 1, 2):
        for q in range(4):
            for c in pieces(kind, q, s_ay, r_ay, me.across()):
                c.wait_send()

            @pl.when((g >= q) & (g < 3))
            def _():
                for c in pieces(kind, q, s_ag.at[0], r_ag, me.across()):
                    c.wait_send()

            @pl.when((g <= q) & (g > 0))
            def _():
                for c in pieces(kind, q, s_ag.at[1], r_ag, me.across()):
                    c.wait_send()

            for c in pieces(kind, q, s_ay, r_ay, me.across(), other=True):
                c.wait_recv()


def tail(slots, attention, x_all, g3, w3, down, rest, up, out, mid, vec):
    dma = pltpu.SemaphoreType.DMA
    v = pltpu.VMEM
    scratch = [
        v((16, 2, 2, 2, 16, 1024), BF), v((16, 2, 2, 16, 1024), BF), v((16, 2, 2, 16, 1024), BF),
        v((8, 2, 16, 1024), BF), v((8, 2, 16, 1024), BF), v((8, 2, 16, 1024), BF), v((8, 2, 16, 1024), BF),
        v((8, 16, 1024), BF), v((8, 16, 1024), BF), v((16, 16, 1024), BF),
        v((2, 128, 1024), BF), v((4, 4, 32, 1024), BF), v((4, 128, 1024), BF), v((2, 4, 128, 1024), BF),
        v((4, 4, 32, 1024), BF), v((2, 4, 4, 32, 1024), BF),
        v((3, 2, 4, 32, 1024), BF), v((2, 4, 32, 1024), BF), v((4, 32, 1024), BF),
        v((4, 32, 1024), BF), v((2, 4, 32, 1024), BF),
        v((4, 3, 4, 64, 128), BF), v((4, 4, 3, 64, 128), BF), v((2, 4, 4, 3, 64, 128), BF),
        v((5, 16, 1024), F32), v((5, 16, 1024), F32),
        dma((6,)), dma((6,)), dma((2, 5)), dma((2, 5)), dma((4,)), dma((2, 4)), dma((4,)), dma((2, 4)),
        dma((3,)), dma((4,)), dma((3,)), dma((3,)), dma((4,)), dma((2, 4)), dma((4,)), dma((2, 4)),
        dma((3,)), dma((4,)), dma((5,)), dma((5,)), dma((2, 4, 4)), dma((4, 4)), dma((4, 4)), dma((4, 4)), dma((2,)),
        v((2048, 1024), BF),
    ]
    if slots:
        scratch += [v((2048, 3 * PAIR), BF), v((2048, PAIR), F32), v((2048, PAIR), F32)]
        operands = (*attention, x_all)
    else:
        operands = (x_all, g3)
    operands += (
        w3, down.reshape(4, 128, 1024), rest.reshape(2, 128, 1024), up.reshape(4, 2, 4, 32, 1024), out.reshape(4, 2, 4, 32, 1024),
        mid.reshape(16, 16, 1024), vec,
    )
    return pl.pallas_call(
        functools.partial(tail_kernel, slots),
        out_shape=(
            jax.ShapeDtypeStruct((1024, 1024), BF),
            jax.ShapeDtypeStruct((256, 4096), BF),
            jax.ShapeDtypeStruct((256, 1024), BF),
            jax.ShapeDtypeStruct((3, 256, 1024), BF),
            jax.ShapeDtypeStruct((16, 16, 1024), BF),
            jax.ShapeDtypeStruct((16, 1024), F32),
        ),
        in_specs=[pl.BlockSpec(memory_space=pl.ANY) if ref is x_all else VMEM for ref in operands],
        out_specs=(VMEM,) * 6,
        scratch_shapes=scratch,
        compiler_params=pltpu.CompilerParams(collective_id=1, has_side_effects=True, vmem_limit_bytes=60 * 2**20),
        cost_estimate=pl.CostEstimate(flops=4 * 10**9, bytes_accessed=40 * 2**20, transcendentals=0),
    )(*operands)


def tile_cols(i, size):
    return pl.ds(pl.multiple_of(i * size, size), size)


def middle_kernel(
    heads_ref, x_in, cot_ref, wo_ref, wu_in, wd_ref, *refs,
):
    middle_steps(heads_ref, x_in, cot_ref, wo_ref, wu_in, wd_ref, refs[:6], *refs[6:])


def middle_steps(
    heads_ref, x_in, cot_ref, wo_ref, wu_in, wd_ref, rows_ref, eb_ref,
    layer_ref, down_out, rest_out, upg_out, og_out, gatt_ref, mid1_ref, vec_ref,
    att, nl, gff, slope, hid, gpre, normed, xhat, rstd, work, moved_buf, gbr, gas, ps, pr, down, down_y, wu_ref, up_ref, x_ref,
    s_a, r_a, s_b, r_b, s_g, r_g, s_p, r_p, s_m, r_m, s_y, r_y, loc, s_u, r_u, s_l,
):
    me = Place()
    f, b = me.f, me.b
    sib = f + 1 - 2 * me.core
    xs = (f + 2) % 4
    xo = xs + 1 - 2 * me.core
    peers = [me.at(f=(f + k % 4) % 4, b=(b + k // 4) % 2) for k in range(1, 8)]
    meet(me, peers, True)
    slot = swapped(f) * 2 + b
    unit = b * 4 + swapped(f)

    def peer_slot(k, sign):
        pf, pb = (f + sign * (k % 4) + 4) % 4, (b + k // 4) % 2
        return swapped(pf) * 2 + pb, pb * 4 + swapped(pf)

    def lanes(index):
        return pl.ds(pl.multiple_of(index * PAIR, PAIR), PAIR)

    for k in range(1, 8):
        where, _ = peer_slot(k, 1)
        remote(heads_ref.at[:, where], att.at[:, :, lanes(unit)], s_a.at[k - 1], r_a.at[k - 1], peers[k - 1]).start()
    att[:, :, lanes(unit)] = heads_ref[:, slot]

    def unit_rows(src, half):
        return pl.ds(pl.multiple_of(src * 256 + half * 128, 128), 128)

    u_out = [
        remote(wu_in.at[unit_rows(src, b)], wu_ref.at[unit_rows(src, b)], s_u.at[i], r_u.at[i], me.across())
        for i, src in enumerate((xs, xo))
    ]
    for c in u_out:
        c.start()
    cot_there = remote(cot_ref, up_ref, s_m.at[1], r_m.at[1], me.moved())
    cot_here = pltpu.make_async_copy(cot_ref, up_ref, loc.at[1])

    @pl.when(me.stays())
    def _():
        cot_here.start()

    @pl.when(jnp.logical_not(me.stays()))
    def _():
        cot_there.start()

    kept = [unit_rows(f, 0), unit_rows(f, 1), unit_rows(sib, 0), unit_rows(sib, 1), unit_rows(xs, b), unit_rows(xo, b)]
    u_kept = [pltpu.make_async_copy(wu_in.at[rows], wu_ref.at[rows], s_l.at[i]) for i, rows in enumerate(kept)]
    x_copy = pltpu.make_async_copy(x_in.at[:, slot], x_ref, s_l.at[6])
    for c in u_kept + [x_copy]:
        c.start()
    for k in range(1, 8):
        _, theirs = peer_slot(k, -1)
        remote(heads_ref.at[:, slot], att.at[:, :, lanes(theirs)], s_a.at[k - 1], r_a.at[k - 1], peers[k - 1]).wait()

    def row(i):
        return rows_ref[i][...]

    def att_rows():
        return att[...].reshape(256, 1024)

    def proj(i, carry):
        cols = tile_cols(i, 512)
        work[:, cols] = dense(att_rows(), wo_ref[:, cols])
        return carry

    lax.fori_loop(0, 2, proj, 0)
    x_copy.wait()
    value, x_hat, inv = norm_fwd(x_ref[...].reshape(256, 1024).astype(F32) + work[...] + row(0), row(1), row(2))
    normed[...] = value
    xhat[...] = x_hat
    rstd[...] = inv
    nl[f] = value.astype(BF)

    whole, halves = pl.ds(0, 256), (pl.ds(0, 128), pl.ds(128, 128))

    def passed(buf, t, i, src, rows, where):
        return remote(buf.at[src, rows], buf.at[src, rows], s_g.at[t, i], r_g.at[t, i], where)

    def scatter(t, i, part, rows, where):
        return remote(ps.at[t, part, rows], pr.at[t, part, rows], s_p.at[t, i], r_p.at[t, i], where)

    def run(t, block, buf, beside_x):
        for i, rows in enumerate(halves):
            passed(buf, t, 1 + i, f, rows, me.beside()).start()
        passed(buf, t, 0, f, whole, me.sibling()).start()
        block(f, 3, whole)
        passed(buf, t, 0, f, whole, me.sibling()).wait_send()
        passed(buf, t, 0, sib, whole, me.sibling()).wait_recv()
        block(sib, 0, whole)
        scatter(t, 0, 0, whole, me.sibling()).start()

        def from_x(i):
            passed(buf, t, 1 + i, f, halves[i], me.beside()).wait_send()
            passed(buf, t, 1 + i, xs, halves[i], me.beside()).wait_recv()
            passed(buf, t, 3 + i, xs, halves[i], me.sibling()).start()

        def from_other(i):
            passed(buf, t, 3 + i, xs, halves[i], me.sibling()).wait_send()
            passed(buf, t, 3 + i, xo, halves[i], me.sibling()).wait_recv()

        def chip_sum(i):
            rows = halves[i]
            scatter(t, 1 + i, 1, rows, me.sibling()).wait()
            ps[t, 2, rows] = (ps[t, 2, rows].astype(F32) + pr[t, 1, rows].astype(F32)).astype(BF)
            scatter(t, 3 + i, 2, rows, me.beside()).start()

        from_x(0)
        block(xs, 2, halves[0])
        from_other(0)
        block(xo, 1, halves[0])
        scatter(t, 1, 1, halves[0], me.sibling()).start()
        from_x(1)
        chip_sum(0)
        block(xs, 2, halves[1])
        from_other(1)
        block(xo, 1, halves[1])
        scatter(t, 2, 1, halves[1], me.sibling()).start()
        chip_sum(1)
        beside_x()
        scatter(t, 0, 0, whole, me.sibling()).wait()
        for i, rows in enumerate(halves):
            scatter(t, 3 + i, 2, rows, me.beside()).wait()
        return ps[t, 3].astype(F32) + pr[t, 0].astype(F32) + pr[t, 2].astype(F32)

    def forward(index, into, rows):
        def up_tile(i, carry):
            cols = tile_cols(i, 256)
            pre = dense(nl[index, rows], wu_ref[:, cols]) + eb_ref[:, pl.ds(pl.multiple_of(f * 1024 + i * 256, 256), 256)]
            cdf = 0.5 * (1.0 + lax.erf(pre * 0.7071067811865476))
            hid[index, rows, cols] = (pre * cdf).astype(BF)
            slope[index, rows, cols] = cdf + pre * jnp.exp(-0.5 * pre * pre) * 0.3989422804014327
            return carry

        def down_tile(i, carry):
            cols = tile_cols(i, 512)
            ps[0, into, rows, cols] = dense(hid[index, rows], wd_ref[:, cols]).astype(BF)
            return carry

        lax.fori_loop(0, 4, up_tile, 0)
        lax.fori_loop(0, 2, down_tile, 0)

    for c in u_out + u_kept:
        c.wait()
    ffn = run(0, forward, nl, lambda: None)

    @pl.when(me.stays())
    def _():
        cot_here.wait()

    @pl.when(jnp.logical_not(me.stays()))
    def _():
        cot_there.wait()

    value, x_hat, inv = norm_fwd(normed[...] + ffn + row(3), row(4), row(5))
    moved_buf[...] = value.astype(BF)

    @pl.when(me.stays())
    def _():
        pltpu.make_async_copy(moved_buf, layer_ref, loc.at[0]).start()

    @pl.when(jnp.logical_not(me.stays()))
    def _():
        remote(moved_buf, layer_ref, s_m.at[0], r_m.at[0], me.moved()).start()

    grad2, gain2, shift2 = norm_back(up_ref[...].astype(F32), x_hat, inv, row(4))
    work[...] = grad2
    low2 = grad2.astype(BF)
    gff[f] = low2
    vec_ref[pl.ds(4, 1), :] = jnp.sum(low2.astype(F32), axis=0, keepdims=True)
    vec_ref[pl.ds(5, 1), :] = gain2[None]
    vec_ref[pl.ds(6, 1), :] = shift2[None]

    def backward(index, into, rows):
        def pre_tile(i, carry):
            cols = tile_cols(i, 512)
            part = dense_back(gff[index, rows], wd_ref[cols, :])
            gpre[index, rows, cols] = (part * slope[index, rows, cols]).astype(BF)
            return carry

        def in_tile(i, carry):
            cols = tile_cols(i, 512)
            ps[1, into, rows, cols] = dense_back(gpre[index, rows], wu_ref[cols, :]).astype(BF)
            return carry

        lax.fori_loop(0, 2, pre_tile, 0)
        lax.fori_loop(0, 2, in_tile, 0)

    first = pl.ds(pl.multiple_of(jnp.where(me.g < 2, 256, 0), 256), 256)
    later = pl.ds(pl.multiple_of(jnp.where(me.g < 2, 0, 256), 256), 256)
    c_down = remote(down.at[1 - b, first], down_y, s_y.at[0], r_y.at[0], me.across())

    def weight_grads():
        def down_tile(i, carry):
            cols = tile_cols(i, 256)
            part = dense_in(hid[:, :, cols].reshape(1024, 256), gff[...].reshape(1024, 1024)).astype(BF)
            down[i // 2, pl.ds(pl.multiple_of(i % 2 * 256, 256), 256)] = part
            return carry

        def up_tile(i, carry):
            cols = tile_cols(i, 256)
            upg_out[cols, :] = dense_in(nl[:, :, cols].reshape(1024, 256), gpre[...].reshape(1024, 1024)).astype(BF)
            return carry

        lax.fori_loop(0, 4, down_tile, 0)
        c_down.start()
        lax.fori_loop(0, 4, up_tile, 0)
        vec_ref[pl.ds(3, 1), :] = jnp.sum(gpre[...].reshape(1024, 1024).astype(F32), axis=0, keepdims=True)

    back = run(1, backward, gff, weight_grads)
    grad1, gain1, shift1 = norm_back(back + work[...], xhat[...], rstd[...], row(1))
    mid1_ref[...] = grad1
    low1 = grad1.astype(BF)
    gbr[...] = low1
    vec_ref[pl.ds(0, 1), :] = jnp.sum(low1.astype(F32), axis=0, keepdims=True)
    vec_ref[pl.ds(1, 1), :] = gain1[None]
    vec_ref[pl.ds(2, 1), :] = shift1[None]
    vec_ref[pl.ds(7, 1), :] = jnp.zeros((1, 1024), F32)

    def att_tile(i, carry):
        part = dense_back(gbr[...], wo_ref[tile_cols(i, 256), :]).astype(BF)
        for j in range(2):
            gas[2 * i + j] = part[:, j * PAIR : (j + 1) * PAIR].reshape(16, 16, PAIR)
        return carry

    lax.fori_loop(0, 4, att_tile, 0)
    for k in range(1, 8):
        _, theirs = peer_slot(k, 1)
        remote(gas.at[theirs], gatt_ref.at[:, slot], s_b.at[k - 1], r_b.at[k - 1], peers[k - 1]).start()
    gatt_ref[:, slot] = gas[unit]

    def o_tile(i, carry):
        cols = tile_cols(i, 256)
        og_out[cols, :] = dense_in(att[:, :, cols].reshape(256, 256), gbr[...]).astype(BF)
        return carry

    lax.fori_loop(0, 4, o_tile, 0)
    for k in range(1, 8):
        where, _ = peer_slot(k, -1)
        remote(gas.at[0], gatt_ref.at[:, where], s_b.at[k - 1], r_b.at[k - 1], peers[k - 1]).wait()
    c_down.wait()
    down_out[first, :] = (down[b, first].astype(F32) + down_y[...].astype(F32)).astype(BF)
    down_out[later, :] = down[b, later]
    rest_out[...] = down[1 - b, later]

    @pl.when(me.stays())
    def _():
        pltpu.make_async_copy(moved_buf, layer_ref, loc.at[0]).wait()

    @pl.when(jnp.logical_not(me.stays()))
    def _():
        remote(moved_buf, layer_ref, s_m.at[0], r_m.at[0], me.moved()).wait()


def middle(heads, x, upstream, w_output, w_up, w_down, params):
    dma = pltpu.SemaphoreType.DMA
    v = pltpu.VMEM
    block = (4, 256, 1024)
    scratch = [
        v((16, 16, 1024), BF), v(block, BF), v(block, BF), v(block, F32), v(block, BF), v(block, BF),
        v((256, 1024), F32), v((256, 1024), F32), v((256, 1), F32), v((256, 1024), F32), v((256, 1024), BF),
        v((256, 1024), BF), v((8, 16, 16, PAIR), BF), v((2, 4, 256, 1024), BF), v((2, 3, 256, 1024), BF),
        v((2, 512, 1024), BF), v((256, 1024), BF), v((1024, 1024), BF), v((256, 1024), BF),
        v((16, 16, 1024), BF),
        dma((7,)), dma((7,)), dma((7,)), dma((7,)), dma((2, 5)), dma((2, 5)), dma((2, 5)), dma((2, 5)),
        dma((2,)), dma((2,)), dma((1,)), dma((1,)), dma((2,)), dma((2,)), dma((2,)), dma((7,)),
    ]
    hbm = pl.BlockSpec(memory_space=pl.ANY)
    square = jax.ShapeDtypeStruct((1024, 1024), BF)
    return pl.pallas_call(
        middle_kernel,
        out_shape=(
            jax.ShapeDtypeStruct((256, 1024), BF), jax.ShapeDtypeStruct((512, 1024), BF),
            jax.ShapeDtypeStruct((256, 1024), BF), square, square,
            jax.ShapeDtypeStruct((16, 8, 16, PAIR), BF),
            jax.ShapeDtypeStruct((256, 1024), F32),
            jax.ShapeDtypeStruct((8, 1024), F32),
        ),
        in_specs=[VMEM, hbm, hbm, VMEM, hbm, VMEM] + [VMEM] * len(params),
        out_specs=(VMEM,) * 8,
        scratch_shapes=scratch,
        compiler_params=pltpu.CompilerParams(collective_id=2, has_side_effects=True, vmem_limit_bytes=60 * 2**20),
        cost_estimate=pl.CostEstimate(flops=14 * 10**9, bytes_accessed=20 * 2**20, transcendentals=2**21),
    )(heads.reshape(16, 8, 16, PAIR), x, upstream, w_output, w_up, w_down, *params)


def start_kernel(
    slots, tok_ref, ends_ref, qw_ref, kw_ref, vw_ref, ow_ref, ew_ref, qb_ref, vb_ref,
    x_ref, ends_out, q_ref, k_ref, v_ref, w3_ref, wo_ref, wu_ref, att_ref, lse_ref,
    s_m, r_m, s_w, r_w, s_u, r_u, s_o, r_o, s_x, r_x, loc,
):
    me = Place()
    g, b, f = me.g, me.b, me.f
    sib = f + 1 - 2 * me.core
    xs = (f + 2) % 4
    xo = xs + 1 - 2 * me.core
    meet(me, [me.across()] + [me.fsdp(k) for k in (1, 2, 3)], True)
    slot = me.core * 4 + me.x * 2 + b
    slot_x = me.core * 4 + (1 - me.x) * 2 + b
    slot_y = slot + 1 - 2 * b
    slot_d = slot_x + 1 - 2 * b
    other = 4 - 8 * me.core
    lo, hi = pl.ds(0, 8), pl.ds(8, 8)

    def moves(i, src, dst):
        return remote(src, dst, s_m.at[i], r_m.at[i], me.moved())

    def relocate(i, src, dst):
        @pl.when(me.stays())
        def _():
            pltpu.make_async_copy(src, dst, loc.at[i]).start()

        @pl.when(jnp.logical_not(me.stays()))
        def _():
            moves(i, src, dst).start()

    def relocated(i, src, dst):
        @pl.when(me.stays())
        def _():
            pltpu.make_async_copy(src, dst, loc.at[i]).wait()

        @pl.when(jnp.logical_not(me.stays()))
        def _():
            moves(i, src, dst).wait()

    theirs = x_ref.at[:, g * 2 + b]
    relocate(0, tok_ref, theirs)
    relocate(1, ends_ref, ends_out)

    def cols(index, size):
        return pl.ds(pl.multiple_of(index * size, size), size)

    def w3_rows(src):
        return cols(src, 256)

    def wo_rows(src, which):
        return pl.ds(pl.multiple_of(src * 256 + which * 128, 128), 128)

    half = cols(b, 128)
    u_x = [
        remote(ew_ref.at[half, cols(xs, 1024)], wu_ref.at[wo_rows(f, b)], s_u.at[1], r_u.at[1], me.beside()),
        remote(ew_ref.at[half, cols(xo, 1024)], wu_ref.at[wo_rows(f, b)], s_u.at[2], r_u.at[2], me.at(f=xo)),
    ]
    o_x = remote(ow_ref.at[half], wo_ref.at[wo_rows(f, b)], s_o.at[1], r_o.at[1], me.beside())
    u_sib = remote(ew_ref.at[:, cols(sib, 1024)], wu_ref.at[w3_rows(f)], s_u.at[0], r_u.at[0], me.sibling())
    o_sib = remote(ow_ref, wo_ref.at[w3_rows(f)], s_o.at[0], r_o.at[0], me.sibling())
    for c in (o_x, u_sib, o_sib):
        c.start()
    o_own = pltpu.make_async_copy(ow_ref, wo_ref.at[w3_rows(f)], loc.at[5])
    u_own = pltpu.make_async_copy(ew_ref.at[:, cols(f, 1024)], wu_ref.at[w3_rows(f)], loc.at[6])
    o_own.start()
    u_own.start()
    weights = (qw_ref, kw_ref, vw_ref)

    def w3_own(j):
        return pltpu.make_async_copy(
            weights[j].at[:, cols(b * 4 + swapped(f), 128)], w3_ref.at[w3_rows(f), pl.ds(128 * j, 128)], loc.at[2 + j]
        )

    for j in range(3):
        w3_own(j).start()
    for k in (2, 3, 1):
        dest = b * 4 + swapped((f + k) % 4)
        for j in range(3):
            remote(
                weights[j].at[:, cols(dest, 128)], w3_ref.at[w3_rows(f), pl.ds(128 * j, 128)],
                s_w.at[j, k - 1], r_w.at[j, k - 1], me.fsdp(k),
            ).start()

    def piece(i, ref, where):
        return remote(ref, ref, s_x.at[i], r_x.at[i], where)

    relocated(0, tok_ref, theirs)
    own = x_ref.at[:, slot]
    sends = [piece(1, own, me.beside()), piece(2, own, me.across()), piece(0, own, me.sibling())]
    for c in sends:
        c.start()

    here = cols(b * 4 + swapped(f), PAIR)
    bias = jnp.concatenate([qb_ref[:, here], jnp.zeros((1, PAIR), F32), vb_ref[:, here]], axis=1)

    def project(which):
        part = dense(x_ref[:, which].reshape(256, 1024), w3_ref[...]) + bias
        part = part.astype(BF).reshape(16, 16, 3 * PAIR)
        q_ref[:, which] = part[:, :, :PAIR]
        k_ref[:, which] = part[:, :, PAIR : 2 * PAIR]
        v_ref[:, which] = part[:, :, 2 * PAIR :]

    piece(1, x_ref.at[:, slot_x], me.beside()).wait_recv()
    more = [piece(4, x_ref.at[hi, slot_x], me.across()), piece(3, x_ref.at[:, slot_x], me.sibling())]
    for c in more:
        c.start()
    sends += more
    piece(2, x_ref.at[:, slot_y], me.across()).wait_recv()
    more = [piece(6, x_ref.at[lo, slot_y], me.beside()), piece(5, x_ref.at[:, slot_y], me.sibling())]
    for c in more:
        c.start()
    sends += more
    for c in u_x:
        c.start()
    o_x.wait()
    o_fwd = [
        remote(wo_ref.at[wo_rows(xs, b)], wo_ref.at[wo_rows(xs, b)], s_o.at[2], r_o.at[2], me.sibling()),
        remote(wo_ref.at[wo_rows(xs, b)], wo_ref.at[wo_rows(xs, b)], s_o.at[3], r_o.at[3], me.across()),
    ]
    for c in o_fwd:
        c.start()
    for k in (1, 2, 3):
        src = (f + 4 - k) % 4
        for j in range(3):
            remote(
                weights[j].at[:, cols(0, 128)], w3_ref.at[w3_rows(src), pl.ds(128 * j, 128)],
                s_w.at[j, k - 1], r_w.at[j, k - 1], me.fsdp(k),
            ).wait()
    for j in range(3):
        w3_own(j).wait()
    project(slot)
    project(slot_x)
    piece(4, x_ref.at[hi, slot_d], me.across()).wait_recv()
    more = [piece(8, x_ref.at[hi, slot_d], me.sibling())]
    more[0].start()
    piece(6, x_ref.at[lo, slot_d], me.beside()).wait_recv()
    more.append(piece(7, x_ref.at[lo, slot_d], me.sibling()))
    more[1].start()
    sends += more
    project(slot_y)
    for i, part in ((0, slot + other), (3, slot_x + other), (5, slot_y + other)):
        piece(i, x_ref.at[:, part], me.sibling()).wait_recv()
        project(part)
    project(slot_d)
    piece(8, x_ref.at[hi, slot_d + other], me.sibling()).wait_recv()
    piece(7, x_ref.at[lo, slot_d + other], me.sibling()).wait_recv()
    project(slot_d + other)
    for c in sends:
        c.wait_send()
    relocated(1, ends_ref, ends_out)

    segments = segments_from(ends_out, slots)

    def attend_quarter(quarter):
        first, last = QUARTERS[quarter]

        rows, lse = attend_wide(quarter, WIDE, first * 512, (last - first) * 512, q_ref, k_ref, v_ref, *segments)
        att_ref[pl.ds(quarter * 4, 4)] = rows.astype(BF).reshape(4, GROUP, 16, PAIR)
        for part in range(WIDE // BQ):
            for head in range(2):
                to = 2 * (quarter * WIDE + part * BQ) + head * BQ
                lse_ref[pl.ds(to, BQ), :] = lse[head * WIDE + part * BQ : head * WIDE + (part + 1) * BQ]

    if slots:
        attend_quarter(0)
    if slots:
        attend_quarter(1)
        attend_quarter(2)
    o_fwd[0].wait()
    o_fwd[1].wait()
    late = remote(wo_ref.at[wo_rows(xs, 1 - b)], wo_ref.at[wo_rows(xs, 1 - b)], s_o.at[4], r_o.at[4], me.sibling())
    late.start()
    if slots:
        attend_quarter(3)
    late.wait()
    o_own.wait()
    o_sib.wait()
    u_own.wait()
    u_sib.wait()
    for c in u_x:
        c.wait()


def start(slots, tokens, ends, query_w, key_w, value_w, output_w, expand_w, query_b, value_b):
    dma = pltpu.SemaphoreType.DMA
    hbm = pl.BlockSpec(memory_space=pl.ANY)
    heads = jax.ShapeDtypeStruct((16, GROUP, 16, PAIR), BF)
    square = jax.ShapeDtypeStruct((1024, 1024), BF)
    return pl.pallas_call(
        functools.partial(start_kernel, slots),
        out_shape=(
            jax.ShapeDtypeStruct((16, GROUP, 16, 1024), BF), jax.ShapeDtypeStruct((8, 128), jnp.int32), heads, heads, heads,
            jax.ShapeDtypeStruct((1024, 3 * PAIR), BF), square, square,
            heads, jax.ShapeDtypeStruct((4096, 1), F32),
        ),
        in_specs=[hbm, VMEM] + [hbm] * 5 + [VMEM, VMEM],
        out_specs=(VMEM, VMEM, VMEM, VMEM, VMEM, VMEM, hbm, hbm, VMEM, VMEM),
        scratch_shapes=[
            dma((2,)), dma((2,)), dma((3, 3)), dma((3, 3)), dma((3,)), dma((3,)), dma((5,)), dma((5,)),
            dma((9,)), dma((9,)), dma((7,)),
        ],
        compiler_params=pltpu.CompilerParams(collective_id=3, has_side_effects=True, vmem_limit_bytes=60 * 2**20),
        cost_estimate=pl.CostEstimate(flops=2 * 10**9, bytes_accessed=20 * 2**20, transcendentals=0),
    )(tokens, ends, query_w, key_w, value_w, output_w, expand_w, query_b[None], value_b[None])


def body(
    tokens, lengths, packing, query_w, query_b, key_w, value_w, value_b, output_w, output_b,
    attn_gain, attn_shift, expand_w, expand_b, reduce_w, reduce_b, ffn_gain, ffn_shift, cotangent,
):
    tok_shape = tokens.shape
    laps, stripe, width = tok_shape[1], tok_shape[2], tok_shape[3]
    mine = laps * stripe
    n_ctx = lax.axis_size("ctx")
    n_f = lax.axis_size("fsdp")
    per_group = n_ctx // n_f
    chunks = per_group // 2
    ctx = lax.axis_index("ctx")
    f = lax.axis_index("fsdp")
    g = ctx // per_group
    chunk = ctx % per_group // 2
    b = ctx % 2
    same_place = [
        [(gg * chunks + s) * 2 + bb for s in range(chunks)] for gg in range(n_f) for bb in range(2)
    ]
    units = expand_w.shape[1] // n_f

    ordered = jnp.sum(
        jnp.where(
            packing[0][:, None] == jnp.arange(lengths.shape[1], dtype=jnp.int32)[None, :],
            lengths[0][None, :],
            0,
        ),
        axis=1,
    )
    slots = jnp.arange(ordered.shape[0], dtype=jnp.int32)
    own_ends = jnp.sum(jnp.where(slots[None, :] <= slots[:, None], ordered[None, :], 0), axis=1)
    own_ends = jnp.pad(own_ends[None], ((0, 7), (0, 128 - own_ends.shape[0])))

    acts = (laps, stripe, width)
    n_slots = lengths.shape[1] if chunks == 1 else 0
    x_all, ends, q, k_own, v_own, w_three, w_output, w_up, att_heads, lse = start(
        n_slots, tokens.reshape(acts), own_ends, query_w, key_w, value_w, output_w, expand_w, query_b, value_b
    )
    q, k_own, v_own = (part.reshape(GROUP * mine, PAIR) for part in (q, k_own, v_own))
    x_slots = x_all
    x_all = x_all.reshape(GROUP * mine, width)
    upstream = cotangent.reshape(mine, width)
    slot_ends = ends[0, : ordered.shape[0]]

    span = GROUP * mine
    index = jnp.arange(span, dtype=jnp.int32)

    def segments(which):
        lap, rest = index // (GROUP * stripe), index % (GROUP * stripe)
        unit, place = rest // stripe, rest % stripe
        owner = unit // 2 * per_group + which * 2 + unit % 2
        position = lap * (n_ctx * stripe) + owner * stripe + place
        return jnp.sum((position[:, None] >= slot_ends[None, :]).astype(jnp.int32), axis=1)

    attention = (q, k_own, v_own, ends, att_heads.reshape(span, PAIR), lse)
    if chunks > 1:
        seg_q = segments(chunk)
        seg_k = jnp.concatenate([segments(s) for s in range(chunks)])
        q_first, q_last = seg_q[::BQ], seg_q[BQ - 1 :: BQ]
        k_first = seg_k[::BK].reshape(chunks, -1)
        k_last = seg_k[BK - 1 :: BK].reshape(chunks, -1)
        lo = jnp.sum((k_last[None] < q_first[:, None, None]).astype(jnp.int32), axis=2)
        hi = jnp.sum((k_first[None] <= q_last[:, None, None]).astype(jnp.int32), axis=2)
        bounds = (lo, hi)
        k = lax.all_gather(k_own, "ctx", axis_index_groups=same_place, tiled=True)
        v = lax.all_gather(v_own, "ctx", axis_index_groups=same_place, tiled=True)
        keyed = (q, k, v, seg_q[:, None], seg_k[None, :])
        att_heads, lse = attend(bounds, *keyed, chunks)

    params = [p[None] for p in (output_b, attn_gain, attn_shift, reduce_b, ffn_gain, ffn_shift, expand_b)]
    layer_out, part_down, rest_down, part_up, part_out, grad_att, grad_mid1, vec = middle(
        att_heads, x_slots, upstream, w_output, w_up, reduce_w, params
    )
    layer_out = layer_out.reshape(tok_shape)
    grad_att = grad_att.reshape(GROUP * mine, PAIR)

    attention += (grad_att,)
    grad_three = None
    if chunks > 1:
        grad_q, grad_k, grad_v = attend_back(bounds, *keyed, att_heads, lse, grad_att, chunks)
        attention = None
        grad_k = lax.psum_scatter(
            grad_k.astype(BF), "ctx", axis_index_groups=same_place, tiled=True
        )
        grad_v = lax.psum_scatter(
            grad_v.astype(BF), "ctx", axis_index_groups=same_place, tiled=True
        )
        grad_three = jnp.concatenate([grad_q, grad_k, grad_v], axis=1)
    share_down, share_up, share_out, share_three, moved, sums = tail(
        n_slots, attention, x_all, grad_three, w_three, part_down, rest_down, part_up, part_out, grad_mid1, vec
    )
    grad_inputs = moved.reshape(tok_shape).astype(F32)
    shares = tuple(part.astype(F32) for part in (share_three, share_out, share_up, share_down)) + (sums,)
    if chunks > 1:
        shares = lax.psum(shares, "ctx", axis_index_groups=same_place)
    share_three, share_out, share_up, share_down, sums = shares
    (
        grad_query_b, grad_value_b, grad_output_b, grad_attn_gain, grad_attn_shift, grad_reduce_b,
        grad_ffn_gain, grad_ffn_shift,
    ) = (sums[i] for i in range(8))
    grad_expand_b = sums[8 : 8 + n_f].reshape(-1)
    return (
        layer_out,
        grad_inputs,
        share_three[0],
        grad_query_b,
        share_three[1],
        share_three[2],
        grad_value_b,
        share_out,
        grad_output_b,
        grad_attn_gain,
        grad_attn_shift,
        share_up,
        grad_expand_b,
        share_down,
        grad_reduce_b,
        grad_ffn_gain,
        grad_ffn_shift,
    )


def solution(mesh):
    acts = P("fsdp", None, "ctx", None)
    rows = P("fsdp", None)
    return jax.shard_map(
        body,
        mesh=mesh,
        in_specs=(
            acts, rows, rows, rows, P(), rows, rows, P(), rows, P(),
            P(), P(), rows, P(), rows, P(), P(), P(), acts,
        ),
        out_specs=(
            acts, acts, rows, P(), rows, rows, P(), rows, P(),
            P(), P(), rows, P(), rows, P(), P(), P(),
        ),
        check_vma=False,
    )
```
